32 devices in a mesh: rep: 2 (over y), expert: 8 (over z, x), group: 2 (over core).
Axes of the slice: x: 2, y: 2, z: 4, core: 2. Of those that a mesh axis runs over, the one named last changes fastest.
Arguments:
- tokens: bfloat16 [4096, 1024], P(('rep', 'expert', 'group')), parts along dimension 0, may hold values from -6 to 6
- w_gate: bfloat16 [16, 1024, 384], P('expert', 'group'), may hold values from -0.1875 to 0.1875
- w_up: bfloat16 [16, 1024, 384], P('expert', 'group'), may hold values from -0.1875 to 0.1875
- w_down: bfloat16 [16, 384, 1024], P('expert', 'group'), may hold values from -0.45927933 to 0.45927933
- route_ids: int32 [4096, 8], P(('rep', 'expert', 'group')), parts along dimension 0, may hold values from 0 to 15, all different within a row; in each aligned block of 128 rows (0 to 127, 128 to 255, ...) at most 80 rows name the same one
- route_scores: float32 [4096, 8], P(('rep', 'expert', 'group')), parts along dimension 0, may hold values from 0.05 to 1
- norm_gain: float32 [1024], replicated, may hold values from 0.5 to 1.5
- class_head: bfloat16 [1024, 2000], P(None, 'expert'), may hold values from -0.59765625 to 0.59765625
- targets: int32 [16, 2, 2000], P('rep', 'group', 'expert'), parts along dimension 0, may hold values 0 or 1
Outputs:
- token_grad: bfloat16 [4096, 1024], P(('rep', 'expert', 'group')), parts along dimension 0
- head_grad: float32 [2048, 2000], P('rep', 'expert'), parts along dimension 0
The draws below stay inside these ranges and needn't reach their ends.
There are 2 independent parts, one for each index of `rep`. The reference program is written for one: setup_inputs(seed, part) draws one part's arguments, and reference() takes and returns one part's arrays. A program takes and returns all parts, laid end to end along the dimension named above; an argument that names none is the same for every part. Nothing has to cross between parts.
Inputs may be any that keep to these rules, and one draw needn't show every extreme that they name: `route_ids`: each row names 8 different experts; among the 128 tokens of one sequence no expert is named by more than 80 tokens, and in some sequences one expert is named by exactly 80.
All inputs are finite; a program needn't handle non-finite values. No bound on the sum of `targets` on one device may be relied on, other than what follows from the above.
Results may differ from the reference program's by a relative error of at most 0.022.
Values may be sent and summed in bfloat16 or wider, within the bound.
No kernel may reach another device: no remote copies, remote signals or barrier semaphores. Data moves between devices by JAX's collectives and lax.ppermute only.
A program may use at most 64 MiB of HBM per device.

```python
import math
import jax
import jax.numpy as jnp
import numpy as np
from jax import lax

D = 1024
FF = 384
TOP = 8
LABELS = 2000
TOK_DEV = 128
EXPERTS = 16
SEQS = 16
TOKENS = 2048
CAP = 80
N_EXPERT = 8
N_GROUP = 2


def draw_tokens(key, part):
    shared = jnp.clip(jax.random.normal(jax.random.fold_in(key, 11), (SEQS, 1, D), jnp.float32), -3.0, 3.0)
    noise = jnp.clip(jax.random.normal(jax.random.fold_in(key, 12), (SEQS, TOK_DEV, D), jnp.float32), -3.0, 3.0)
    values = jnp.clip(1.5 * shared + noise, -6.0, 6.0)
    return values.reshape(TOKENS, D).astype(jnp.bfloat16)


def mixed_weight(key, salt, rows, cols, scale):
    common = jnp.clip(jax.random.normal(jax.random.fold_in(key, salt), (1, rows, cols), jnp.float32), -4.0, 4.0)
    own = jnp.clip(jax.random.normal(jax.random.fold_in(key, salt + 1), (EXPERTS, rows, cols), jnp.float32), -4.0, 4.0)
    limit = 6.0 * scale * rows ** (-0.5)
    values = (0.9 * common + 0.45 * own) * (scale * rows ** (-0.5))
    return jnp.clip(values, -limit, limit).astype(jnp.bfloat16)


def draw_w_gate(key, part):
    return mixed_weight(key, 101, D, FF, 1.0)


def draw_w_up(key, part):
    return mixed_weight(key, 201, D, FF, 1.0)


def draw_w_down(key, part):
    return mixed_weight(key, 301, FF, D, 1.5)


def place_ends(result, rng, least, high):
    shape = result.shape
    index_at = [jax.random.randint(jax.random.fold_in(rng, axis), (), 0, shape[axis]) for axis in range(len(shape))]
    result = result.at[tuple(index_at)].set(least)
    longest = shape.index(max(shape))
    index_at[longest] = (index_at[longest] + 1) % shape[longest]
    return result.at[tuple(index_at)].set(high)


def level_of(own_key, shape, cuts, smallest, top_value):
    def one(dim, blocks):
        steps = jax.random.uniform(jax.random.fold_in(jax.random.fold_in(own_key, 6), dim), (blocks,), jnp.float32, smallest / len(cuts), top_value / len(cuts))
        return jnp.repeat(jnp.exp(steps), shape[dim] // blocks).reshape((-1,) + (1,) * (len(shape) - dim - 1))

    gain = one(*cuts[0])
    for cut in cuts[1:]:
        gain = gain * one(*cut)
    return gain


def shared_out(own_key, own, number, rows, amount, top, most, lean):
    ranking = jax.random.permutation(own_key, amount)
    heavy_load, ordinary = shares(amount, rows * top, most, lean, True), shares(amount, rows * top, most, lean, False)
    places = jnp.arange(amount)

    def named(tallies, rotation):
        used = int((tallies > 0).sum())
        fixed = max(1, used // 4)
        passed = fixed + (places - fixed + rotation * (used - fixed)) % max(1, amount - fixed)
        return jnp.zeros((amount,), jnp.int32).at[ranking[jnp.where(places < fixed, places, passed)]].set(jnp.asarray(tallies, jnp.int32))

    tallies = jnp.where(number % 4 == 0, named(heavy_load, number // 4), named(ordinary, number - number // 4 - 1))
    mixed = jax.random.permutation(jax.random.fold_in(own, 3), amount)
    source_of, sink = mixed[0:amount // 2 * 2:2], mixed[1:amount // 2 * 2:2]
    room = jnp.minimum(tallies[source_of] - 1, most - tallies[sink]) // 2
    room = jnp.where((source_of == ranking[0]) | (sink == ranking[0]) | (tallies[sink] == 0), 0, jnp.maximum(room, 0))
    passed = jax.random.randint(jax.random.fold_in(own, 4), (amount // 2,), 0, 1 << 20) % (room + 1)
    tallies = tallies.at[source_of].add(-passed).at[sink].add(passed)
    members = jnp.searchsorted(jnp.cumsum(tallies), jnp.arange(rows * top), side="right").astype(jnp.int32)
    grid = members.reshape(top, rows).T
    grid = grid[jax.random.permutation(jax.random.fold_in(own, 1), rows)]
    rotation = jax.random.randint(jax.random.fold_in(own, 2), (rows, 1), 0, top)
    return jnp.take_along_axis(grid, (jnp.arange(top)[None, :] + rotation) % top, axis=1)


def shares(count, total, most, skew, full):
    weights = [(1 << 20) // math.isqrt(standing ** skew) + 1 for standing in range(1, count + 1)]
    largest = most if full else min(most, max(-(-total // count), total * weights[0] // sum(weights)))
    least = 1 if total - largest >= count - 1 else 0
    holding, rest = [largest] + [least] * (count - 1), total - largest - least * (count - 1)
    while rest > 0:
        free = [i for i in range(1, count) if holding[i] < largest] or [i for i in range(1, count) if holding[i] < most]
        mass, budget = sum([weights[i] for i in free]), rest
        for i in free:
            extra = min(most - holding[i], max(1, budget * weights[i] // mass), rest)
            holding[i] = holding[i] + extra
            rest = rest - extra
    return np.array(holding)


def centred(stream_key, dims, spread, bound, split=(), held_as=jnp.bfloat16):
    drawn = spread * jax.random.normal(stream_key, dims, jnp.float32)
    if split:
        drawn = drawn * level_of(stream_key, dims, split, -0.22, 0.18)
    return jnp.clip(drawn, -bound, bound).astype(held_as)


def setup_inputs(seed: int = 0, part: int = 0) -> dict:
    key_list = jax.random.split(jax.random.key(seed), 10)
    own_keys = jax.random.split(jax.random.fold_in(key_list[9], part), 10)
    tokens = draw_tokens(jax.random.fold_in(jax.random.fold_in(key_list[9], part), 71), part)
    w_gate = draw_w_gate(jax.random.fold_in(key_list[9], 71), part)
    w_up = draw_w_up(jax.random.fold_in(key_list[9], 71), part)
    w_down = draw_w_down(jax.random.fold_in(key_list[9], 71), part)
    route_ids_keys = jax.random.split(jax.random.fold_in(own_keys[4], 1), TOKENS // TOK_DEV)
    route_ids_turns = jax.random.permutation(jax.random.fold_in(own_keys[4], 3), TOKENS // TOK_DEV)
    route_ids = jax.vmap(lambda own, number: shared_out(jax.random.fold_in(own_keys[4], 2), own, number, TOK_DEV, EXPERTS, TOP, CAP, 2))(route_ids_keys, route_ids_turns).reshape((TOKENS, TOP))
    route_scores = jnp.clip(jnp.exp(math.log(1.0) - 2.9957323 * jax.random.uniform(own_keys[5], (TOKENS, TOP), jnp.float32) ** level_of(own_keys[5], (TOKENS, TOP), ((0, 16),), -0.2, 0.2)), 0.05, 1.0)
    norm_gain = jnp.clip(1.0 + 0.1 * jax.random.normal(key_list[6], (D,), jnp.float32), 0.5, 1.5)
    class_head = centred(key_list[7], (D, LABELS), 0.1, 0.59765625, ((1, 8),))
    targets = place_ends((jax.random.randint(own_keys[8], (N_EXPERT, N_GROUP, LABELS), 0, 8) < 1).astype(jnp.int32), jax.random.fold_in(own_keys[8], 1), 0, 1)
    return dict(tokens=tokens, w_gate=w_gate, w_up=w_up, w_down=w_down, route_ids=route_ids, route_scores=route_scores, norm_gain=norm_gain, class_head=class_head, targets=targets)


LOSS_SCALE = 8.0
NORM_EPS = 1e-06

def silu_parts(gate_act):
    sigmoid_gate = jax.nn.sigmoid(gate_act)
    return (gate_act * sigmoid_gate, sigmoid_gate * (1.0 + gate_act * (1.0 - sigmoid_gate)))

def reference(tokens, w_gate, w_up, w_down, route_ids, route_scores, norm_gain, class_head, targets):
    token_float = tokens.astype(jnp.float32).reshape(SEQS, TOK_DEV, D)
    expert_ids = route_ids.reshape(SEQS, TOK_DEV, TOP)
    route_weight = (route_scores / lax.optimization_barrier(jnp.sum(route_scores, axis=-1, keepdims=True))).reshape(SEQS, TOK_DEV, TOP)
    expert_iota = jnp.arange(EXPERTS, dtype=jnp.int32)
    matches = (expert_ids[..., None] == expert_iota).astype(jnp.int32)
    named_count = lax.optimization_barrier(jnp.sum(matches, axis=2))
    before = jnp.cumsum(named_count, axis=1) - named_count
    weight_by = lax.optimization_barrier(jnp.sum(matches.astype(jnp.float32) * route_weight[..., None], axis=2))
    slot_iota = jnp.arange(CAP, dtype=jnp.int32)

    def placement(expert):
        chosen = named_count[:, :, expert]
        slot_pos = before[:, :, expert]
        hit = (slot_pos[:, None, :] == slot_iota[None, :, None]) & (chosen[:, None, :] == 1)
        return hit.astype(jnp.float32)

    def expert_rows(placement_map):
        slot_rows = jnp.einsum('sct,std->scd', placement_map, token_float)
        return slot_rows.astype(jnp.bfloat16).reshape(SEQS * CAP, D)

    def forward_expert(running, expert):
        placement_map = placement(expert)
        slot_rows = expert_rows(placement_map)
        gate_act = jnp.dot(slot_rows, w_gate[expert], preferred_element_type=jnp.float32)
        up_act = jnp.dot(slot_rows, w_up[expert], preferred_element_type=jnp.float32)
        silu_val, silu_slope = silu_parts(gate_act)
        hidden = (silu_val * up_act).astype(jnp.bfloat16)
        expert_out = jnp.dot(hidden, w_down[expert], preferred_element_type=jnp.float32).astype(jnp.bfloat16)
        weighted_place = placement_map * weight_by[:, :, expert][:, None, :]
        expert_float = expert_out.astype(jnp.float32).reshape(SEQS, CAP, D)
        running = running + jnp.einsum('sct,scd->std', weighted_place, expert_float)
        return (running, None)
    moe_out, _ = lax.scan(forward_expert, jnp.zeros((SEQS, TOK_DEV, D), jnp.float32), expert_iota)
    residual = token_float + moe_out
    inv_rms = lax.rsqrt(lax.optimization_barrier(jnp.mean(residual * residual, axis=-1, keepdims=True)) + NORM_EPS)
    normed = residual * inv_rms * norm_gain
    pooled = lax.optimization_barrier(jnp.mean(normed, axis=1)).astype(jnp.bfloat16)
    logits = jnp.dot(pooled, class_head, preferred_element_type=jnp.float32)
    target_rows = targets.reshape(SEQS, LABELS).astype(jnp.float32)
    logit_grad = (LOSS_SCALE * (jax.nn.sigmoid(logits) - target_rows)).astype(jnp.bfloat16)
    head_grad = jnp.dot(pooled.T, logit_grad, preferred_element_type=jnp.float32)
    pooled_grad = jnp.dot(logit_grad, class_head.T, preferred_element_type=jnp.float32)
    scaled = norm_gain * pooled_grad[:, None, :] / TOK_DEV
    cube = inv_rms * inv_rms * inv_rms
    resid_grad = inv_rms * scaled - residual * cube * lax.optimization_barrier(jnp.mean(residual * scaled, axis=-1, keepdims=True))

    def backward_expert(running, expert):
        placement_map = placement(expert)
        slot_rows = expert_rows(placement_map)
        gate_act = jnp.dot(slot_rows, w_gate[expert], preferred_element_type=jnp.float32)
        up_act = jnp.dot(slot_rows, w_up[expert], preferred_element_type=jnp.float32)
        silu_val, silu_slope = silu_parts(gate_act)
        weighted_place = placement_map * weight_by[:, :, expert][:, None, :]
        slot_grad = jnp.einsum('sct,std->scd', weighted_place, resid_grad).astype(jnp.bfloat16).reshape(SEQS * CAP, D)
        down_back = jnp.dot(slot_grad, w_down[expert].T, preferred_element_type=jnp.float32)
        gate_grad = (down_back * up_act * silu_slope).astype(jnp.bfloat16)
        up_grad = (down_back * silu_val).astype(jnp.bfloat16)
        input_grad = jnp.dot(gate_grad, w_gate[expert].T, preferred_element_type=jnp.float32)
        input_grad = input_grad + jnp.dot(up_grad, w_up[expert].T, preferred_element_type=jnp.float32)
        input_grad = input_grad.astype(jnp.bfloat16).astype(jnp.float32).reshape(SEQS, CAP, D)
        running = running + jnp.einsum('sct,scd->std', placement_map, input_grad)
        return (running, None)
    expert_grads, _ = lax.scan(backward_expert, jnp.zeros((SEQS, TOK_DEV, D), jnp.float32), expert_iota)
    token_grad = (resid_grad + expert_grads).astype(jnp.bfloat16).reshape(TOKENS, D)
    return (token_grad, head_grad)
```

```python
import jax
import jax.numpy as jnp
from jax import lax
from jax.sharding import PartitionSpec as P

LOSS_SCALE = 8.0
NORM_EPS = 1e-06
F32 = jnp.float32
BF16 = jnp.bfloat16


def dot(left, right):
    return jnp.dot(left, right, preferred_element_type=F32)


def dot_t(left, right):
    return lax.dot_general(left, right, (((1,), (1,)), ((), ())), preferred_element_type=F32)


def joined(shard, group_count, axis):
    if group_count != 2:
        return lax.all_gather(shard, "group", axis=axis, tiled=True)
    other = lax.ppermute(shard, "group", [(0, 1), (1, 0)])
    first = lax.axis_index("group") == 0
    return jnp.concatenate(
        [jnp.where(first, shard, other), jnp.where(first, other, shard)], axis=axis
    )


def body(tokens, w_gate, w_up, w_down, route_ids, route_scores, norm_gain, class_head, targets):
    rows_here, feature_dim = tokens.shape
    top_count = route_ids.shape[1]
    expert_count = lax.axis_size("expert")
    group_count = lax.axis_size("group")
    local_experts = w_gate.shape[0]
    experts_all = expert_count * local_experts

    route_weight = route_scores / jnp.sum(route_scores, axis=-1, keepdims=True)
    expert_iota = jnp.arange(experts_all, dtype=jnp.int32)
    weight_by = jnp.zeros((rows_here, experts_all), F32)
    for choice_k in range(top_count):
        hit = route_ids[:, choice_k][:, None] == expert_iota[None, :]
        weight_by = weight_by + jnp.where(hit, route_weight[:, choice_k][:, None], 0.0)
    weight_out = weight_by.reshape(rows_here, expert_count, local_experts).transpose(1, 0, 2)
    weight_in = lax.all_to_all(weight_out, "expert", split_axis=0, concat_axis=0, tiled=True)
    weight_in = weight_in.reshape(expert_count * rows_here, local_experts)

    tokens_all = lax.all_gather(tokens, "expert", axis=0, tiled=True)
    gate_full = joined(w_gate, group_count, 1)
    up_full = joined(w_up, group_count, 1)
    down_full = joined(w_down, group_count, 1)

    gate_list = []
    up_list = []
    part = None
    for local in range(local_experts):
        gate_act = dot(tokens_all, gate_full[local])
        up_act = dot(tokens_all, up_full[local])
        gate_list.append(gate_act)
        up_list.append(up_act)
        hidden = gate_act * jax.nn.sigmoid(gate_act) * up_act * weight_in[:, local][:, None]
        term = dot(hidden.astype(BF16), down_full[local])
        part = term if part is None else part + term
    moe_out = lax.psum_scatter(part.astype(BF16), "expert", scatter_dimension=0, tiled=True)
    moe_all = lax.all_gather(moe_out, "expert", axis=0, tiled=True)

    residual = tokens_all.astype(F32) + moe_all.astype(F32)
    inv_rms = lax.rsqrt(jnp.mean(residual * residual, axis=-1, keepdims=True) + NORM_EPS)
    normed = residual * inv_rms * norm_gain
    pooled = jnp.mean(normed.reshape(expert_count, rows_here, feature_dim), axis=1).astype(BF16)
    logits = dot(pooled, class_head)
    target_rows = targets.reshape(expert_count, -1).astype(F32)
    logit_grad = (LOSS_SCALE * (jax.nn.sigmoid(logits) - target_rows)).astype(BF16)
    pooled_terms = dot_t(logit_grad, class_head)
    pooled_grad = lax.psum(pooled_terms.astype(BF16), "expert").astype(F32)

    both = jnp.concatenate([pooled, logit_grad], axis=1)
    if group_count == 2:
        both = jnp.concatenate([both, lax.ppermute(both, "group", [(0, 1), (1, 0)])], axis=0)
    else:
        both = lax.all_gather(both, "group", axis=0, tiled=True)
    head_grad = lax.dot_general(
        both[:, :feature_dim],
        both[:, feature_dim:],
        (((0,), (0,)), ((), ())),
        preferred_element_type=F32,
    )

    scaled = jnp.repeat(norm_gain * pooled_grad / rows_here, rows_here, axis=0)
    cube = inv_rms * inv_rms * inv_rms
    slope = cube * jnp.mean(residual * scaled, axis=-1, keepdims=True)
    resid_grad = inv_rms * scaled - residual * slope
    grad_rows = resid_grad.astype(BF16)

    back = None
    for local in range(local_experts):
        gate_act = gate_list[local]
        sigmoid_gate = jax.nn.sigmoid(gate_act)
        down_back = dot_t(grad_rows, down_full[local]) * weight_in[:, local][:, None]
        silu_slope = sigmoid_gate * (1.0 + gate_act * (1.0 - sigmoid_gate))
        gate_grad = (down_back * up_list[local] * silu_slope).astype(BF16)
        up_grad = (down_back * gate_act * sigmoid_gate).astype(BF16)
        term = dot_t(gate_grad, gate_full[local]) + dot_t(up_grad, up_full[local])
        back = term if back is None else back + term
    input_grad = lax.psum_scatter(back.astype(BF16), "expert", scatter_dimension=0, tiled=True)
    own = lax.dynamic_slice_in_dim(
        resid_grad, lax.axis_index("expert") * rows_here, rows_here, axis=0
    )
    token_grad = (own + input_grad.astype(F32)).astype(BF16)
    return (token_grad, head_grad)


def solution(mesh):
    in_specs = (
        P(("rep", "expert", "group"), None),
        P("expert", "group", None),
        P("expert", "group", None),
        P("expert", "group", None),
        P(("rep", "expert", "group"), None),
        P(("rep", "expert", "group"), None),
        P(),
        P(None, "expert"),
        P("rep", "group", "expert"),
    )
    out_specs = (P(("rep", "expert", "group"), None), P("rep", "expert"))
    return jax.shard_map(body, mesh=mesh, in_specs=in_specs, out_specs=out_specs, check_vma=False)
```

```python
import jax
import jax.numpy as jnp
from jax import lax
from jax.sharding import PartitionSpec as P

LOSS_SCALE = 8.0
NORM_EPS = 1e-06
F32 = jnp.float32
BF16 = jnp.bfloat16


def dot(left, right):
    return jnp.dot(left, right, preferred_element_type=F32)


def dot_t(left, right):
    return lax.dot_general(left, right, (((1,), (1,)), ((), ())), preferred_element_type=F32)


def ring_order(expert_count, group_count):
    if group_count == 2:
        return list(range(0, expert_count, 2)) + list(range(expert_count - 1, 0, -2))
    return list(range(expert_count))


def shift_perm(order, distance):
    count = len(order)
    return [(order[i], order[(i + distance) % count]) for i in range(count)]


def send(value, order, distance):
    return lax.ppermute(value, "expert", shift_perm(order, distance))


def ring_gather(block, order):
    half = len(order) // 2
    mid = block.shape[0] // 2
    blocks = {0: block}
    from_left = from_right = block
    for step in range(1, half):
        from_left = send(from_left, order, 1)
        from_right = send(from_right, order, -1)
        blocks[-step] = from_left
        blocks[step] = from_right
    top = send(from_left[:mid], order, 1)
    bottom = send(from_right[mid:], order, -1)
    blocks[half] = jnp.concatenate([top, bottom], axis=0)
    return blocks


def ring_scatter(partial, order):
    half = len(order) // 2
    last = partial(half).astype(BF16)
    mid = last.shape[0] // 2
    from_left = send(last[:mid], order, 1)
    from_right = send(last[mid:], order, -1)
    for step in range(half - 1, 0, -1):
        right = partial(step)
        left = partial(-step)
        if step == half - 1:
            right = jnp.concatenate([right[:mid] + from_left.astype(F32), right[mid:]], axis=0)
            left = jnp.concatenate([left[:mid], left[mid:] + from_right.astype(F32)], axis=0)
        else:
            right = right + from_left.astype(F32)
            left = left + from_right.astype(F32)
        from_left = send(right.astype(BF16), order, 1)
        from_right = send(left.astype(BF16), order, -1)
    return partial(0) + from_left.astype(F32) + from_right.astype(F32)


def full_weights(w_gate, w_up, w_down, group_count):
    local_experts = w_gate.shape[0]
    gate_up = [w_gate, w_up]
    if group_count != 2:
        parts = [lax.all_gather(w, "group", axis=1, tiled=True) for w in gate_up]
        wide = jnp.concatenate([w[e] for e in range(local_experts) for w in parts], axis=1)
        down = lax.all_gather(w_down, "group", axis=1, tiled=True)
        return wide, down.reshape(-1, down.shape[-1])
    swap = [(0, 1), (1, 0)]
    first = lax.axis_index("group") == 0
    others = [lax.ppermute(w, "group", swap) for w in gate_up]
    down_other = lax.ppermute(w_down, "group", swap)
    own_wide = jnp.concatenate([w[e] for e in range(local_experts) for w in gate_up], axis=1)
    other_wide = jnp.concatenate([w[e] for e in range(local_experts) for w in others], axis=1)
    wide = jnp.concatenate(
        [jnp.where(first, own_wide, other_wide), jnp.where(first, other_wide, own_wide)], axis=0
    )
    down = jnp.concatenate(
        [jnp.where(first, w_down, down_other), jnp.where(first, down_other, w_down)], axis=1
    )
    return wide, down.reshape(-1, down.shape[-1])


def body(tokens, w_gate, w_up, w_down, route_ids, route_scores, norm_gain, class_head, targets):
    rows_here, feature_dim = tokens.shape
    top_count = route_ids.shape[1]
    expert_count = lax.axis_size("expert")
    group_count = lax.axis_size("group")
    local_experts, _, hidden_dim = w_gate.shape
    experts_all = expert_count * local_experts
    order = ring_order(expert_count, group_count)
    half = expert_count // 2
    distances = list(range(-half + 1, half + 1))
    place = [order.index(e) for e in range(expert_count)]
    here = jnp.array(place, jnp.int32)[lax.axis_index("expert")]
    order_twice = jnp.array(order * 2, jnp.int32)
    device_at = {k: order_twice[here + (k % expert_count)] for k in distances}

    tokens_at = ring_gather(tokens, order)
    wide, down = full_weights(w_gate, w_up, w_down, group_count)

    route_weight = route_scores / jnp.sum(route_scores, axis=-1, keepdims=True)
    expert_iota = jnp.arange(experts_all, dtype=jnp.int32)
    weight_by = jnp.zeros((experts_all, rows_here), F32)
    for choice_k in range(top_count):
        hit = route_ids[:, choice_k][None, :] == expert_iota[:, None]
        weight_by = weight_by + jnp.where(hit, route_weight[:, choice_k][None, :], 0.0)
    weight_at = {}
    for k in distances:
        rows = lax.dynamic_slice_in_dim(
            weight_by, device_at[k] * local_experts, local_experts, axis=0
        )
        weight_at[-k if k != half else k] = rows if k == 0 else send(rows, order, k)

    gate_at, up_at, scale_at, part_at = {}, {}, {}, {}
    for k in sorted(distances, key=lambda k: (abs(k), k)):
        act = dot(tokens_at[k], wide).reshape(rows_here, local_experts, 2, hidden_dim)
        gate_act, up_act = act[:, :, 0], act[:, :, 1]
        scale = weight_at[k].T[:, :, None]
        hidden = gate_act * jax.nn.sigmoid(gate_act) * up_act * scale
        gate_at[k], up_at[k], scale_at[k] = gate_act, up_act, scale
        part_at[k] = dot(hidden.astype(BF16).reshape(rows_here, -1), down)
    moe_out = ring_scatter(lambda k: part_at[k], order).astype(BF16)
    moe_at = ring_gather(moe_out, order)

    residual_at, inv_at = {}, {}
    pooled = jnp.zeros((expert_count, feature_dim), F32)
    row_iota = jnp.arange(expert_count, dtype=jnp.int32)[:, None]
    for k in distances:
        residual = tokens_at[k].astype(F32) + moe_at[k].astype(F32)
        inv_rms = lax.rsqrt(jnp.mean(residual * residual, axis=-1, keepdims=True) + NORM_EPS)
        mean = jnp.mean(residual * inv_rms * norm_gain, axis=0, keepdims=True)
        pooled = jnp.where(row_iota == device_at[k], mean, pooled)
        residual_at[k], inv_at[k] = residual, inv_rms
    pooled = pooled.astype(BF16)
    logits = dot(pooled, class_head)
    target_rows = targets.reshape(expert_count, -1).astype(F32)
    logit_grad = (LOSS_SCALE * (jax.nn.sigmoid(logits) - target_rows)).astype(BF16)
    pooled_terms = dot_t(logit_grad, class_head).astype(BF16)
    pooled_grad = pooled_terms.astype(F32)
    for k in distances:
        if k != 0:
            pooled_grad = pooled_grad + send(pooled_terms, order, k).astype(F32)

    both = jnp.concatenate([pooled, logit_grad], axis=1)
    if group_count == 2:
        both = jnp.concatenate([both, lax.ppermute(both, "group", [(0, 1), (1, 0)])], axis=0)
    else:
        both = lax.all_gather(both, "group", axis=0, tiled=True)
    head_grad = lax.dot_general(
        both[:, :feature_dim],
        both[:, feature_dim:],
        (((0,), (0,)), ((), ())),
        preferred_element_type=F32,
    )

    scaled_all = norm_gain * pooled_grad / rows_here
    resid_grad_at = {}

    def back_part(k):
        scaled = lax.dynamic_slice_in_dim(scaled_all, device_at[k], 1, axis=0)
        residual, inv_rms = residual_at[k], inv_at[k]
        cube = inv_rms * inv_rms * inv_rms
        slope = cube * jnp.mean(residual * scaled, axis=-1, keepdims=True)
        resid_grad = inv_rms * scaled - residual * slope
        resid_grad_at[k] = resid_grad
        gate_act, up_act = gate_at[k], up_at[k]
        sigmoid_gate = jax.nn.sigmoid(gate_act)
        down_back = dot_t(resid_grad.astype(BF16), down)
        down_back = down_back.reshape(rows_here, local_experts, hidden_dim) * scale_at[k]
        silu_slope = sigmoid_gate * (1.0 + gate_act * (1.0 - sigmoid_gate))
        gate_grad = (down_back * up_act * silu_slope).astype(BF16)
        up_grad = (down_back * gate_act * sigmoid_gate).astype(BF16)
        act_grad = jnp.stack([gate_grad, up_grad], axis=2).reshape(rows_here, -1)
        return dot_t(act_grad, wide)

    input_grad = ring_scatter(back_part, order)
    token_grad = (resid_grad_at[0] + input_grad).astype(BF16)
    return (token_grad, head_grad)


def solution(mesh):
    in_specs = (
        P(("rep", "expert", "group"), None),
        P("expert", "group", None),
        P("expert", "group", None),
        P("expert", "group", None),
        P(("rep", "expert", "group"), None),
        P(("rep", "expert", "group"), None),
        P(),
        P(None, "expert"),
        P("rep", "group", "expert"),
    )
    out_specs = (P(("rep", "expert", "group"), None), P("rep", "expert"))
    return jax.shard_map(body, mesh=mesh, in_specs=in_specs, out_specs=out_specs, check_vma=False)
```

```python
import functools

import jax
import jax.numpy as jnp
from jax import lax
from jax.experimental import pallas as pl
from jax.experimental.pallas import tpu as pltpu
from jax.sharding import PartitionSpec as P

LOSS_SCALE = 8.0
NORM_EPS = 1e-06
F32 = jnp.float32
BF16 = jnp.bfloat16
LANES = 128
VMEM_LIMIT = 32 * 1024 * 1024


def dot(left, right):
    return jnp.dot(left, right, preferred_element_type=F32)


def dot_t(left, right):
    return lax.dot_general(left, right, (((1,), (1,)), ((), ())), preferred_element_type=F32)


def call(kernel, outs, *args, flops=0, scratch=(), in_any=False):
    if in_any:
        specs = [pl.BlockSpec(memory_space=pl.ANY)] * len(args)
    else:
        specs = [pl.BlockSpec(memory_space=pltpu.VMEM)] * len(args)
        args = [pltpu.with_memory_space_constraint(a, pltpu.VMEM) for a in args]
    size = sum(a.size * a.dtype.itemsize for a in args)
    return pl.pallas_call(
        kernel,
        out_shape=[pltpu.VMEM(shape, dtype) for shape, dtype in outs],
        in_specs=specs,
        out_specs=[pl.BlockSpec(memory_space=pltpu.VMEM)] * len(outs),
        scratch_shapes=list(scratch),
        compiler_params=pltpu.CompilerParams(vmem_limit_bytes=VMEM_LIMIT),
        cost_estimate=pl.CostEstimate(flops=flops, bytes_accessed=size, transcendentals=0),
    )(*args)


class Ring:
    def __init__(self, expert_count, group_count):
        self.count = expert_count
        self.half = expert_count // 2
        self.snake = group_count == 2
        if self.snake:
            self.order = list(range(0, expert_count, 2)) + list(range(expert_count - 1, 0, -2))
        else:
            self.order = list(range(expert_count))

    def send(self, value, distance):
        pairs = [
            (self.order[i], self.order[(i + distance) % self.count]) for i in range(self.count)
        ]
        return lax.ppermute(value, "expert", pairs)

    def device_at(self, distance):
        here = lax.axis_index("expert")
        count = self.count
        if self.snake:
            here = jnp.where(here % 2 == 0, here // 2, count - 1 - here // 2)
        there = lax.rem(here + distance % count, count)
        if self.snake:
            there = jnp.where(there < self.half, 2 * there, 2 * (count - 1 - there) + 1)
        return there

    def gather(self, block, use):
        mid = block.shape[0] // 2
        from_left = from_right = block
        use((0,), (block,))
        for step in range(1, self.half):
            from_left = self.send(from_left, 1)
            from_right = self.send(from_right, -1)
            use((-step, step), (from_left, from_right))
        top = self.send(from_left[:mid], 1)
        bottom = self.send(from_right[mid:], -1)
        use((self.half,), (top, bottom))

    def scatter(self, ends, partial):
        from_left = self.send(ends[0], 1)
        from_right = self.send(ends[1], -1)
        for step in range(self.half - 1, 0, -1):
            right = add_rows(partial(step), from_left, 0)
            left = add_rows(partial(-step), from_right, 1)
            from_left = self.send(right, 1)
            from_right = self.send(left, -1)
        return from_left, from_right


def add_rows(block, arrived, at_end):
    rows, cols = block.shape
    some = arrived.shape[0]

    def kernel(block_ref, arrived_ref, out_ref):
        if some == rows:
            out_ref[...] = (block_ref[...] + arrived_ref[...].astype(F32)).astype(BF16)
            return
        begin = rows - some if at_end else 0
        rest = 0 if at_end else some
        own = pl.ds(begin, some)
        other = pl.ds(rest, rows - some)
        out_ref[own, :] = (block_ref[own, :] + arrived_ref[...].astype(F32)).astype(BF16)
        out_ref[other, :] = block_ref[other, :].astype(BF16)

    return call(kernel, [((rows, cols), BF16)], block, arrived)[0]


def pack_kernel(ids_ref, scores_ref, tokens_ref, out_ref):
    rows, cols = tokens_ref.shape
    scores = scores_ref[...]
    ids = ids_ref[...]
    route_weight = scores / jnp.sum(scores, axis=-1, keepdims=True)
    lane = lax.broadcasted_iota(jnp.int32, (rows, LANES), 1)
    weight_by = jnp.zeros((rows, LANES), F32)
    for choice_k in range(scores.shape[1]):
        one = slice(choice_k, choice_k + 1)
        weight_by = weight_by + jnp.where(ids[:, one] == lane, route_weight[:, one], 0.0)
    high = weight_by.astype(BF16).astype(F32)
    low = pltpu.roll(weight_by - high, LANES // 2, 1)
    out_ref[:, :cols] = tokens_ref[...]
    out_ref[:, cols:] = (high + low).astype(BF16)


def assemble_kernel(shards, local_experts, *refs):
    gates, ups, downs = refs[:shards], refs[shards : 2 * shards], refs[2 * shards : 3 * shards]
    wide_ref, down_ref, sems = refs[3 * shards :]
    hidden_dim = gates[0].shape[2]
    copies = []

    def start(source, target):
        copies.append(pltpu.make_async_copy(source, target, sems.at[len(copies)]))
        copies[-1].start()

    for i in range(shards):
        place = 0
        if shards == 2:
            group = lax.axis_index("group")
            place = group if i == 0 else 1 - group
        depth, height = gates[i].shape[1], downs[i].shape[1]
        rows = pl.ds(pl.multiple_of(place * depth, 16), depth)
        for local in range(local_experts):
            begin = local * 2 * hidden_dim
            start(gates[i].at[local], wide_ref.at[rows, pl.ds(begin, hidden_dim)])
            start(ups[i].at[local], wide_ref.at[rows, pl.ds(begin + hidden_dim, hidden_dim)])
            top = pl.multiple_of(local * hidden_dim + place * height, 16)
            start(downs[i].at[local], down_ref.at[pl.ds(top, height), :])
    for copy in copies:
        copy.wait()


def full_weights(w_gate, w_up, w_down, group_count):
    local_experts, _, hidden_dim = w_gate.shape
    feature_dim = w_down.shape[2]
    shards = []
    for shard in (w_gate, w_up, w_down):
        if group_count == 2:
            shards += [shard, lax.ppermute(shard, "group", [(0, 1), (1, 0)])]
        else:
            shards += [lax.all_gather(shard, "group", axis=1, tiled=True)]
    count = len(shards) // 3
    return call(
        functools.partial(assemble_kernel, count, local_experts),
        [
            ((feature_dim, 2 * local_experts * hidden_dim), BF16),
            ((local_experts * hidden_dim, feature_dim), BF16),
        ],
        *shards,
        scratch=[pltpu.SemaphoreType.DMA((3 * count * local_experts,))],
        in_any=True,
    )


def body(tokens, w_gate, w_up, w_down, route_ids, route_scores, norm_gain, class_head, targets):
    rows_here, feature_dim = tokens.shape
    expert_count = lax.axis_size("expert")
    group_count = lax.axis_size("group")
    local_experts, _, hidden_dim = w_gate.shape
    pair_dim = 2 * hidden_dim
    ring = Ring(expert_count, group_count)
    block = (rows_here, feature_dim)
    mid = rows_here // 2

    packed = call(
        pack_kernel,
        [((rows_here, feature_dim + LANES), BF16)],
        route_ids,
        route_scores,
        tokens,
    )[0]
    wide, down = full_weights(w_gate, w_up, w_down, group_count)

    def rows_of(refs):
        return jnp.concatenate([ref[...] for ref in refs], axis=0) if len(refs) > 1 else refs[0][...]

    def forward_kernel(halves, count, *refs):
        token_refs, (wide_ref, down_ref), outs = refs[:count], refs[count : count + 2], refs[count + 2 :]
        x = rows_of([ref.at[:, :feature_dim] for ref in token_refs])
        weights = rows_of([ref.at[:, feature_dim:] for ref in token_refs]).astype(F32)
        lane = lax.broadcasted_iota(jnp.int32, weights.shape, 1)
        total = None
        for local in range(local_experts):
            expert = lax.axis_index("expert") * local_experts + local
            mine = (lane == expert) | (lane == expert + LANES // 2)
            scale = jnp.sum(jnp.where(mine, weights, 0.0), axis=1, keepdims=True)
            act = dot(x, wide_ref[:, pl.ds(local * pair_dim, pair_dim)])
            gate_act, up_act = act[:, :hidden_dim], act[:, hidden_dim:]
            sigmoid_gate = jax.nn.sigmoid(gate_act)
            silu = gate_act * sigmoid_gate * scale
            slope = sigmoid_gate * (1.0 + gate_act * (1.0 - sigmoid_gate)) * scale
            cols = pl.ds(local * hidden_dim, hidden_dim)
            outs[0][:, cols] = (up_act * slope).astype(BF16)
            outs[1][:, cols] = silu.astype(BF16)
            hidden = (silu * up_act).astype(BF16)
            term = dot(hidden, down_ref[cols, :])
            total = term if total is None else total + term
        rows = total.shape[0] // len(outs[2:])
        for i, out in enumerate(outs[2:]):
            out[...] = total[i * rows : (i + 1) * rows].astype(out.dtype)

    tokens_at, saved_at, part_at = {}, {}, {}
    flops = 2 * rows_here * feature_dim * hidden_dim * local_experts * 3

    def forward(distances, blocks):
        ends = distances == (ring.half,)
        rows = sum(b.shape[0] for b in blocks)
        outs = [((rows, local_experts * hidden_dim), BF16)] * 2
        outs += [((mid, feature_dim), BF16)] * 2 if ends else [(block, F32)] * len(blocks)
        result = call(
            functools.partial(forward_kernel, ends, len(blocks)),
            outs,
            *blocks,
            wide,
            down,
            flops=flops * rows // rows_here,
        )
        tokens_at[distances] = blocks
        saved_at[distances] = result[:2]
        if ends:
            part_at["ends"] = result[2:]
        else:
            part_at.update(zip(distances, result[2:]))

    ring.gather(packed, forward)
    from_left, from_right = ring.scatter(part_at["ends"], lambda k: part_at[k])

    def moe_kernel(part_ref, left_ref, right_ref, out_ref):
        arrived = left_ref[...].astype(F32) + right_ref[...].astype(F32)
        out_ref[...] = (part_ref[...] + arrived).astype(BF16)

    moe_out = call(moe_kernel, [(block, BF16)], part_at[0], from_left, from_right)[0]

    gain = norm_gain.reshape(1, feature_dim)
    moe_at, mean_at = {}, {}

    def residual_of(token_refs, moe_refs):
        token_rows = rows_of([ref.at[:, :feature_dim] for ref in token_refs]).astype(F32)
        return token_rows + rows_of(moe_refs).astype(F32)

    def inv_rms_of(residual):
        return lax.rsqrt(jnp.mean(residual * residual, axis=-1, keepdims=True) + NORM_EPS)

    def norm_kernel(distances, count, *refs):
        residual = residual_of(refs[:count], refs[count : 2 * count])
        gain_ref, so_far, out_ref = refs[2 * count :]
        normed = residual * inv_rms_of(residual) * gain_ref[...]
        pooled = so_far[...]
        row = lax.broadcasted_iota(jnp.int32, pooled.shape, 0)
        for i, k in enumerate(distances):
            part = normed[i * rows_here : (i + 1) * rows_here]
            mean = jnp.mean(part, axis=0, keepdims=True)
            pooled = jnp.where(row == ring.device_at(k), mean, pooled)
        out_ref[...] = pooled

    pooled_shape = (expert_count, feature_dim)
    mean_at["pooled"] = jnp.zeros(pooled_shape, F32)

    def norm(distances, blocks):
        moe_at[distances] = blocks
        mean_at["pooled"] = call(
            functools.partial(norm_kernel, distances, len(blocks)),
            [(pooled_shape, F32)],
            *tokens_at[distances],
            *blocks,
            gain,
            mean_at["pooled"],
        )[0]

    ring.gather(moe_out, norm)
    pooled = mean_at["pooled"].astype(BF16)
    logits = dot(pooled, class_head)
    target_rows = targets.reshape(expert_count, -1).astype(F32)
    logit_grad = (LOSS_SCALE * (jax.nn.sigmoid(logits) - target_rows)).astype(BF16)
    pooled_grad = dot_t(logit_grad, class_head)
    distance = 1
    while distance < expert_count:
        pairs = [(e, e ^ distance) for e in range(expert_count)]
        mine = pooled_grad.astype(BF16)
        other = lax.ppermute(mine, "expert", pairs)
        pooled_grad = mine.astype(F32) + other.astype(F32)
        distance *= 2

    both = jnp.concatenate([pooled, logit_grad], axis=1)
    if group_count == 2:
        both = jnp.concatenate([both, lax.ppermute(both, "group", [(0, 1), (1, 0)])], axis=0)
    else:
        both = lax.all_gather(both, "group", axis=0, tiled=True)
    head_grad = lax.dot_general(
        both[:, :feature_dim],
        both[:, feature_dim:],
        (((0,), (0,)), ((), ())),
        preferred_element_type=F32,
    )

    def backward_kernel(distances, count, *refs):
        residual = residual_of(refs[:count], refs[count : 2 * count])
        gate_save, up_save, grad_ref, gain_ref, wide_ref, down_ref = refs[2 * count : 2 * count + 6]
        outs = refs[2 * count + 6 :]
        inv_rms = inv_rms_of(residual)
        cube = inv_rms * inv_rms * inv_rms
        parts = []
        for i, k in enumerate(distances):
            rows = slice(i * rows_here, (i + 1) * rows_here)
            scaled = gain_ref[...] * grad_ref[pl.ds(ring.device_at(k), 1), :] / rows_here
            slope = cube[rows] * jnp.mean(residual[rows] * scaled, axis=-1, keepdims=True)
            parts.append(inv_rms[rows] * scaled - residual[rows] * slope)
        resid_grad = jnp.concatenate(parts, axis=0) if len(parts) > 1 else parts[0]
        down_back = dot_t(resid_grad.astype(BF16), down_ref[...])
        total = resid_grad if distances == (0,) else None
        for local in range(local_experts):
            cols = slice(local * hidden_dim, (local + 1) * hidden_dim)
            gate_grad = (down_back[:, cols] * gate_save[:, cols].astype(F32)).astype(BF16)
            up_grad = (down_back[:, cols] * up_save[:, cols].astype(F32)).astype(BF16)
            grads = jnp.concatenate([gate_grad, up_grad], axis=1)
            term = dot_t(grads, wide_ref[:, pl.ds(local * pair_dim, pair_dim)])
            total = term if total is None else total + term
        rows = total.shape[0] // len(outs)
        for i, out in enumerate(outs):
            out[...] = total[i * rows : (i + 1) * rows].astype(out.dtype)

    back_at = {}

    def backward(distances):
        blocks = tokens_at[distances]
        ends = distances == (ring.half,)
        outs = [((mid, feature_dim), BF16)] * 2 if ends else [(block, F32)] * len(blocks)
        result = call(
            functools.partial(backward_kernel, distances, len(blocks)),
            outs,
            *blocks,
            *moe_at[distances],
            *saved_at[distances],
            pooled_grad,
            gain,
            wide,
            down,
            flops=flops * len(distances),
        )
        if ends:
            back_at["ends"] = result
        else:
            back_at.update(zip(distances, result))

    for step in range(ring.half, 0, -1):
        backward((step,) if step == ring.half else (-step, step))
    backward((0,))
    from_left, from_right = ring.scatter(back_at["ends"], lambda k: back_at[k])
    token_grad = call(moe_kernel, [(block, BF16)], back_at[0], from_left, from_right)[0]
    return (token_grad, head_grad)


def solution(mesh):
    in_specs = (
        P(("rep", "expert", "group"), None),
        P("expert", "group", None),
        P("expert", "group", None),
        P("expert", "group", None),
        P(("rep", "expert", "group"), None),
        P(("rep", "expert", "group"), None),
        P(),
        P(None, "expert"),
        P("rep", "group", "expert"),
    )
    out_specs = (P(("rep", "expert", "group"), None), P("rep", "expert"))
    return jax.shard_map(body, mesh=mesh, in_specs=in_specs, out_specs=out_specs, check_vma=False)
```

```python
import functools

import jax
import jax.numpy as jnp
from jax import lax
from jax.experimental import pallas as pl
from jax.experimental.pallas import tpu as pltpu
from jax.sharding import PartitionSpec as P

LOSS_SCALE = 8.0
NORM_EPS = 1e-06
F32 = jnp.float32
BF16 = jnp.bfloat16
LANES = 128
VMEM_LIMIT = 32 * 1024 * 1024


def dot(left, right):
    return jnp.dot(left, right, preferred_element_type=F32)


def dot_t(left, right):
    return lax.dot_general(left, right, (((1,), (1,)), ((), ())), preferred_element_type=F32)


def call(kernel, outs, *args, flops=0):
    args = [pltpu.with_memory_space_constraint(a, pltpu.VMEM) for a in args]
    size = sum(a.size * a.dtype.itemsize for a in args)
    return pl.pallas_call(
        kernel,
        out_shape=[pltpu.VMEM(shape, dtype) for shape, dtype in outs],
        in_specs=[pl.BlockSpec(memory_space=pltpu.VMEM)] * len(args),
        out_specs=[pl.BlockSpec(memory_space=pltpu.VMEM)] * len(outs),
        compiler_params=pltpu.CompilerParams(vmem_limit_bytes=VMEM_LIMIT),
        cost_estimate=pl.CostEstimate(flops=flops, bytes_accessed=size, transcendentals=0),
    )(*args)


class Ring:
    def __init__(self, expert_count, group_count):
        self.count = expert_count
        self.half = expert_count // 2
        self.snake = group_count == 2
        if self.snake:
            self.order = list(range(0, expert_count, 2)) + list(range(expert_count - 1, 0, -2))
        else:
            self.order = list(range(expert_count))

    def send(self, value, distance):
        pairs = [
            (self.order[i], self.order[(i + distance) % self.count]) for i in range(self.count)
        ]
        return lax.ppermute(value, "expert", pairs)

    def device_at(self, distance):
        here = lax.axis_index("expert")
        count = self.count
        if self.snake:
            here = jnp.where(here % 2 == 0, here // 2, count - 1 - here // 2)
        there = lax.rem(here + distance % count, count)
        if self.snake:
            there = jnp.where(there < self.half, 2 * there, 2 * (count - 1 - there) + 1)
        return there

    def gather(self, top, bottom, use, first=None):
        top_left = top_right = top
        bottom_left = bottom_right = bottom
        use((0,), (top, bottom))
        for step in range(1, self.half):
            top_left = self.send(top_left, 1)
            top_right = self.send(top_right, -1)
            bottom_left = self.send(bottom_left, 1)
            bottom_right = self.send(bottom_right, -1)
            if first is not None and step == min(2, self.half - 1):
                bottom_left = first(bottom_left)
            use((-step, step), (top_left, bottom_left, top_right, bottom_right))
        use((self.half,), (self.send(top_left, 1), self.send(bottom_right, -1)))

    def scatter(self, parts):
        most = self.half - 1
        top_left = self.send(parts[self.half][0], 1)
        bottom_right = self.send(parts[self.half][1], -1)
        bottom_left = self.send(parts[most][1], 1)
        top_right = self.send(parts[-most][0], -1)
        for step in range(most, 0, -1):
            top_left = self.send(add(parts[step][0], top_left), 1)
            bottom_right = self.send(add(parts[-step][1], bottom_right), -1)
            if step > 1:
                bottom_left = self.send(add(parts[step - 1][1], bottom_left), 1)
                top_right = self.send(add(parts[1 - step][0], top_right), -1)
        return (top_left, top_right), (bottom_left, bottom_right)

    def part_types(self, distances):
        types = []
        for k in distances:
            first = BF16 if k == self.half or k == 1 - self.half else F32
            second = BF16 if k == self.half or k == self.half - 1 else F32
            types += [first, second]
        return types


def add_kernel(block_ref, arrived_ref, out_ref):
    out_ref[...] = (block_ref[...] + arrived_ref[...].astype(F32)).astype(BF16)


def add(block, arrived):
    return call(add_kernel, [(block.shape, BF16)], block, arrived)[0]


def sum_kernel(*refs):
    out_ref = refs[-1]
    rows = refs[0].shape[0]
    for i in range(len(refs) // 3):
        own, left, right = refs[3 * i : 3 * i + 3]
        arrived = left[...].astype(F32) + right[...].astype(F32)
        out_ref[pl.ds(i * rows, rows), :] = (own[...] + arrived).astype(BF16)


def pack_kernel(ids_ref, scores_ref, tokens_ref, top_ref, bottom_ref, sems):
    rows, cols = tokens_ref.shape
    mid = rows // 2
    copies = []
    for i, ref in enumerate((top_ref, bottom_ref)):
        source = tokens_ref.at[pl.ds(i * mid, mid), :]
        copies.append(pltpu.make_async_copy(source, ref.at[:, pl.ds(0, cols)], sems.at[i]))
        copies[-1].start()
    scores = scores_ref[...]
    ids = ids_ref[...]
    route_weight = scores / jnp.sum(scores, axis=0, keepdims=True)
    expert = lax.broadcasted_iota(jnp.int32, (LANES // 2, rows), 0)
    weight_by = jnp.zeros((LANES // 2, rows), F32)
    for choice_k in range(scores.shape[0]):
        one = slice(choice_k, choice_k + 1)
        weight_by = weight_by + jnp.where(ids[one] == expert, route_weight[one], 0.0)
    high = weight_by.astype(BF16).astype(F32)
    weights = jnp.concatenate([high, weight_by - high], axis=0).T.astype(BF16)
    top_ref[:, cols:] = weights[:mid]
    bottom_ref[:, cols:] = weights[mid:]
    for copy in copies:
        copy.wait()


def assemble_kernel(shards, local_experts, *refs):
    gates, ups, downs = refs[:shards], refs[shards : 2 * shards], refs[2 * shards : 3 * shards]
    wide_ref, down_ref, _, sems = refs[3 * shards + 1 :]
    hidden_dim = gates[0].shape[2]
    copies = []

    def start(source, target):
        copies.append(pltpu.make_async_copy(source, target, sems.at[len(copies)]))
        copies[-1].start()

    for i in range(shards):
        place = 0
        if shards == 2:
            group = lax.axis_index("group")
            place = group if i == 0 else 1 - group
        depth, height = gates[i].shape[1], downs[i].shape[1]
        rows = pl.ds(pl.multiple_of(place * depth, 16), depth)
        for local in range(local_experts):
            begin = local * 2 * hidden_dim
            start(gates[i].at[local], wide_ref.at[rows, pl.ds(begin, hidden_dim)])
            start(ups[i].at[local], wide_ref.at[rows, pl.ds(begin + hidden_dim, hidden_dim)])
            top = pl.multiple_of(local * hidden_dim + place * height, 16)
            start(downs[i].at[local], down_ref.at[pl.ds(top, height), :])
    for copy in copies:
        copy.wait()


def exchange_shards(w_gate, w_up, w_down, group_count):
    shards = []
    for shard in (w_gate, w_up, w_down):
        if group_count == 2:
            shards += [shard, lax.ppermute(shard, "group", [(0, 1), (1, 0)])]
        else:
            shards += [lax.all_gather(shard, "group", axis=1, tiled=True)]
    return shards


def assemble(shards, local_experts, passed):
    count = len(shards) // 3
    hidden_dim = shards[0].shape[2]
    feature_dim = shards[-1].shape[2]
    if count == 2:
        shards = [
            pltpu.with_memory_space_constraint(w, pltpu.VMEM) if i % 2 else w
            for i, w in enumerate(shards)
        ]
    return pl.pallas_call(
        functools.partial(assemble_kernel, count, local_experts),
        out_shape=[
            pltpu.VMEM((feature_dim, 2 * local_experts * hidden_dim), BF16),
            pltpu.VMEM((local_experts * hidden_dim, feature_dim), BF16),
            pltpu.VMEM(passed.shape, passed.dtype),
        ],
        in_specs=[
            pl.BlockSpec(memory_space=pltpu.VMEM if count == 2 and i % 2 else pl.ANY)
            for i in range(len(shards))
        ]
        + [pl.BlockSpec(memory_space=pltpu.VMEM)],
        out_specs=[pl.BlockSpec(memory_space=pltpu.VMEM)] * 3,
        scratch_shapes=[pltpu.SemaphoreType.DMA((3 * count * local_experts,))],
        input_output_aliases={len(shards): 2},
        compiler_params=pltpu.CompilerParams(vmem_limit_bytes=VMEM_LIMIT),
    )(*shards, pltpu.with_memory_space_constraint(passed, pltpu.VMEM))


def body(tokens, w_gate, w_up, w_down, route_ids, route_scores, norm_gain, class_head, targets):
    rows_here, feature_dim = tokens.shape
    expert_count = lax.axis_size("expert")
    group_count = lax.axis_size("group")
    local_experts, _, hidden_dim = w_gate.shape
    pair_dim = 2 * hidden_dim
    ring = Ring(expert_count, group_count)
    block = (rows_here, feature_dim)
    mid = rows_here // 2

    shards = exchange_shards(w_gate, w_up, w_down, group_count)
    top, bottom = pl.pallas_call(
        pack_kernel,
        out_shape=[pltpu.VMEM((mid, feature_dim + LANES), BF16)] * 2,
        in_specs=[pl.BlockSpec(memory_space=pltpu.VMEM)] * 2 + [pl.BlockSpec(memory_space=pl.ANY)],
        out_specs=[pl.BlockSpec(memory_space=pltpu.VMEM)] * 2,
        scratch_shapes=[pltpu.SemaphoreType.DMA((2,))],
        compiler_params=pltpu.CompilerParams(vmem_limit_bytes=VMEM_LIMIT),
    )(route_ids.T, route_scores.T, tokens)
    weights_at = []

    def assemble_now(passed):
        wide, down, passed = assemble(shards, local_experts, passed)
        weights_at.extend([wide, down])
        return passed

    def rows_of(refs):
        return jnp.concatenate([ref[...] for ref in refs], axis=0) if len(refs) > 1 else refs[0][...]

    def forward_kernel(count, *refs):
        token_refs, (wide_ref, down_ref), outs = refs[:count], refs[count : count + 2], refs[count + 2 :]
        x = rows_of([ref.at[:, :feature_dim] for ref in token_refs])
        weights = rows_of([ref.at[:, feature_dim:] for ref in token_refs]).astype(F32)
        lane = lax.broadcasted_iota(jnp.int32, weights.shape, 1)
        total = None
        for local in range(local_experts):
            expert = lax.axis_index("expert") * local_experts + local
            mine = (lane == expert) | (lane == expert + LANES // 2)
            scale = jnp.sum(jnp.where(mine, weights, 0.0), axis=1, keepdims=True)
            act = dot(x, wide_ref[:, pl.ds(local * pair_dim, pair_dim)])
            gate_act, up_act = act[:, :hidden_dim], act[:, hidden_dim:]
            sigmoid_gate = jax.nn.sigmoid(gate_act)
            silu = gate_act * sigmoid_gate * scale
            slope = sigmoid_gate * (1.0 + gate_act * (1.0 - sigmoid_gate)) * scale
            cols = pl.ds(local * hidden_dim, hidden_dim)
            outs[0][:, cols] = (up_act * slope).astype(BF16)
            outs[1][:, cols] = silu.astype(BF16)
            hidden = (silu * up_act).astype(BF16)
            term = dot(hidden, down_ref[cols, :])
            total = term if total is None else total + term
        for i, out in enumerate(outs[2:]):
            out[...] = total[i * mid : (i + 1) * mid].astype(out.dtype)

    tokens_at, saved_at, part_at = {}, {}, {}
    flops = 2 * rows_here * feature_dim * hidden_dim * local_experts * 3

    def hold(distances, blocks):
        tokens_at[distances] = blocks

    def keep_parts(parts, distances, halves):
        parts.update({k: halves[2 * i : 2 * i + 2] for i, k in enumerate(distances)})

    def part_outs(distances):
        return [((mid, feature_dim), dtype) for dtype in ring.part_types(distances)]

    def forward(distances):
        blocks = tokens_at[distances]
        rows = mid * len(blocks)
        result = call(
            functools.partial(forward_kernel, len(blocks)),
            [((rows, local_experts * hidden_dim), BF16)] * 2 + part_outs(distances),
            *blocks,
            *weights_at,
            flops=flops * rows // rows_here,
        )
        saved_at[distances] = result[:2]
        keep_parts(part_at, distances, result[2:])

    ring.gather(top, bottom, hold, assemble_now)
    wide, down = weights_at
    for distances in tokens_at:
        forward(distances)
    gain = norm_gain.reshape(1, feature_dim)
    half_shape = (mid, feature_dim)
    moe_top, moe_bottom = [
        call(sum_kernel, [(half_shape, BF16)], own, *arrived)[0]
        for own, arrived in zip(part_at[0], ring.scatter(part_at))
    ]

    moe_at, mean_at = {}, {}

    def residual_of(token_refs, moe_refs):
        token_rows = rows_of([ref.at[:, :feature_dim] for ref in token_refs]).astype(F32)
        return token_rows + rows_of(moe_refs).astype(F32)

    def inv_rms_of(residual):
        return lax.rsqrt(jnp.mean(residual * residual, axis=-1, keepdims=True) + NORM_EPS)

    def norm_kernel(distances, count, *refs):
        residual = residual_of(refs[:count], refs[count : 2 * count])
        gain_ref, so_far, out_ref = refs[2 * count :]
        normed = residual * inv_rms_of(residual) * gain_ref[...]
        pooled = so_far[...]
        row = lax.broadcasted_iota(jnp.int32, pooled.shape, 0)
        for i, k in enumerate(distances):
            part = normed[i * rows_here : (i + 1) * rows_here]
            mean = jnp.mean(part, axis=0, keepdims=True)
            pooled = jnp.where(row == ring.device_at(k), mean, pooled)
        out_ref[...] = pooled

    pooled_shape = (expert_count, feature_dim)
    mean_at["pooled"] = jnp.zeros(pooled_shape, F32)

    def norm(distances, blocks):
        moe_at[distances] = blocks
        mean_at["pooled"] = call(
            functools.partial(norm_kernel, distances, len(blocks)),
            [(pooled_shape, F32)],
            *tokens_at[distances],
            *blocks,
            gain,
            mean_at["pooled"],
        )[0]

    ring.gather(moe_top, moe_bottom, norm)
    pooled = mean_at["pooled"].astype(BF16)
    logits = dot(pooled, class_head)
    target_rows = targets.reshape(expert_count, -1).astype(F32)
    logit_grad = (LOSS_SCALE * (jax.nn.sigmoid(logits) - target_rows)).astype(BF16)
    pooled_grad = dot_t(logit_grad, class_head)
    distance = 1
    while distance < expert_count:
        pairs = [(e, e ^ distance) for e in range(expert_count)]
        mine = pooled_grad.astype(BF16)
        other = lax.ppermute(mine, "expert", pairs)
        pooled_grad = mine.astype(F32) + other.astype(F32)
        distance *= 2

    both = jnp.concatenate([pooled, logit_grad], axis=1)
    if group_count == 2:
        both = jnp.concatenate([both, lax.ppermute(both, "group", [(0, 1), (1, 0)])], axis=0)
    else:
        both = lax.all_gather(both, "group", axis=0, tiled=True)
    head_grad = lax.dot_general(
        both[:, :feature_dim],
        both[:, feature_dim:],
        (((0,), (0,)), ((), ())),
        preferred_element_type=F32,
    )

    def backward_kernel(distances, count, *refs):
        residual = residual_of(refs[:count], refs[count : 2 * count])
        gate_save, up_save, grad_ref, gain_ref, wide_ref, down_ref = refs[2 * count : 2 * count + 6]
        outs = refs[2 * count + 6 :]
        inv_rms = inv_rms_of(residual)
        cube = inv_rms * inv_rms * inv_rms
        parts = []
        for i, k in enumerate(distances):
            rows = slice(i * rows_here, (i + 1) * rows_here)
            scaled = gain_ref[...] * grad_ref[pl.ds(ring.device_at(k), 1), :] / rows_here
            slope = cube[rows] * jnp.mean(residual[rows] * scaled, axis=-1, keepdims=True)
            parts.append(inv_rms[rows] * scaled - residual[rows] * slope)
        resid_grad = jnp.concatenate(parts, axis=0) if len(parts) > 1 else parts[0]
        down_back = dot_t(resid_grad.astype(BF16), down_ref[...])
        total = resid_grad if distances == (0,) else None
        for local in range(local_experts):
            cols = slice(local * hidden_dim, (local + 1) * hidden_dim)
            gate_grad = (down_back[:, cols] * gate_save[:, cols].astype(F32)).astype(BF16)
            up_grad = (down_back[:, cols] * up_save[:, cols].astype(F32)).astype(BF16)
            grads = jnp.concatenate([gate_grad, up_grad], axis=1)
            term = dot_t(grads, wide_ref[:, pl.ds(local * pair_dim, pair_dim)])
            total = term if total is None else total + term
        for i, out in enumerate(outs):
            out[...] = total[i * mid : (i + 1) * mid].astype(out.dtype)

    back_at = {}

    def backward(distances):
        blocks = tokens_at[distances]
        result = call(
            functools.partial(backward_kernel, distances, len(blocks)),
            part_outs(distances),
            *blocks,
            *moe_at[distances],
            *saved_at[distances],
            pooled_grad,
            gain,
            wide,
            down,
            flops=flops * len(distances),
        )
        keep_parts(back_at, distances, result)

    for distances in reversed(list(tokens_at)):
        backward(distances)
    (top_left, top_right), (bottom_left, bottom_right) = ring.scatter(back_at)
    token_grad = pl.pallas_call(
        sum_kernel,
        out_shape=jax.ShapeDtypeStruct(block, BF16),
        in_specs=[pl.BlockSpec(memory_space=pltpu.VMEM)] * 6,
        out_specs=pl.BlockSpec(memory_space=pltpu.VMEM),
        compiler_params=pltpu.CompilerParams(vmem_limit_bytes=VMEM_LIMIT),
    )(back_at[0][0], top_left, top_right, back_at[0][1], bottom_left, bottom_right)
    return (token_grad, head_grad)


def solution(mesh):
    in_specs = (
        P(("rep", "expert", "group"), None),
        P("expert", "group", None),
        P("expert", "group", None),
        P("expert", "group", None),
        P(("rep", "expert", "group"), None),
        P(("rep", "expert", "group"), None),
        P(),
        P(None, "expert"),
        P("rep", "group", "expert"),
    )
    out_specs = (P(("rep", "expert", "group"), None), P("rep", "expert"))
    return jax.shard_map(body, mesh=mesh, in_specs=in_specs, out_specs=out_specs, check_vma=False)
```

```python
import functools

import jax
import jax.numpy as jnp
from jax import lax
from jax.experimental import pallas as pl
from jax.experimental.pallas import tpu as pltpu
from jax.sharding import PartitionSpec as P

LOSS_SCALE = 8.0
NORM_EPS = 1e-06
F32 = jnp.float32
BF16 = jnp.bfloat16
LANES = 128
VMEM_LIMIT = 32 * 1024 * 1024


def dot(left, right):
    return jnp.dot(left, right, preferred_element_type=F32)


def dot_t(left, right):
    return lax.dot_general(left, right, (((1,), (1,)), ((), ())), preferred_element_type=F32)


def call(kernel, outs, *args, flops=0):
    args = [pltpu.with_memory_space_constraint(a, pltpu.VMEM) for a in args]
    size = sum(a.size * a.dtype.itemsize for a in args)
    return pl.pallas_call(
        kernel,
        out_shape=[pltpu.VMEM(shape, dtype) for shape, dtype in outs],
        in_specs=[pl.BlockSpec(memory_space=pltpu.VMEM)] * len(args),
        out_specs=[pl.BlockSpec(memory_space=pltpu.VMEM)] * len(outs),
        compiler_params=pltpu.CompilerParams(vmem_limit_bytes=VMEM_LIMIT),
        cost_estimate=pl.CostEstimate(flops=flops, bytes_accessed=size, transcendentals=0),
    )(*args)


class Ring:
    def __init__(self, expert_count, group_count):
        self.count = expert_count
        self.half = expert_count // 2
        self.groups = group_count
        self.snake = group_count == 2
        if self.snake:
            self.order = list(range(0, expert_count, 2)) + list(range(expert_count - 1, 0, -2))
        else:
            self.order = list(range(expert_count))

    def send(self, value, away):
        pairs = []
        for i in range(self.count):
            for g in range(self.groups):
                there = self.order[(i + (1 if (g % 2 == 0) == away else -1)) % self.count]
                pairs.append((self.order[i] * self.groups + g, there * self.groups + g))
        return lax.ppermute(value, ("expert", "group"), pairs)

    def swap(self, value):
        return lax.ppermute(value, "group", [(g, g ^ 1) for g in range(self.groups)])

    def total(self, value):
        distance = 1
        while distance < self.count:
            other = lax.ppermute(
                value, "expert", [(e, e ^ distance) for e in range(self.count)]
            )
            value = (value.astype(F32) + other.astype(F32)).astype(BF16)
            distance *= 2
        return value

    def core(self):
        return lax.rem(lax.axis_index("group"), 2)

    def device_at(self, distance):
        here = lax.axis_index("expert")
        count = self.count
        if self.snake:
            here = jnp.where(here % 2 == 0, here // 2, count - 1 - here // 2)
        step = jnp.where(self.core() == 0, count - distance, distance)
        there = lax.rem(here + step, count)
        if self.snake:
            there = jnp.where(there < self.half, 2 * there, 2 * (count - 1 - there) + 1)
        return there

    def row_at(self, distance, other):
        core = self.core()
        return (1 - core if other else core) * self.count + self.device_at(distance)

    def gather(self, own, use, first=None):
        mid = own.shape[0] // 2
        mine, theirs = own, self.swap(own)
        use(0, (mine, theirs))
        for step in range(1, self.half):
            mine, theirs = self.send(mine, True), self.send(theirs, True)
            if first is not None and step == min(2, self.half - 1):
                theirs = first(theirs)
            use(step, (mine, theirs))

        def half_kernel(block_ref, out_ref):
            out_ref[...] = block_ref[pl.ds(pl.multiple_of(self.core() * mid, mid), mid), :]

        halves = [call(half_kernel, [((mid, own.shape[1]), own.dtype)], b)[0] for b in (mine, theirs)]
        use(self.half, tuple(self.send(h, True) for h in halves))

    def scatter(self, parts):
        mid = parts[self.half][0].shape[0]
        shape = parts[1][0].shape

        def half_kernel(block_ref, arrived_ref, out_ref):
            out_ref[...] = block_ref[...].astype(BF16)
            rows = pl.ds(pl.multiple_of(self.core() * mid, mid), mid)
            out_ref[rows, :] = (block_ref[rows, :] + arrived_ref[...].astype(F32)).astype(BF16)

        def add_kernel(block_ref, arrived_ref, out_ref):
            out_ref[...] = (block_ref[...] + arrived_ref[...].astype(F32)).astype(BF16)

        mine, theirs = parts[self.half]
        theirs, mine = self.send(theirs, False), self.send(mine, False)
        for step in range(self.half - 1, 0, -1):
            kernel = half_kernel if step == self.half - 1 else add_kernel
            theirs = self.send(call(kernel, [(shape, BF16)], parts[step][1], theirs)[0], False)
            mine = self.send(call(kernel, [(shape, BF16)], parts[step][0], mine)[0], False)
        return mine, self.swap(theirs)


def sum_kernel(own_ref, left_ref, right_ref, out_ref):
    arrived = left_ref[...].astype(F32) + right_ref[...].astype(F32)
    out_ref[...] = (own_ref[...] + arrived).astype(BF16)


def pack_kernel(ids_hbm, scores_hbm, tokens_hbm, out_ref, ids_ref, scores_ref, sems):
    rows, cols = tokens_hbm.shape
    token_copy = pltpu.make_async_copy(tokens_hbm, out_ref.at[:, pl.ds(0, cols)], sems.at[0])
    ids_copy = pltpu.make_async_copy(ids_hbm, ids_ref, sems.at[1])
    scores_copy = pltpu.make_async_copy(scores_hbm, scores_ref, sems.at[2])
    for copy in (ids_copy, scores_copy, token_copy):
        copy.start()
    ids_copy.wait()
    scores_copy.wait()
    scores = scores_ref[...]
    ids = ids_ref[...]
    route_weight = scores / jnp.sum(scores, axis=0, keepdims=True)
    expert = lax.broadcasted_iota(jnp.int32, (LANES // 2, rows), 0)
    weight_by = jnp.zeros((LANES // 2, rows), F32)
    for choice_k in range(scores.shape[0]):
        one = slice(choice_k, choice_k + 1)
        weight_by = weight_by + jnp.where(ids[one] == expert, route_weight[one], 0.0)
    high = weight_by.astype(BF16).astype(F32)
    out_ref[:, cols:] = jnp.concatenate([high, weight_by - high], axis=0).T.astype(BF16)
    token_copy.wait()


def pack(ids, scores, tokens):
    rows, cols = tokens.shape
    args = [pltpu.with_memory_space_constraint(a, pltpu.HBM) for a in (ids, scores, tokens)]
    return pl.pallas_call(
        pack_kernel,
        out_shape=pltpu.VMEM((rows, cols + LANES), BF16),
        in_specs=[pl.BlockSpec(memory_space=pl.ANY)] * 3,
        out_specs=pl.BlockSpec(memory_space=pltpu.VMEM),
        scratch_shapes=[
            pltpu.VMEM(ids.shape, ids.dtype),
            pltpu.VMEM(scores.shape, F32),
            pltpu.SemaphoreType.DMA((3,)),
        ],
        compiler_params=pltpu.CompilerParams(vmem_limit_bytes=VMEM_LIMIT),
    )(*args)


def assemble_kernel(shards, local_experts, *refs):
    gates, ups, downs = refs[:shards], refs[shards : 2 * shards], refs[2 * shards : 3 * shards]
    wide_ref, down_ref, _, sems = refs[3 * shards + 1 :]
    hidden_dim = gates[0].shape[2]
    copies = []

    def start(source, target):
        copies.append(pltpu.make_async_copy(source, target, sems.at[len(copies)]))
        copies[-1].start()

    for i in range(shards):
        place = 0
        if shards == 2:
            group = lax.axis_index("group")
            place = group if i == 0 else 1 - group
        depth, height = gates[i].shape[1], downs[i].shape[1]
        rows = pl.ds(pl.multiple_of(place * depth, 16), depth)
        for local in range(local_experts):
            begin = local * 2 * hidden_dim
            start(gates[i].at[local], wide_ref.at[rows, pl.ds(begin, hidden_dim)])
            start(ups[i].at[local], wide_ref.at[rows, pl.ds(begin + hidden_dim, hidden_dim)])
            top = pl.multiple_of(local * hidden_dim + place * height, 16)
            start(downs[i].at[local], down_ref.at[pl.ds(top, height), :])
    for copy in copies:
        copy.wait()


def exchange_shards(w_gate, w_up, w_down, group_count):
    shards = []
    for shard in (w_gate, w_up, w_down):
        if group_count == 2:
            shards += [shard, lax.ppermute(shard, "group", [(0, 1), (1, 0)])]
        else:
            shards += [lax.all_gather(shard, "group", axis=1, tiled=True)]
    return shards


def assemble(shards, local_experts, passed):
    count = len(shards) // 3
    hidden_dim = shards[0].shape[2]
    feature_dim = shards[-1].shape[2]
    if count == 2:
        shards = [
            pltpu.with_memory_space_constraint(w, pltpu.VMEM if i % 2 else pltpu.HBM)
            for i, w in enumerate(shards)
        ]
    return pl.pallas_call(
        functools.partial(assemble_kernel, count, local_experts),
        out_shape=[
            pltpu.VMEM((feature_dim, 2 * local_experts * hidden_dim), BF16),
            pltpu.VMEM((local_experts * hidden_dim, feature_dim), BF16),
            pltpu.VMEM(passed.shape, passed.dtype),
        ],
        in_specs=[
            pl.BlockSpec(memory_space=pltpu.VMEM if count == 2 and i % 2 else pl.ANY)
            for i in range(len(shards))
        ]
        + [pl.BlockSpec(memory_space=pltpu.VMEM)],
        out_specs=[pl.BlockSpec(memory_space=pltpu.VMEM)] * 3,
        scratch_shapes=[pltpu.SemaphoreType.DMA((3 * count * local_experts,))],
        input_output_aliases={len(shards): 2},
        compiler_params=pltpu.CompilerParams(vmem_limit_bytes=VMEM_LIMIT),
    )(*shards, pltpu.with_memory_space_constraint(passed, pltpu.VMEM))


def body(tokens, w_gate, w_up, w_down, route_ids, route_scores, norm_gain, class_head, targets):
    rows_here, feature_dim = tokens.shape
    expert_count = lax.axis_size("expert")
    group_count = lax.axis_size("group")
    local_experts, _, hidden_dim = w_gate.shape
    pair_dim = 2 * hidden_dim
    ring = Ring(expert_count, group_count)
    block = (rows_here, feature_dim)
    mid = rows_here // 2

    packed = pack(route_ids.T, route_scores.T, tokens)
    shards = exchange_shards(w_gate, w_up, w_down, group_count)
    weights_at = []

    def assemble_now(passed):
        wide, down, passed = assemble(shards, local_experts, passed)
        weights_at.extend([wide, down])
        return passed

    def rows_of(refs):
        return jnp.concatenate([ref[...] for ref in refs], axis=0) if len(refs) > 1 else refs[0][...]

    def forward_kernel(count, *refs):
        token_refs, (wide_ref, down_ref), outs = refs[:count], refs[count : count + 2], refs[count + 2 :]
        x = rows_of([ref.at[:, :feature_dim] for ref in token_refs])
        weights = rows_of([ref.at[:, feature_dim:] for ref in token_refs]).astype(F32)
        lane = lax.broadcasted_iota(jnp.int32, weights.shape, 1)
        total = None
        for local in range(local_experts):
            expert = lax.axis_index("expert") * local_experts + local
            mine = (lane == expert) | (lane == expert + LANES // 2)
            scale = jnp.sum(jnp.where(mine, weights, 0.0), axis=1, keepdims=True)
            act = dot(x, wide_ref[:, pl.ds(local * pair_dim, pair_dim)])
            gate_act, up_act = act[:, :hidden_dim], act[:, hidden_dim:]
            sigmoid_gate = jax.nn.sigmoid(gate_act)
            silu = gate_act * sigmoid_gate * scale
            slope = sigmoid_gate * (1.0 + gate_act * (1.0 - sigmoid_gate)) * scale
            cols = pl.ds(local * hidden_dim, hidden_dim)
            outs[0][:, cols] = (up_act * slope).astype(BF16)
            outs[1][:, cols] = silu.astype(BF16)
            hidden = (silu * up_act).astype(BF16)
            term = dot(hidden, down_ref[cols, :])
            total = term if total is None else total + term
        rows = total.shape[0] // len(outs[2:])
        for i, out in enumerate(outs[2:]):
            out[...] = total[i * rows : (i + 1) * rows].astype(out.dtype)

    tokens_at, part_at, saved_at = {}, {}, {}
    flops = 2 * feature_dim * hidden_dim * local_experts * 3

    def mine_at(blocks_at, k):
        return blocks_at[k][:1] if k == 0 else blocks_at[k]

    def part_outs(k):
        rows, dtype = (mid, BF16) if k == ring.half else (rows_here, F32)
        return [((rows, feature_dim), dtype)] * (1 if k == 0 else 2)

    def forward(k):
        blocks = mine_at(tokens_at, k)
        rows = sum(b.shape[0] for b in blocks)
        result = call(
            functools.partial(forward_kernel, len(blocks)),
            [((rows, local_experts * hidden_dim), BF16)] * 2 + part_outs(k),
            *blocks,
            *weights_at,
            flops=flops * rows,
        )
        saved_at[k] = result[:2]
        part_at[k] = result[2:]

    ring.gather(packed, tokens_at.__setitem__, assemble_now)
    wide, down = weights_at
    for k in tokens_at:
        forward(k)
    gain = norm_gain.reshape(1, feature_dim)
    moe_out = call(sum_kernel, [(block, BF16)], part_at[0][0], *ring.scatter(part_at))[0]
    moe_at = {}
    ring.gather(moe_out, moe_at.__setitem__)

    def residual_of(token_refs, moe_refs):
        token_rows = rows_of([ref.at[:, :feature_dim] for ref in token_refs]).astype(F32)
        return token_rows + rows_of(moe_refs).astype(F32)

    def inv_rms_of(residual):
        return lax.rsqrt(jnp.mean(residual * residual, axis=-1, keepdims=True) + NORM_EPS)

    def norm_kernel(*refs):
        residual = residual_of(refs[:2], refs[2:4])
        gain_ref, out_ref = refs[4:]
        normed = residual * inv_rms_of(residual) * gain_ref[...]
        row = lax.broadcasted_iota(jnp.int32, out_ref.shape, 0)
        pooled = jnp.zeros(out_ref.shape, F32)
        for i in range(2):
            part = normed[i * rows_here : (i + 1) * rows_here]
            mean = jnp.mean(part, axis=0, keepdims=True)
            pooled = jnp.where(row == ring.row_at(0, i), mean, pooled)
        out_ref[...] = pooled.astype(BF16)

    pooled_shape = (2 * expert_count, feature_dim)
    pooled = call(norm_kernel, [(pooled_shape, BF16)], *tokens_at[0], *moe_at[0], gain)[0]
    pooled = ring.total(pooled)
    target_own = targets.reshape(expert_count, -1).astype(F32)

    def target_kernel(own_ref, other_ref, out_ref):
        for i, ref in enumerate((own_ref, other_ref)):
            begin = (1 - ring.core() if i else ring.core()) * expert_count
            out_ref[pl.ds(pl.multiple_of(begin, expert_count), expert_count), :] = ref[...]

    target_shape = (2 * expert_count, target_own.shape[1])
    target_rows = call(target_kernel, [(target_shape, F32)], target_own, ring.swap(target_own))[0]
    logits = dot(pooled, class_head)
    logit_grad = (LOSS_SCALE * (jax.nn.sigmoid(logits) - target_rows)).astype(BF16)
    pooled_grad = ring.total(dot_t(logit_grad, class_head).astype(BF16)).astype(F32)

    if group_count > 2:
        both = jnp.concatenate([pooled, logit_grad], axis=1)
        both = lax.all_gather(both, "group", axis=0)[::2].reshape(-1, both.shape[1])
        pooled, logit_grad = both[:, :feature_dim], both[:, feature_dim:]
    head_grad = lax.dot_general(
        pooled, logit_grad, (((0,), (0,)), ((), ())), preferred_element_type=F32
    )

    def backward_kernel(k, count, *refs):
        residual = residual_of(refs[:count], refs[count : 2 * count])
        gate_save, up_save, grad_ref, gain_ref, wide_ref, down_ref = refs[2 * count : 2 * count + 6]
        outs = refs[2 * count + 6 :]
        inv_rms = inv_rms_of(residual)
        cube = inv_rms * inv_rms * inv_rms
        parts = []
        for i in range(count):
            some = residual.shape[0] // count
            rows = slice(i * some, (i + 1) * some)
            scaled = gain_ref[...] * grad_ref[pl.ds(ring.row_at(k, i), 1), :] / rows_here
            slope = cube[rows] * jnp.mean(residual[rows] * scaled, axis=-1, keepdims=True)
            parts.append(inv_rms[rows] * scaled - residual[rows] * slope)
        resid_grad = jnp.concatenate(parts, axis=0) if count > 1 else parts[0]
        down_back = dot_t(resid_grad.astype(BF16), down_ref[...])
        total = resid_grad if k == 0 else None
        for local in range(local_experts):
            cols = slice(local * hidden_dim, (local + 1) * hidden_dim)
            gate_grad = (down_back[:, cols] * gate_save[:, cols].astype(F32)).astype(BF16)
            up_grad = (down_back[:, cols] * up_save[:, cols].astype(F32)).astype(BF16)
            grads = jnp.concatenate([gate_grad, up_grad], axis=1)
            term = dot_t(grads, wide_ref[:, pl.ds(local * pair_dim, pair_dim)])
            total = term if total is None else total + term
        rows = total.shape[0] // len(outs)
        for i, out in enumerate(outs):
            out[...] = total[i * rows : (i + 1) * rows].astype(out.dtype)

    back_at = {}
    for k in reversed(list(tokens_at)):
        blocks = mine_at(tokens_at, k)
        back_at[k] = call(
            functools.partial(backward_kernel, k, len(blocks)),
            part_outs(k),
            *blocks,
            *mine_at(moe_at, k),
            *saved_at[k],
            pooled_grad,
            gain,
            wide,
            down,
            flops=flops * sum(b.shape[0] for b in blocks),
        )
    token_grad = pl.pallas_call(
        sum_kernel,
        out_shape=jax.ShapeDtypeStruct(block, BF16),
        in_specs=[pl.BlockSpec(memory_space=pltpu.VMEM)] * 3,
        out_specs=pl.BlockSpec(memory_space=pltpu.VMEM),
        compiler_params=pltpu.CompilerParams(vmem_limit_bytes=VMEM_LIMIT),
    )(back_at[0][0], *ring.scatter(back_at))
    return (token_grad, head_grad)


def solution(mesh):
    in_specs = (
        P(("rep", "expert", "group"), None),
        P("expert", "group", None),
        P("expert", "group", None),
        P("expert", "group", None),
        P(("rep", "expert", "group"), None),
        P(("rep", "expert", "group"), None),
        P(),
        P(None, "expert"),
        P("rep", "group", "expert"),
    )
    out_specs = (P(("rep", "expert", "group"), None), P("rep", "expert"))
    return jax.shard_map(body, mesh=mesh, in_specs=in_specs, out_specs=out_specs, check_vma=False)
```

```python
import functools

import jax
import jax.numpy as jnp
from jax import lax
from jax.experimental import pallas as pl
from jax.experimental.pallas import tpu as pltpu
from jax.sharding import PartitionSpec as P

LOSS_SCALE = 8.0
NORM_EPS = 1e-06
F32 = jnp.float32
BF16 = jnp.bfloat16
LANES = 128
VMEM_LIMIT = 32 * 1024 * 1024


def dot(left, right):
    return jnp.dot(left, right, preferred_element_type=F32)


def dot_t(left, right):
    return lax.dot_general(left, right, (((1,), (1,)), ((), ())), preferred_element_type=F32)


def call(kernel, outs, *args, flops=0):
    args = [pltpu.with_memory_space_constraint(a, pltpu.VMEM) for a in args]
    size = sum(a.size * a.dtype.itemsize for a in args)
    return pl.pallas_call(
        kernel,
        out_shape=[pltpu.VMEM(shape, dtype) for shape, dtype in outs],
        in_specs=[pl.BlockSpec(memory_space=pltpu.VMEM)] * len(args),
        out_specs=[pl.BlockSpec(memory_space=pltpu.VMEM)] * len(outs),
        compiler_params=pltpu.CompilerParams(vmem_limit_bytes=VMEM_LIMIT),
        cost_estimate=pl.CostEstimate(flops=flops, bytes_accessed=size, transcendentals=0),
    )(*args)


class Ring:
    def __init__(self, expert_count, group_count):
        self.count = expert_count
        self.half = expert_count // 2
        self.groups = group_count
        self.snake = group_count == 2
        if self.snake:
            self.order = list(range(0, expert_count, 2)) + list(range(expert_count - 1, 0, -2))
        else:
            self.order = list(range(expert_count))

    def send(self, value, away, cross=False):
        pairs = []
        for i in range(self.count):
            for g in range(self.groups):
                right = (g % 2 == 0) == (away != (cross and away))
                there = self.order[(i + (1 if right else -1)) % self.count]
                pairs.append((self.order[i] * self.groups + g, there * self.groups + (g ^ cross)))
        return lax.ppermute(value, ("expert", "group"), pairs)

    def swap(self, value):
        return lax.ppermute(value, "group", [(g, g ^ 1) for g in range(self.groups)])

    def total(self, value, guards):
        def round_kernel(mine_ref, other_ref, guard_ref, out_ref):
            out_ref[...] = (mine_ref[...].astype(F32) + other_ref[...].astype(F32)).astype(BF16)

        distance = 1
        while distance < self.count:
            other = lax.ppermute(
                value, "expert", [(e, e ^ distance) for e in range(self.count)]
            )
            guard = guards.pop(0) if len(guards) > 1 else guards[0]
            value = call(round_kernel, [(value.shape, BF16)], value, other, guard)[0]
            distance *= 2
        return value

    def core(self):
        return lax.rem(lax.axis_index("group"), 2)

    def device_at(self, distance):
        here = lax.axis_index("expert")
        count = self.count
        if self.snake:
            here = jnp.where(here % 2 == 0, here // 2, count - 1 - here // 2)
        step = jnp.where(self.core() == 0, count - distance, distance)
        there = lax.rem(here + step, count)
        if self.snake:
            there = jnp.where(there < self.half, 2 * there, 2 * (count - 1 - there) + 1)
        return there

    def gather(self, own, use):
        mid = own.shape[0] // 2
        use(0, (own,))
        mine, theirs = self.send(own, True), self.send(own, True, True)
        use(1, (mine, theirs))
        for step in range(2, self.half):
            mine, theirs = self.send(mine, True), self.send(theirs, True)
            use(step, (mine, theirs))

        def half_kernel(block_ref, out_ref):
            out_ref[...] = block_ref[pl.ds(pl.multiple_of(self.core() * mid, mid), mid), :]

        halves = [call(half_kernel, [((mid, own.shape[1]), own.dtype)], b)[0] for b in (mine, theirs)]
        use(self.half, tuple(self.send(h, True) for h in halves))

    def scatter(self, parts):
        rows, cols = parts[1][0].shape
        mid = rows // 2

        def half_kernel(place, block_ref, arrived_ref, out_ref):
            out_ref[...] = block_ref[...].astype(BF16)
            some = pl.ds(pl.multiple_of(self.core() * mid, mid), mid)
            arrived = arrived_ref[pl.ds(place * mid, mid), :].astype(F32)
            out_ref[some, :] = (block_ref[some, :] + arrived).astype(BF16)

        def add_kernel(place, block_ref, arrived_ref, out_ref):
            out_ref[...] = (block_ref[...] + arrived_ref[...].astype(F32)).astype(BF16)

        sums = [self.send(parts[self.half][0], False)] * 2
        for step in range(self.half - 1, 0, -1):
            kernel = half_kernel if step == self.half - 1 else add_kernel
            for i in range(2):
                added = call(
                    functools.partial(kernel, i), [((rows, cols), BF16)], parts[step][i], sums[i]
                )[0]
                sums[i] = self.send(added, False, step == 1 and i == 1)
        return sums


def sum_kernel(own_ref, left_ref, right_ref, out_ref):
    arrived = left_ref[...].astype(F32) + right_ref[...].astype(F32)
    out_ref[...] = (own_ref[...] + arrived).astype(BF16)


def pack_kernel(ids_hbm, scores_hbm, tokens_hbm, out_ref, ids_ref, scores_ref, sems):
    rows, cols = tokens_hbm.shape
    token_copy = pltpu.make_async_copy(tokens_hbm, out_ref.at[:, pl.ds(0, cols)], sems.at[0])
    ids_copy = pltpu.make_async_copy(ids_hbm, ids_ref, sems.at[1])
    scores_copy = pltpu.make_async_copy(scores_hbm, scores_ref, sems.at[2])
    for copy in (ids_copy, scores_copy, token_copy):
        copy.start()
    ids_copy.wait()
    scores_copy.wait()
    scores = scores_ref[...]
    ids = ids_ref[...]
    route_weight = scores / jnp.sum(scores, axis=0, keepdims=True)
    expert = lax.broadcasted_iota(jnp.int32, (LANES // 2, rows), 0)
    weight_by = jnp.zeros((LANES // 2, rows), F32)
    for choice_k in range(scores.shape[0]):
        one = slice(choice_k, choice_k + 1)
        weight_by = weight_by + jnp.where(ids[one] == expert, route_weight[one], 0.0)
    high = weight_by.astype(BF16).astype(F32)
    out_ref[:, cols:] = jnp.concatenate([high, weight_by - high], axis=0).T.astype(BF16)
    token_copy.wait()


def pack(ids, scores, tokens):
    rows, cols = tokens.shape
    args = [pltpu.with_memory_space_constraint(a, pltpu.HBM) for a in (ids, scores, tokens)]
    return pl.pallas_call(
        pack_kernel,
        out_shape=pltpu.VMEM((rows, cols + LANES), BF16),
        in_specs=[pl.BlockSpec(memory_space=pl.ANY)] * 3,
        out_specs=pl.BlockSpec(memory_space=pltpu.VMEM),
        scratch_shapes=[
            pltpu.VMEM(ids.shape, ids.dtype),
            pltpu.VMEM(scores.shape, F32),
            pltpu.SemaphoreType.DMA((3,)),
        ],
        compiler_params=pltpu.CompilerParams(vmem_limit_bytes=VMEM_LIMIT),
    )(*args)


def assemble_kernel(shards, local_experts, *refs):
    gates, ups, downs = refs[:shards], refs[shards : 2 * shards], refs[2 * shards : 3 * shards]
    wide_ref, down_ref, sems = refs[3 * shards :]
    hidden_dim = gates[0].shape[2]
    copies = []

    def start(source, target):
        copies.append(pltpu.make_async_copy(source, target, sems.at[len(copies)]))
        copies[-1].start()

    for i in range(shards):
        place = 0
        if shards == 2:
            group = lax.axis_index("group")
            place = group if i == 0 else 1 - group
        depth, height = gates[i].shape[1], downs[i].shape[1]
        rows = pl.ds(pl.multiple_of(place * depth, 16), depth)
        for local in range(local_experts):
            begin = local * 2 * hidden_dim
            start(gates[i].at[local], wide_ref.at[rows, pl.ds(begin, hidden_dim)])
            start(ups[i].at[local], wide_ref.at[rows, pl.ds(begin + hidden_dim, hidden_dim)])
            top = pl.multiple_of(local * hidden_dim + place * height, 16)
            start(downs[i].at[local], down_ref.at[pl.ds(top, height), :])
    for copy in copies:
        copy.wait()


def exchange_shards(w_gate, w_up, w_down, group_count):
    shards = []
    for shard in (w_gate, w_up, w_down):
        if group_count == 2:
            shards += [shard, lax.ppermute(shard, "group", [(0, 1), (1, 0)])]
        else:
            shards += [lax.all_gather(shard, "group", axis=1, tiled=True)]
    return shards


def assemble(shards, local_experts):
    count = len(shards) // 3
    hidden_dim = shards[0].shape[2]
    feature_dim = shards[-1].shape[2]
    if count == 2:
        shards = [
            pltpu.with_memory_space_constraint(w, pltpu.VMEM if i % 2 else pltpu.HBM)
            for i, w in enumerate(shards)
        ]
    return pl.pallas_call(
        functools.partial(assemble_kernel, count, local_experts),
        out_shape=[
            pltpu.VMEM((feature_dim, 2 * local_experts * hidden_dim), BF16),
            pltpu.VMEM((local_experts * hidden_dim, feature_dim), BF16),
        ],
        in_specs=[
            pl.BlockSpec(memory_space=pltpu.VMEM if count == 2 and i % 2 else pl.ANY)
            for i in range(len(shards))
        ],
        out_specs=[pl.BlockSpec(memory_space=pltpu.VMEM)] * 2,
        scratch_shapes=[pltpu.SemaphoreType.DMA((3 * count * local_experts,))],
        compiler_params=pltpu.CompilerParams(vmem_limit_bytes=VMEM_LIMIT),
    )(*shards)


def transpose_kernel(from_ref, to_ref):
    strip = 2 * LANES

    @pl.loop(0, to_ref.shape[0] // strip)
    def _(i):
        some = pl.ds(pl.multiple_of(i * strip, strip), strip)
        to_ref[some, :] = from_ref[:, some].T


def transposed(weights):
    rows, cols = weights.shape
    return call(transpose_kernel, [((cols, rows), BF16)], weights)[0]


def body(tokens, w_gate, w_up, w_down, route_ids, route_scores, norm_gain, class_head, targets):
    rows_here, feature_dim = tokens.shape
    expert_count = lax.axis_size("expert")
    group_count = lax.axis_size("group")
    local_experts, _, hidden_dim = w_gate.shape
    pair_dim = 2 * hidden_dim
    ring = Ring(expert_count, group_count)
    block = (rows_here, feature_dim)
    mid = rows_here // 2

    packed = pack(route_ids.T, route_scores.T, tokens)
    shards = exchange_shards(w_gate, w_up, w_down, group_count)
    wide, down = assemble(shards, local_experts)

    def rows_of(refs):
        return jnp.concatenate([ref[...] for ref in refs], axis=0) if len(refs) > 1 else refs[0][...]

    def forward_kernel(count, *refs):
        token_refs, (wide_ref, down_ref), outs = refs[:count], refs[count : count + 2], refs[count + 2 :]
        x = rows_of([ref.at[:, :feature_dim] for ref in token_refs])
        weights = rows_of([ref.at[:, feature_dim:] for ref in token_refs]).astype(F32)
        lane = lax.broadcasted_iota(jnp.int32, weights.shape, 1)
        total = None
        for local in range(local_experts):
            expert = lax.axis_index("expert") * local_experts + local
            mine = (lane == expert) | (lane == expert + LANES // 2)
            scale = jnp.sum(jnp.where(mine, weights, 0.0), axis=1, keepdims=True)
            act = dot(x, wide_ref[:, pl.ds(local * pair_dim, pair_dim)])
            gate_act, up_act = act[:, :hidden_dim], act[:, hidden_dim:]
            sigmoid_gate = jax.nn.sigmoid(gate_act)
            silu = gate_act * sigmoid_gate * scale
            slope = sigmoid_gate * (1.0 + gate_act * (1.0 - sigmoid_gate)) * scale
            cols = pl.ds(local * hidden_dim, hidden_dim)
            outs[0][:, cols] = (up_act * slope).astype(BF16)
            outs[1][:, cols] = silu.astype(BF16)
            hidden = (silu * up_act).astype(BF16)
            term = dot(hidden, down_ref[cols, :])
            total = term if total is None else total + term
        rows = total.shape[0] // len(outs[2:])
        for i, out in enumerate(outs[2:]):
            out[...] = total[i * rows : (i + 1) * rows].astype(out.dtype)

    tokens_at, part_at, saved_at, moe_at = {}, {}, {}, {}
    flops = 2 * feature_dim * hidden_dim * local_experts * 3

    def part_outs(k):
        if k == ring.half:
            return [(block, BF16)]
        return [(block, F32)] * (1 if k == 0 else 2)

    def forward(k):
        blocks = tokens_at[k]
        rows = sum(b.shape[0] for b in blocks)
        result = call(
            functools.partial(forward_kernel, len(blocks)),
            [((rows, local_experts * hidden_dim), BF16)] * 2 + part_outs(k),
            *blocks,
            wide,
            down,
            flops=flops * rows,
        )
        saved_at[k] = result[:2]
        part_at[k] = result[2:]

    ring.gather(packed, tokens_at.__setitem__)
    for k in tokens_at:
        forward(k)
    gain = norm_gain.reshape(1, feature_dim)
    moe_out = call(sum_kernel, [(block, BF16)], part_at[0][0], *ring.scatter(part_at))[0]
    ring.gather(moe_out, moe_at.__setitem__)

    def residual_of(token_refs, moe_refs):
        token_rows = rows_of([ref.at[:, :feature_dim] for ref in token_refs]).astype(F32)
        return token_rows + rows_of(moe_refs).astype(F32)

    def inv_rms_of(residual):
        return lax.rsqrt(jnp.mean(residual * residual, axis=-1, keepdims=True) + NORM_EPS)

    def norm_kernel(tokens_ref, moe_ref, gain_ref, out_ref):
        residual = residual_of([tokens_ref], [moe_ref])
        normed = residual * inv_rms_of(residual) * gain_ref[...]
        row = lax.broadcasted_iota(jnp.int32, out_ref.shape, 0)
        mean = jnp.mean(normed, axis=0, keepdims=True)
        out_ref[...] = jnp.where(row == ring.device_at(0), mean, 0.0).astype(BF16)

    guards = [b for k in range(1, ring.half) for b in moe_at[k]]
    pooled_shape = (expert_count, feature_dim)
    pooled = call(norm_kernel, [(pooled_shape, BF16)], packed, moe_out, gain)[0]
    pooled = ring.total(pooled, guards)
    logits = dot(pooled, class_head)
    target_rows = targets.reshape(expert_count, -1).astype(F32)
    logit_grad = (LOSS_SCALE * (jax.nn.sigmoid(logits) - target_rows)).astype(BF16)
    pooled_grad = ring.total(dot_t(logit_grad, class_head).astype(BF16), guards)
    pooled_grads = [pooled_grad, ring.swap(pooled_grad)]

    both = jnp.concatenate([pooled, logit_grad], axis=1)
    if group_count == 2:
        both = jnp.concatenate([both, ring.swap(both)], axis=0)
    else:
        both = lax.all_gather(both, "group", axis=0, tiled=True)
    head_grad = lax.dot_general(
        both[:, :feature_dim],
        both[:, feature_dim:],
        (((0,), (0,)), ((), ())),
        preferred_element_type=F32,
    )

    def backward_kernel(k, count, *refs):
        residual = residual_of(refs[:count], refs[count : 2 * count])
        gate_save, up_save, *grad_refs = refs[2 * count : 2 * count + 4]
        gain_ref, wide_ref, down_ref, *outs = refs[2 * count + 4 :]
        inv_rms = inv_rms_of(residual)
        cube = inv_rms * inv_rms * inv_rms
        parts = []
        for i in range(count):
            some = residual.shape[0] // count
            rows = slice(i * some, (i + 1) * some)
            scaled = gain_ref[...] * grad_refs[i][pl.ds(ring.device_at(k), 1), :] / rows_here
            slope = cube[rows] * jnp.mean(residual[rows] * scaled, axis=-1, keepdims=True)
            parts.append(inv_rms[rows] * scaled - residual[rows] * slope)
        resid_grad = jnp.concatenate(parts, axis=0) if count > 1 else parts[0]
        down_back = dot(resid_grad.astype(BF16), down_ref[...])
        total = resid_grad if k == 0 else None
        for local in range(local_experts):
            cols = slice(local * hidden_dim, (local + 1) * hidden_dim)
            gate_grad = (down_back[:, cols] * gate_save[:, cols].astype(F32)).astype(BF16)
            up_grad = (down_back[:, cols] * up_save[:, cols].astype(F32)).astype(BF16)
            grads = jnp.concatenate([gate_grad, up_grad], axis=1)
            term = dot(grads, wide_ref[pl.ds(local * pair_dim, pair_dim), :])
            total = term if total is None else total + term
        rows = total.shape[0] // len(outs)
        for i, out in enumerate(outs):
            out[...] = total[i * rows : (i + 1) * rows].astype(out.dtype)

    wide_t, down_t = transposed(wide), transposed(down)
    pooled_grads = [g.astype(F32) for g in pooled_grads]
    back_at = {}
    for k in reversed(list(tokens_at)):
        blocks = tokens_at[k]
        back_at[k] = call(
            functools.partial(backward_kernel, k, len(blocks)),
            part_outs(k),
            *blocks,
            *moe_at[k],
            *saved_at[k],
            *pooled_grads,
            gain,
            wide_t,
            down_t,
            flops=flops * sum(b.shape[0] for b in blocks),
        )
    token_grad = pl.pallas_call(
        sum_kernel,
        out_shape=jax.ShapeDtypeStruct(block, BF16),
        in_specs=[pl.BlockSpec(memory_space=pltpu.VMEM)] * 3,
        out_specs=pl.BlockSpec(memory_space=pltpu.VMEM),
        compiler_params=pltpu.CompilerParams(vmem_limit_bytes=VMEM_LIMIT),
    )(back_at[0][0], *ring.scatter(back_at))
    return (token_grad, head_grad)


def solution(mesh):
    in_specs = (
        P(("rep", "expert", "group"), None),
        P("expert", "group", None),
        P("expert", "group", None),
        P("expert", "group", None),
        P(("rep", "expert", "group"), None),
        P(("rep", "expert", "group"), None),
        P(),
        P(None, "expert"),
        P("rep", "group", "expert"),
    )
    out_specs = (P(("rep", "expert", "group"), None), P("rep", "expert"))
    return jax.shard_map(body, mesh=mesh, in_specs=in_specs, out_specs=out_specs, check_vma=False)
```

```python
import functools

import jax
import jax.numpy as jnp
from jax import lax
from jax.experimental import pallas as pl
from jax.experimental.pallas import tpu as pltpu
from jax.sharding import PartitionSpec as P

LOSS_SCALE = 8.0
NORM_EPS = 1e-06
F32 = jnp.float32
BF16 = jnp.bfloat16
LANES = 128
VMEM_LIMIT = 32 * 1024 * 1024


def dot(left, right):
    return jnp.dot(left, right, preferred_element_type=F32)


def dot_t(left, right):
    return lax.dot_general(left, right, (((1,), (1,)), ((), ())), preferred_element_type=F32)


def call(kernel, outs, *args, flops=0):
    args = [pltpu.with_memory_space_constraint(a, pltpu.VMEM) for a in args]
    size = sum(a.size * a.dtype.itemsize for a in args)
    return pl.pallas_call(
        kernel,
        out_shape=[pltpu.VMEM(shape, dtype) for shape, dtype in outs],
        in_specs=[pl.BlockSpec(memory_space=pltpu.VMEM)] * len(args),
        out_specs=[pl.BlockSpec(memory_space=pltpu.VMEM)] * len(outs),
        compiler_params=pltpu.CompilerParams(vmem_limit_bytes=VMEM_LIMIT),
        cost_estimate=pl.CostEstimate(flops=flops, bytes_accessed=size, transcendentals=0),
    )(*args)


class Ring:
    def __init__(self, expert_count, group_count):
        self.count = expert_count
        self.half = expert_count // 2
        self.snake = group_count == 2
        if self.snake:
            self.order = list(range(0, expert_count, 2)) + list(range(expert_count - 1, 0, -2))
        else:
            self.order = list(range(expert_count))

    def send(self, value, distance):
        pairs = [
            (self.order[i], self.order[(i + distance) % self.count]) for i in range(self.count)
        ]
        return lax.ppermute(value, "expert", pairs)

    def device_at(self, distance):
        here = lax.axis_index("expert")
        count = self.count
        if self.snake:
            here = jnp.where(here % 2 == 0, here // 2, count - 1 - here // 2)
        there = lax.rem(here + distance % count, count)
        if self.snake:
            there = jnp.where(there < self.half, 2 * there, 2 * (count - 1 - there) + 1)
        return there

    def gather(self, top, bottom, use):
        top_left = top_right = top
        bottom_left = bottom_right = bottom
        use((0,), (top, bottom))
        for step in range(1, self.half):
            top_left = self.send(top_left, 1)
            top_right = self.send(top_right, -1)
            bottom_left = self.send(bottom_left, 1)
            bottom_right = self.send(bottom_right, -1)
            use((-step, step), (top_left, bottom_left, top_right, bottom_right))
        use((self.half,), (self.send(top_left, 1), self.send(bottom_right, -1)))

    def scatter(self, parts):
        most = self.half - 1
        top_left = self.send(parts[self.half][0], 1)
        bottom_right = self.send(parts[self.half][1], -1)
        bottom_left = self.send(parts[most][1], 1)
        top_right = self.send(parts[-most][0], -1)
        for step in range(most, 0, -1):
            top_left = self.send(add(parts[step][0], top_left), 1)
            bottom_right = self.send(add(parts[-step][1], bottom_right), -1)
            if step > 1:
                bottom_left = self.send(add(parts[step - 1][1], bottom_left), 1)
                top_right = self.send(add(parts[1 - step][0], top_right), -1)
        return (top_left, top_right), (bottom_left, bottom_right)

    def part_types(self, distances):
        types = []
        for k in distances:
            first = BF16 if k == self.half or k == 1 - self.half else F32
            second = BF16 if k == self.half or k == self.half - 1 else F32
            types += [first, second]
        return types


def add_kernel(block_ref, arrived_ref, out_ref):
    out_ref[...] = (block_ref[...] + arrived_ref[...].astype(F32)).astype(BF16)


def add(block, arrived):
    return call(add_kernel, [(block.shape, BF16)], block, arrived)[0]


def sum_kernel(*refs):
    out_ref = refs[-1]
    rows = refs[0].shape[0]
    for i in range(len(refs) // 3):
        own, left, right = refs[3 * i : 3 * i + 3]
        arrived = left[...].astype(F32) + right[...].astype(F32)
        out_ref[pl.ds(i * rows, rows), :] = (own[...] + arrived).astype(BF16)


def pack_kernel(ids_hbm, scores_hbm, tokens_hbm, top_ref, bottom_ref, ids_ref, scores_ref, sems):
    rows, cols = tokens_hbm.shape
    mid = rows // 2
    quarter = LANES // 4
    copies = [
        pltpu.make_async_copy(ids_hbm, ids_ref, sems.at[0]),
        pltpu.make_async_copy(scores_hbm, scores_ref, sems.at[1]),
        pltpu.make_async_copy(
            tokens_hbm.at[pl.ds(0, mid), :], top_ref.at[:, pl.ds(0, cols)], sems.at[2]
        ),
        pltpu.make_async_copy(tokens_hbm.at[pl.ds(mid, mid), :], bottom_ref, sems.at[3]),
    ]
    for copy in copies:
        copy.start()
    copies[0].wait()
    copies[1].wait()
    scores = scores_ref[...]
    ids = ids_ref[...]
    route_weight = scores / jnp.sum(scores, axis=0, keepdims=True)
    expert = lax.broadcasted_iota(jnp.int32, (quarter, rows), 0)
    weight_by = jnp.zeros((quarter, rows), F32)
    for choice_k in range(scores.shape[0]):
        one = slice(choice_k, choice_k + 1)
        weight_by = weight_by + jnp.where(ids[one] == expert, route_weight[one], 0.0)
    high = weight_by.astype(BF16).astype(F32)
    weights = jnp.concatenate([high, weight_by - high] * 2, axis=0).T
    lane = lax.broadcasted_iota(jnp.int32, (mid, LANES), 1)
    both = jnp.where(lane < 2 * quarter, weights[:mid], weights[mid:])
    top_ref[:, cols:] = both.astype(BF16)
    copies[2].wait()
    copies[3].wait()


def pack(ids, scores, tokens):
    rows, cols = tokens.shape
    args = [pltpu.with_memory_space_constraint(a, pltpu.HBM) for a in (ids, scores, tokens)]
    return pl.pallas_call(
        pack_kernel,
        out_shape=[
            pltpu.VMEM((rows // 2, cols + LANES), BF16),
            pltpu.VMEM((rows // 2, cols), BF16),
        ],
        in_specs=[pl.BlockSpec(memory_space=pl.ANY)] * 3,
        out_specs=[pl.BlockSpec(memory_space=pltpu.VMEM)] * 2,
        scratch_shapes=[
            pltpu.VMEM(ids.shape, ids.dtype),
            pltpu.VMEM(scores.shape, F32),
            pltpu.SemaphoreType.DMA((4,)),
        ],
        compiler_params=pltpu.CompilerParams(vmem_limit_bytes=VMEM_LIMIT),
    )(*args)


class Copies:
    def __init__(self, sems):
        self.sems, self.started = sems, []

    def start(self, source, target):
        copy = pltpu.make_async_copy(source, target, self.sems.at[len(self.started)])
        copy.start()
        self.started.append(copy)

    def wait(self):
        for copy in self.started:
            copy.wait()


def strips(gate_shape, down_shape):
    local_experts, depth, hidden_dim = gate_shape
    _, height, feature_dim = down_shape
    row, places = 0, []
    for _ in range(local_experts):
        pair = [(row, depth), (row + depth, depth)]
        row += 2 * depth
        downs = []
        for begin in range(0, feature_dim, hidden_dim):
            downs.append((row, height, begin, min(hidden_dim, feature_dim - begin)))
            row += height
        places.append((pair, downs))
    return row, places


def pack_weights(w_gate, w_up, w_down):
    rows, places = strips(w_gate.shape, w_down.shape)
    hidden_dim = w_gate.shape[2]

    def kernel(gate_hbm, up_hbm, down_hbm, out_ref, sems):
        copies = Copies(sems)
        for local, (pair, downs) in enumerate(places):
            for source, (row, some) in zip((gate_hbm, up_hbm), pair):
                copies.start(source.at[local], out_ref.at[pl.ds(row, some), :])
            for row, some, begin, cols in downs:
                source = down_hbm.at[local, :, pl.ds(begin, cols)]
                copies.start(source, out_ref.at[pl.ds(row, some), pl.ds(0, cols)])
                if cols < hidden_dim:
                    out_ref[pl.ds(row, some), pl.ds(cols, hidden_dim - cols)] = jnp.zeros(
                        (some, hidden_dim - cols), BF16
                    )
        copies.wait()

    shards = [pltpu.with_memory_space_constraint(w, pltpu.HBM) for w in (w_gate, w_up, w_down)]
    count = sum(len(pair) + len(downs) for pair, downs in places)
    return pl.pallas_call(
        kernel,
        out_shape=pltpu.VMEM((rows, hidden_dim), BF16),
        in_specs=[pl.BlockSpec(memory_space=pl.ANY)] * 3,
        out_specs=pl.BlockSpec(memory_space=pltpu.VMEM),
        scratch_shapes=[pltpu.SemaphoreType.DMA((count,))],
        compiler_params=pltpu.CompilerParams(vmem_limit_bytes=VMEM_LIMIT),
    )(*shards)


def full_weights(w_gate, w_up, w_down, group_count):
    local_experts, _, hidden_dim = w_gate.shape
    feature_dim = w_down.shape[2]
    paired = group_count == 2
    if paired:
        other = lax.ppermute(pack_weights(w_gate, w_up, w_down), "group", [(0, 1), (1, 0)])
        other = pltpu.with_memory_space_constraint(other, pltpu.VMEM)
        shards = [w_gate, w_up, w_down]
    else:
        shards = [lax.all_gather(w, "group", axis=1, tiled=True) for w in (w_gate, w_up, w_down)]
    _, places = strips(shards[0].shape, shards[2].shape)
    depth, height = shards[0].shape[1], shards[2].shape[1]

    def kernel(*refs):
        gate_hbm, up_hbm, down_hbm, *rest = refs
        wide_ref, down_ref, sems = rest[-3:]
        copies = Copies(sems)
        mine = lax.axis_index("group") if paired else 0

        def wide_at(place, local, is_up):
            rows = pl.ds(pl.multiple_of(place * depth, 16), depth)
            return wide_ref.at[rows, pl.ds((2 * local + is_up) * hidden_dim, hidden_dim)]

        def down_at(place, local, begin, cols):
            top = pl.multiple_of(local * hidden_dim + place * height, 16)
            return down_ref.at[pl.ds(top, height), pl.ds(begin, cols)]

        for local in range(local_experts):
            for is_up, source in enumerate((gate_hbm, up_hbm)):
                copies.start(source.at[local], wide_at(mine, local, is_up))
            copies.start(down_hbm.at[local], down_at(mine, local, 0, feature_dim))
        if paired:
            for local, (pair, downs) in enumerate(places):
                for is_up, (row, some) in enumerate(pair):
                    copies.start(rest[0].at[pl.ds(row, some), :], wide_at(1 - mine, local, is_up))
                for row, some, begin, cols in downs:
                    source = rest[0].at[pl.ds(row, some), pl.ds(0, cols)]
                    copies.start(source, down_at(1 - mine, local, begin, cols))
        copies.wait()

    shards = [pltpu.with_memory_space_constraint(w, pltpu.HBM) for w in shards]
    count = 3 * local_experts
    specs = [pl.BlockSpec(memory_space=pl.ANY)] * 3
    if paired:
        count += sum(len(pair) + len(downs) for pair, downs in places)
        specs.append(pl.BlockSpec(memory_space=pltpu.VMEM))
        shards.append(other)
    return pl.pallas_call(
        kernel,
        out_shape=[
            pltpu.VMEM((feature_dim, 2 * local_experts * hidden_dim), BF16),
            pltpu.VMEM((local_experts * hidden_dim, feature_dim), BF16),
        ],
        in_specs=specs,
        out_specs=[pl.BlockSpec(memory_space=pltpu.VMEM)] * 2,
        scratch_shapes=[pltpu.SemaphoreType.DMA((count,))],
        compiler_params=pltpu.CompilerParams(vmem_limit_bytes=VMEM_LIMIT),
    )(*shards)


def transpose_kernel(from_ref, to_ref):
    strip = 2 * LANES

    @pl.loop(0, to_ref.shape[0] // strip)
    def _(i):
        some = pl.ds(pl.multiple_of(i * strip, strip), strip)
        to_ref[some, :] = from_ref[:, some].T


def transposed(weights):
    rows, cols = weights.shape
    return call(transpose_kernel, [((cols, rows), BF16)], weights)[0]


def body(tokens, w_gate, w_up, w_down, route_ids, route_scores, norm_gain, class_head, targets):
    rows_here, feature_dim = tokens.shape
    expert_count = lax.axis_size("expert")
    group_count = lax.axis_size("group")
    local_experts, _, hidden_dim = w_gate.shape
    pair_dim = 2 * hidden_dim
    ring = Ring(expert_count, group_count)
    block = (rows_here, feature_dim)
    mid = rows_here // 2

    top, bottom = pack(route_ids.T, route_scores.T, tokens)
    wide, down = full_weights(w_gate, w_up, w_down, group_count)

    def rows_of(refs):
        return jnp.concatenate([ref[...] for ref in refs], axis=0) if len(refs) > 1 else refs[0][...]

    def forward_kernel(count, *refs):
        token_refs, (wide_ref, down_ref), outs = refs[:count], refs[count : count + 2], refs[count + 2 :]
        x = rows_of([ref.at[:, :feature_dim] for ref in token_refs])
        weights = jnp.concatenate([ref[:, feature_dim:] for ref in token_refs[::2]], axis=0).astype(F32)
        lane = lax.broadcasted_iota(jnp.int32, weights.shape, 1)
        quarter = LANES // 4
        total = None
        for local in range(local_experts):
            expert = lax.axis_index("expert") * local_experts + local
            scales = []
            for begin in (expert, expert + 2 * quarter):
                here = (lane == begin) | (lane == begin + quarter)
                scales.append(jnp.sum(jnp.where(here, weights, 0.0), axis=1, keepdims=True))
            pieces = [s[i : i + mid] for i in range(0, weights.shape[0], mid) for s in scales]
            scale = jnp.concatenate(pieces, axis=0)
            act = dot(x, wide_ref[:, pl.ds(local * pair_dim, pair_dim)])
            gate_act, up_act = act[:, :hidden_dim], act[:, hidden_dim:]
            sigmoid_gate = jax.nn.sigmoid(gate_act)
            silu = gate_act * sigmoid_gate * scale
            slope = sigmoid_gate * (1.0 + gate_act * (1.0 - sigmoid_gate)) * scale
            cols = pl.ds(local * hidden_dim, hidden_dim)
            outs[0][:, cols] = (up_act * slope).astype(BF16)
            outs[1][:, cols] = silu.astype(BF16)
            hidden = (silu * up_act).astype(BF16)
            term = dot(hidden, down_ref[cols, :])
            total = term if total is None else total + term
        for i, out in enumerate(outs[2:]):
            out[...] = total[i * mid : (i + 1) * mid].astype(out.dtype)

    tokens_at, saved_at, part_at = {}, {}, {}
    flops = 2 * rows_here * feature_dim * hidden_dim * local_experts * 3

    def hold(distances, blocks):
        tokens_at[distances] = blocks

    def keep_parts(parts, distances, halves):
        parts.update({k: halves[2 * i : 2 * i + 2] for i, k in enumerate(distances)})

    def part_outs(distances):
        return [((mid, feature_dim), dtype) for dtype in ring.part_types(distances)]

    def forward(distances):
        blocks = tokens_at[distances]
        rows = mid * len(blocks)
        result = call(
            functools.partial(forward_kernel, len(blocks)),
            [((rows, local_experts * hidden_dim), BF16)] * 2 + part_outs(distances),
            *blocks,
            wide,
            down,
            flops=flops * rows // rows_here,
        )
        saved_at[distances] = result[:2]
        keep_parts(part_at, distances, result[2:])

    ring.gather(top, bottom, hold)
    for distances in tokens_at:
        forward(distances)
    gain = norm_gain.reshape(1, feature_dim)
    half_shape = (mid, feature_dim)
    moe_top, moe_bottom = [
        call(sum_kernel, [(half_shape, BF16)], own, *arrived)[0]
        for own, arrived in zip(part_at[0], ring.scatter(part_at))
    ]

    moe_at, mean_at = {}, {}

    def residual_of(token_refs, moe_refs):
        token_rows = rows_of([ref.at[:, :feature_dim] for ref in token_refs]).astype(F32)
        return token_rows + rows_of(moe_refs).astype(F32)

    def inv_rms_of(residual):
        return lax.rsqrt(jnp.mean(residual * residual, axis=-1, keepdims=True) + NORM_EPS)

    def norm_kernel(distances, count, *refs):
        residual = residual_of(refs[:count], refs[count : 2 * count])
        gain_ref, so_far, out_ref = refs[2 * count :]
        normed = residual * inv_rms_of(residual) * gain_ref[...]
        pooled = so_far[...]
        row = lax.broadcasted_iota(jnp.int32, pooled.shape, 0)
        for i, k in enumerate(distances):
            part = normed[i * rows_here : (i + 1) * rows_here]
            mean = jnp.mean(part, axis=0, keepdims=True)
            pooled = jnp.where(row == ring.device_at(k), mean, pooled)
        out_ref[...] = pooled

    pooled_shape = (expert_count, feature_dim)
    mean_at["pooled"] = jnp.zeros(pooled_shape, F32)

    def norm(distances, blocks):
        moe_at[distances] = blocks
        mean_at["pooled"] = call(
            functools.partial(norm_kernel, distances, len(blocks)),
            [(pooled_shape, F32)],
            *tokens_at[distances],
            *blocks,
            gain,
            mean_at["pooled"],
        )[0]

    ring.gather(moe_top, moe_bottom, norm)
    pooled = mean_at["pooled"].astype(BF16)
    logits = dot(pooled, class_head)
    target_rows = targets.reshape(expert_count, -1).astype(F32)
    logit_grad = (LOSS_SCALE * (jax.nn.sigmoid(logits) - target_rows)).astype(BF16)
    pooled_grad = dot_t(logit_grad, class_head)
    distance = 1
    while distance < expert_count:
        pairs = [(e, e ^ distance) for e in range(expert_count)]
        mine = pooled_grad.astype(BF16)
        other = lax.ppermute(mine, "expert", pairs)
        pooled_grad = mine.astype(F32) + other.astype(F32)
        distance *= 2

    both = jnp.concatenate([pooled, logit_grad], axis=1)
    if group_count == 2:
        both = jnp.concatenate([both, lax.ppermute(both, "group", [(0, 1), (1, 0)])], axis=0)
    else:
        both = lax.all_gather(both, "group", axis=0, tiled=True)
    head_grad = lax.dot_general(
        both[:, :feature_dim],
        both[:, feature_dim:],
        (((0,), (0,)), ((), ())),
        preferred_element_type=F32,
    )

    def backward_kernel(distances, count, *refs):
        residual = residual_of(refs[:count], refs[count : 2 * count])
        gate_save, up_save, grad_ref, gain_ref, wide_ref, down_ref = refs[2 * count : 2 * count + 6]
        outs = refs[2 * count + 6 :]
        inv_rms = inv_rms_of(residual)
        cube = inv_rms * inv_rms * inv_rms
        parts = []
        for i, k in enumerate(distances):
            rows = slice(i * rows_here, (i + 1) * rows_here)
            scaled = gain_ref[...] * grad_ref[pl.ds(ring.device_at(k), 1), :] / rows_here
            slope = cube[rows] * jnp.mean(residual[rows] * scaled, axis=-1, keepdims=True)
            parts.append(inv_rms[rows] * scaled - residual[rows] * slope)
        resid_grad = jnp.concatenate(parts, axis=0) if len(parts) > 1 else parts[0]
        down_back = dot(resid_grad.astype(BF16), down_ref[...])
        total = resid_grad if distances == (0,) else None
        for local in range(local_experts):
            cols = slice(local * hidden_dim, (local + 1) * hidden_dim)
            gate_grad = (down_back[:, cols] * gate_save[:, cols].astype(F32)).astype(BF16)
            up_grad = (down_back[:, cols] * up_save[:, cols].astype(F32)).astype(BF16)
            grads = jnp.concatenate([gate_grad, up_grad], axis=1)
            term = dot(grads, wide_ref[pl.ds(local * pair_dim, pair_dim), :])
            total = term if total is None else total + term
        for i, out in enumerate(outs):
            out[...] = total[i * mid : (i + 1) * mid].astype(out.dtype)

    wide_t, down_t = transposed(wide), transposed(down)
    back_at = {}

    def backward(distances):
        blocks = tokens_at[distances]
        result = call(
            functools.partial(backward_kernel, distances, len(blocks)),
            part_outs(distances),
            *blocks,
            *moe_at[distances],
            *saved_at[distances],
            pooled_grad,
            gain,
            wide_t,
            down_t,
            flops=flops * len(distances),
        )
        keep_parts(back_at, distances, result)

    for distances in reversed(list(tokens_at)):
        backward(distances)
    (top_left, top_right), (bottom_left, bottom_right) = ring.scatter(back_at)
    token_grad = pl.pallas_call(
        sum_kernel,
        out_shape=jax.ShapeDtypeStruct(block, BF16),
        in_specs=[pl.BlockSpec(memory_space=pltpu.VMEM)] * 6,
        out_specs=pl.BlockSpec(memory_space=pltpu.VMEM),
        compiler_params=pltpu.CompilerParams(vmem_limit_bytes=VMEM_LIMIT),
    )(back_at[0][0], top_left, top_right, back_at[0][1], bottom_left, bottom_right)
    return (token_grad, head_grad)


def solution(mesh):
    in_specs = (
        P(("rep", "expert", "group"), None),
        P("expert", "group", None),
        P("expert", "group", None),
        P("expert", "group", None),
        P(("rep", "expert", "group"), None),
        P(("rep", "expert", "group"), None),
        P(),
        P(None, "expert"),
        P("rep", "group", "expert"),
    )
    out_specs = (P(("rep", "expert", "group"), None), P("rep", "expert"))
    return jax.shard_map(body, mesh=mesh, in_specs=in_specs, out_specs=out_specs, check_vma=False)
```

```python
import functools

import jax
import jax.numpy as jnp
from jax import lax
from jax.experimental import pallas as pl
from jax.experimental.pallas import tpu as pltpu
from jax.sharding import PartitionSpec as P

LOSS_SCALE = 8.0
NORM_EPS = 1e-06
F32 = jnp.float32
BF16 = jnp.bfloat16
LANES = 128
VMEM_LIMIT = 32 * 1024 * 1024


def dot(left, right):
    return jnp.dot(left, right, preferred_element_type=F32)


def dot_t(left, right):
    return lax.dot_general(left, right, (((1,), (1,)), ((), ())), preferred_element_type=F32)


def call(kernel, outs, *args, flops=0):
    args = [pltpu.with_memory_space_constraint(a, pltpu.VMEM) for a in args]
    size = sum(a.size * a.dtype.itemsize for a in args)
    return pl.pallas_call(
        kernel,
        out_shape=[pltpu.VMEM(shape, dtype) for shape, dtype in outs],
        in_specs=[pl.BlockSpec(memory_space=pltpu.VMEM)] * len(args),
        out_specs=[pl.BlockSpec(memory_space=pltpu.VMEM)] * len(outs),
        compiler_params=pltpu.CompilerParams(vmem_limit_bytes=VMEM_LIMIT),
        cost_estimate=pl.CostEstimate(flops=flops, bytes_accessed=size, transcendentals=0),
    )(*args)


class Ring:
    def __init__(self, expert_count, group_count):
        self.count = expert_count
        self.half = expert_count // 2
        self.snake = group_count == 2
        if self.snake:
            self.order = list(range(0, expert_count, 2)) + list(range(expert_count - 1, 0, -2))
        else:
            self.order = list(range(expert_count))

    def send(self, value, distance):
        pairs = [
            (self.order[i], self.order[(i + distance) % self.count]) for i in range(self.count)
        ]
        return lax.ppermute(value, "expert", pairs)

    def device_at(self, distance):
        here = lax.axis_index("expert")
        count = self.count
        if self.snake:
            here = jnp.where(here % 2 == 0, here // 2, count - 1 - here // 2)
        there = lax.rem(here + distance % count, count)
        if self.snake:
            there = jnp.where(there < self.half, 2 * there, 2 * (count - 1 - there) + 1)
        return there

    def gather(self, top, bottom, use):
        top_left = top_right = top
        bottom_left = bottom_right = bottom
        use((0,), (top, bottom))
        for step in range(1, self.half):
            top_left = self.send(top_left, 1)
            top_right = self.send(top_right, -1)
            bottom_left = self.send(bottom_left, 1)
            bottom_right = self.send(bottom_right, -1)
            use((-step, step), (top_left, bottom_left, top_right, bottom_right))
        use((self.half,), (self.send(top_left, 1), self.send(bottom_right, -1)))

    def scatter(self, parts):
        most = self.half - 1
        top_left = self.send(parts[self.half][0], 1)
        bottom_right = self.send(parts[self.half][1], -1)
        bottom_left = self.send(parts[most][1], 1)
        top_right = self.send(parts[-most][0], -1)
        for step in range(most, 0, -1):
            top_left = self.send(add(parts[step][0], top_left), 1)
            bottom_right = self.send(add(parts[-step][1], bottom_right), -1)
            if step > 1:
                bottom_left = self.send(add(parts[step - 1][1], bottom_left), 1)
                top_right = self.send(add(parts[1 - step][0], top_right), -1)
        return (top_left, top_right), (bottom_left, bottom_right)

    def part_types(self, distances):
        types = []
        for k in distances:
            first = BF16 if k == self.half or k == 1 - self.half else F32
            second = BF16 if k == self.half or k == self.half - 1 else F32
            types += [first, second]
        return types


def add_kernel(block_ref, arrived_ref, out_ref):
    out_ref[...] = (block_ref[...] + arrived_ref[...].astype(F32)).astype(BF16)


def add(block, arrived):
    return call(add_kernel, [(block.shape, BF16)], block, arrived)[0]


def sum_kernel(*refs):
    out_ref = refs[-1]
    rows = refs[0].shape[0]
    for i in range(len(refs) // 3):
        own, left, right = refs[3 * i : 3 * i + 3]
        arrived = left[...].astype(F32) + right[...].astype(F32)
        out_ref[pl.ds(i * rows, rows), :] = (own[...] + arrived).astype(BF16)


class Copies:
    def __init__(self, sems):
        self.sems, self.started = sems, []

    def start(self, source, target):
        copy = pltpu.make_async_copy(source, target, self.sems.at[len(self.started)])
        copy.start()
        self.started.append(copy)

    def wait(self):
        for copy in self.started:
            copy.wait()


def strips(gate_shape, down_shape):
    local_experts, depth, hidden_dim = gate_shape
    _, height, feature_dim = down_shape
    row, places = 0, []
    for _ in range(local_experts):
        pair = [(row, depth), (row + depth, depth)]
        row += 2 * depth
        downs = []
        for begin in range(0, feature_dim, hidden_dim):
            downs.append((row, height, begin, min(hidden_dim, feature_dim - begin)))
            row += height
        places.append((pair, downs))
    return row, places


def pack(ids, scores, tokens, shards):
    rows, cols = tokens.shape
    mid = rows // 2
    quarter = LANES // 4
    inputs = [ids, scores, tokens, *shards]
    packed_shape, places, count = None, [], 0
    if shards:
        hidden_dim = shards[0].shape[2]
        packed_rows, places = strips(shards[0].shape, shards[2].shape)
        packed_shape = (packed_rows, hidden_dim)
        count = sum(len(pair) + len(downs) for pair, downs in places)

    def kernel(*refs):
        ids_hbm, scores_hbm, tokens_hbm, *shards_hbm = refs[: len(inputs)]
        top_ref, bottom_ref, *packed_refs = refs[len(inputs) : -3]
        ids_ref, scores_ref, sems = refs[-3:]
        copies = Copies(sems)
        copies.start(ids_hbm, ids_ref)
        copies.start(scores_hbm, scores_ref)
        copies.start(tokens_hbm.at[pl.ds(0, mid), :], top_ref.at[:, pl.ds(0, cols)])
        copies.start(tokens_hbm.at[pl.ds(mid, mid), :], bottom_ref)
        for local, (pair, downs) in enumerate(places):
            out_ref = packed_refs[0]
            for source, (row, some) in zip(shards_hbm, pair):
                copies.start(source.at[local], out_ref.at[pl.ds(row, some), :])
            for row, some, begin, width in downs:
                source = shards_hbm[2].at[local, :, pl.ds(begin, width)]
                copies.start(source, out_ref.at[pl.ds(row, some), pl.ds(0, width)])
                if width < hidden_dim:
                    rest = hidden_dim - width
                    out_ref[pl.ds(row, some), pl.ds(width, rest)] = jnp.zeros((some, rest), BF16)
        copies.started[0].wait()
        copies.started[1].wait()
        scores = scores_ref[...]
        ids = ids_ref[...]
        route_weight = scores / jnp.sum(scores, axis=0, keepdims=True)
        expert = lax.broadcasted_iota(jnp.int32, (quarter, rows), 0)
        weight_by = jnp.zeros((quarter, rows), F32)
        for choice_k in range(scores.shape[0]):
            one = slice(choice_k, choice_k + 1)
            weight_by = weight_by + jnp.where(ids[one] == expert, route_weight[one], 0.0)
        high = weight_by.astype(BF16).astype(F32)
        weights = jnp.concatenate([high, weight_by - high] * 2, axis=0).T
        lane = lax.broadcasted_iota(jnp.int32, (mid, LANES), 1)
        both = jnp.where(lane < 2 * quarter, weights[:mid], weights[mid:])
        top_ref[:, cols:] = both.astype(BF16)
        for copy in copies.started[2:]:
            copy.wait()

    outs = [pltpu.VMEM((mid, cols + LANES), BF16), pltpu.VMEM((mid, cols), BF16)]
    if shards:
        outs.append(pltpu.VMEM(packed_shape, BF16))
    return pl.pallas_call(
        kernel,
        out_shape=outs,
        in_specs=[pl.BlockSpec(memory_space=pl.ANY)] * len(inputs),
        out_specs=[pl.BlockSpec(memory_space=pltpu.VMEM)] * len(outs),
        scratch_shapes=[
            pltpu.VMEM(ids.shape, ids.dtype),
            pltpu.VMEM(scores.shape, F32),
            pltpu.SemaphoreType.DMA((4 + count,)),
        ],
        compiler_params=pltpu.CompilerParams(vmem_limit_bytes=VMEM_LIMIT),
    )(*[pltpu.with_memory_space_constraint(a, pltpu.HBM) for a in inputs])


def full_weights(shards, packed):
    local_experts, _, hidden_dim = shards[0].shape
    feature_dim = shards[2].shape[2]
    paired = packed is not None
    _, places = strips(shards[0].shape, shards[2].shape)
    depth, height = shards[0].shape[1], shards[2].shape[1]

    def kernel(*refs):
        gate_hbm, up_hbm, down_hbm, *rest = refs
        wide_ref, down_ref, sems = rest[-3:]
        copies = Copies(sems)
        mine = lax.axis_index("group") if paired else 0

        def wide_at(place, local, is_up):
            rows = pl.ds(pl.multiple_of(place * depth, 16), depth)
            return wide_ref.at[rows, pl.ds((2 * local + is_up) * hidden_dim, hidden_dim)]

        def down_at(place, local, begin, cols):
            top = pl.multiple_of(local * hidden_dim + place * height, 16)
            return down_ref.at[pl.ds(top, height), pl.ds(begin, cols)]

        for local in range(local_experts):
            for is_up, source in enumerate((gate_hbm, up_hbm)):
                copies.start(source.at[local], wide_at(mine, local, is_up))
            copies.start(down_hbm.at[local], down_at(mine, local, 0, feature_dim))
        if paired:
            for local, (pair, downs) in enumerate(places):
                for is_up, (row, some) in enumerate(pair):
                    copies.start(rest[0].at[pl.ds(row, some), :], wide_at(1 - mine, local, is_up))
                for row, some, begin, cols in downs:
                    source = rest[0].at[pl.ds(row, some), pl.ds(0, cols)]
                    copies.start(source, down_at(1 - mine, local, begin, cols))
        copies.wait()

    shards = [pltpu.with_memory_space_constraint(w, pltpu.HBM) for w in shards]
    count = 3 * local_experts
    specs = [pl.BlockSpec(memory_space=pl.ANY)] * 3
    if paired:
        count += sum(len(pair) + len(downs) for pair, downs in places)
        specs.append(pl.BlockSpec(memory_space=pltpu.VMEM))
        shards.append(pltpu.with_memory_space_constraint(packed, pltpu.VMEM))
    return pl.pallas_call(
        kernel,
        out_shape=[
            pltpu.VMEM((feature_dim, 2 * local_experts * hidden_dim), BF16),
            pltpu.VMEM((local_experts * hidden_dim, feature_dim), BF16),
        ],
        in_specs=specs,
        out_specs=[pl.BlockSpec(memory_space=pltpu.VMEM)] * 2,
        scratch_shapes=[pltpu.SemaphoreType.DMA((count,))],
        compiler_params=pltpu.CompilerParams(vmem_limit_bytes=VMEM_LIMIT),
    )(*shards)


def transpose_kernel(from_ref, to_ref):
    strip = 2 * LANES

    @pl.loop(0, to_ref.shape[0] // strip)
    def _(i):
        some = pl.ds(pl.multiple_of(i * strip, strip), strip)
        to_ref[some, :] = from_ref[:, some].T


def transposed(weights):
    rows, cols = weights.shape
    return call(transpose_kernel, [((cols, rows), BF16)], weights)[0]


def body(tokens, w_gate, w_up, w_down, route_ids, route_scores, norm_gain, class_head, targets):
    rows_here, feature_dim = tokens.shape
    expert_count = lax.axis_size("expert")
    group_count = lax.axis_size("group")
    local_experts, _, hidden_dim = w_gate.shape
    pair_dim = 2 * hidden_dim
    ring = Ring(expert_count, group_count)
    block = (rows_here, feature_dim)
    mid = rows_here // 2

    shards = [w_gate, w_up, w_down]
    if group_count == 2:
        top, bottom, packed = pack(route_ids.T, route_scores.T, tokens, shards)
        packed = lax.ppermute(packed, "group", [(0, 1), (1, 0)])
    else:
        top, bottom = pack(route_ids.T, route_scores.T, tokens, [])
        shards = [lax.all_gather(w, "group", axis=1, tiled=True) for w in shards]
        packed = None
    wide, down = full_weights(shards, packed)

    def rows_of(refs):
        return jnp.concatenate([ref[...] for ref in refs], axis=0) if len(refs) > 1 else refs[0][...]

    def forward_kernel(count, guards, *refs):
        token_refs, (wide_ref, down_ref) = refs[:count], refs[count : count + 2]
        outs = refs[count + 2 + guards :]
        x = rows_of([ref.at[:, :feature_dim] for ref in token_refs])
        weights = jnp.concatenate([ref[:, feature_dim:] for ref in token_refs[::2]], axis=0).astype(F32)
        lane = lax.broadcasted_iota(jnp.int32, weights.shape, 1)
        quarter = LANES // 4
        total = None
        for local in range(local_experts):
            expert = lax.axis_index("expert") * local_experts + local
            scales = []
            for begin in (expert, expert + 2 * quarter):
                here = (lane == begin) | (lane == begin + quarter)
                scales.append(jnp.sum(jnp.where(here, weights, 0.0), axis=1, keepdims=True))
            pieces = [s[i : i + mid] for i in range(0, weights.shape[0], mid) for s in scales]
            scale = jnp.concatenate(pieces, axis=0)
            act = dot(x, wide_ref[:, pl.ds(local * pair_dim, pair_dim)])
            gate_act, up_act = act[:, :hidden_dim], act[:, hidden_dim:]
            sigmoid_gate = jax.nn.sigmoid(gate_act)
            silu = gate_act * sigmoid_gate * scale
            slope = sigmoid_gate * (1.0 + gate_act * (1.0 - sigmoid_gate)) * scale
            cols = pl.ds(local * hidden_dim, hidden_dim)
            outs[0][:, cols] = (up_act * slope).astype(BF16)
            outs[1][:, cols] = silu.astype(BF16)
            hidden = (silu * up_act).astype(BF16)
            term = dot(hidden, down_ref[cols, :])
            total = term if total is None else total + term
        for i, out in enumerate(outs[2:]):
            out[...] = total[i * mid : (i + 1) * mid].astype(out.dtype)

    tokens_at, saved_at, part_at = {}, {}, {}
    flops = 2 * rows_here * feature_dim * hidden_dim * local_experts * 3

    def hold(distances, blocks):
        tokens_at[distances] = blocks

    def keep_parts(parts, distances, halves):
        parts.update({k: halves[2 * i : 2 * i + 2] for i, k in enumerate(distances)})

    def part_outs(distances):
        return [((mid, feature_dim), dtype) for dtype in ring.part_types(distances)]

    def forward(distances):
        blocks = tokens_at[distances]
        rows = mid * len(blocks)
        guards = [saved_at[d][0] for d in ((0,), (-1, 1))] if distances == (ring.half,) else []
        result = call(
            functools.partial(forward_kernel, len(blocks), len(guards)),
            [((rows, local_experts * hidden_dim), BF16)] * 2 + part_outs(distances),
            *blocks,
            wide,
            down,
            *guards,
            flops=flops * rows // rows_here,
        )
        saved_at[distances] = result[:2]
        keep_parts(part_at, distances, result[2:])

    ring.gather(top, bottom, hold)
    for distances in tokens_at:
        forward(distances)
    gain = norm_gain.reshape(1, feature_dim)
    half_shape = (mid, feature_dim)
    moe_top, moe_bottom = [
        call(sum_kernel, [(half_shape, BF16)], own, *arrived)[0]
        for own, arrived in zip(part_at[0], ring.scatter(part_at))
    ]

    norm_at, mean_at = {}, {}

    def residual_of(token_refs, moe_refs):
        token_rows = rows_of([ref.at[:, :feature_dim] for ref in token_refs]).astype(F32)
        return token_rows + rows_of(moe_refs).astype(F32)

    def inv_rms_of(residual):
        return lax.rsqrt(jnp.mean(residual * residual, axis=-1, keepdims=True) + NORM_EPS)

    def norm_kernel(distances, count, *refs):
        residual = residual_of(refs[:count], refs[count : 2 * count])
        gain_ref, so_far, out_ref, residual_ref, inv_ref = refs[2 * count :]
        inv_rms = inv_rms_of(residual)
        residual_ref[...] = residual
        inv_ref[...] = jnp.broadcast_to(inv_rms, inv_ref.shape)
        normed = residual * inv_rms * gain_ref[...]
        pooled = so_far[...]
        row = lax.broadcasted_iota(jnp.int32, pooled.shape, 0)
        for i, k in enumerate(distances):
            part = normed[i * rows_here : (i + 1) * rows_here]
            mean = jnp.mean(part, axis=0, keepdims=True)
            pooled = jnp.where(row == ring.device_at(k), mean, pooled)
        out_ref[...] = pooled

    pooled_shape = (expert_count, feature_dim)
    mean_at["pooled"] = jnp.zeros(pooled_shape, F32)

    def norm(distances, blocks):
        rows = mid * len(blocks)
        mean_at["pooled"], *norm_at[distances] = call(
            functools.partial(norm_kernel, distances, len(blocks)),
            [(pooled_shape, F32), ((rows, feature_dim), F32), ((rows, LANES), F32)],
            *tokens_at[distances],
            *blocks,
            gain,
            mean_at["pooled"],
        )

    ring.gather(moe_top, moe_bottom, norm)
    pooled = mean_at["pooled"].astype(BF16)
    logits = dot(pooled, class_head)
    target_rows = targets.reshape(expert_count, -1).astype(F32)
    logit_grad = (LOSS_SCALE * (jax.nn.sigmoid(logits) - target_rows)).astype(BF16)
    pooled_grad = dot_t(logit_grad, class_head)
    distance = 1
    while distance < expert_count:
        pairs = [(e, e ^ distance) for e in range(expert_count)]
        mine = pooled_grad.astype(BF16)
        other = lax.ppermute(mine, "expert", pairs)
        pooled_grad = mine.astype(F32) + other.astype(F32)
        distance *= 2

    both = jnp.concatenate([pooled, logit_grad], axis=1)
    if group_count == 2:
        both = jnp.concatenate([both, lax.ppermute(both, "group", [(0, 1), (1, 0)])], axis=0)
    else:
        both = lax.all_gather(both, "group", axis=0, tiled=True)
    head_grad = lax.dot_general(
        both[:, :feature_dim],
        both[:, feature_dim:],
        (((0,), (0,)), ((), ())),
        preferred_element_type=F32,
    )

    def backward_kernel(distances, residual_ref, inv_ref, gate_save, up_save, *refs):
        grad_ref, gain_ref, wide_ref, down_ref, *outs = refs
        residual, inv_rms = residual_ref[...], inv_ref[:, :1]
        cube = inv_rms * inv_rms * inv_rms
        parts = []
        for i, k in enumerate(distances):
            rows = slice(i * rows_here, (i + 1) * rows_here)
            scaled = gain_ref[...] * grad_ref[pl.ds(ring.device_at(k), 1), :] / rows_here
            slope = cube[rows] * jnp.mean(residual[rows] * scaled, axis=-1, keepdims=True)
            parts.append(inv_rms[rows] * scaled - residual[rows] * slope)
        resid_grad = jnp.concatenate(parts, axis=0) if len(parts) > 1 else parts[0]
        down_back = dot(resid_grad.astype(BF16), down_ref[...])
        total = resid_grad if distances == (0,) else None
        for local in range(local_experts):
            cols = slice(local * hidden_dim, (local + 1) * hidden_dim)
            gate_grad = (down_back[:, cols] * gate_save[:, cols].astype(F32)).astype(BF16)
            up_grad = (down_back[:, cols] * up_save[:, cols].astype(F32)).astype(BF16)
            grads = jnp.concatenate([gate_grad, up_grad], axis=1)
            term = dot(grads, wide_ref[pl.ds(local * pair_dim, pair_dim), :])
            total = term if total is None else total + term
        for i, out in enumerate(outs):
            out[...] = total[i * mid : (i + 1) * mid].astype(out.dtype)

    wide_t, down_t = transposed(wide), transposed(down)
    back_at = {}

    def backward(distances):
        result = call(
            functools.partial(backward_kernel, distances),
            part_outs(distances),
            *norm_at[distances],
            *saved_at[distances],
            pooled_grad,
            gain,
            wide_t,
            down_t,
            flops=flops * len(distances),
        )
        keep_parts(back_at, distances, result)

    for distances in reversed(list(tokens_at)):
        backward(distances)
    (top_left, top_right), (bottom_left, bottom_right) = ring.scatter(back_at)
    token_grad = pl.pallas_call(
        sum_kernel,
        out_shape=jax.ShapeDtypeStruct(block, BF16),
        in_specs=[pl.BlockSpec(memory_space=pltpu.VMEM)] * 6,
        out_specs=pl.BlockSpec(memory_space=pltpu.VMEM),
        compiler_params=pltpu.CompilerParams(vmem_limit_bytes=VMEM_LIMIT),
    )(back_at[0][0], top_left, top_right, back_at[0][1], bottom_left, bottom_right)
    return (token_grad, head_grad)


def solution(mesh):
    in_specs = (
        P(("rep", "expert", "group"), None),
        P("expert", "group", None),
        P("expert", "group", None),
        P("expert", "group", None),
        P(("rep", "expert", "group"), None),
        P(("rep", "expert", "group"), None),
        P(),
        P(None, "expert"),
        P("rep", "group", "expert"),
    )
    out_specs = (P(("rep", "expert", "group"), None), P("rep", "expert"))
    return jax.shard_map(body, mesh=mesh, in_specs=in_specs, out_specs=out_specs, check_vma=False)
```

```python
import functools

import jax
import jax.numpy as jnp
from jax import lax
from jax.experimental import pallas as pl
from jax.experimental.pallas import tpu as pltpu
from jax.sharding import PartitionSpec as P

LOSS_SCALE = 8.0
NORM_EPS = 1e-06
F32 = jnp.float32
BF16 = jnp.bfloat16
LANES = 128
VMEM_LIMIT = 32 * 1024 * 1024


def dot(left, right):
    return jnp.dot(left, right, preferred_element_type=F32)


def dot_t(left, right):
    return lax.dot_general(left, right, (((1,), (1,)), ((), ())), preferred_element_type=F32)


def call(kernel, outs, *args, flops=0, scratch=()):
    args = [pltpu.with_memory_space_constraint(a, pltpu.VMEM) for a in args]
    size = sum(a.size * a.dtype.itemsize for a in args)
    return pl.pallas_call(
        kernel,
        out_shape=[pltpu.VMEM(shape, dtype) for shape, dtype in outs],
        in_specs=[pl.BlockSpec(memory_space=pltpu.VMEM)] * len(args),
        out_specs=[pl.BlockSpec(memory_space=pltpu.VMEM)] * len(outs),
        scratch_shapes=list(scratch),
        compiler_params=pltpu.CompilerParams(vmem_limit_bytes=VMEM_LIMIT),
        cost_estimate=pl.CostEstimate(flops=flops, bytes_accessed=size, transcendentals=0),
    )(*args)


def after(value, guard):
    def kernel(value_ref, guard_ref, out_ref):
        pass

    args = [pltpu.with_memory_space_constraint(a, pltpu.VMEM) for a in (value, guard)]
    return pl.pallas_call(
        kernel,
        out_shape=pltpu.VMEM(value.shape, value.dtype),
        in_specs=[pl.BlockSpec(memory_space=pltpu.VMEM)] * 2,
        out_specs=pl.BlockSpec(memory_space=pltpu.VMEM),
        input_output_aliases={0: 0},
        compiler_params=pltpu.CompilerParams(vmem_limit_bytes=VMEM_LIMIT),
    )(*args)


class Ring:
    def __init__(self, expert_count, group_count):
        self.count = expert_count
        self.half = expert_count // 2
        self.snake = group_count == 2
        if self.snake:
            self.order = list(range(0, expert_count, 2)) + list(range(expert_count - 1, 0, -2))
        else:
            self.order = list(range(expert_count))

    def send(self, value, distance):
        pairs = [
            (self.order[i], self.order[(i + distance) % self.count]) for i in range(self.count)
        ]
        return lax.ppermute(value, "expert", pairs)

    def device_at(self, distance):
        here = lax.axis_index("expert")
        count = self.count
        if self.snake:
            here = jnp.where(here % 2 == 0, here // 2, count - 1 - here // 2)
        there = lax.rem(here + distance % count, count)
        if self.snake:
            there = jnp.where(there < self.half, 2 * there, 2 * (count - 1 - there) + 1)
        return there

    def gather(self, top, bottom, use, waits=None):
        top_left = top_right = top
        bottom_left = bottom_right = bottom
        use((0,), (top, bottom))
        for step in range(1, self.half):
            if waits and step in waits:
                *others, last = waits[step]()
                top_right = after(top_right, others[0]) if others else top_right
                bottom_left = after(bottom_left, last)
            top_left = self.send(top_left, 1)
            top_right = self.send(top_right, -1)
            bottom_left = self.send(bottom_left, 1)
            bottom_right = self.send(bottom_right, -1)
            use((-step, step), (top_left, bottom_left, top_right, bottom_right))
        use((self.half,), (self.send(top_left, 1), self.send(bottom_right, -1)))

    def scatter(self, parts):
        most = self.half - 1
        top_left = self.send(parts[self.half][0], 1)
        bottom_right = self.send(parts[self.half][1], -1)
        bottom_left = self.send(parts[most][1], 1)
        top_right = self.send(parts[-most][0], -1)
        for step in range(most, 0, -1):
            top_left = self.send(add(parts[step][0], top_left), 1)
            bottom_right = self.send(add(parts[-step][1], bottom_right), -1)
            if step > 1:
                bottom_left = self.send(add(parts[step - 1][1], bottom_left), 1)
                top_right = self.send(add(parts[1 - step][0], top_right), -1)
        return (top_left, top_right), (bottom_left, bottom_right)

    def part_types(self, distances):
        types = []
        for k in distances:
            first = BF16 if k == self.half or k == 1 - self.half else F32
            second = BF16 if k == self.half or k == self.half - 1 else F32
            types += [first, second]
        return types


def add_kernel(block_ref, arrived_ref, out_ref):
    out_ref[...] = (block_ref[...] + arrived_ref[...].astype(F32)).astype(BF16)


def add(block, arrived):
    return call(add_kernel, [(block.shape, BF16)], block, arrived)[0]


def sum_kernel(*refs):
    out_ref = refs[-1]
    rows = refs[0].shape[0]
    for i in range(len(refs) // 3):
        own, left, right = refs[3 * i : 3 * i + 3]
        arrived = left[...].astype(F32) + right[...].astype(F32)
        out_ref[pl.ds(i * rows, rows), :] = (own[...] + arrived).astype(BF16)


class Copies:
    def __init__(self, sems):
        self.sems, self.started = sems, []

    def start(self, source, target):
        copy = pltpu.make_async_copy(source, target, self.sems.at[len(self.started)])
        copy.start()
        self.started.append(copy)

    def wait(self):
        for copy in self.started:
            copy.wait()


def strips(gate_shape, down_shape):
    local_experts, depth, hidden_dim = gate_shape
    _, height, feature_dim = down_shape
    row, places = 0, []
    for _ in range(local_experts):
        pair = [(row, depth), (row + depth, depth)]
        row += 2 * depth
        downs = []
        for begin in range(0, feature_dim, hidden_dim):
            downs.append((row, height, begin, min(hidden_dim, feature_dim - begin)))
            row += height
        places.append((pair, downs))
    return row, places


def pack(ids, scores, tokens, shards):
    rows, cols = tokens.shape
    mid = rows // 2
    quarter = LANES // 4
    inputs = [ids, scores, tokens, *shards]
    packed_shape, places, count = None, [], 0
    if shards:
        hidden_dim = shards[0].shape[2]
        packed_rows, places = strips(shards[0].shape, shards[2].shape)
        packed_shape = (packed_rows, hidden_dim)
        count = sum(len(pair) + len(downs) for pair, downs in places)

    def kernel(*refs):
        ids_hbm, scores_hbm, tokens_hbm, *shards_hbm = refs[: len(inputs)]
        top_ref, bottom_ref, *packed_refs = refs[len(inputs) : -3]
        ids_ref, scores_ref, sems = refs[-3:]
        copies = Copies(sems)
        copies.start(ids_hbm, ids_ref)
        copies.start(scores_hbm, scores_ref)
        copies.start(tokens_hbm.at[pl.ds(0, mid), :], top_ref.at[:, pl.ds(0, cols)])
        copies.start(tokens_hbm.at[pl.ds(mid, mid), :], bottom_ref)
        for local, (pair, downs) in enumerate(places):
            out_ref = packed_refs[0]
            for source, (row, some) in zip(shards_hbm, pair):
                copies.start(source.at[local], out_ref.at[pl.ds(row, some), :])
            for row, some, begin, width in downs:
                source = shards_hbm[2].at[local, :, pl.ds(begin, width)]
                copies.start(source, out_ref.at[pl.ds(row, some), pl.ds(0, width)])
                if width < hidden_dim:
                    rest = hidden_dim - width
                    out_ref[pl.ds(row, some), pl.ds(width, rest)] = jnp.zeros((some, rest), BF16)
        copies.started[0].wait()
        copies.started[1].wait()
        scores = scores_ref[...]
        ids = ids_ref[...]
        route_weight = scores / jnp.sum(scores, axis=0, keepdims=True)
        expert = lax.broadcasted_iota(jnp.int32, (quarter, rows), 0)
        weight_by = jnp.zeros((quarter, rows), F32)
        for choice_k in range(scores.shape[0]):
            one = slice(choice_k, choice_k + 1)
            weight_by = weight_by + jnp.where(ids[one] == expert, route_weight[one], 0.0)
        high = weight_by.astype(BF16).astype(F32)
        weights = jnp.concatenate([high, weight_by - high] * 2, axis=0).T
        lane = lax.broadcasted_iota(jnp.int32, (mid, LANES), 1)
        both = jnp.where(lane < 2 * quarter, weights[:mid], weights[mid:])
        top_ref[:, cols:] = both.astype(BF16)
        for copy in copies.started[2:]:
            copy.wait()

    outs = [pltpu.VMEM((mid, cols + LANES), BF16), pltpu.VMEM((mid, cols), BF16)]
    if shards:
        outs.append(pltpu.VMEM(packed_shape, BF16))
    return pl.pallas_call(
        kernel,
        out_shape=outs,
        in_specs=[pl.BlockSpec(memory_space=pl.ANY)] * len(inputs),
        out_specs=[pl.BlockSpec(memory_space=pltpu.VMEM)] * len(outs),
        scratch_shapes=[
            pltpu.VMEM(ids.shape, ids.dtype),
            pltpu.VMEM(scores.shape, F32),
            pltpu.SemaphoreType.DMA((4 + count,)),
        ],
        compiler_params=pltpu.CompilerParams(vmem_limit_bytes=VMEM_LIMIT),
    )(*[pltpu.with_memory_space_constraint(a, pltpu.HBM) for a in inputs])


def full_weights(shards, packed):
    local_experts, _, hidden_dim = shards[0].shape
    feature_dim = shards[2].shape[2]
    paired = packed is not None
    _, places = strips(shards[0].shape, shards[2].shape)
    depth, height = shards[0].shape[1], shards[2].shape[1]

    def kernel(*refs):
        gate_hbm, up_hbm, down_hbm, *rest = refs
        wide_ref, down_ref, sems = rest[-3:]
        copies = Copies(sems)
        mine = lax.axis_index("group") if paired else 0

        def wide_at(place, local, is_up):
            rows = pl.ds(pl.multiple_of(place * depth, 16), depth)
            return wide_ref.at[rows, pl.ds((2 * local + is_up) * hidden_dim, hidden_dim)]

        def down_at(place, local, begin, cols):
            top = pl.multiple_of(local * hidden_dim + place * height, 16)
            return down_ref.at[pl.ds(top, height), pl.ds(begin, cols)]

        for local in range(local_experts):
            for is_up, source in enumerate((gate_hbm, up_hbm)):
                copies.start(source.at[local], wide_at(mine, local, is_up))
            copies.start(down_hbm.at[local], down_at(mine, local, 0, feature_dim))
        if paired:
            for local, (pair, downs) in enumerate(places):
                for is_up, (row, some) in enumerate(pair):
                    copies.start(rest[0].at[pl.ds(row, some), :], wide_at(1 - mine, local, is_up))
                for row, some, begin, cols in downs:
                    source = rest[0].at[pl.ds(row, some), pl.ds(0, cols)]
                    copies.start(source, down_at(1 - mine, local, begin, cols))
        copies.wait()

    shards = [pltpu.with_memory_space_constraint(w, pltpu.HBM) for w in shards]
    count = 3 * local_experts
    specs = [pl.BlockSpec(memory_space=pl.ANY)] * 3
    if paired:
        count += sum(len(pair) + len(downs) for pair, downs in places)
        specs.append(pl.BlockSpec(memory_space=pltpu.VMEM))
        shards.append(pltpu.with_memory_space_constraint(packed, pltpu.VMEM))
    return pl.pallas_call(
        kernel,
        out_shape=[
            pltpu.VMEM((feature_dim, 2 * local_experts * hidden_dim), BF16),
            pltpu.VMEM((local_experts * hidden_dim, feature_dim), BF16),
        ],
        in_specs=specs,
        out_specs=[pl.BlockSpec(memory_space=pltpu.VMEM)] * 2,
        scratch_shapes=[pltpu.SemaphoreType.DMA((count,))],
        compiler_params=pltpu.CompilerParams(vmem_limit_bytes=VMEM_LIMIT),
    )(*shards)


def transpose_kernel(from_ref, to_ref):
    strip = 2 * LANES

    @pl.loop(0, to_ref.shape[0] // strip)
    def _(i):
        some = pl.ds(pl.multiple_of(i * strip, strip), strip)
        to_ref[some, :] = from_ref[:, some].T


def transposed(weights):
    rows, cols = weights.shape
    return call(transpose_kernel, [((cols, rows), BF16)], weights)[0]


def body(tokens, w_gate, w_up, w_down, route_ids, route_scores, norm_gain, class_head, targets):
    rows_here, feature_dim = tokens.shape
    expert_count = lax.axis_size("expert")
    group_count = lax.axis_size("group")
    local_experts, _, hidden_dim = w_gate.shape
    pair_dim = 2 * hidden_dim
    ring = Ring(expert_count, group_count)
    block = (rows_here, feature_dim)
    mid = rows_here // 2

    shards = [w_gate, w_up, w_down]
    if group_count == 2:
        top, bottom, packed = pack(route_ids.T, route_scores.T, tokens, shards)
        packed = lax.ppermute(packed, "group", [(0, 1), (1, 0)])
    else:
        top, bottom = pack(route_ids.T, route_scores.T, tokens, [])
        shards = [lax.all_gather(w, "group", axis=1, tiled=True) for w in shards]
        packed = None
    wide, down = full_weights(shards, packed)

    def rows_of(refs):
        return jnp.concatenate([ref[...] for ref in refs], axis=0) if len(refs) > 1 else refs[0][...]

    def forward_kernel(count, guards, *refs):
        token_refs, (wide_ref, down_ref) = refs[:count], refs[count : count + 2]
        outs = refs[count + 2 + guards :]
        x = rows_of([ref.at[:, :feature_dim] for ref in token_refs])
        weights = jnp.concatenate([ref[:, feature_dim:] for ref in token_refs[::2]], axis=0).astype(F32)
        lane = lax.broadcasted_iota(jnp.int32, weights.shape, 1)
        quarter = LANES // 4
        total = None
        for local in range(local_experts):
            expert = lax.axis_index("expert") * local_experts + local
            scales = []
            for begin in (expert, expert + 2 * quarter):
                here = (lane == begin) | (lane == begin + quarter)
                scales.append(jnp.sum(jnp.where(here, weights, 0.0), axis=1, keepdims=True))
            pieces = [s[i : i + mid] for i in range(0, weights.shape[0], mid) for s in scales]
            scale = jnp.concatenate(pieces, axis=0)
            act = dot(x, wide_ref[:, pl.ds(local * pair_dim, pair_dim)])
            gate_act, up_act = act[:, :hidden_dim], act[:, hidden_dim:]
            sigmoid_gate = jax.nn.sigmoid(gate_act)
            silu = gate_act * sigmoid_gate * scale
            slope = sigmoid_gate * (1.0 + gate_act * (1.0 - sigmoid_gate)) * scale
            cols = pl.ds(local * hidden_dim, hidden_dim)
            outs[0][:, cols] = (up_act * slope).astype(BF16)
            outs[1][:, cols] = silu.astype(BF16)
            hidden = (silu * up_act).astype(BF16)
            term = dot(hidden, down_ref[cols, :])
            total = term if total is None else total + term
        for i, out in enumerate(outs[2:]):
            out[...] = total[i * mid : (i + 1) * mid].astype(out.dtype)

    tokens_at, saved_at, part_at = {}, {}, {}
    flops = 2 * rows_here * feature_dim * hidden_dim * local_experts * 3

    def hold(distances, blocks):
        tokens_at[distances] = blocks

    def keep_parts(parts, distances, halves):
        parts.update({k: halves[2 * i : 2 * i + 2] for i, k in enumerate(distances)})

    def part_outs(distances):
        return [((mid, feature_dim), dtype) for dtype in ring.part_types(distances)]

    def forward(distances):
        blocks = tokens_at[distances]
        rows = mid * len(blocks)
        guards = [saved_at[1 - ring.half, ring.half - 1][0]] if distances == (ring.half,) else []
        result = call(
            functools.partial(forward_kernel, len(blocks), len(guards)),
            [((rows, local_experts * hidden_dim), BF16)] * 2 + part_outs(distances),
            *blocks,
            wide,
            down,
            *guards,
            flops=flops * rows // rows_here,
        )
        saved_at[distances] = result[:2]
        keep_parts(part_at, distances, result[2:])

    def early(*done):
        for distances in done:
            forward(distances)
        return [saved_at[d][0] for d in done]

    waits = {}
    if packed is not None and ring.half > 3:
        waits = {2: lambda: [packed], 3: lambda: early((0,), (-1, 1))}
    ring.gather(top, bottom, hold, waits)
    for distances in tokens_at:
        if distances not in saved_at:
            forward(distances)
    gain = norm_gain.reshape(1, feature_dim)
    half_shape = (mid, feature_dim)
    moe_top, moe_bottom = [
        call(sum_kernel, [(half_shape, BF16)], own, *arrived)[0]
        for own, arrived in zip(part_at[0], ring.scatter(part_at))
    ]

    norm_at, mean_at = {}, {}

    def residual_of(token_refs, moe_refs):
        token_rows = rows_of([ref.at[:, :feature_dim] for ref in token_refs]).astype(F32)
        return token_rows + rows_of(moe_refs).astype(F32)

    def inv_rms_of(residual):
        return lax.rsqrt(jnp.mean(residual * residual, axis=-1, keepdims=True) + NORM_EPS)

    def norm_kernel(distances, count, *refs):
        residual = residual_of(refs[:count], refs[count : 2 * count])
        gain_ref, so_far, out_ref, residual_ref, inv_ref = refs[2 * count :]
        inv_rms = inv_rms_of(residual)
        residual_ref[...] = residual
        inv_ref[...] = jnp.broadcast_to(inv_rms, inv_ref.shape)
        normed = residual * inv_rms * gain_ref[...]
        pooled = so_far[...]
        row = lax.broadcasted_iota(jnp.int32, pooled.shape, 0)
        for i, k in enumerate(distances):
            part = normed[i * rows_here : (i + 1) * rows_here]
            mean = jnp.mean(part, axis=0, keepdims=True)
            pooled = jnp.where(row == ring.device_at(k), mean, pooled)
        out_ref[...] = pooled

    pooled_shape = (expert_count, feature_dim)
    mean_at["pooled"] = jnp.zeros(pooled_shape, F32)

    def norm(distances, blocks):
        rows = mid * len(blocks)
        mean_at["pooled"], *norm_at[distances] = call(
            functools.partial(norm_kernel, distances, len(blocks)),
            [(pooled_shape, F32), ((rows, feature_dim), F32), ((rows, LANES), F32)],
            *tokens_at[distances],
            *blocks,
            gain,
            mean_at["pooled"],
        )

    ring.gather(moe_top, moe_bottom, norm)
    pooled = mean_at["pooled"].astype(BF16)
    logits = dot(pooled, class_head)
    target_rows = targets.reshape(expert_count, -1).astype(F32)
    logit_grad = (LOSS_SCALE * (jax.nn.sigmoid(logits) - target_rows)).astype(BF16)
    pooled_grad = dot_t(logit_grad, class_head)
    span = 2
    for masks in ([1], list(range(span, expert_count, span))):
        mine = pooled_grad.astype(BF16)
        pooled_grad = mine.astype(F32)
        for mask in masks:
            pairs = [(e, e ^ mask) for e in range(expert_count)]
            pooled_grad = pooled_grad + lax.ppermute(mine, "expert", pairs).astype(F32)

    both = jnp.concatenate([pooled, logit_grad], axis=1)
    if group_count == 2:
        both = jnp.concatenate([both, lax.ppermute(both, "group", [(0, 1), (1, 0)])], axis=0)
    else:
        both = lax.all_gather(both, "group", axis=0, tiled=True)
    head_grad = lax.dot_general(
        both[:, :feature_dim],
        both[:, feature_dim:],
        (((0,), (0,)), ((), ())),
        preferred_element_type=F32,
    )

    def backward_kernel(distances, residual_ref, inv_ref, gate_save, up_save, *refs):
        grad_ref, gain_ref, wide_ref, down_ref, *outs = refs[:-1]
        rows_ref = refs[-1]
        piece = 32
        for i, k in enumerate(distances):
            scaled = gain_ref[...] * grad_ref[pl.ds(ring.device_at(k), 1), :] / rows_here
            for begin in range(0, rows_here, piece):
                rows = pl.ds(i * rows_here + begin, piece)
                residual, inv_rms = residual_ref[rows, :], inv_ref[rows, :1]
                cube = inv_rms * inv_rms * inv_rms
                slope = cube * jnp.mean(residual * scaled, axis=-1, keepdims=True)
                resid_grad = inv_rms * scaled - residual * slope
                rows_ref[rows, :] = resid_grad.astype(BF16)
                if distances == (0,):
                    outs[begin // mid][pl.ds(begin % mid, piece), :] = resid_grad
        down_back = dot(rows_ref[...], down_ref[...])
        total = None
        for local in range(local_experts):
            cols = slice(local * hidden_dim, (local + 1) * hidden_dim)
            gate_grad = (down_back[:, cols] * gate_save[:, cols].astype(F32)).astype(BF16)
            up_grad = (down_back[:, cols] * up_save[:, cols].astype(F32)).astype(BF16)
            grads = jnp.concatenate([gate_grad, up_grad], axis=1)
            term = dot(grads, wide_ref[pl.ds(local * pair_dim, pair_dim), :])
            total = term if total is None else total + term
        for i, out in enumerate(outs):
            part = total[i * mid : (i + 1) * mid]
            out[...] = out[...] + part if distances == (0,) else part.astype(out.dtype)

    wide_t, down_t = transposed(wide), transposed(down)
    back_at = {}

    def backward(distances):
        result = call(
            functools.partial(backward_kernel, distances),
            part_outs(distances),
            *norm_at[distances],
            *saved_at[distances],
            pooled_grad,
            gain,
            wide_t,
            down_t,
            flops=flops * len(distances),
            scratch=[pltpu.VMEM((rows_here * len(distances), feature_dim), BF16)],
        )
        keep_parts(back_at, distances, result)

    for distances in reversed(list(tokens_at)):
        backward(distances)
    (top_left, top_right), (bottom_left, bottom_right) = ring.scatter(back_at)
    token_grad = pl.pallas_call(
        sum_kernel,
        out_shape=jax.ShapeDtypeStruct(block, BF16),
        in_specs=[pl.BlockSpec(memory_space=pltpu.VMEM)] * 6,
        out_specs=pl.BlockSpec(memory_space=pltpu.VMEM),
        compiler_params=pltpu.CompilerParams(vmem_limit_bytes=VMEM_LIMIT),
    )(back_at[0][0], top_left, top_right, back_at[0][1], bottom_left, bottom_right)
    return (token_grad, head_grad)


def solution(mesh):
    in_specs = (
        P(("rep", "expert", "group"), None),
        P("expert", "group", None),
        P("expert", "group", None),
        P("expert", "group", None),
        P(("rep", "expert", "group"), None),
        P(("rep", "expert", "group"), None),
        P(),
        P(None, "expert"),
        P("rep", "group", "expert"),
    )
    out_specs = (P(("rep", "expert", "group"), None), P("rep", "expert"))
    return jax.shard_map(body, mesh=mesh, in_specs=in_specs, out_specs=out_specs, check_vma=False)
```

```python
import functools

import jax
import jax.numpy as jnp
from jax import lax
from jax.experimental import pallas as pl
from jax.experimental.pallas import tpu as pltpu
from jax.sharding import PartitionSpec as P

LOSS_SCALE = 8.0
NORM_EPS = 1e-06
F32 = jnp.float32
BF16 = jnp.bfloat16
LANES = 128
VMEM_LIMIT = 32 * 1024 * 1024


def dot(left, right):
    return jnp.dot(left, right, preferred_element_type=F32)


def dot_t(left, right):
    return lax.dot_general(left, right, (((1,), (1,)), ((), ())), preferred_element_type=F32)


def call(kernel, outs, *args, flops=0):
    args = [pltpu.with_memory_space_constraint(a, pltpu.VMEM) for a in args]
    size = sum(a.size * a.dtype.itemsize for a in args)
    return pl.pallas_call(
        kernel,
        out_shape=[pltpu.VMEM(shape, dtype) for shape, dtype in outs],
        in_specs=[pl.BlockSpec(memory_space=pltpu.VMEM)] * len(args),
        out_specs=[pl.BlockSpec(memory_space=pltpu.VMEM)] * len(outs),
        compiler_params=pltpu.CompilerParams(vmem_limit_bytes=VMEM_LIMIT),
        cost_estimate=pl.CostEstimate(flops=flops, bytes_accessed=size, transcendentals=0),
    )(*args)


class Ring:
    def __init__(self, expert_count, group_count):
        self.count = expert_count
        self.half = expert_count // 2
        self.snake = group_count == 2
        if self.snake:
            self.order = list(range(0, expert_count, 2)) + list(range(expert_count - 1, 0, -2))
        else:
            self.order = list(range(expert_count))

    def send(self, value, distance):
        pairs = [
            (self.order[i], self.order[(i + distance) % self.count]) for i in range(self.count)
        ]
        return lax.ppermute(value, "expert", pairs)

    def device_at(self, distance):
        here = lax.axis_index("expert")
        count = self.count
        if self.snake:
            here = jnp.where(here % 2 == 0, here // 2, count - 1 - here // 2)
        there = lax.rem(here + distance % count, count)
        if self.snake:
            there = jnp.where(there < self.half, 2 * there, 2 * (count - 1 - there) + 1)
        return there

    def gather(self, top, bottom, use):
        top_left = top_right = top
        bottom_left = bottom_right = bottom
        use((0,), (top, bottom))
        for step in range(1, self.half):
            top_left = self.send(top_left, 1)
            top_right = self.send(top_right, -1)
            bottom_left = self.send(bottom_left, 1)
            bottom_right = self.send(bottom_right, -1)
            use((-step, step), (top_left, bottom_left, top_right, bottom_right))
        use((self.half,), (self.send(top_left, 1), self.send(bottom_right, -1)))

    def scatter(self, parts):
        most = self.half - 1
        top_left = self.send(parts[self.half][0], 1)
        bottom_right = self.send(parts[self.half][1], -1)
        bottom_left = self.send(parts[most][1], 1)
        top_right = self.send(parts[-most][0], -1)
        for step in range(most, 0, -1):
            top_left = self.send(add(parts[step][0], top_left), 1)
            bottom_right = self.send(add(parts[-step][1], bottom_right), -1)
            if step > 1:
                bottom_left = self.send(add(parts[step - 1][1], bottom_left), 1)
                top_right = self.send(add(parts[1 - step][0], top_right), -1)
        return (top_left, top_right), (bottom_left, bottom_right)

    def scatter_whole(self, ends, parts):
        mid = ends[0].shape[0]

        def half_kernel(first, block_ref, arrived_ref, out_ref):
            added, kept = pl.ds(first, mid), pl.ds(mid - first, mid)
            out_ref[added, :] = (block_ref[added, :] + arrived_ref[...].astype(F32)).astype(BF16)
            out_ref[kept, :] = block_ref[kept, :].astype(BF16)

        left, right = self.send(ends[0], 1), self.send(ends[1], -1)
        for step in range(self.half - 1, 0, -1):
            blocks = parts[step], parts[-step]
            if step == self.half - 1:
                halves = [functools.partial(half_kernel, first) for first in (0, mid)]
                shape = blocks[0].shape
                left, right = [
                    call(kernel, [(shape, BF16)], block, arrived)[0]
                    for kernel, block, arrived in zip(halves, blocks, (left, right))
                ]
            else:
                left, right = add(blocks[0], left), add(blocks[1], right)
            left, right = self.send(left, 1), self.send(right, -1)
        return left, right

    def part_types(self, distances):
        types = []
        for k in distances:
            first = BF16 if k == self.half or k == 1 - self.half else F32
            second = BF16 if k == self.half or k == self.half - 1 else F32
            types += [first, second]
        return types


def add_kernel(block_ref, arrived_ref, out_ref):
    out_ref[...] = (block_ref[...] + arrived_ref[...].astype(F32)).astype(BF16)


def add(block, arrived):
    return call(add_kernel, [(block.shape, BF16)], block, arrived)[0]


def sum_kernel(*refs):
    out_ref = refs[-1]
    rows = refs[0].shape[0]
    for i in range(len(refs) // 3):
        own, left, right = refs[3 * i : 3 * i + 3]
        arrived = left[...].astype(F32) + right[...].astype(F32)
        out_ref[pl.ds(i * rows, rows), :] = (own[...] + arrived).astype(BF16)


class Copies:
    def __init__(self, sems):
        self.sems, self.started = sems, []

    def start(self, source, target):
        copy = pltpu.make_async_copy(source, target, self.sems.at[len(self.started)])
        copy.start()
        self.started.append(copy)

    def wait(self):
        for copy in self.started:
            copy.wait()


def strips(gate_shape, down_shape):
    local_experts, depth, hidden_dim = gate_shape
    _, height, feature_dim = down_shape
    row, places = 0, []
    for _ in range(local_experts):
        pair = [(row, depth), (row + depth, depth)]
        row += 2 * depth
        downs = []
        for begin in range(0, feature_dim, hidden_dim):
            downs.append((row, height, begin, min(hidden_dim, feature_dim - begin)))
            row += height
        places.append((pair, downs))
    return row, places


def pack(ids, scores, tokens, shards):
    rows, cols = tokens.shape
    mid = rows // 2
    quarter = LANES // 4
    inputs = [ids, scores, tokens, *shards]
    packed_shape, places, count = None, [], 0
    if shards:
        hidden_dim = shards[0].shape[2]
        packed_rows, places = strips(shards[0].shape, shards[2].shape)
        packed_shape = (packed_rows, hidden_dim)
        count = sum(len(pair) + len(downs) for pair, downs in places)

    def kernel(*refs):
        ids_hbm, scores_hbm, tokens_hbm, *shards_hbm = refs[: len(inputs)]
        top_ref, bottom_ref, *packed_refs = refs[len(inputs) : -3]
        ids_ref, scores_ref, sems = refs[-3:]
        copies = Copies(sems)
        copies.start(ids_hbm, ids_ref)
        copies.start(scores_hbm, scores_ref)
        copies.start(tokens_hbm.at[pl.ds(0, mid), :], top_ref.at[:, pl.ds(0, cols)])
        copies.start(tokens_hbm.at[pl.ds(mid, mid), :], bottom_ref)
        for local, (pair, downs) in enumerate(places):
            out_ref = packed_refs[0]
            for source, (row, some) in zip(shards_hbm, pair):
                copies.start(source.at[local], out_ref.at[pl.ds(row, some), :])
            for row, some, begin, width in downs:
                source = shards_hbm[2].at[local, :, pl.ds(begin, width)]
                copies.start(source, out_ref.at[pl.ds(row, some), pl.ds(0, width)])
                if width < hidden_dim:
                    rest = hidden_dim - width
                    out_ref[pl.ds(row, some), pl.ds(width, rest)] = jnp.zeros((some, rest), BF16)
        copies.started[0].wait()
        copies.started[1].wait()
        scores = scores_ref[...]
        ids = ids_ref[...]
        route_weight = scores / jnp.sum(scores, axis=0, keepdims=True)
        expert = lax.broadcasted_iota(jnp.int32, (quarter, rows), 0)
        weight_by = jnp.zeros((quarter, rows), F32)
        for choice_k in range(scores.shape[0]):
            one = slice(choice_k, choice_k + 1)
            weight_by = weight_by + jnp.where(ids[one] == expert, route_weight[one], 0.0)
        high = weight_by.astype(BF16).astype(F32)
        weights = jnp.concatenate([high, weight_by - high] * 2, axis=0).T
        lane = lax.broadcasted_iota(jnp.int32, (mid, LANES), 1)
        both = jnp.where(lane < 2 * quarter, weights[:mid], weights[mid:])
        top_ref[:, cols:] = both.astype(BF16)
        for copy in copies.started[2:]:
            copy.wait()

    outs = [pltpu.VMEM((mid, cols + LANES), BF16), pltpu.VMEM((mid, cols), BF16)]
    if shards:
        outs.append(pltpu.VMEM(packed_shape, BF16))
    return pl.pallas_call(
        kernel,
        out_shape=outs,
        in_specs=[pl.BlockSpec(memory_space=pl.ANY)] * len(inputs),
        out_specs=[pl.BlockSpec(memory_space=pltpu.VMEM)] * len(outs),
        scratch_shapes=[
            pltpu.VMEM(ids.shape, ids.dtype),
            pltpu.VMEM(scores.shape, F32),
            pltpu.SemaphoreType.DMA((4 + count,)),
        ],
        compiler_params=pltpu.CompilerParams(vmem_limit_bytes=VMEM_LIMIT),
    )(*[pltpu.with_memory_space_constraint(a, pltpu.HBM) for a in inputs])


def full_weights(shards, packed):
    local_experts, _, hidden_dim = shards[0].shape
    feature_dim = shards[2].shape[2]
    paired = packed is not None
    _, places = strips(shards[0].shape, shards[2].shape)
    depth, height = shards[0].shape[1], shards[2].shape[1]

    def kernel(*refs):
        gate_hbm, up_hbm, down_hbm, *rest = refs
        wide_ref, down_ref, sems = rest[-3:]
        copies = Copies(sems)
        mine = lax.axis_index("group") if paired else 0

        def wide_at(place, local, is_up):
            rows = pl.ds(pl.multiple_of(place * depth, 16), depth)
            return wide_ref.at[rows, pl.ds((2 * local + is_up) * hidden_dim, hidden_dim)]

        def down_at(place, local, begin, cols):
            top = pl.multiple_of(local * hidden_dim + place * height, 16)
            return down_ref.at[pl.ds(top, height), pl.ds(begin, cols)]

        for local in range(local_experts):
            for is_up, source in enumerate((gate_hbm, up_hbm)):
                copies.start(source.at[local], wide_at(mine, local, is_up))
            copies.start(down_hbm.at[local], down_at(mine, local, 0, feature_dim))
        if paired:
            for local, (pair, downs) in enumerate(places):
                for is_up, (row, some) in enumerate(pair):
                    copies.start(rest[0].at[pl.ds(row, some), :], wide_at(1 - mine, local, is_up))
                for row, some, begin, cols in downs:
                    source = rest[0].at[pl.ds(row, some), pl.ds(0, cols)]
                    copies.start(source, down_at(1 - mine, local, begin, cols))
        copies.wait()

    shards = [pltpu.with_memory_space_constraint(w, pltpu.HBM) for w in shards]
    count = 3 * local_experts
    specs = [pl.BlockSpec(memory_space=pl.ANY)] * 3
    if paired:
        count += sum(len(pair) + len(downs) for pair, downs in places)
        specs.append(pl.BlockSpec(memory_space=pltpu.VMEM))
        shards.append(pltpu.with_memory_space_constraint(packed, pltpu.VMEM))
    return pl.pallas_call(
        kernel,
        out_shape=[
            pltpu.VMEM((feature_dim, 2 * local_experts * hidden_dim), BF16),
            pltpu.VMEM((local_experts * hidden_dim, feature_dim), BF16),
        ],
        in_specs=specs,
        out_specs=[pl.BlockSpec(memory_space=pltpu.VMEM)] * 2,
        scratch_shapes=[pltpu.SemaphoreType.DMA((count,))],
        compiler_params=pltpu.CompilerParams(vmem_limit_bytes=VMEM_LIMIT),
    )(*shards)


def transpose_kernel(from_ref, to_ref):
    strip = 2 * LANES

    @pl.loop(0, to_ref.shape[0] // strip)
    def _(i):
        some = pl.ds(pl.multiple_of(i * strip, strip), strip)
        to_ref[some, :] = from_ref[:, some].T


def transposed(weights):
    rows, cols = weights.shape
    return call(transpose_kernel, [((cols, rows), BF16)], weights)[0]


def body(tokens, w_gate, w_up, w_down, route_ids, route_scores, norm_gain, class_head, targets):
    rows_here, feature_dim = tokens.shape
    expert_count = lax.axis_size("expert")
    group_count = lax.axis_size("group")
    local_experts, _, hidden_dim = w_gate.shape
    pair_dim = 2 * hidden_dim
    ring = Ring(expert_count, group_count)
    block = (rows_here, feature_dim)
    mid = rows_here // 2

    shards = [w_gate, w_up, w_down]
    if group_count == 2:
        top, bottom, packed = pack(route_ids.T, route_scores.T, tokens, shards)
        packed = lax.ppermute(packed, "group", [(0, 1), (1, 0)])
    else:
        top, bottom = pack(route_ids.T, route_scores.T, tokens, [])
        shards = [lax.all_gather(w, "group", axis=1, tiled=True) for w in shards]
        packed = None
    wide, down = full_weights(shards, packed)

    def rows_of(refs):
        return jnp.concatenate([ref[...] for ref in refs], axis=0) if len(refs) > 1 else refs[0][...]

    def forward_kernel(count, *refs):
        token_refs, (wide_ref, down_ref) = refs[:count], refs[count : count + 2]
        outs = refs[count + 2 :]
        x = rows_of([ref.at[:, :feature_dim] for ref in token_refs])
        weights = jnp.concatenate([ref[:, feature_dim:] for ref in token_refs[::2]], axis=0).astype(F32)
        lane = lax.broadcasted_iota(jnp.int32, weights.shape, 1)
        quarter = LANES // 4
        hidden = []
        for local in range(local_experts):
            expert = lax.axis_index("expert") * local_experts + local
            scales = []
            for begin in (expert, expert + 2 * quarter):
                here = (lane == begin) | (lane == begin + quarter)
                scales.append(jnp.sum(jnp.where(here, weights, 0.0), axis=1, keepdims=True))
            pieces = [s[i : i + mid] for i in range(0, weights.shape[0], mid) for s in scales]
            scale = jnp.concatenate(pieces, axis=0)
            act = dot(x, wide_ref[:, pl.ds(local * pair_dim, pair_dim)])
            gate_act, up_act = act[:, :hidden_dim], act[:, hidden_dim:]
            sigmoid_gate = jax.nn.sigmoid(gate_act)
            silu = gate_act * sigmoid_gate * scale
            slope = sigmoid_gate * (1.0 + gate_act * (1.0 - sigmoid_gate)) * scale
            cols = pl.ds(local * hidden_dim, hidden_dim)
            outs[0][:, cols] = (up_act * slope).astype(BF16)
            outs[1][:, cols] = silu.astype(BF16)
            hidden.append((silu * up_act).astype(BF16))
        total = dot(jnp.concatenate(hidden, axis=1), down_ref[...])
        for i, out in enumerate(outs[2:]):
            out[...] = total[i * mid : (i + 1) * mid].astype(out.dtype)

    tokens_at, saved_at, part_at = {}, {}, {}
    flops = 2 * rows_here * feature_dim * hidden_dim * local_experts * 3

    def hold(distances, blocks):
        tokens_at[distances] = blocks

    def keep_parts(parts, distances, halves):
        parts.update({k: halves[2 * i : 2 * i + 2] for i, k in enumerate(distances)})

    def part_outs(distances):
        return [((mid, feature_dim), dtype) for dtype in ring.part_types(distances)]

    def forward(distances):
        blocks = tokens_at[distances]
        rows = mid * len(blocks)
        result = call(
            functools.partial(forward_kernel, len(blocks)),
            [((rows, local_experts * hidden_dim), BF16)] * 2 + part_outs(distances),
            *blocks,
            wide,
            down,
            flops=flops * rows // rows_here,
        )
        saved_at[distances] = result[:2]
        keep_parts(part_at, distances, result[2:])

    ring.gather(top, bottom, hold)
    for distances in tokens_at:
        forward(distances)
    gain = norm_gain.reshape(1, feature_dim)
    half_shape = (mid, feature_dim)
    moe_top, moe_bottom = [
        call(sum_kernel, [(half_shape, BF16)], own, *arrived)[0]
        for own, arrived in zip(part_at[0], ring.scatter(part_at))
    ]

    norm_at, mean_at = {}, {}

    def residual_of(token_refs, moe_refs):
        token_rows = rows_of([ref.at[:, :feature_dim] for ref in token_refs]).astype(F32)
        return token_rows + rows_of(moe_refs).astype(F32)

    def inv_rms_of(residual):
        return lax.rsqrt(jnp.mean(residual * residual, axis=-1, keepdims=True) + NORM_EPS)

    def norm_kernel(distances, count, *refs):
        residual = residual_of(refs[:count], refs[count : 2 * count])
        gain_ref, so_far, out_ref, residual_ref, inv_ref = refs[2 * count :]
        inv_rms = inv_rms_of(residual)
        residual_ref[...] = residual
        inv_ref[...] = jnp.broadcast_to(inv_rms, inv_ref.shape)
        normed = residual * inv_rms * gain_ref[...]
        pooled = so_far[...]
        row = lax.broadcasted_iota(jnp.int32, pooled.shape, 0)
        for i, k in enumerate(distances):
            part = normed[i * rows_here : (i + 1) * rows_here]
            mean = jnp.mean(part, axis=0, keepdims=True)
            pooled = jnp.where(row == ring.device_at(k), mean, pooled)
        out_ref[...] = pooled

    pooled_shape = (expert_count, feature_dim)
    mean_at["pooled"] = jnp.zeros(pooled_shape, F32)

    def norm(distances, blocks):
        rows = mid * len(blocks)
        mean_at["pooled"], *norm_at[distances] = call(
            functools.partial(norm_kernel, distances, len(blocks)),
            [(pooled_shape, F32), ((rows, feature_dim), F32), ((rows, LANES), F32)],
            *tokens_at[distances],
            *blocks,
            gain,
            mean_at["pooled"],
        )

    ring.gather(moe_top, moe_bottom, norm)
    pooled = mean_at["pooled"].astype(BF16)
    logits = dot(pooled, class_head)
    target_rows = targets.reshape(expert_count, -1).astype(F32)
    logit_grad = (LOSS_SCALE * (jax.nn.sigmoid(logits) - target_rows)).astype(BF16)
    pooled_grad = dot_t(logit_grad, class_head)
    span = 2
    for masks in ([1], list(range(span, expert_count, span))):
        mine = pooled_grad.astype(BF16)
        pooled_grad = mine.astype(F32)
        for mask in masks:
            pairs = [(e, e ^ mask) for e in range(expert_count)]
            pooled_grad = pooled_grad + lax.ppermute(mine, "expert", pairs).astype(F32)

    both = jnp.concatenate([pooled, logit_grad], axis=1)
    if group_count == 2:
        both = jnp.concatenate([both, lax.ppermute(both, "group", [(0, 1), (1, 0)])], axis=0)
    else:
        both = lax.all_gather(both, "group", axis=0, tiled=True)
    head_grad = lax.dot_general(
        both[:, :feature_dim],
        both[:, feature_dim:],
        (((0,), (0,)), ((), ())),
        preferred_element_type=F32,
    )

    def backward_kernel(distances, residual_ref, inv_ref, gate_save, up_save, *refs):
        grad_ref, gain_ref, wide_ref, down_ref, *outs = refs
        residual, inv_rms = residual_ref[...], inv_ref[:, :1]
        cube = inv_rms * inv_rms * inv_rms
        parts = []
        for i, k in enumerate(distances):
            rows = slice(i * rows_here, (i + 1) * rows_here)
            scaled = gain_ref[...] * grad_ref[pl.ds(ring.device_at(k), 1), :] / rows_here
            slope = cube[rows] * jnp.mean(residual[rows] * scaled, axis=-1, keepdims=True)
            parts.append(inv_rms[rows] * scaled - residual[rows] * slope)
        resid_grad = jnp.concatenate(parts, axis=0) if len(parts) > 1 else parts[0]
        down_back = dot(resid_grad.astype(BF16), down_ref[...])
        grads = []
        for local in range(local_experts):
            cols = slice(local * hidden_dim, (local + 1) * hidden_dim)
            for save in (gate_save, up_save):
                grads.append((down_back[:, cols] * save[:, cols].astype(F32)).astype(BF16))
        total = dot(jnp.concatenate(grads, axis=1), wide_ref[...])
        if distances == (0,):
            total = total + resid_grad
        rows = total.shape[0] // len(outs)
        for i, out in enumerate(outs):
            out[...] = total[i * rows : (i + 1) * rows].astype(out.dtype)

    wide_t, down_t = transposed(wide), transposed(down)
    back_at = {}

    def backward(distances):
        if distances == (ring.half,):
            outs = [((mid, feature_dim), BF16)] * 2
        else:
            outs = [(block, F32)] * len(distances)
        result = call(
            functools.partial(backward_kernel, distances),
            outs,
            *norm_at[distances],
            *saved_at[distances],
            pooled_grad,
            gain,
            wide_t,
            down_t,
            flops=flops * len(distances),
        )
        if distances == (ring.half,):
            back_at["ends"] = result
        else:
            back_at.update(zip(distances, result))

    for distances in reversed(list(tokens_at)):
        backward(distances)
    token_grad = pl.pallas_call(
        sum_kernel,
        out_shape=jax.ShapeDtypeStruct(block, BF16),
        in_specs=[pl.BlockSpec(memory_space=pltpu.VMEM)] * 3,
        out_specs=pl.BlockSpec(memory_space=pltpu.VMEM),
        compiler_params=pltpu.CompilerParams(vmem_limit_bytes=VMEM_LIMIT),
    )(back_at[0], *ring.scatter_whole(back_at["ends"], back_at))
    return (token_grad, head_grad)


def solution(mesh):
    in_specs = (
        P(("rep", "expert", "group"), None),
        P("expert", "group", None),
        P("expert", "group", None),
        P("expert", "group", None),
        P(("rep", "expert", "group"), None),
        P(("rep", "expert", "group"), None),
        P(),
        P(None, "expert"),
        P("rep", "group", "expert"),
    )
    out_specs = (P(("rep", "expert", "group"), None), P("rep", "expert"))
    return jax.shard_map(body, mesh=mesh, in_specs=in_specs, out_specs=out_specs, check_vma=False)
```

```python
import functools

import jax
import jax.numpy as jnp
from jax import lax
from jax.experimental import pallas as pl
from jax.experimental.pallas import tpu as pltpu
from jax.sharding import PartitionSpec as P

LOSS_SCALE = 8.0
NORM_EPS = 1e-06
F32 = jnp.float32
BF16 = jnp.bfloat16
LANES = 128
VMEM_LIMIT = 32 * 1024 * 1024


def dot(left, right):
    return jnp.dot(left, right, preferred_element_type=F32)


def dot_t(left, right):
    return lax.dot_general(left, right, (((1,), (1,)), ((), ())), preferred_element_type=F32)


def call(kernel, outs, *args, flops=0):
    args = [pltpu.with_memory_space_constraint(a, pltpu.VMEM) for a in args]
    size = sum(a.size * a.dtype.itemsize for a in args)
    return pl.pallas_call(
        kernel,
        out_shape=[pltpu.VMEM(shape, dtype) for shape, dtype in outs],
        in_specs=[pl.BlockSpec(memory_space=pltpu.VMEM)] * len(args),
        out_specs=[pl.BlockSpec(memory_space=pltpu.VMEM)] * len(outs),
        compiler_params=pltpu.CompilerParams(vmem_limit_bytes=VMEM_LIMIT),
        cost_estimate=pl.CostEstimate(flops=flops, bytes_accessed=size, transcendentals=0),
    )(*args)


def after(value, guard):
    def kernel(value_ref, guard_ref, out_ref):
        pass

    args = [pltpu.with_memory_space_constraint(a, pltpu.VMEM) for a in (value, guard)]
    return pl.pallas_call(
        kernel,
        out_shape=pltpu.VMEM(value.shape, value.dtype),
        in_specs=[pl.BlockSpec(memory_space=pltpu.VMEM)] * 2,
        out_specs=pl.BlockSpec(memory_space=pltpu.VMEM),
        input_output_aliases={0: 0},
        compiler_params=pltpu.CompilerParams(vmem_limit_bytes=VMEM_LIMIT),
    )(*args)


class Ring:
    def __init__(self, expert_count, group_count):
        self.count = expert_count
        self.half = expert_count // 2
        self.snake = group_count == 2
        if self.snake:
            self.order = list(range(0, expert_count, 2)) + list(range(expert_count - 1, 0, -2))
        else:
            self.order = list(range(expert_count))

    def send(self, value, distance):
        pairs = [
            (self.order[i], self.order[(i + distance) % self.count]) for i in range(self.count)
        ]
        return lax.ppermute(value, "expert", pairs)

    def device_at(self, distance):
        here = lax.axis_index("expert")
        count = self.count
        if self.snake:
            here = jnp.where(here % 2 == 0, here // 2, count - 1 - here // 2)
        there = lax.rem(here + distance % count, count)
        if self.snake:
            there = jnp.where(there < self.half, 2 * there, 2 * (count - 1 - there) + 1)
        return there

    def gather(self, top, bottom, use):
        top_left = top_right = top
        bottom_left = bottom_right = bottom
        use((0,), (top, bottom))
        for step in range(1, self.half):
            top_left = self.send(top_left, 1)
            top_right = self.send(top_right, -1)
            bottom_left = self.send(bottom_left, 1)
            bottom_right = self.send(bottom_right, -1)
            use((-step, step), (top_left, bottom_left, top_right, bottom_right))
        use((self.half,), (self.send(top_left, 1), self.send(bottom_right, -1)))

    def scatter(self, parts):
        most = self.half - 1
        top_left = self.send(parts[self.half][0], 1)
        bottom_right = self.send(parts[self.half][1], -1)
        bottom_left = self.send(parts[most][1], 1)
        top_right = self.send(parts[-most][0], -1)
        for step in range(most, 0, -1):
            top_left = self.send(add(parts[step][0], top_left), 1)
            bottom_right = self.send(add(parts[-step][1], bottom_right), -1)
            if step > 1:
                bottom_left = self.send(add(parts[step - 1][1], bottom_left), 1)
                top_right = self.send(add(parts[1 - step][0], top_right), -1)
        return (top_left, top_right), (bottom_left, bottom_right)

    def scatter_whole(self, ends, parts):
        mid = ends[0].shape[0]

        def half_kernel(first, block_ref, arrived_ref, out_ref):
            added, kept = pl.ds(first, mid), pl.ds(mid - first, mid)
            out_ref[added, :] = (block_ref[added, :] + arrived_ref[...].astype(F32)).astype(BF16)
            out_ref[kept, :] = block_ref[kept, :].astype(BF16)

        left, right = self.send(ends[0], 1), self.send(ends[1], -1)
        for step in range(self.half - 1, 0, -1):
            blocks = parts[step], parts[-step]
            if step == self.half - 1:
                halves = [functools.partial(half_kernel, first) for first in (0, mid)]
                shape = blocks[0].shape
                left, right = [
                    call(kernel, [(shape, BF16)], block, arrived)[0]
                    for kernel, block, arrived in zip(halves, blocks, (left, right))
                ]
            else:
                left, right = add(blocks[0], left), add(blocks[1], right)
            last = left
            left, right = self.send(left, 1), self.send(right, -1)
        return left, right, last

    def part_types(self, distances):
        types = []
        for k in distances:
            first = BF16 if k == self.half or k == 1 - self.half else F32
            second = BF16 if k == self.half or k == self.half - 1 else F32
            types += [first, second]
        return types


def add_kernel(block_ref, arrived_ref, out_ref):
    out_ref[...] = (block_ref[...] + arrived_ref[...].astype(F32)).astype(BF16)


def add(block, arrived):
    return call(add_kernel, [(block.shape, BF16)], block, arrived)[0]


def sum_kernel(*refs):
    out_ref = refs[-1]
    rows = refs[0].shape[0]
    for i in range(len(refs) // 3):
        own, left, right = refs[3 * i : 3 * i + 3]
        arrived = left[...].astype(F32) + right[...].astype(F32)
        out_ref[pl.ds(i * rows, rows), :] = (own[...] + arrived).astype(BF16)


class Copies:
    def __init__(self, sems):
        self.sems, self.started = sems, []

    def start(self, source, target):
        copy = pltpu.make_async_copy(source, target, self.sems.at[len(self.started)])
        copy.start()
        self.started.append(copy)

    def wait(self):
        for copy in self.started:
            copy.wait()


def strips(gate_shape, down_shape):
    local_experts, depth, hidden_dim = gate_shape
    _, height, feature_dim = down_shape
    row, places = 0, []
    for _ in range(local_experts):
        pair = [(row, depth), (row + depth, depth)]
        row += 2 * depth
        downs = []
        for begin in range(0, feature_dim, hidden_dim):
            downs.append((row, height, begin, min(hidden_dim, feature_dim - begin)))
            row += height
        places.append((pair, downs))
    return row, places


def pack(ids, scores, tokens, shards):
    rows, cols = tokens.shape
    mid = rows // 2
    quarter = LANES // 4
    inputs = [ids, scores, tokens, *shards]
    packed_shape, places, count = None, [], 0
    if shards:
        hidden_dim = shards[0].shape[2]
        packed_rows, places = strips(shards[0].shape, shards[2].shape)
        packed_shape = (packed_rows, hidden_dim)
        count = sum(len(pair) + len(downs) for pair, downs in places)

    def kernel(*refs):
        ids_hbm, scores_hbm, tokens_hbm, *shards_hbm = refs[: len(inputs)]
        top_ref, bottom_ref, *packed_refs = refs[len(inputs) : -3]
        ids_ref, scores_ref, sems = refs[-3:]
        copies = Copies(sems)
        copies.start(ids_hbm, ids_ref)
        copies.start(scores_hbm, scores_ref)
        copies.start(tokens_hbm.at[pl.ds(0, mid), :], top_ref.at[:, pl.ds(0, cols)])
        copies.start(tokens_hbm.at[pl.ds(mid, mid), :], bottom_ref)
        for local, (pair, downs) in enumerate(places):
            out_ref = packed_refs[0]
            for source, (row, some) in zip(shards_hbm, pair):
                copies.start(source.at[local], out_ref.at[pl.ds(row, some), :])
            for row, some, begin, width in downs:
                source = shards_hbm[2].at[local, :, pl.ds(begin, width)]
                copies.start(source, out_ref.at[pl.ds(row, some), pl.ds(0, width)])
                if width < hidden_dim:
                    rest = hidden_dim - width
                    out_ref[pl.ds(row, some), pl.ds(width, rest)] = jnp.zeros((some, rest), BF16)
        copies.started[0].wait()
        copies.started[1].wait()
        scores = scores_ref[...]
        ids = ids_ref[...]
        route_weight = scores / jnp.sum(scores, axis=0, keepdims=True)
        expert = lax.broadcasted_iota(jnp.int32, (quarter, rows), 0)
        weight_by = jnp.zeros((quarter, rows), F32)
        for choice_k in range(scores.shape[0]):
            one = slice(choice_k, choice_k + 1)
            weight_by = weight_by + jnp.where(ids[one] == expert, route_weight[one], 0.0)
        high = weight_by.astype(BF16).astype(F32)
        weights = jnp.concatenate([high, weight_by - high] * 2, axis=0).T
        lane = lax.broadcasted_iota(jnp.int32, (mid, LANES), 1)
        both = jnp.where(lane < 2 * quarter, weights[:mid], weights[mid:])
        top_ref[:, cols:] = both.astype(BF16)
        for copy in copies.started[2:]:
            copy.wait()

    outs = [pltpu.VMEM((mid, cols + LANES), BF16), pltpu.VMEM((mid, cols), BF16)]
    if shards:
        outs.append(pltpu.VMEM(packed_shape, BF16))
    return pl.pallas_call(
        kernel,
        out_shape=outs,
        in_specs=[pl.BlockSpec(memory_space=pl.ANY)] * len(inputs),
        out_specs=[pl.BlockSpec(memory_space=pltpu.VMEM)] * len(outs),
        scratch_shapes=[
            pltpu.VMEM(ids.shape, ids.dtype),
            pltpu.VMEM(scores.shape, F32),
            pltpu.SemaphoreType.DMA((4 + count,)),
        ],
        compiler_params=pltpu.CompilerParams(vmem_limit_bytes=VMEM_LIMIT),
    )(*[pltpu.with_memory_space_constraint(a, pltpu.HBM) for a in inputs])


def full_weights(shards, packed):
    local_experts, _, hidden_dim = shards[0].shape
    feature_dim = shards[2].shape[2]
    paired = packed is not None
    _, places = strips(shards[0].shape, shards[2].shape)
    depth, height = shards[0].shape[1], shards[2].shape[1]

    def kernel(*refs):
        gate_hbm, up_hbm, down_hbm, *rest = refs
        wide_ref, down_ref, sems = rest[-3:]
        copies = Copies(sems)
        mine = lax.axis_index("group") if paired else 0

        def wide_at(place, local, is_up):
            rows = pl.ds(pl.multiple_of(place * depth, 16), depth)
            return wide_ref.at[rows, pl.ds((2 * local + is_up) * hidden_dim, hidden_dim)]

        def down_at(place, local, begin, cols):
            top = pl.multiple_of(local * hidden_dim + place * height, 16)
            return down_ref.at[pl.ds(top, height), pl.ds(begin, cols)]

        for local in range(local_experts):
            for is_up, source in enumerate((gate_hbm, up_hbm)):
                copies.start(source.at[local], wide_at(mine, local, is_up))
            copies.start(down_hbm.at[local], down_at(mine, local, 0, feature_dim))
        if paired:
            for local, (pair, downs) in enumerate(places):
                for is_up, (row, some) in enumerate(pair):
                    copies.start(rest[0].at[pl.ds(row, some), :], wide_at(1 - mine, local, is_up))
                for row, some, begin, cols in downs:
                    source = rest[0].at[pl.ds(row, some), pl.ds(0, cols)]
                    copies.start(source, down_at(1 - mine, local, begin, cols))
        copies.wait()

    shards = [pltpu.with_memory_space_constraint(w, pltpu.HBM) for w in shards]
    count = 3 * local_experts
    specs = [pl.BlockSpec(memory_space=pl.ANY)] * 3
    if paired:
        count += sum(len(pair) + len(downs) for pair, downs in places)
        specs.append(pl.BlockSpec(memory_space=pltpu.VMEM))
        shards.append(pltpu.with_memory_space_constraint(packed, pltpu.VMEM))
    return pl.pallas_call(
        kernel,
        out_shape=[
            pltpu.VMEM((feature_dim, 2 * local_experts * hidden_dim), BF16),
            pltpu.VMEM((local_experts * hidden_dim, feature_dim), BF16),
        ],
        in_specs=specs,
        out_specs=[pl.BlockSpec(memory_space=pltpu.VMEM)] * 2,
        scratch_shapes=[pltpu.SemaphoreType.DMA((count,))],
        compiler_params=pltpu.CompilerParams(vmem_limit_bytes=VMEM_LIMIT),
    )(*shards)


def transpose_kernel(from_ref, to_ref):
    strip = 2 * LANES

    @pl.loop(0, to_ref.shape[0] // strip)
    def _(i):
        some = pl.ds(pl.multiple_of(i * strip, strip), strip)
        to_ref[some, :] = from_ref[:, some].T


def transposed(weights):
    rows, cols = weights.shape
    return call(transpose_kernel, [((cols, rows), BF16)], weights)[0]


def body(tokens, w_gate, w_up, w_down, route_ids, route_scores, norm_gain, class_head, targets):
    rows_here, feature_dim = tokens.shape
    expert_count = lax.axis_size("expert")
    group_count = lax.axis_size("group")
    local_experts, _, hidden_dim = w_gate.shape
    pair_dim = 2 * hidden_dim
    ring = Ring(expert_count, group_count)
    block = (rows_here, feature_dim)
    mid = rows_here // 2

    shards = [w_gate, w_up, w_down]
    if group_count == 2:
        top, bottom, packed = pack(route_ids.T, route_scores.T, tokens, shards)
        packed = lax.ppermute(packed, "group", [(0, 1), (1, 0)])
    else:
        top, bottom = pack(route_ids.T, route_scores.T, tokens, [])
        shards = [lax.all_gather(w, "group", axis=1, tiled=True) for w in shards]
        packed = None
    wide, down = full_weights(shards, packed)

    def rows_of(refs):
        return jnp.concatenate([ref[...] for ref in refs], axis=0) if len(refs) > 1 else refs[0][...]

    def forward_kernel(count, *refs):
        token_refs, (wide_ref, down_ref) = refs[:count], refs[count : count + 2]
        outs = refs[count + 2 :]
        x = rows_of([ref.at[:, :feature_dim] for ref in token_refs])
        weights = jnp.concatenate([ref[:, feature_dim:] for ref in token_refs[::2]], axis=0).astype(F32)
        lane = lax.broadcasted_iota(jnp.int32, weights.shape, 1)
        quarter = LANES // 4
        hidden = []
        for local in range(local_experts):
            expert = lax.axis_index("expert") * local_experts + local
            scales = []
            for begin in (expert, expert + 2 * quarter):
                here = (lane == begin) | (lane == begin + quarter)
                scales.append(jnp.sum(jnp.where(here, weights, 0.0), axis=1, keepdims=True))
            pieces = [s[i : i + mid] for i in range(0, weights.shape[0], mid) for s in scales]
            scale = jnp.concatenate(pieces, axis=0)
            act = dot(x, wide_ref[:, pl.ds(local * pair_dim, pair_dim)])
            gate_act, up_act = act[:, :hidden_dim], act[:, hidden_dim:]
            sigmoid_gate = jax.nn.sigmoid(gate_act)
            silu = gate_act * sigmoid_gate * scale
            slope = sigmoid_gate * (1.0 + gate_act * (1.0 - sigmoid_gate)) * scale
            cols = pl.ds(local * hidden_dim, hidden_dim)
            outs[0][:, cols] = (up_act * slope).astype(BF16)
            outs[1][:, cols] = silu.astype(BF16)
            hidden.append((silu * up_act).astype(BF16))
        total = dot(jnp.concatenate(hidden, axis=1), down_ref[...])
        for i, out in enumerate(outs[2:]):
            out[...] = total[i * mid : (i + 1) * mid].astype(out.dtype)

    tokens_at, saved_at, part_at = {}, {}, {}
    flops = 2 * rows_here * feature_dim * hidden_dim * local_experts * 3

    def hold(distances, blocks):
        tokens_at[distances] = blocks

    def keep_parts(parts, distances, halves):
        parts.update({k: halves[2 * i : 2 * i + 2] for i, k in enumerate(distances)})

    def part_outs(distances):
        return [((mid, feature_dim), dtype) for dtype in ring.part_types(distances)]

    def forward(distances):
        blocks = tokens_at[distances]
        rows = mid * len(blocks)
        result = call(
            functools.partial(forward_kernel, len(blocks)),
            [((rows, local_experts * hidden_dim), BF16)] * 2 + part_outs(distances),
            *blocks,
            wide,
            down,
            flops=flops * rows // rows_here,
        )
        saved_at[distances] = result[:2]
        keep_parts(part_at, distances, result[2:])

    ring.gather(top, bottom, hold)
    for distances in tokens_at:
        forward(distances)
    gain = norm_gain.reshape(1, feature_dim)
    half_shape = (mid, feature_dim)
    moe_top, moe_bottom = [
        call(sum_kernel, [(half_shape, BF16)], own, *arrived)[0]
        for own, arrived in zip(part_at[0], ring.scatter(part_at))
    ]

    norm_at, mean_at = {}, {}

    def residual_of(token_refs, moe_refs):
        token_rows = rows_of([ref.at[:, :feature_dim] for ref in token_refs]).astype(F32)
        return token_rows + rows_of(moe_refs).astype(F32)

    def inv_rms_of(residual):
        return lax.rsqrt(jnp.mean(residual * residual, axis=-1, keepdims=True) + NORM_EPS)

    def norm_kernel(distances, count, *refs):
        residual = residual_of(refs[:count], refs[count : 2 * count])
        gain_ref, so_far, out_ref, residual_ref, inv_ref = refs[2 * count :]
        inv_rms = inv_rms_of(residual)
        residual_ref[...] = residual
        inv_ref[...] = jnp.broadcast_to(inv_rms, inv_ref.shape)
        normed = residual * inv_rms * gain_ref[...]
        pooled = so_far[...]
        row = lax.broadcasted_iota(jnp.int32, pooled.shape, 0)
        for i, k in enumerate(distances):
            part = normed[i * rows_here : (i + 1) * rows_here]
            mean = jnp.mean(part, axis=0, keepdims=True)
            pooled = jnp.where(row == ring.device_at(k), mean, pooled)
        out_ref[...] = pooled

    pooled_shape = (expert_count, feature_dim)
    mean_at["pooled"] = jnp.zeros(pooled_shape, F32)

    def norm(distances, blocks):
        rows = mid * len(blocks)
        mean_at["pooled"], *norm_at[distances] = call(
            functools.partial(norm_kernel, distances, len(blocks)),
            [(pooled_shape, F32), ((rows, feature_dim), F32), ((rows, LANES), F32)],
            *tokens_at[distances],
            *blocks,
            gain,
            mean_at["pooled"],
        )

    ring.gather(moe_top, moe_bottom, norm)
    pooled = mean_at["pooled"].astype(BF16)
    logits = dot(pooled, class_head)
    target_rows = targets.reshape(expert_count, -1).astype(F32)
    logit_grad = (LOSS_SCALE * (jax.nn.sigmoid(logits) - target_rows)).astype(BF16)
    pooled_grad = dot_t(logit_grad, class_head)
    span = 2
    for masks in ([1], list(range(span, expert_count, span))):
        mine = pooled_grad.astype(BF16)
        pooled_grad = mine.astype(F32)
        for mask in masks:
            pairs = [(e, e ^ mask) for e in range(expert_count)]
            pooled_grad = pooled_grad + lax.ppermute(mine, "expert", pairs).astype(F32)

    def backward_kernel(distances, residual_ref, inv_ref, gate_save, up_save, *refs):
        grad_ref, gain_ref, wide_ref, down_ref, *outs = refs
        residual, inv_rms = residual_ref[...], inv_ref[:, :1]
        cube = inv_rms * inv_rms * inv_rms
        parts = []
        for i, k in enumerate(distances):
            rows = slice(i * rows_here, (i + 1) * rows_here)
            scaled = gain_ref[...] * grad_ref[pl.ds(ring.device_at(k), 1), :] / rows_here
            slope = cube[rows] * jnp.mean(residual[rows] * scaled, axis=-1, keepdims=True)
            parts.append(inv_rms[rows] * scaled - residual[rows] * slope)
        resid_grad = jnp.concatenate(parts, axis=0) if len(parts) > 1 else parts[0]
        down_back = dot(resid_grad.astype(BF16), down_ref[...])
        grads = []
        for local in range(local_experts):
            cols = slice(local * hidden_dim, (local + 1) * hidden_dim)
            for save in (gate_save, up_save):
                grads.append((down_back[:, cols] * save[:, cols].astype(F32)).astype(BF16))
        total = dot(jnp.concatenate(grads, axis=1), wide_ref[...])
        if distances == (0,):
            total = total + resid_grad
        rows = total.shape[0] // len(outs)
        for i, out in enumerate(outs):
            out[...] = total[i * rows : (i + 1) * rows].astype(out.dtype)

    wide_t, down_t = transposed(wide), transposed(down)
    back_at = {}

    def backward(distances):
        if distances == (ring.half,):
            outs = [((mid, feature_dim), BF16)] * 2
        else:
            outs = [(block, F32)] * len(distances)
        result = call(
            functools.partial(backward_kernel, distances),
            outs,
            *norm_at[distances],
            *saved_at[distances],
            pooled_grad,
            gain,
            wide_t,
            down_t,
            flops=flops * len(distances),
        )
        if distances == (ring.half,):
            back_at["ends"] = result
        else:
            back_at.update(zip(distances, result))

    for distances in reversed(list(tokens_at)):
        backward(distances)
    left, right, last = ring.scatter_whole(back_at["ends"], back_at)
    token_grad = pl.pallas_call(
        sum_kernel,
        out_shape=jax.ShapeDtypeStruct(block, BF16),
        in_specs=[pl.BlockSpec(memory_space=pltpu.VMEM)] * 3,
        out_specs=pl.BlockSpec(memory_space=pltpu.VMEM),
        compiler_params=pltpu.CompilerParams(vmem_limit_bytes=VMEM_LIMIT),
    )(back_at[0], left, right)

    both = after(jnp.concatenate([pooled, logit_grad], axis=1), last)
    if group_count == 2:
        both = jnp.concatenate([both, lax.ppermute(both, "group", [(0, 1), (1, 0)])], axis=0)
    else:
        both = lax.all_gather(both, "group", axis=0, tiled=True)
    head_grad = lax.dot_general(
        both[:, :feature_dim],
        both[:, feature_dim:],
        (((0,), (0,)), ((), ())),
        preferred_element_type=F32,
    )
    return (token_grad, head_grad)


def solution(mesh):
    in_specs = (
        P(("rep", "expert", "group"), None),
        P("expert", "group", None),
        P("expert", "group", None),
        P("expert", "group", None),
        P(("rep", "expert", "group"), None),
        P(("rep", "expert", "group"), None),
        P(),
        P(None, "expert"),
        P("rep", "group", "expert"),
    )
    out_specs = (P(("rep", "expert", "group"), None), P("rep", "expert"))
    return jax.shard_map(body, mesh=mesh, in_specs=in_specs, out_specs=out_specs, check_vma=False)
```

```python
import functools

import jax
import jax.numpy as jnp
from jax import lax
from jax.experimental import pallas as pl
from jax.experimental.pallas import tpu as pltpu
from jax.sharding import PartitionSpec as P

LOSS_SCALE = 8.0
NORM_EPS = 1e-06
F32 = jnp.float32
BF16 = jnp.bfloat16
LANES = 128
VMEM_LIMIT = 32 * 1024 * 1024


def dot(left, right):
    return jnp.dot(left, right, preferred_element_type=F32)


def dot_t(left, right):
    return lax.dot_general(left, right, (((1,), (1,)), ((), ())), preferred_element_type=F32)


def call(kernel, outs, *args, flops=0):
    args = [pltpu.with_memory_space_constraint(a, pltpu.VMEM) for a in args]
    size = sum(a.size * a.dtype.itemsize for a in args)
    return pl.pallas_call(
        kernel,
        out_shape=[pltpu.VMEM(shape, dtype) for shape, dtype in outs],
        in_specs=[pl.BlockSpec(memory_space=pltpu.VMEM)] * len(args),
        out_specs=[pl.BlockSpec(memory_space=pltpu.VMEM)] * len(outs),
        compiler_params=pltpu.CompilerParams(vmem_limit_bytes=VMEM_LIMIT),
        cost_estimate=pl.CostEstimate(flops=flops, bytes_accessed=size, transcendentals=0),
    )(*args)


def after(value, guard):
    def kernel(value_ref, guard_ref, out_ref):
        pass

    args = [pltpu.with_memory_space_constraint(a, pltpu.VMEM) for a in (value, guard)]
    return pl.pallas_call(
        kernel,
        out_shape=pltpu.VMEM(value.shape, value.dtype),
        in_specs=[pl.BlockSpec(memory_space=pltpu.VMEM)] * 2,
        out_specs=pl.BlockSpec(memory_space=pltpu.VMEM),
        input_output_aliases={0: 0},
        compiler_params=pltpu.CompilerParams(vmem_limit_bytes=VMEM_LIMIT),
    )(*args)


class Ring:
    def __init__(self, expert_count, group_count):
        self.count = expert_count
        self.half = expert_count // 2
        self.snake = group_count == 2
        if self.snake:
            self.order = list(range(0, expert_count, 2)) + list(range(expert_count - 1, 0, -2))
        else:
            self.order = list(range(expert_count))

    def send(self, value, distance):
        pairs = [
            (self.order[i], self.order[(i + distance) % self.count]) for i in range(self.count)
        ]
        return lax.ppermute(value, "expert", pairs)

    def device_at(self, distance):
        here = lax.axis_index("expert")
        count = self.count
        if self.snake:
            here = jnp.where(here % 2 == 0, here // 2, count - 1 - here // 2)
        there = lax.rem(here + distance % count, count)
        if self.snake:
            there = jnp.where(there < self.half, 2 * there, 2 * (count - 1 - there) + 1)
        return there

    def gather(self, top, bottom, use):
        top_left = top_right = top
        bottom_left = bottom_right = bottom
        use((0,), (top, bottom))
        for step in range(1, self.half):
            top_left = self.send(top_left, 1)
            top_right = self.send(top_right, -1)
            bottom_left = self.send(bottom_left, 1)
            bottom_right = self.send(bottom_right, -1)
            use((-step, step), (top_left, bottom_left, top_right, bottom_right))
        use((self.half,), (self.send(top_left, 1), self.send(bottom_right, -1)))

    def scatter(self, ends, parts):
        mid = ends[0].shape[0]

        def half_kernel(first, block_ref, arrived_ref, out_ref):
            added, kept = pl.ds(first, mid), pl.ds(mid - first, mid)
            out_ref[added, :] = (block_ref[added, :] + arrived_ref[...].astype(F32)).astype(BF16)
            out_ref[kept, :] = block_ref[kept, :].astype(BF16)

        def right_kernel(first, block_ref, arrived_ref, guard_ref, out_ref):
            if arrived_ref.shape[0] == mid:
                half_kernel(first, block_ref, arrived_ref, out_ref)
            else:
                add_kernel(block_ref, arrived_ref, out_ref)

        most = self.half - 1
        from_right = self.send(ends[1], -1)
        from_left = self.send(after(ends[0], parts[max(most - 1, 0)]), 1)
        for step in range(most, 0, -1):
            shape = [(parts[step].shape, BF16)]
            kernel = functools.partial(half_kernel, mid) if step == most else add_kernel
            leftward = call(kernel, shape, parts[-step], from_right)[0]
            from_right = self.send(leftward, -1)
            kernel = functools.partial(right_kernel, 0)
            rightward = call(kernel, shape, parts[step], from_left, parts[max(step - 2, 0)])[0]
            from_left = self.send(rightward, 1)
        return from_left, from_right, rightward


def add_kernel(block_ref, arrived_ref, out_ref):
    out_ref[...] = (block_ref[...] + arrived_ref[...].astype(F32)).astype(BF16)


def add(block, arrived):
    return call(add_kernel, [(block.shape, BF16)], block, arrived)[0]


def sum_kernel(own_ref, left_ref, right_ref, *outs):
    arrived = left_ref[...].astype(F32) + right_ref[...].astype(F32)
    total = (own_ref[...] + arrived).astype(BF16)
    rows = total.shape[0] // len(outs)
    for i, out in enumerate(outs):
        out[...] = total[i * rows : (i + 1) * rows]


class Copies:
    def __init__(self, sems):
        self.sems, self.started = sems, []

    def start(self, source, target):
        copy = pltpu.make_async_copy(source, target, self.sems.at[len(self.started)])
        copy.start()
        self.started.append(copy)

    def wait(self):
        for copy in self.started:
            copy.wait()


def strips(gate_shape, down_shape):
    local_experts, depth, hidden_dim = gate_shape
    _, height, feature_dim = down_shape
    row, places = 0, []
    for _ in range(local_experts):
        pair = [(row, depth), (row + depth, depth)]
        row += 2 * depth
        downs = []
        for begin in range(0, feature_dim, hidden_dim):
            downs.append((row, height, begin, min(hidden_dim, feature_dim - begin)))
            row += height
        places.append((pair, downs))
    return row, places


def pack(ids, scores, tokens, shards):
    rows, cols = tokens.shape
    mid = rows // 2
    quarter = LANES // 4
    inputs = [ids, scores, tokens, *shards]
    packed_shape, places, count = None, [], 0
    if shards:
        hidden_dim = shards[0].shape[2]
        packed_rows, places = strips(shards[0].shape, shards[2].shape)
        packed_shape = (packed_rows, hidden_dim)
        count = sum(len(pair) + len(downs) for pair, downs in places)

    def kernel(*refs):
        ids_hbm, scores_hbm, tokens_hbm, *shards_hbm = refs[: len(inputs)]
        top_ref, bottom_ref, *packed_refs = refs[len(inputs) : -3]
        ids_ref, scores_ref, sems = refs[-3:]
        copies = Copies(sems)
        copies.start(ids_hbm, ids_ref)
        copies.start(scores_hbm, scores_ref)
        copies.start(tokens_hbm.at[pl.ds(0, mid), :], top_ref.at[:, pl.ds(0, cols)])
        copies.start(tokens_hbm.at[pl.ds(mid, mid), :], bottom_ref)
        for local, (pair, downs) in enumerate(places):
            out_ref = packed_refs[0]
            for source, (row, some) in zip(shards_hbm, pair):
                copies.start(source.at[local], out_ref.at[pl.ds(row, some), :])
            for row, some, begin, width in downs:
                source = shards_hbm[2].at[local, :, pl.ds(begin, width)]
                copies.start(source, out_ref.at[pl.ds(row, some), pl.ds(0, width)])
                if width < hidden_dim:
                    rest = hidden_dim - width
                    out_ref[pl.ds(row, some), pl.ds(width, rest)] = jnp.zeros((some, rest), BF16)
        copies.started[0].wait()
        copies.started[1].wait()
        scores = scores_ref[...]
        ids = ids_ref[...]
        route_weight = scores / jnp.sum(scores, axis=0, keepdims=True)
        expert = lax.broadcasted_iota(jnp.int32, (quarter, rows), 0)
        weight_by = jnp.zeros((quarter, rows), F32)
        for choice_k in range(scores.shape[0]):
            one = slice(choice_k, choice_k + 1)
            weight_by = weight_by + jnp.where(ids[one] == expert, route_weight[one], 0.0)
        high = weight_by.astype(BF16).astype(F32)
        weights = jnp.concatenate([high, weight_by - high] * 2, axis=0).T
        lane = lax.broadcasted_iota(jnp.int32, (mid, LANES), 1)
        both = jnp.where(lane < 2 * quarter, weights[:mid], weights[mid:])
        top_ref[:, cols:] = both.astype(BF16)
        for copy in copies.started[2:]:
            copy.wait()

    outs = [pltpu.VMEM((mid, cols + LANES), BF16), pltpu.VMEM((mid, cols), BF16)]
    if shards:
        outs.append(pltpu.VMEM(packed_shape, BF16))
    return pl.pallas_call(
        kernel,
        out_shape=outs,
        in_specs=[pl.BlockSpec(memory_space=pl.ANY)] * len(inputs),
        out_specs=[pl.BlockSpec(memory_space=pltpu.VMEM)] * len(outs),
        scratch_shapes=[
            pltpu.VMEM(ids.shape, ids.dtype),
            pltpu.VMEM(scores.shape, F32),
            pltpu.SemaphoreType.DMA((4 + count,)),
        ],
        compiler_params=pltpu.CompilerParams(vmem_limit_bytes=VMEM_LIMIT),
    )(*[pltpu.with_memory_space_constraint(a, pltpu.HBM) for a in inputs])


def full_weights(shards, packed):
    local_experts, _, hidden_dim = shards[0].shape
    feature_dim = shards[2].shape[2]
    paired = packed is not None
    _, places = strips(shards[0].shape, shards[2].shape)
    depth, height = shards[0].shape[1], shards[2].shape[1]

    def kernel(*refs):
        gate_hbm, up_hbm, down_hbm, *rest = refs
        wide_ref, down_ref, sems = rest[-3:]
        copies = Copies(sems)
        mine = lax.axis_index("group") if paired else 0

        def wide_at(place, local, is_up):
            rows = pl.ds(pl.multiple_of(place * depth, 16), depth)
            return wide_ref.at[rows, pl.ds((2 * local + is_up) * hidden_dim, hidden_dim)]

        def down_at(place, local, begin, cols):
            top = pl.multiple_of(local * hidden_dim + place * height, 16)
            return down_ref.at[pl.ds(top, height), pl.ds(begin, cols)]

        for local in range(local_experts):
            for is_up, source in enumerate((gate_hbm, up_hbm)):
                copies.start(source.at[local], wide_at(mine, local, is_up))
            copies.start(down_hbm.at[local], down_at(mine, local, 0, feature_dim))
        if paired:
            for local, (pair, downs) in enumerate(places):
                for is_up, (row, some) in enumerate(pair):
                    copies.start(rest[0].at[pl.ds(row, some), :], wide_at(1 - mine, local, is_up))
                for row, some, begin, cols in downs:
                    source = rest[0].at[pl.ds(row, some), pl.ds(0, cols)]
                    copies.start(source, down_at(1 - mine, local, begin, cols))
        copies.wait()

    shards = [pltpu.with_memory_space_constraint(w, pltpu.HBM) for w in shards]
    count = 3 * local_experts
    specs = [pl.BlockSpec(memory_space=pl.ANY)] * 3
    if paired:
        count += sum(len(pair) + len(downs) for pair, downs in places)
        specs.append(pl.BlockSpec(memory_space=pltpu.VMEM))
        shards.append(pltpu.with_memory_space_constraint(packed, pltpu.VMEM))
    return pl.pallas_call(
        kernel,
        out_shape=[
            pltpu.VMEM((feature_dim, 2 * local_experts * hidden_dim), BF16),
            pltpu.VMEM((local_experts * hidden_dim, feature_dim), BF16),
        ],
        in_specs=specs,
        out_specs=[pl.BlockSpec(memory_space=pltpu.VMEM)] * 2,
        scratch_shapes=[pltpu.SemaphoreType.DMA((count,))],
        compiler_params=pltpu.CompilerParams(vmem_limit_bytes=VMEM_LIMIT),
    )(*shards)


def transpose_kernel(from_ref, to_ref):
    strip = 2 * LANES

    @pl.loop(0, to_ref.shape[0] // strip)
    def _(i):
        some = pl.ds(pl.multiple_of(i * strip, strip), strip)
        to_ref[some, :] = from_ref[:, some].T


def transposed(weights):
    rows, cols = weights.shape
    return call(transpose_kernel, [((cols, rows), BF16)], weights)[0]


def body(tokens, w_gate, w_up, w_down, route_ids, route_scores, norm_gain, class_head, targets):
    rows_here, feature_dim = tokens.shape
    expert_count = lax.axis_size("expert")
    group_count = lax.axis_size("group")
    local_experts, _, hidden_dim = w_gate.shape
    pair_dim = 2 * hidden_dim
    ring = Ring(expert_count, group_count)
    block = (rows_here, feature_dim)
    mid = rows_here // 2

    shards = [w_gate, w_up, w_down]
    if group_count == 2:
        top, bottom, packed = pack(route_ids.T, route_scores.T, tokens, shards)
        packed = lax.ppermute(packed, "group", [(0, 1), (1, 0)])
    else:
        top, bottom = pack(route_ids.T, route_scores.T, tokens, [])
        shards = [lax.all_gather(w, "group", axis=1, tiled=True) for w in shards]
        packed = None
    wide, down = full_weights(shards, packed)

    def rows_of(refs):
        return jnp.concatenate([ref[...] for ref in refs], axis=0) if len(refs) > 1 else refs[0][...]

    def forward_kernel(count, *refs):
        token_refs, (wide_ref, down_ref) = refs[:count], refs[count : count + 2]
        outs = refs[count + 2 :]
        x = rows_of([ref.at[:, :feature_dim] for ref in token_refs])
        weights = jnp.concatenate([ref[:, feature_dim:] for ref in token_refs[::2]], axis=0).astype(F32)
        lane = lax.broadcasted_iota(jnp.int32, weights.shape, 1)
        quarter = LANES // 4
        hidden = []
        for local in range(local_experts):
            expert = lax.axis_index("expert") * local_experts + local
            scales = []
            for begin in (expert, expert + 2 * quarter):
                here = (lane == begin) | (lane == begin + quarter)
                scales.append(jnp.sum(jnp.where(here, weights, 0.0), axis=1, keepdims=True))
            pieces = [s[i : i + mid] for i in range(0, weights.shape[0], mid) for s in scales]
            scale = jnp.concatenate(pieces, axis=0)
            act = dot(x, wide_ref[:, pl.ds(local * pair_dim, pair_dim)])
            gate_act, up_act = act[:, :hidden_dim], act[:, hidden_dim:]
            sigmoid_gate = jax.nn.sigmoid(gate_act)
            silu = gate_act * sigmoid_gate * scale
            slope = sigmoid_gate * (1.0 + gate_act * (1.0 - sigmoid_gate)) * scale
            cols = pl.ds(local * hidden_dim, hidden_dim)
            outs[0][:, cols] = (up_act * slope).astype(BF16)
            outs[1][:, cols] = silu.astype(BF16)
            hidden.append((silu * up_act).astype(BF16))
        total = dot(jnp.concatenate(hidden, axis=1), down_ref[...])
        rows = total.shape[0] // len(outs[2:])
        for i, out in enumerate(outs[2:]):
            out[...] = total[i * rows : (i + 1) * rows].astype(out.dtype)

    tokens_at, saved_at, part_at = {}, {}, {}
    flops = 2 * rows_here * feature_dim * hidden_dim * local_experts * 3

    def hold(distances, blocks):
        tokens_at[distances] = blocks

    def part_outs(distances):
        if distances == (ring.half,):
            return [((mid, feature_dim), BF16)] * 2
        return [(block, F32)] * len(distances)

    def keep_parts(parts, distances, results):
        if distances == (ring.half,):
            parts["ends"] = results
        else:
            parts.update(zip(distances, results))

    def forward(distances):
        blocks = tokens_at[distances]
        rows = mid * len(blocks)
        result = call(
            functools.partial(forward_kernel, len(blocks)),
            [((rows, local_experts * hidden_dim), BF16)] * 2 + part_outs(distances),
            *blocks,
            wide,
            down,
            flops=flops * rows // rows_here,
        )
        saved_at[distances] = result[:2]
        keep_parts(part_at, distances, result[2:])

    ring.gather(top, bottom, hold)
    for distances in tokens_at:
        forward(distances)
    gain = norm_gain.reshape(1, feature_dim)
    from_left, from_right, _ = ring.scatter(part_at["ends"], part_at)
    halves = [((mid, feature_dim), BF16)] * 2
    moe_top, moe_bottom = call(sum_kernel, halves, part_at[0], from_left, from_right)

    norm_at, mean_at = {}, {}

    def residual_of(token_refs, moe_refs):
        token_rows = rows_of([ref.at[:, :feature_dim] for ref in token_refs]).astype(F32)
        return token_rows + rows_of(moe_refs).astype(F32)

    def inv_rms_of(residual):
        return lax.rsqrt(jnp.mean(residual * residual, axis=-1, keepdims=True) + NORM_EPS)

    def norm_kernel(distances, count, *refs):
        residual = residual_of(refs[:count], refs[count : 2 * count])
        gain_ref, so_far, out_ref, residual_ref, inv_ref = refs[2 * count :]
        inv_rms = inv_rms_of(residual)
        residual_ref[...] = residual
        inv_ref[...] = jnp.broadcast_to(inv_rms, inv_ref.shape)
        normed = residual * inv_rms * gain_ref[...]
        pooled = so_far[...]
        row = lax.broadcasted_iota(jnp.int32, pooled.shape, 0)
        for i, k in enumerate(distances):
            part = normed[i * rows_here : (i + 1) * rows_here]
            mean = jnp.mean(part, axis=0, keepdims=True)
            pooled = jnp.where(row == ring.device_at(k), mean, pooled)
        out_ref[...] = pooled

    pooled_shape = (expert_count, feature_dim)
    mean_at["pooled"] = jnp.zeros(pooled_shape, F32)

    def norm(distances, blocks):
        rows = mid * len(blocks)
        mean_at["pooled"], *norm_at[distances] = call(
            functools.partial(norm_kernel, distances, len(blocks)),
            [(pooled_shape, F32), ((rows, feature_dim), F32), ((rows, LANES), F32)],
            *tokens_at[distances],
            *blocks,
            gain,
            mean_at["pooled"],
        )

    ring.gather(moe_top, moe_bottom, norm)
    pooled = mean_at["pooled"].astype(BF16)
    logits = dot(pooled, class_head)
    target_rows = targets.reshape(expert_count, -1).astype(F32)
    logit_grad = (LOSS_SCALE * (jax.nn.sigmoid(logits) - target_rows)).astype(BF16)
    pooled_grad = dot_t(logit_grad, class_head)
    span = 2
    for masks in ([1], list(range(span, expert_count, span))):
        mine = pooled_grad.astype(BF16)
        pooled_grad = mine.astype(F32)
        for mask in masks:
            pairs = [(e, e ^ mask) for e in range(expert_count)]
            pooled_grad = pooled_grad + lax.ppermute(mine, "expert", pairs).astype(F32)

    def backward_kernel(distances, residual_ref, inv_ref, gate_save, up_save, *refs):
        grad_ref, gain_ref, wide_ref, down_ref, *outs = refs
        residual, inv_rms = residual_ref[...], inv_ref[:, :1]
        cube = inv_rms * inv_rms * inv_rms
        parts = []
        for i, k in enumerate(distances):
            rows = slice(i * rows_here, (i + 1) * rows_here)
            scaled = gain_ref[...] * grad_ref[pl.ds(ring.device_at(k), 1), :] / rows_here
            slope = cube[rows] * jnp.mean(residual[rows] * scaled, axis=-1, keepdims=True)
            parts.append(inv_rms[rows] * scaled - residual[rows] * slope)
        resid_grad = jnp.concatenate(parts, axis=0) if len(parts) > 1 else parts[0]
        down_back = dot(resid_grad.astype(BF16), down_ref[...])
        grads = []
        for local in range(local_experts):
            cols = slice(local * hidden_dim, (local + 1) * hidden_dim)
            for save in (gate_save, up_save):
                grads.append((down_back[:, cols] * save[:, cols].astype(F32)).astype(BF16))
        total = dot(jnp.concatenate(grads, axis=1), wide_ref[...])
        if distances == (0,):
            total = total + resid_grad
        rows = total.shape[0] // len(outs)
        for i, out in enumerate(outs):
            out[...] = total[i * rows : (i + 1) * rows].astype(out.dtype)

    wide_t, down_t = transposed(wide), transposed(down)
    back_at = {}

    def backward(distances):
        result = call(
            functools.partial(backward_kernel, distances),
            part_outs(distances),
            *norm_at[distances],
            *saved_at[distances],
            pooled_grad,
            gain,
            wide_t,
            down_t,
            flops=flops * len(distances),
        )
        keep_parts(back_at, distances, result)

    for distances in reversed(list(tokens_at)):
        backward(distances)
    from_left, from_right, last = ring.scatter(back_at["ends"], back_at)
    token_grad = pl.pallas_call(
        sum_kernel,
        out_shape=jax.ShapeDtypeStruct(block, BF16),
        in_specs=[pl.BlockSpec(memory_space=pltpu.VMEM)] * 3,
        out_specs=pl.BlockSpec(memory_space=pltpu.VMEM),
        compiler_params=pltpu.CompilerParams(vmem_limit_bytes=VMEM_LIMIT),
    )(back_at[0], from_left, from_right)

    both = after(jnp.concatenate([pooled, logit_grad], axis=1), last)
    if group_count == 2:
        both = jnp.concatenate([both, lax.ppermute(both, "group", [(0, 1), (1, 0)])], axis=0)
    else:
        both = lax.all_gather(both, "group", axis=0, tiled=True)
    head_grad = lax.dot_general(
        both[:, :feature_dim],
        both[:, feature_dim:],
        (((0,), (0,)), ((), ())),
        preferred_element_type=F32,
    )
    return (token_grad, head_grad)


def solution(mesh):
    in_specs = (
        P(("rep", "expert", "group"), None),
        P("expert", "group", None),
        P("expert", "group", None),
        P("expert", "group", None),
        P(("rep", "expert", "group"), None),
        P(("rep", "expert", "group"), None),
        P(),
        P(None, "expert"),
        P("rep", "group", "expert"),
    )
    out_specs = (P(("rep", "expert", "group"), None), P("rep", "expert"))
    return jax.shard_map(body, mesh=mesh, in_specs=in_specs, out_specs=out_specs, check_vma=False)
```

```python
import functools

import jax
import jax.numpy as jnp
from jax import lax
from jax.experimental import pallas as pl
from jax.experimental.pallas import tpu as pltpu
from jax.sharding import PartitionSpec as P

LOSS_SCALE = 8.0
NORM_EPS = 1e-06
F32 = jnp.float32
BF16 = jnp.bfloat16
LANES = 128
VMEM_LIMIT = 32 * 1024 * 1024


def dot(left, right):
    return jnp.dot(left, right, preferred_element_type=F32)


def dot_t(left, right):
    return lax.dot_general(left, right, (((1,), (1,)), ((), ())), preferred_element_type=F32)


def call(kernel, outs, *args, flops=0):
    args = [pltpu.with_memory_space_constraint(a, pltpu.VMEM) for a in args]
    size = sum(a.size * a.dtype.itemsize for a in args)
    return pl.pallas_call(
        kernel,
        out_shape=[pltpu.VMEM(shape, dtype) for shape, dtype in outs],
        in_specs=[pl.BlockSpec(memory_space=pltpu.VMEM)] * len(args),
        out_specs=[pl.BlockSpec(memory_space=pltpu.VMEM)] * len(outs),
        compiler_params=pltpu.CompilerParams(vmem_limit_bytes=VMEM_LIMIT),
        cost_estimate=pl.CostEstimate(flops=flops, bytes_accessed=size, transcendentals=0),
    )(*args)


class Ring:
    def __init__(self, expert_count, group_count):
        self.count = expert_count
        self.half = expert_count // 2
        self.snake = group_count == 2
        if self.snake:
            self.order = list(range(0, expert_count, 2)) + list(range(expert_count - 1, 0, -2))
        else:
            self.order = list(range(expert_count))

    def send(self, value, distance):
        pairs = [
            (self.order[i], self.order[(i + distance) % self.count]) for i in range(self.count)
        ]
        return lax.ppermute(value, "expert", pairs)

    def device_at(self, distance):
        here = lax.axis_index("expert")
        count = self.count
        if self.snake:
            here = jnp.where(here % 2 == 0, here // 2, count - 1 - here // 2)
        there = lax.rem(here + distance % count, count)
        if self.snake:
            there = jnp.where(there < self.half, 2 * there, 2 * (count - 1 - there) + 1)
        return there

    def gather(self, top, bottom, use):
        top_left = top_right = top
        bottom_left = bottom_right = bottom
        use((0,), (top, bottom))
        for step in range(1, self.half):
            top_left = self.send(top_left, 1)
            top_right = self.send(top_right, -1)
            bottom_left = self.send(bottom_left, 1)
            bottom_right = self.send(bottom_right, -1)
            use((-step, step), (top_left, bottom_left, top_right, bottom_right))
        use((self.half,), (self.send(top_left, 1), self.send(bottom_right, -1)))

    def scatter(self, ends, parts):
        mid = ends[0].shape[0]

        def half_kernel(first, block_ref, arrived_ref, out_ref):
            added, kept = pl.ds(first, mid), pl.ds(mid - first, mid)
            out_ref[added, :] = (block_ref[added, :] + arrived_ref[...].astype(F32)).astype(BF16)
            out_ref[kept, :] = block_ref[kept, :].astype(BF16)

        from_right, from_left = self.send(ends[1], -1), self.send(ends[0], 1)
        for step in range(self.half - 1, 0, -1):
            kernels = [add_kernel, add_kernel]
            if step == self.half - 1:
                kernels = [functools.partial(half_kernel, first) for first in (mid, 0)]
            shape = [(parts[step].shape, BF16)]
            leftward = call(kernels[0], shape, parts[-step], from_right)[0]
            from_right = self.send(leftward, -1)
            rightward = call(kernels[1], shape, parts[step], from_left)[0]
            from_left = self.send(rightward, 1)
        return from_left, from_right


def add_kernel(block_ref, arrived_ref, out_ref):
    out_ref[...] = (block_ref[...] + arrived_ref[...].astype(F32)).astype(BF16)


def sum_kernel(own_ref, left_ref, right_ref, *outs):
    arrived = left_ref[...].astype(F32) + right_ref[...].astype(F32)
    total = (own_ref[...] + arrived).astype(BF16)
    rows = total.shape[0] // len(outs)
    for i, out in enumerate(outs):
        out[...] = total[i * rows : (i + 1) * rows]


class Copies:
    def __init__(self, sems):
        self.sems, self.started = sems, []

    def start(self, source, target):
        copy = pltpu.make_async_copy(source, target, self.sems.at[len(self.started)])
        copy.start()
        self.started.append(copy)

    def wait(self):
        for copy in self.started:
            copy.wait()


def strips(gate_shape, down_shape):
    local_experts, depth, hidden_dim = gate_shape
    _, height, feature_dim = down_shape
    row, places = 0, []
    for _ in range(local_experts):
        pair = [(row, depth), (row + depth, depth)]
        row += 2 * depth
        downs = []
        for begin in range(0, feature_dim, hidden_dim):
            downs.append((row, height, begin, min(hidden_dim, feature_dim - begin)))
            row += height
        places.append((pair, downs))
    return row, places


def pack(ids, scores, tokens, shards):
    rows, cols = tokens.shape
    mid = rows // 2
    quarter = LANES // 4
    inputs = [ids, scores, tokens, *shards]
    packed_shape, places, count = None, [], 0
    if shards:
        hidden_dim = shards[0].shape[2]
        packed_rows, places = strips(shards[0].shape, shards[2].shape)
        packed_shape = (packed_rows, hidden_dim)
        count = sum(len(pair) + len(downs) for pair, downs in places)

    def kernel(*refs):
        ids_hbm, scores_hbm, tokens_hbm, *shards_hbm = refs[: len(inputs)]
        top_ref, bottom_ref, *packed_refs = refs[len(inputs) : -3]
        ids_ref, scores_ref, sems = refs[-3:]
        copies = Copies(sems)
        copies.start(ids_hbm, ids_ref)
        copies.start(scores_hbm, scores_ref)
        copies.start(tokens_hbm.at[pl.ds(0, mid), :], top_ref.at[:, pl.ds(0, cols)])
        copies.start(tokens_hbm.at[pl.ds(mid, mid), :], bottom_ref)
        for local, (pair, downs) in enumerate(places):
            out_ref = packed_refs[0]
            for source, (row, some) in zip(shards_hbm, pair):
                copies.start(source.at[local], out_ref.at[pl.ds(row, some), :])
            for row, some, begin, width in downs:
                source = shards_hbm[2].at[local, :, pl.ds(begin, width)]
                copies.start(source, out_ref.at[pl.ds(row, some), pl.ds(0, width)])
                if width < hidden_dim:
                    rest = hidden_dim - width
                    out_ref[pl.ds(row, some), pl.ds(width, rest)] = jnp.zeros((some, rest), BF16)
        copies.started[0].wait()
        copies.started[1].wait()
        scores = scores_ref[...]
        ids = ids_ref[...]
        route_weight = scores / jnp.sum(scores, axis=0, keepdims=True)
        expert = lax.broadcasted_iota(jnp.int32, (quarter, rows), 0)
        weight_by = jnp.zeros((quarter, rows), F32)
        for choice_k in range(scores.shape[0]):
            one = slice(choice_k, choice_k + 1)
            weight_by = weight_by + jnp.where(ids[one] == expert, route_weight[one], 0.0)
        high = weight_by.astype(BF16).astype(F32)
        weights = jnp.concatenate([high, weight_by - high] * 2, axis=0).T
        lane = lax.broadcasted_iota(jnp.int32, (mid, LANES), 1)
        both = jnp.where(lane < 2 * quarter, weights[:mid], weights[mid:])
        top_ref[:, cols:] = both.astype(BF16)
        for copy in copies.started[2:]:
            copy.wait()

    outs = [pltpu.VMEM((mid, cols + LANES), BF16), pltpu.VMEM((mid, cols), BF16)]
    if shards:
        outs.append(pltpu.VMEM(packed_shape, BF16))
    return pl.pallas_call(
        kernel,
        out_shape=outs,
        in_specs=[pl.BlockSpec(memory_space=pl.ANY)] * len(inputs),
        out_specs=[pl.BlockSpec(memory_space=pltpu.VMEM)] * len(outs),
        scratch_shapes=[
            pltpu.VMEM(ids.shape, ids.dtype),
            pltpu.VMEM(scores.shape, F32),
            pltpu.SemaphoreType.DMA((4 + count,)),
        ],
        compiler_params=pltpu.CompilerParams(vmem_limit_bytes=VMEM_LIMIT),
    )(*[pltpu.with_memory_space_constraint(a, pltpu.HBM) for a in inputs])


def full_weights(shards, packed):
    local_experts, _, hidden_dim = shards[0].shape
    feature_dim = shards[2].shape[2]
    paired = packed is not None
    _, places = strips(shards[0].shape, shards[2].shape)
    depth, height = shards[0].shape[1], shards[2].shape[1]

    def kernel(*refs):
        gate_hbm, up_hbm, down_hbm, *rest = refs
        wide_ref, down_ref, sems = rest[-3:]
        copies = Copies(sems)
        mine = lax.axis_index("group") if paired else 0

        def wide_at(place, local, is_up):
            rows = pl.ds(pl.multiple_of(place * depth, 16), depth)
            return wide_ref.at[rows, pl.ds((2 * local + is_up) * hidden_dim, hidden_dim)]

        def down_at(place, local, begin, cols):
            top = pl.multiple_of(local * hidden_dim + place * height, 16)
            return down_ref.at[pl.ds(top, height), pl.ds(begin, cols)]

        for local in range(local_experts):
            for is_up, source in enumerate((gate_hbm, up_hbm)):
                copies.start(source.at[local], wide_at(mine, local, is_up))
            copies.start(down_hbm.at[local], down_at(mine, local, 0, feature_dim))
        if paired:
            for local, (pair, downs) in enumerate(places):
                for is_up, (row, some) in enumerate(pair):
                    copies.start(rest[0].at[pl.ds(row, some), :], wide_at(1 - mine, local, is_up))
                for row, some, begin, cols in downs:
                    source = rest[0].at[pl.ds(row, some), pl.ds(0, cols)]
                    copies.start(source, down_at(1 - mine, local, begin, cols))
        copies.wait()

    shards = [pltpu.with_memory_space_constraint(w, pltpu.HBM) for w in shards]
    count = 3 * local_experts
    specs = [pl.BlockSpec(memory_space=pl.ANY)] * 3
    if paired:
        count += sum(len(pair) + len(downs) for pair, downs in places)
        specs.append(pl.BlockSpec(memory_space=pltpu.VMEM))
        shards.append(pltpu.with_memory_space_constraint(packed, pltpu.VMEM))
    return pl.pallas_call(
        kernel,
        out_shape=[
            pltpu.VMEM((feature_dim, 2 * local_experts * hidden_dim), BF16),
            pltpu.VMEM((local_experts * hidden_dim, feature_dim), BF16),
        ],
        in_specs=specs,
        out_specs=[pl.BlockSpec(memory_space=pltpu.VMEM)] * 2,
        scratch_shapes=[pltpu.SemaphoreType.DMA((count,))],
        compiler_params=pltpu.CompilerParams(vmem_limit_bytes=VMEM_LIMIT),
    )(*shards)


def transpose_kernel(from_ref, to_ref):
    strip = 2 * LANES

    @pl.loop(0, to_ref.shape[0] // strip)
    def _(i):
        some = pl.ds(pl.multiple_of(i * strip, strip), strip)
        to_ref[some, :] = from_ref[:, some].T


def transposed(weights):
    rows, cols = weights.shape
    return call(transpose_kernel, [((cols, rows), BF16)], weights)[0]


def body(tokens, w_gate, w_up, w_down, route_ids, route_scores, norm_gain, class_head, targets):
    rows_here, feature_dim = tokens.shape
    expert_count = lax.axis_size("expert")
    group_count = lax.axis_size("group")
    local_experts, _, hidden_dim = w_gate.shape
    pair_dim = 2 * hidden_dim
    ring = Ring(expert_count, group_count)
    block = (rows_here, feature_dim)
    mid = rows_here // 2

    shards = [w_gate, w_up, w_down]
    if group_count == 2:
        top, bottom, packed = pack(route_ids.T, route_scores.T, tokens, shards)
        packed = lax.ppermute(packed, "group", [(0, 1), (1, 0)])
    else:
        top, bottom = pack(route_ids.T, route_scores.T, tokens, [])
        shards = [lax.all_gather(w, "group", axis=1, tiled=True) for w in shards]
        packed = None
    wide, down = full_weights(shards, packed)

    far, bottom_half, top_half = ring.half, "bottom", "top"
    units = [(bottom_half,), (top_half, 1 - far, far - 1)]
    units += [(-k, k) for k in range(far - 2, 0, -1)] + [(0,)]

    def half_rows(item):
        return {top_half: (0,), bottom_half: (1,)}.get(item, (0, 1))

    def distance_of(item):
        return far if item in (top_half, bottom_half) else item

    def rows_of(unit):
        return sum(mid * len(half_rows(item)) for item in unit)

    def part_outs(unit):
        return [
            ((mid * len(half_rows(item)), feature_dim), F32 if item == distance_of(item) else BF16)
            for item in unit
        ]

    def store_parts(total, unit, outs):
        begin = 0
        for out in outs:
            out[...] = total[begin : begin + out.shape[0]].astype(out.dtype)
            begin += out.shape[0]

    def forward_kernel(unit, *refs):
        wide_ref, down_ref, gate_save, up_save, *outs = refs[2 * len(unit) :]
        rows, scales = [], [[] for _ in range(local_experts)]
        quarter = LANES // 4
        lane = lax.broadcasted_iota(jnp.int32, (mid, LANES), 1)
        for i, item in enumerate(unit):
            top_ref, bottom_ref = refs[2 * i : 2 * i + 2]
            weights = top_ref[:, feature_dim:].astype(F32)
            for half in half_rows(item):
                rows.append(bottom_ref[...] if half else top_ref[:, :feature_dim])
                for local in range(local_experts):
                    begin = lax.axis_index("expert") * local_experts + local + 2 * quarter * half
                    here = (lane == begin) | (lane == begin + quarter)
                    scale = jnp.sum(jnp.where(here, weights, 0.0), axis=1, keepdims=True)
                    scales[local].append(scale)
        x = jnp.concatenate(rows, axis=0) if len(rows) > 1 else rows[0]
        hidden = []
        for local in range(local_experts):
            scale = jnp.concatenate(scales[local], axis=0) if len(rows) > 1 else scales[local][0]
            act = dot(x, wide_ref[:, pl.ds(local * pair_dim, pair_dim)])
            gate_act, up_act = act[:, :hidden_dim], act[:, hidden_dim:]
            sigmoid_gate = jax.nn.sigmoid(gate_act)
            silu = gate_act * sigmoid_gate * scale
            slope = sigmoid_gate * (1.0 + gate_act * (1.0 - sigmoid_gate)) * scale
            cols = pl.ds(local * hidden_dim, hidden_dim)
            gate_save[:, cols] = (up_act * slope).astype(BF16)
            up_save[:, cols] = silu.astype(BF16)
            hidden.append((silu * up_act).astype(BF16))
        store_parts(dot(jnp.concatenate(hidden, axis=1), down_ref[...]), unit, outs)

    tokens_at, saved_at, part_at = {}, {}, {}
    flops = 2 * feature_dim * hidden_dim * local_experts * 3

    def hold(distances, blocks):
        tokens_at.update({k: blocks[2 * i : 2 * i + 2] for i, k in enumerate(distances)})

    ring.gather(top, bottom, hold)
    for unit in units:
        rows = rows_of(unit)
        results = call(
            functools.partial(forward_kernel, unit),
            [((rows, local_experts * hidden_dim), BF16)] * 2 + part_outs(unit),
            *[half for item in unit for half in tokens_at[distance_of(item)]],
            wide,
            down,
            flops=flops * rows,
        )
        saved_at[unit] = results[:2]
        part_at.update(zip(unit, results[2:]))
    gain = norm_gain.reshape(1, feature_dim)
    from_left, from_right = ring.scatter((part_at[top_half], part_at[bottom_half]), part_at)
    halves = [((mid, feature_dim), BF16)] * 2
    moe_top, moe_bottom = call(sum_kernel, halves, part_at[0], from_left, from_right)

    norm_at, mean_at = {}, {}

    def norm_kernel(distances, *refs):
        count = 2 * len(distances)
        tokens_here = [ref[:, :feature_dim].astype(F32) for ref in refs[:count]]
        residual = jnp.concatenate(
            [rows + ref[...].astype(F32) for rows, ref in zip(tokens_here, refs[count : 2 * count])], axis=0
        )
        gain_ref, so_far, out_ref, residual_ref, inv_ref = refs[2 * count :]
        inv_rms = lax.rsqrt(jnp.mean(residual * residual, axis=-1, keepdims=True) + NORM_EPS)
        residual_ref[...] = residual
        inv_ref[...] = jnp.broadcast_to(inv_rms, inv_ref.shape)
        normed = residual * inv_rms * gain_ref[...]
        pooled = so_far[...]
        row = lax.broadcasted_iota(jnp.int32, pooled.shape, 0)
        for i, k in enumerate(distances):
            part = normed[i * rows_here : (i + 1) * rows_here]
            mean = jnp.mean(part, axis=0, keepdims=True)
            pooled = jnp.where(row == ring.device_at(k), mean, pooled)
        out_ref[...] = pooled

    pooled_shape = (expert_count, feature_dim)
    mean_at["pooled"] = jnp.zeros(pooled_shape, F32)

    def norm(distances, blocks):
        rows = mid * len(blocks)
        mean_at["pooled"], *kept = call(
            functools.partial(norm_kernel, distances),
            [(pooled_shape, F32), ((rows, feature_dim), F32), ((rows, LANES), F32)],
            *[half for k in distances for half in tokens_at[k]],
            *blocks,
            gain,
            mean_at["pooled"],
        )
        norm_at.update({k: (i * rows_here, kept) for i, k in enumerate(distances)})

    ring.gather(moe_top, moe_bottom, norm)
    pooled = mean_at["pooled"].astype(BF16)
    logits = dot(pooled, class_head)
    target_rows = targets.reshape(expert_count, -1).astype(F32)
    logit_grad = (LOSS_SCALE * (jax.nn.sigmoid(logits) - target_rows)).astype(BF16)
    pooled_grad = dot_t(logit_grad, class_head)
    span = 2
    for masks in ([1], list(range(span, expert_count, span))):
        mine = pooled_grad.astype(BF16)
        pooled_grad = mine.astype(F32)
        for mask in masks:
            pairs = [(e, e ^ mask) for e in range(expert_count)]
            pooled_grad = pooled_grad + lax.ppermute(mine, "expert", pairs).astype(F32)

    def backward_kernel(unit, *refs):
        gate_save, up_save, grad_ref, gain_ref, wide_ref, down_ref, *outs = refs[2 * len(unit) :]
        parts = []
        for i, item in enumerate(unit):
            k, some = distance_of(item), half_rows(item)
            rows = pl.ds(norm_at[k][0] + some[0] * mid, len(some) * mid)
            residual, inv_rms = refs[2 * i][rows, :], refs[2 * i + 1][rows, :1]
            scaled = gain_ref[...] * grad_ref[pl.ds(ring.device_at(k), 1), :] / rows_here
            cube = inv_rms * inv_rms * inv_rms
            slope = cube * jnp.mean(residual * scaled, axis=-1, keepdims=True)
            parts.append(inv_rms * scaled - residual * slope)
        resid_grad = jnp.concatenate(parts, axis=0) if len(parts) > 1 else parts[0]
        down_back = dot(resid_grad.astype(BF16), down_ref[...])
        grads = []
        for local in range(local_experts):
            cols = slice(local * hidden_dim, (local + 1) * hidden_dim)
            for save in (gate_save, up_save):
                grads.append((down_back[:, cols] * save[:, cols].astype(F32)).astype(BF16))
        total = dot(jnp.concatenate(grads, axis=1), wide_ref[...])
        store_parts(total + resid_grad if unit == (0,) else total, unit, outs)

    wide_t, down_t = transposed(wide), transposed(down)
    back_at = {}
    for unit in units:
        results = call(
            functools.partial(backward_kernel, unit),
            part_outs(unit),
            *[kept for item in unit for kept in norm_at[distance_of(item)][1]],
            *saved_at[unit],
            pooled_grad,
            gain,
            wide_t,
            down_t,
            flops=flops * rows_of(unit),
        )
        back_at.update(zip(unit, results))
    token_grad = pl.pallas_call(
        sum_kernel,
        out_shape=jax.ShapeDtypeStruct(block, BF16),
        in_specs=[pl.BlockSpec(memory_space=pltpu.VMEM)] * 3,
        out_specs=pl.BlockSpec(memory_space=pltpu.VMEM),
        compiler_params=pltpu.CompilerParams(vmem_limit_bytes=VMEM_LIMIT),
    )(back_at[0], *ring.scatter((back_at[top_half], back_at[bottom_half]), back_at))

    both = jnp.concatenate([pooled, logit_grad], axis=1)
    if group_count == 2:
        both = jnp.concatenate([both, lax.ppermute(both, "group", [(0, 1), (1, 0)])], axis=0)
    else:
        both = lax.all_gather(both, "group", axis=0, tiled=True)
    head_grad = lax.dot_general(
        both[:, :feature_dim],
        both[:, feature_dim:],
        (((0,), (0,)), ((), ())),
        preferred_element_type=F32,
    )
    return (token_grad, head_grad)


def solution(mesh):
    in_specs = (
        P(("rep", "expert", "group"), None),
        P("expert", "group", None),
        P("expert", "group", None),
        P("expert", "group", None),
        P(("rep", "expert", "group"), None),
        P(("rep", "expert", "group"), None),
        P(),
        P(None, "expert"),
        P("rep", "group", "expert"),
    )
    out_specs = (P(("rep", "expert", "group"), None), P("rep", "expert"))
    return jax.shard_map(body, mesh=mesh, in_specs=in_specs, out_specs=out_specs, check_vma=False)
```

```python
import functools

import jax
import jax.numpy as jnp
from jax import lax
from jax.experimental import pallas as pl
from jax.experimental.pallas import tpu as pltpu
from jax.sharding import PartitionSpec as P

LOSS_SCALE = 8.0
NORM_EPS = 1e-06
F32 = jnp.float32
BF16 = jnp.bfloat16
LANES = 128
VMEM_LIMIT = 32 * 1024 * 1024


def dot(left, right):
    return jnp.dot(left, right, preferred_element_type=F32)


def dot_t(left, right):
    return lax.dot_general(left, right, (((1,), (1,)), ((), ())), preferred_element_type=F32)


def call(kernel, outs, *args, flops=0):
    args = [pltpu.with_memory_space_constraint(a, pltpu.VMEM) for a in args]
    size = sum(a.size * a.dtype.itemsize for a in args)
    return pl.pallas_call(
        kernel,
        out_shape=[pltpu.VMEM(shape, dtype) for shape, dtype in outs],
        in_specs=[pl.BlockSpec(memory_space=pltpu.VMEM)] * len(args),
        out_specs=[pl.BlockSpec(memory_space=pltpu.VMEM)] * len(outs),
        compiler_params=pltpu.CompilerParams(vmem_limit_bytes=VMEM_LIMIT),
        cost_estimate=pl.CostEstimate(flops=flops, bytes_accessed=size, transcendentals=0),
    )(*args)


class Ring:
    def __init__(self, expert_count, group_count):
        self.count = expert_count
        self.half = expert_count // 2
        self.groups = group_count
        self.snake = group_count == 2
        if self.snake:
            self.order = list(range(0, expert_count, 2)) + list(range(expert_count - 1, 0, -2))
        else:
            self.order = list(range(expert_count))

    def send(self, value, distance):
        pairs = []
        for i in range(self.count):
            for g in range(self.groups):
                there = self.order[(i + (-distance if g % 2 else distance)) % self.count]
                pairs.append((self.order[i] * self.groups + g, there * self.groups + g))
        return lax.ppermute(value, ("expert", "group"), pairs)

    def device_at(self, distance):
        here = lax.axis_index("expert")
        count = self.count
        if self.snake:
            here = jnp.where(here % 2 == 0, here // 2, count - 1 - here // 2)
        ahead = distance % count
        step = jnp.where(lax.rem(lax.axis_index("group"), 2) == 0, ahead, count - ahead)
        there = lax.rem(here + step, count)
        if self.snake:
            there = jnp.where(there < self.half, 2 * there, 2 * (count - 1 - there) + 1)
        return there

    def signed(self, behind):
        return -behind if behind < self.half else self.count - behind

    def gather_round(self, own):
        blocks = {0: own}
        for behind in range(1, self.count):
            own = self.send(own, 1)
            blocks[self.signed(behind)] = own
        return blocks

    def scatter_round(self, parts):
        total = parts[self.signed(1)]
        for behind in range(2, self.count):
            total = add(parts[self.signed(behind)], self.send(total, 1))
        return self.send(total, 1)

    def gather(self, top, bottom, use):
        top_left = top_right = top
        bottom_left = bottom_right = bottom
        use((0,), (top, bottom))
        for step in range(1, self.half):
            top_left = self.send(top_left, 1)
            top_right = self.send(top_right, -1)
            bottom_left = self.send(bottom_left, 1)
            bottom_right = self.send(bottom_right, -1)
            use((-step, step), (top_left, bottom_left, top_right, bottom_right))
        use((self.half,), (self.send(top_left, 1), self.send(bottom_right, -1)))

    def scatter_whole(self, ends, parts):
        mid = ends[0].shape[0]

        def half_kernel(first, block_ref, arrived_ref, out_ref):
            added, kept = pl.ds(first, mid), pl.ds(mid - first, mid)
            out_ref[added, :] = (block_ref[added, :] + arrived_ref[...].astype(F32)).astype(BF16)
            out_ref[kept, :] = block_ref[kept, :].astype(BF16)

        left, right = self.send(ends[0], 1), self.send(ends[1], -1)
        for step in range(self.half - 1, 0, -1):
            blocks = parts[step], parts[-step]
            if step == self.half - 1:
                halves = [functools.partial(half_kernel, first) for first in (0, mid)]
                shape = blocks[0].shape
                left, right = [
                    call(kernel, [(shape, BF16)], block, arrived)[0]
                    for kernel, block, arrived in zip(halves, blocks, (left, right))
                ]
            else:
                left, right = add(blocks[0], left), add(blocks[1], right)
            left, right = self.send(left, 1), self.send(right, -1)
        return left, right


def add_kernel(block_ref, arrived_ref, out_ref):
    out_ref[...] = (block_ref[...] + arrived_ref[...].astype(F32)).astype(BF16)


def add(block, arrived):
    return call(add_kernel, [(block.shape, BF16)], block, arrived)[0]


def sum_kernel(count, *refs):
    total = refs[0][...]
    for ref in refs[1:count]:
        total = total + ref[...].astype(F32)
    outs = refs[count:]
    rows = total.shape[0] // len(outs)
    for i, out in enumerate(outs):
        out[...] = total[i * rows : (i + 1) * rows].astype(BF16)


class Copies:
    def __init__(self, sems):
        self.sems, self.started = sems, []

    def start(self, source, target):
        copy = pltpu.make_async_copy(source, target, self.sems.at[len(self.started)])
        copy.start()
        self.started.append(copy)

    def wait(self):
        for copy in self.started:
            copy.wait()


def strips(gate_shape, down_shape):
    local_experts, depth, hidden_dim = gate_shape
    _, height, feature_dim = down_shape
    row, places = 0, []
    for _ in range(local_experts):
        pair = [(row, depth), (row + depth, depth)]
        row += 2 * depth
        downs = []
        for begin in range(0, feature_dim, hidden_dim):
            downs.append((row, height, begin, min(hidden_dim, feature_dim - begin)))
            row += height
        places.append((pair, downs))
    return row, places


def pack(ids, scores, tokens, shards):
    rows, cols = tokens.shape
    inputs = [ids, scores, tokens, *shards]
    packed_shape, places, count = None, [], 0
    if shards:
        hidden_dim = shards[0].shape[2]
        packed_rows, places = strips(shards[0].shape, shards[2].shape)
        packed_shape = (packed_rows, hidden_dim)
        count = sum(len(pair) + len(downs) for pair, downs in places)

    def kernel(*refs):
        ids_hbm, scores_hbm, tokens_hbm, *shards_hbm = refs[: len(inputs)]
        block_ref, *packed_refs = refs[len(inputs) : -3]
        ids_ref, scores_ref, sems = refs[-3:]
        copies = Copies(sems)
        copies.start(ids_hbm, ids_ref)
        copies.start(scores_hbm, scores_ref)
        copies.start(tokens_hbm, block_ref.at[:, pl.ds(0, cols)])
        for local, (pair, downs) in enumerate(places):
            out_ref = packed_refs[0]
            for source, (row, some) in zip(shards_hbm, pair):
                copies.start(source.at[local], out_ref.at[pl.ds(row, some), :])
            for row, some, begin, width in downs:
                source = shards_hbm[2].at[local, :, pl.ds(begin, width)]
                copies.start(source, out_ref.at[pl.ds(row, some), pl.ds(0, width)])
                if width < hidden_dim:
                    rest = hidden_dim - width
                    out_ref[pl.ds(row, some), pl.ds(width, rest)] = jnp.zeros((some, rest), BF16)
        copies.started[0].wait()
        copies.started[1].wait()
        scores = scores_ref[...]
        ids = ids_ref[...]
        route_weight = scores / jnp.sum(scores, axis=0, keepdims=True)
        expert = lax.broadcasted_iota(jnp.int32, (LANES // 2, rows), 0)
        weight_by = jnp.zeros((LANES // 2, rows), F32)
        for choice_k in range(scores.shape[0]):
            one = slice(choice_k, choice_k + 1)
            weight_by = weight_by + jnp.where(ids[one] == expert, route_weight[one], 0.0)
        high = weight_by.astype(BF16).astype(F32)
        block_ref[:, cols:] = jnp.concatenate([high, weight_by - high], axis=0).T.astype(BF16)
        for copy in copies.started[2:]:
            copy.wait()

    outs = [pltpu.VMEM((rows, cols + LANES), BF16)]
    if shards:
        outs.append(pltpu.VMEM(packed_shape, BF16))
    return pl.pallas_call(
        kernel,
        out_shape=outs,
        in_specs=[pl.BlockSpec(memory_space=pl.ANY)] * len(inputs),
        out_specs=[pl.BlockSpec(memory_space=pltpu.VMEM)] * len(outs),
        scratch_shapes=[
            pltpu.VMEM(ids.shape, ids.dtype),
            pltpu.VMEM(scores.shape, F32),
            pltpu.SemaphoreType.DMA((3 + count,)),
        ],
        compiler_params=pltpu.CompilerParams(vmem_limit_bytes=VMEM_LIMIT),
    )(*[pltpu.with_memory_space_constraint(a, pltpu.HBM) for a in inputs])


def full_weights(shards, packed):
    local_experts, _, hidden_dim = shards[0].shape
    feature_dim = shards[2].shape[2]
    paired = packed is not None
    _, places = strips(shards[0].shape, shards[2].shape)
    depth, height = shards[0].shape[1], shards[2].shape[1]

    def kernel(*refs):
        gate_hbm, up_hbm, down_hbm, *rest = refs
        wide_ref, down_ref, sems = rest[-3:]
        copies = Copies(sems)
        mine = lax.axis_index("group") if paired else 0

        def wide_at(place, local, is_up):
            rows = pl.ds(pl.multiple_of(place * depth, 16), depth)
            return wide_ref.at[rows, pl.ds((2 * local + is_up) * hidden_dim, hidden_dim)]

        def down_at(place, local, begin, cols):
            top = pl.multiple_of(local * hidden_dim + place * height, 16)
            return down_ref.at[pl.ds(top, height), pl.ds(begin, cols)]

        for local in range(local_experts):
            for is_up, source in enumerate((gate_hbm, up_hbm)):
                copies.start(source.at[local], wide_at(mine, local, is_up))
            copies.start(down_hbm.at[local], down_at(mine, local, 0, feature_dim))
        if paired:
            for local, (pair, downs) in enumerate(places):
                for is_up, (row, some) in enumerate(pair):
                    copies.start(rest[0].at[pl.ds(row, some), :], wide_at(1 - mine, local, is_up))
                for row, some, begin, cols in downs:
                    source = rest[0].at[pl.ds(row, some), pl.ds(0, cols)]
                    copies.start(source, down_at(1 - mine, local, begin, cols))
        copies.wait()

    shards = [pltpu.with_memory_space_constraint(w, pltpu.HBM) for w in shards]
    count = 3 * local_experts
    specs = [pl.BlockSpec(memory_space=pl.ANY)] * 3
    if paired:
        count += sum(len(pair) + len(downs) for pair, downs in places)
        specs.append(pl.BlockSpec(memory_space=pltpu.VMEM))
        shards.append(pltpu.with_memory_space_constraint(packed, pltpu.VMEM))
    return pl.pallas_call(
        kernel,
        out_shape=[
            pltpu.VMEM((feature_dim, 2 * local_experts * hidden_dim), BF16),
            pltpu.VMEM((local_experts * hidden_dim, feature_dim), BF16),
        ],
        in_specs=specs,
        out_specs=[pl.BlockSpec(memory_space=pltpu.VMEM)] * 2,
        scratch_shapes=[pltpu.SemaphoreType.DMA((count,))],
        compiler_params=pltpu.CompilerParams(vmem_limit_bytes=VMEM_LIMIT),
    )(*shards)


def transpose_kernel(from_ref, to_ref):
    strip = 2 * LANES

    @pl.loop(0, to_ref.shape[0] // strip)
    def _(i):
        some = pl.ds(pl.multiple_of(i * strip, strip), strip)
        to_ref[some, :] = from_ref[:, some].T


def transposed(weights):
    rows, cols = weights.shape
    return call(transpose_kernel, [((cols, rows), BF16)], weights)[0]


def body(tokens, w_gate, w_up, w_down, route_ids, route_scores, norm_gain, class_head, targets):
    rows_here, feature_dim = tokens.shape
    expert_count = lax.axis_size("expert")
    group_count = lax.axis_size("group")
    local_experts, _, hidden_dim = w_gate.shape
    pair_dim = 2 * hidden_dim
    ring = Ring(expert_count, group_count)
    block = (rows_here, feature_dim)
    mid = rows_here // 2

    shards = [w_gate, w_up, w_down]
    if group_count == 2:
        own, packed = pack(route_ids.T, route_scores.T, tokens, shards)
        packed = lax.ppermute(packed, "group", [(0, 1), (1, 0)])
    else:
        (own,) = pack(route_ids.T, route_scores.T, tokens, [])
        shards = [lax.all_gather(w, "group", axis=1, tiled=True) for w in shards]
        packed = None
    wide, down = full_weights(shards, packed)

    def forward_kernel(block_ref, wide_ref, down_ref, gate_save, up_save, out_ref):
        x = block_ref[:, :feature_dim]
        weights = block_ref[:, feature_dim:].astype(F32)
        lane = lax.broadcasted_iota(jnp.int32, weights.shape, 1)
        hidden = []
        for local in range(local_experts):
            expert = lax.axis_index("expert") * local_experts + local
            mine = (lane == expert) | (lane == expert + LANES // 2)
            scale = jnp.sum(jnp.where(mine, weights, 0.0), axis=1, keepdims=True)
            act = dot(x, wide_ref[:, pl.ds(local * pair_dim, pair_dim)])
            gate_act, up_act = act[:, :hidden_dim], act[:, hidden_dim:]
            sigmoid_gate = jax.nn.sigmoid(gate_act)
            silu = gate_act * sigmoid_gate * scale
            slope = sigmoid_gate * (1.0 + gate_act * (1.0 - sigmoid_gate)) * scale
            cols = pl.ds(local * hidden_dim, hidden_dim)
            gate_save[:, cols] = (up_act * slope).astype(BF16)
            up_save[:, cols] = silu.astype(BF16)
            hidden.append((silu * up_act).astype(BF16))
        out_ref[...] = dot(jnp.concatenate(hidden, axis=1), down_ref[...]).astype(out_ref.dtype)

    tokens_at = ring.gather_round(own)
    part_at, saved_at = {}, {}
    flops = 2 * rows_here * feature_dim * hidden_dim * local_experts * 3
    for k, rows in tokens_at.items():
        *saved_at[k], part_at[k] = call(
            forward_kernel,
            [((rows_here, local_experts * hidden_dim), BF16)] * 2
            + [(block, BF16 if k == ring.signed(1) else F32)],
            rows,
            wide,
            down,
            flops=flops,
        )
    gain = norm_gain.reshape(1, feature_dim)
    moe_top, moe_bottom = call(
        functools.partial(sum_kernel, 2),
        [((mid, feature_dim), BF16)] * 2,
        part_at[0],
        ring.scatter_round(part_at),
    )

    norm_at, mean_at = {}, {}

    def inv_rms_of(residual):
        return lax.rsqrt(jnp.mean(residual * residual, axis=-1, keepdims=True) + NORM_EPS)

    def norm_kernel(distances, *refs):
        count = len(distances)
        residual = jnp.concatenate([ref[:, :feature_dim].astype(F32) for ref in refs[:count]], axis=0)
        moe_rows = [ref[...].astype(F32) for ref in refs[count : 3 * count]]
        residual = residual + jnp.concatenate(moe_rows, axis=0)
        gain_ref, so_far, out_ref, residual_ref, inv_ref = refs[3 * count :]
        inv_rms = inv_rms_of(residual)
        residual_ref[...] = residual
        inv_ref[...] = jnp.broadcast_to(inv_rms, inv_ref.shape)
        normed = residual * inv_rms * gain_ref[...]
        pooled = so_far[...]
        row = lax.broadcasted_iota(jnp.int32, pooled.shape, 0)
        for i, k in enumerate(distances):
            part = normed[i * rows_here : (i + 1) * rows_here]
            mean = jnp.mean(part, axis=0, keepdims=True)
            pooled = jnp.where(row == ring.device_at(k), mean, pooled)
        out_ref[...] = pooled

    pooled_shape = (expert_count, feature_dim)
    mean_at["pooled"] = jnp.zeros(pooled_shape, F32)

    def norm(distances, blocks):
        rows = mid * len(blocks)
        mean_at["pooled"], *norm_at[distances] = call(
            functools.partial(norm_kernel, distances),
            [(pooled_shape, F32), ((rows, feature_dim), F32), ((rows, LANES), F32)],
            *[tokens_at[k] for k in distances],
            *blocks,
            gain,
            mean_at["pooled"],
        )

    ring.gather(moe_top, moe_bottom, norm)
    pooled = mean_at["pooled"].astype(BF16)
    logits = dot(pooled, class_head)
    target_rows = targets.reshape(expert_count, -1).astype(F32)
    logit_grad = (LOSS_SCALE * (jax.nn.sigmoid(logits) - target_rows)).astype(BF16)
    pooled_grad = dot_t(logit_grad, class_head)
    span = 2
    for masks in ([1], list(range(span, expert_count, span))):
        mine = pooled_grad.astype(BF16)
        pooled_grad = mine.astype(F32)
        for mask in masks:
            pairs = [(e, e ^ mask) for e in range(expert_count)]
            pooled_grad = pooled_grad + lax.ppermute(mine, "expert", pairs).astype(F32)

    both = jnp.concatenate([pooled, logit_grad], axis=1)
    if group_count == 2:
        both = jnp.concatenate([both, lax.ppermute(both, "group", [(0, 1), (1, 0)])], axis=0)
    else:
        both = lax.all_gather(both, "group", axis=0, tiled=True)
    head_grad = lax.dot_general(
        both[:, :feature_dim],
        both[:, feature_dim:],
        (((0,), (0,)), ((), ())),
        preferred_element_type=F32,
    )

    def backward_kernel(distances, residual_ref, inv_ref, *refs):
        saved, (grad_ref, gain_ref, wide_ref, down_ref, *outs) = refs[: 2 * len(distances)], refs[2 * len(distances) :]
        residual, inv_rms = residual_ref[...], inv_ref[:, :1]
        cube = inv_rms * inv_rms * inv_rms
        parts = []
        for i, k in enumerate(distances):
            rows = slice(i * rows_here, (i + 1) * rows_here)
            scaled = gain_ref[...] * grad_ref[pl.ds(ring.device_at(k), 1), :] / rows_here
            slope = cube[rows] * jnp.mean(residual[rows] * scaled, axis=-1, keepdims=True)
            parts.append(inv_rms[rows] * scaled - residual[rows] * slope)
        resid_grad = jnp.concatenate(parts, axis=0) if len(parts) > 1 else parts[0]
        down_back = dot(resid_grad.astype(BF16), down_ref[...])
        grads = []
        for local in range(local_experts):
            cols = slice(local * hidden_dim, (local + 1) * hidden_dim)
            for saves in (saved[::2], saved[1::2]):
                save = jnp.concatenate([ref[:, cols] for ref in saves], axis=0).astype(F32)
                grads.append((down_back[:, cols] * save).astype(BF16))
        total = dot(jnp.concatenate(grads, axis=1), wide_ref[...])
        if distances == (0,):
            total = total + resid_grad
        rows = total.shape[0] // len(outs)
        for i, out in enumerate(outs):
            out[...] = total[i * rows : (i + 1) * rows].astype(out.dtype)

    wide_t, down_t = transposed(wide), transposed(down)
    back_at = {}

    def backward(distances):
        if distances == (ring.half,):
            outs = [((mid, feature_dim), BF16)] * 2
        else:
            outs = [(block, F32)] * len(distances)
        result = call(
            functools.partial(backward_kernel, distances),
            outs,
            *norm_at[distances],
            *[save for k in distances for save in saved_at[k]],
            pooled_grad,
            gain,
            wide_t,
            down_t,
            flops=flops * len(distances),
        )
        if distances == (ring.half,):
            back_at["ends"] = result
        else:
            back_at.update(zip(distances, result))

    for distances in reversed(list(norm_at)):
        backward(distances)
    token_grad = pl.pallas_call(
        functools.partial(sum_kernel, 3),
        out_shape=jax.ShapeDtypeStruct(block, BF16),
        in_specs=[pl.BlockSpec(memory_space=pltpu.VMEM)] * 3,
        out_specs=pl.BlockSpec(memory_space=pltpu.VMEM),
        compiler_params=pltpu.CompilerParams(vmem_limit_bytes=VMEM_LIMIT),
    )(back_at[0], *ring.scatter_whole(back_at["ends"], back_at))
    return (token_grad, head_grad)


def solution(mesh):
    in_specs = (
        P(("rep", "expert", "group"), None),
        P("expert", "group", None),
        P("expert", "group", None),
        P("expert", "group", None),
        P(("rep", "expert", "group"), None),
        P(("rep", "expert", "group"), None),
        P(),
        P(None, "expert"),
        P("rep", "group", "expert"),
    )
    out_specs = (P(("rep", "expert", "group"), None), P("rep", "expert"))
    return jax.shard_map(body, mesh=mesh, in_specs=in_specs, out_specs=out_specs, check_vma=False)
```

```python
import functools

import jax
import jax.numpy as jnp
from jax import lax
from jax.experimental import pallas as pl
from jax.experimental.pallas import tpu as pltpu
from jax.sharding import PartitionSpec as P

LOSS_SCALE = 8.0
NORM_EPS = 1e-06
F32 = jnp.float32
BF16 = jnp.bfloat16
LANES = 128
VMEM_LIMIT = 32 * 1024 * 1024


def dot(left, right):
    return jnp.dot(left, right, preferred_element_type=F32)


def dot_t(left, right):
    return lax.dot_general(left, right, (((1,), (1,)), ((), ())), preferred_element_type=F32)


def call(kernel, outs, *args, flops=0):
    args = [pltpu.with_memory_space_constraint(a, pltpu.VMEM) for a in args]
    size = sum(a.size * a.dtype.itemsize for a in args)
    return pl.pallas_call(
        kernel,
        out_shape=[pltpu.VMEM(shape, dtype) for shape, dtype in outs],
        in_specs=[pl.BlockSpec(memory_space=pltpu.VMEM)] * len(args),
        out_specs=[pl.BlockSpec(memory_space=pltpu.VMEM)] * len(outs),
        compiler_params=pltpu.CompilerParams(vmem_limit_bytes=VMEM_LIMIT),
        cost_estimate=pl.CostEstimate(flops=flops, bytes_accessed=size, transcendentals=0),
    )(*args)


def after(value, guards):
    def kernel(*refs):
        pass

    args = [pltpu.with_memory_space_constraint(a, pltpu.VMEM) for a in (value, *guards)]
    return pl.pallas_call(
        kernel,
        out_shape=pltpu.VMEM(value.shape, value.dtype),
        in_specs=[pl.BlockSpec(memory_space=pltpu.VMEM)] * len(args),
        out_specs=pl.BlockSpec(memory_space=pltpu.VMEM),
        input_output_aliases={0: 0},
        compiler_params=pltpu.CompilerParams(vmem_limit_bytes=VMEM_LIMIT),
    )(*args)


class Ring:
    def __init__(self, expert_count, group_count):
        self.count = expert_count
        self.half = expert_count // 2
        self.groups = group_count
        self.snake = group_count == 2
        if self.snake:
            self.order = list(range(0, expert_count, 2)) + list(range(expert_count - 1, 0, -2))
        else:
            self.order = list(range(expert_count))

    def send(self, value, distance):
        pairs = []
        for i in range(self.count):
            for g in range(self.groups):
                there = self.order[(i + (-distance if g % 2 else distance)) % self.count]
                pairs.append((self.order[i] * self.groups + g, there * self.groups + g))
        return lax.ppermute(value, ("expert", "group"), pairs)

    def device_at(self, distance):
        here = lax.axis_index("expert")
        count = self.count
        if self.snake:
            here = jnp.where(here % 2 == 0, here // 2, count - 1 - here // 2)
        ahead = distance % count
        step = jnp.where(lax.rem(lax.axis_index("group"), 2) == 0, ahead, count - ahead)
        there = lax.rem(here + step, count)
        if self.snake:
            there = jnp.where(there < self.half, 2 * there, 2 * (count - 1 - there) + 1)
        return there

    def signed(self, distance):
        distance %= self.count
        return distance if distance <= self.half else distance - self.count

    def gather_whole(self, own, meanwhile):
        blocks = {0: own}
        from_left = from_right = own
        for step in range(1, self.half + 1):
            if step > 2:
                guards = meanwhile(step - 2, blocks)
                from_left = after(from_left, guards)
                from_right = after(from_right, guards) if step < self.half else from_right
            from_left = self.send(from_left, 1)
            blocks[self.signed(-step)] = from_left
            if step < self.half:
                from_right = self.send(from_right, -1)
                blocks[step] = from_right
        return blocks

    def scatter_hop(self, step, parts, arrived):
        top, bottom = parts[self.signed(-step)][0], parts[self.signed(step)][1]
        if arrived:
            top, bottom = add(top, arrived[0]), add(bottom, arrived[1])
        return self.send(top, 1), self.send(bottom, -1)

    def gather(self, top, bottom, use):
        top_left = top_right = top
        bottom_left = bottom_right = bottom
        use((0,), (top, bottom))
        for step in range(1, self.half):
            top_left = self.send(top_left, 1)
            top_right = self.send(top_right, -1)
            bottom_left = self.send(bottom_left, 1)
            bottom_right = self.send(bottom_right, -1)
            use((-step, step), (top_left, bottom_left, top_right, bottom_right))
        use((self.half,), (self.send(top_left, 1), self.send(bottom_right, -1)))

    def scatter_whole(self, ends, parts):
        mid = ends[0].shape[0]

        def half_kernel(first, block_ref, arrived_ref, out_ref):
            added, kept = pl.ds(first, mid), pl.ds(mid - first, mid)
            out_ref[added, :] = (block_ref[added, :] + arrived_ref[...].astype(F32)).astype(BF16)
            out_ref[kept, :] = block_ref[kept, :].astype(BF16)

        left, right = self.send(ends[0], 1), self.send(ends[1], -1)
        for step in range(self.half - 1, 0, -1):
            blocks = parts[step], parts[-step]
            if step == self.half - 1:
                halves = [functools.partial(half_kernel, first) for first in (0, mid)]
                shape = blocks[0].shape
                left, right = [
                    call(kernel, [(shape, BF16)], block, arrived)[0]
                    for kernel, block, arrived in zip(halves, blocks, (left, right))
                ]
            else:
                left, right = add(blocks[0], left), add(blocks[1], right)
            left, right = self.send(left, 1), self.send(right, -1)
        return left, right


def add_kernel(block_ref, arrived_ref, out_ref):
    out_ref[...] = (block_ref[...] + arrived_ref[...].astype(F32)).astype(BF16)


def add(block, arrived):
    return call(add_kernel, [(block.shape, BF16)], block, arrived)[0]


def sum_kernel(count, *refs):
    total = refs[0][...]
    for ref in refs[1:count]:
        total = total + ref[...].astype(F32)
    outs = refs[count:]
    rows = total.shape[0] // len(outs)
    for i, out in enumerate(outs):
        out[...] = total[i * rows : (i + 1) * rows].astype(BF16)


class Copies:
    def __init__(self, sems):
        self.sems, self.started = sems, []

    def start(self, source, target):
        copy = pltpu.make_async_copy(source, target, self.sems.at[len(self.started)])
        copy.start()
        self.started.append(copy)

    def wait(self):
        for copy in self.started:
            copy.wait()


def strips(gate_shape, down_shape):
    local_experts, depth, hidden_dim = gate_shape
    _, height, feature_dim = down_shape
    row, places = 0, []
    for _ in range(local_experts):
        pair = [(row, depth), (row + depth, depth)]
        row += 2 * depth
        downs = []
        for begin in range(0, feature_dim, hidden_dim):
            downs.append((row, height, begin, min(hidden_dim, feature_dim - begin)))
            row += height
        places.append((pair, downs))
    return row, places


def pack(ids, scores, tokens, shards):
    rows, cols = tokens.shape
    inputs = [ids, scores, tokens, *shards]
    packed_shape, places, count = None, [], 0
    if shards:
        hidden_dim = shards[0].shape[2]
        packed_rows, places = strips(shards[0].shape, shards[2].shape)
        packed_shape = (packed_rows, hidden_dim)
        count = sum(len(pair) + len(downs) for pair, downs in places)

    def kernel(*refs):
        ids_hbm, scores_hbm, tokens_hbm, *shards_hbm = refs[: len(inputs)]
        block_ref, *packed_refs = refs[len(inputs) : -3]
        ids_ref, scores_ref, sems = refs[-3:]
        copies = Copies(sems)
        copies.start(ids_hbm, ids_ref)
        copies.start(scores_hbm, scores_ref)
        copies.start(tokens_hbm, block_ref.at[:, pl.ds(0, cols)])
        for local, (pair, downs) in enumerate(places):
            out_ref = packed_refs[0]
            for source, (row, some) in zip(shards_hbm, pair):
                copies.start(source.at[local], out_ref.at[pl.ds(row, some), :])
            for row, some, begin, width in downs:
                source = shards_hbm[2].at[local, :, pl.ds(begin, width)]
                copies.start(source, out_ref.at[pl.ds(row, some), pl.ds(0, width)])
                if width < hidden_dim:
                    rest = hidden_dim - width
                    out_ref[pl.ds(row, some), pl.ds(width, rest)] = jnp.zeros((some, rest), BF16)
        copies.started[0].wait()
        copies.started[1].wait()
        scores = scores_ref[...]
        ids = ids_ref[...]
        route_weight = scores / jnp.sum(scores, axis=0, keepdims=True)
        expert = lax.broadcasted_iota(jnp.int32, (LANES // 2, rows), 0)
        weight_by = jnp.zeros((LANES // 2, rows), F32)
        for choice_k in range(scores.shape[0]):
            one = slice(choice_k, choice_k + 1)
            weight_by = weight_by + jnp.where(ids[one] == expert, route_weight[one], 0.0)
        high = weight_by.astype(BF16).astype(F32)
        block_ref[:, cols:] = jnp.concatenate([high, weight_by - high], axis=0).T.astype(BF16)
        for copy in copies.started[2:]:
            copy.wait()

    outs = [pltpu.VMEM((rows, cols + LANES), BF16)]
    if shards:
        outs.append(pltpu.VMEM(packed_shape, BF16))
    return pl.pallas_call(
        kernel,
        out_shape=outs,
        in_specs=[pl.BlockSpec(memory_space=pl.ANY)] * len(inputs),
        out_specs=[pl.BlockSpec(memory_space=pltpu.VMEM)] * len(outs),
        scratch_shapes=[
            pltpu.VMEM(ids.shape, ids.dtype),
            pltpu.VMEM(scores.shape, F32),
            pltpu.SemaphoreType.DMA((3 + count,)),
        ],
        compiler_params=pltpu.CompilerParams(vmem_limit_bytes=VMEM_LIMIT),
    )(*[pltpu.with_memory_space_constraint(a, pltpu.HBM) for a in inputs])


def full_weights(shards, packed):
    local_experts, _, hidden_dim = shards[0].shape
    feature_dim = shards[2].shape[2]
    paired = packed is not None
    _, places = strips(shards[0].shape, shards[2].shape)
    depth, height = shards[0].shape[1], shards[2].shape[1]

    def kernel(*refs):
        gate_hbm, up_hbm, down_hbm, *rest = refs
        wide_ref, down_ref, sems = rest[-3:]
        copies = Copies(sems)
        mine = lax.axis_index("group") if paired else 0

        def wide_at(place, local, is_up):
            rows = pl.ds(pl.multiple_of(place * depth, 16), depth)
            return wide_ref.at[rows, pl.ds((2 * local + is_up) * hidden_dim, hidden_dim)]

        def down_at(place, local, begin, cols):
            top = pl.multiple_of(local * hidden_dim + place * height, 16)
            return down_ref.at[pl.ds(top, height), pl.ds(begin, cols)]

        for local in range(local_experts):
            for is_up, source in enumerate((gate_hbm, up_hbm)):
                copies.start(source.at[local], wide_at(mine, local, is_up))
            copies.start(down_hbm.at[local], down_at(mine, local, 0, feature_dim))
        if paired:
            for local, (pair, downs) in enumerate(places):
                for is_up, (row, some) in enumerate(pair):
                    copies.start(rest[0].at[pl.ds(row, some), :], wide_at(1 - mine, local, is_up))
                for row, some, begin, cols in downs:
                    source = rest[0].at[pl.ds(row, some), pl.ds(0, cols)]
                    copies.start(source, down_at(1 - mine, local, begin, cols))
        copies.wait()

    shards = [pltpu.with_memory_space_constraint(w, pltpu.HBM) for w in shards]
    count = 3 * local_experts
    specs = [pl.BlockSpec(memory_space=pl.ANY)] * 3
    if paired:
        count += sum(len(pair) + len(downs) for pair, downs in places)
        specs.append(pl.BlockSpec(memory_space=pltpu.VMEM))
        shards.append(pltpu.with_memory_space_constraint(packed, pltpu.VMEM))
    return pl.pallas_call(
        kernel,
        out_shape=[
            pltpu.VMEM((feature_dim, 2 * local_experts * hidden_dim), BF16),
            pltpu.VMEM((local_experts * hidden_dim, feature_dim), BF16),
        ],
        in_specs=specs,
        out_specs=[pl.BlockSpec(memory_space=pltpu.VMEM)] * 2,
        scratch_shapes=[pltpu.SemaphoreType.DMA((count,))],
        compiler_params=pltpu.CompilerParams(vmem_limit_bytes=VMEM_LIMIT),
    )(*shards)


def transpose_kernel(from_ref, to_ref):
    strip = 2 * LANES

    @pl.loop(0, to_ref.shape[0] // strip)
    def _(i):
        some = pl.ds(pl.multiple_of(i * strip, strip), strip)
        to_ref[some, :] = from_ref[:, some].T


def transposed(weights):
    rows, cols = weights.shape
    return call(transpose_kernel, [((cols, rows), BF16)], weights)[0]


def body(tokens, w_gate, w_up, w_down, route_ids, route_scores, norm_gain, class_head, targets):
    rows_here, feature_dim = tokens.shape
    expert_count = lax.axis_size("expert")
    group_count = lax.axis_size("group")
    local_experts, _, hidden_dim = w_gate.shape
    pair_dim = 2 * hidden_dim
    ring = Ring(expert_count, group_count)
    block = (rows_here, feature_dim)
    mid = rows_here // 2

    shards = [w_gate, w_up, w_down]
    if group_count == 2:
        own, packed = pack(route_ids.T, route_scores.T, tokens, shards)
        packed = lax.ppermute(packed, "group", [(0, 1), (1, 0)])
    else:
        (own,) = pack(route_ids.T, route_scores.T, tokens, [])
        shards = [lax.all_gather(w, "group", axis=1, tiled=True) for w in shards]
        packed = None
    wide, down = full_weights(shards, packed)

    def forward_kernel(count, *refs):
        wide_ref, down_ref, gate_save, up_save, *outs = refs[count:]
        blocks = [ref[...] for ref in refs[:count]]
        rows = jnp.concatenate(blocks, axis=0) if count > 1 else blocks[0]
        x, weights = rows[:, :feature_dim], rows[:, feature_dim:].astype(F32)
        lane = lax.broadcasted_iota(jnp.int32, weights.shape, 1)
        hidden = []
        for local in range(local_experts):
            expert = lax.axis_index("expert") * local_experts + local
            mine = (lane == expert) | (lane == expert + LANES // 2)
            scale = jnp.sum(jnp.where(mine, weights, 0.0), axis=1, keepdims=True)
            act = dot(x, wide_ref[:, pl.ds(local * pair_dim, pair_dim)])
            gate_act, up_act = act[:, :hidden_dim], act[:, hidden_dim:]
            sigmoid_gate = jax.nn.sigmoid(gate_act)
            silu = gate_act * sigmoid_gate * scale
            slope = sigmoid_gate * (1.0 + gate_act * (1.0 - sigmoid_gate)) * scale
            cols = pl.ds(local * hidden_dim, hidden_dim)
            gate_save[:, cols] = (up_act * slope).astype(BF16)
            up_save[:, cols] = silu.astype(BF16)
            hidden.append((silu * up_act).astype(BF16))
        total = dot(jnp.concatenate(hidden, axis=1), down_ref[...])
        for i, out in enumerate(outs):
            out[...] = total[i * mid : (i + 1) * mid].astype(out.dtype)

    part_at, saved_at = {}, {}
    flops = 2 * rows_here * feature_dim * hidden_dim * local_experts * 3

    def forward(distances, blocks):
        count = len(distances)
        first_sends = ((ring.signed(-1), 0), (ring.signed(1), 1))
        results = call(
            functools.partial(forward_kernel, count),
            [((rows_here * count, local_experts * hidden_dim), BF16)] * 2
            + [
                ((mid, feature_dim), BF16 if (k, half) in first_sends else F32)
                for k in distances
                for half in (0, 1)
            ],
            *[blocks[k] for k in distances],
            wide,
            down,
            flops=flops * count,
        )
        saved_at[distances] = results[:2]
        part_at.update({k: results[2 + 2 * i : 4 + 2 * i] for i, k in enumerate(distances)})

    arrived = []

    def scatter_on(step, blocks):
        forward((-step, step), blocks)
        arrived[:] = ring.scatter_hop(step, part_at, arrived)
        return arrived

    tokens_at = ring.gather_whole(own, scatter_on)
    for distances in [(0,)] + [(-k, k) for k in range(1, ring.half)] + [(ring.half,)]:
        if distances not in saved_at:
            forward(distances, tokens_at)
    for step in range(max(1, ring.half - 1), expert_count):
        arrived[:] = ring.scatter_hop(step, part_at, arrived)
    gain = norm_gain.reshape(1, feature_dim)
    moe_top, moe_bottom = [
        call(functools.partial(sum_kernel, 2), [((mid, feature_dim), BF16)], part, others)[0]
        for part, others in zip(part_at[0], arrived)
    ]

    norm_at, mean_at = {}, {}

    def inv_rms_of(residual):
        return lax.rsqrt(jnp.mean(residual * residual, axis=-1, keepdims=True) + NORM_EPS)

    def norm_kernel(distances, *refs):
        count = len(distances)
        residual = jnp.concatenate([ref[:, :feature_dim].astype(F32) for ref in refs[:count]], axis=0)
        moe_rows = [ref[...].astype(F32) for ref in refs[count : 3 * count]]
        residual = residual + jnp.concatenate(moe_rows, axis=0)
        gain_ref, so_far, out_ref, residual_ref, inv_ref = refs[3 * count :]
        inv_rms = inv_rms_of(residual)
        residual_ref[...] = residual
        inv_ref[...] = jnp.broadcast_to(inv_rms, inv_ref.shape)
        normed = residual * inv_rms * gain_ref[...]
        pooled = so_far[...]
        row = lax.broadcasted_iota(jnp.int32, pooled.shape, 0)
        for i, k in enumerate(distances):
            part = normed[i * rows_here : (i + 1) * rows_here]
            mean = jnp.mean(part, axis=0, keepdims=True)
            pooled = jnp.where(row == ring.device_at(k), mean, pooled)
        out_ref[...] = pooled

    pooled_shape = (expert_count, feature_dim)
    mean_at["pooled"] = jnp.zeros(pooled_shape, F32)

    def norm(distances, blocks):
        rows = mid * len(blocks)
        mean_at["pooled"], *norm_at[distances] = call(
            functools.partial(norm_kernel, distances),
            [(pooled_shape, F32), ((rows, feature_dim), F32), ((rows, LANES), F32)],
            *[tokens_at[k] for k in distances],
            *blocks,
            gain,
            mean_at["pooled"],
        )

    ring.gather(moe_top, moe_bottom, norm)
    pooled = mean_at["pooled"].astype(BF16)
    logits = dot(pooled, class_head)
    target_rows = targets.reshape(expert_count, -1).astype(F32)
    logit_grad = (LOSS_SCALE * (jax.nn.sigmoid(logits) - target_rows)).astype(BF16)
    pooled_grad = dot_t(logit_grad, class_head)
    span = 2
    for masks in ([1], list(range(span, expert_count, span))):
        mine = pooled_grad.astype(BF16)
        pooled_grad = mine.astype(F32)
        for mask in masks:
            pairs = [(e, e ^ mask) for e in range(expert_count)]
            pooled_grad = pooled_grad + lax.ppermute(mine, "expert", pairs).astype(F32)

    both = jnp.concatenate([pooled, logit_grad], axis=1)
    if group_count == 2:
        both = jnp.concatenate([both, lax.ppermute(both, "group", [(0, 1), (1, 0)])], axis=0)
    else:
        both = lax.all_gather(both, "group", axis=0, tiled=True)
    head_grad = lax.dot_general(
        both[:, :feature_dim],
        both[:, feature_dim:],
        (((0,), (0,)), ((), ())),
        preferred_element_type=F32,
    )

    def backward_kernel(distances, residual_ref, inv_ref, gate_save, up_save, *refs):
        grad_ref, gain_ref, wide_ref, down_ref, *outs = refs
        residual, inv_rms = residual_ref[...], inv_ref[:, :1]
        cube = inv_rms * inv_rms * inv_rms
        parts = []
        for i, k in enumerate(distances):
            rows = slice(i * rows_here, (i + 1) * rows_here)
            scaled = gain_ref[...] * grad_ref[pl.ds(ring.device_at(k), 1), :] / rows_here
            slope = cube[rows] * jnp.mean(residual[rows] * scaled, axis=-1, keepdims=True)
            parts.append(inv_rms[rows] * scaled - residual[rows] * slope)
        resid_grad = jnp.concatenate(parts, axis=0) if len(parts) > 1 else parts[0]
        down_back = dot(resid_grad.astype(BF16), down_ref[...])
        grads = []
        for local in range(local_experts):
            cols = slice(local * hidden_dim, (local + 1) * hidden_dim)
            for save in (gate_save, up_save):
                grads.append((down_back[:, cols] * save[:, cols].astype(F32)).astype(BF16))
        total = dot(jnp.concatenate(grads, axis=1), wide_ref[...])
        if distances == (0,):
            total = total + resid_grad
        rows = total.shape[0] // len(outs)
        for i, out in enumerate(outs):
            out[...] = total[i * rows : (i + 1) * rows].astype(out.dtype)

    wide_t, down_t = transposed(wide), transposed(down)
    back_at = {}

    def backward(distances):
        if distances == (ring.half,):
            outs = [((mid, feature_dim), BF16)] * 2
        else:
            outs = [(block, F32)] * len(distances)
        result = call(
            functools.partial(backward_kernel, distances),
            outs,
            *norm_at[distances],
            *saved_at[distances],
            pooled_grad,
            gain,
            wide_t,
            down_t,
            flops=flops * len(distances),
        )
        if distances == (ring.half,):
            back_at["ends"] = result
        else:
            back_at.update(zip(distances, result))

    for distances in reversed(list(norm_at)):
        backward(distances)
    token_grad = pl.pallas_call(
        functools.partial(sum_kernel, 3),
        out_shape=jax.ShapeDtypeStruct(block, BF16),
        in_specs=[pl.BlockSpec(memory_space=pltpu.VMEM)] * 3,
        out_specs=pl.BlockSpec(memory_space=pltpu.VMEM),
        compiler_params=pltpu.CompilerParams(vmem_limit_bytes=VMEM_LIMIT),
    )(back_at[0], *ring.scatter_whole(back_at["ends"], back_at))
    return (token_grad, head_grad)


def solution(mesh):
    in_specs = (
        P(("rep", "expert", "group"), None),
        P("expert", "group", None),
        P("expert", "group", None),
        P("expert", "group", None),
        P(("rep", "expert", "group"), None),
        P(("rep", "expert", "group"), None),
        P(),
        P(None, "expert"),
        P("rep", "group", "expert"),
    )
    out_specs = (P(("rep", "expert", "group"), None), P("rep", "expert"))
    return jax.shard_map(body, mesh=mesh, in_specs=in_specs, out_specs=out_specs, check_vma=False)
```

```python
import functools

import jax
import jax.numpy as jnp
from jax import lax
from jax.experimental import pallas as pl
from jax.experimental.pallas import tpu as pltpu
from jax.sharding import PartitionSpec as P

LOSS_SCALE = 8.0
NORM_EPS = 1e-06
F32 = jnp.float32
BF16 = jnp.bfloat16
LANES = 128
VMEM_LIMIT = 32 * 1024 * 1024


def dot(left, right):
    return jnp.dot(left, right, preferred_element_type=F32)


def dot_t(left, right):
    return lax.dot_general(left, right, (((1,), (1,)), ((), ())), preferred_element_type=F32)


def call(kernel, outs, *args, flops=0):
    args = [pltpu.with_memory_space_constraint(a, pltpu.VMEM) for a in args]
    size = sum(a.size * a.dtype.itemsize for a in args)
    return pl.pallas_call(
        kernel,
        out_shape=[pltpu.VMEM(shape, dtype) for shape, dtype in outs],
        in_specs=[pl.BlockSpec(memory_space=pltpu.VMEM)] * len(args),
        out_specs=[pl.BlockSpec(memory_space=pltpu.VMEM)] * len(outs),
        compiler_params=pltpu.CompilerParams(vmem_limit_bytes=VMEM_LIMIT),
        cost_estimate=pl.CostEstimate(flops=flops, bytes_accessed=size, transcendentals=0),
    )(*args)


def after(value, guards):
    def kernel(*refs):
        pass

    args = [pltpu.with_memory_space_constraint(a, pltpu.VMEM) for a in (value, *guards)]
    return pl.pallas_call(
        kernel,
        out_shape=pltpu.VMEM(value.shape, value.dtype),
        in_specs=[pl.BlockSpec(memory_space=pltpu.VMEM)] * len(args),
        out_specs=pl.BlockSpec(memory_space=pltpu.VMEM),
        input_output_aliases={0: 0},
        compiler_params=pltpu.CompilerParams(vmem_limit_bytes=VMEM_LIMIT),
    )(*args)


class Ring:
    def __init__(self, expert_count, group_count):
        self.count = expert_count
        self.half = expert_count // 2
        self.snake = group_count == 2
        if self.snake:
            self.order = list(range(0, expert_count, 2)) + list(range(expert_count - 1, 0, -2))
        else:
            self.order = list(range(expert_count))

    def send(self, value, distance):
        pairs = [
            (self.order[i], self.order[(i + distance) % self.count]) for i in range(self.count)
        ]
        return lax.ppermute(value, "expert", pairs)

    def device_at(self, distance):
        here = lax.axis_index("expert")
        count = self.count
        if self.snake:
            here = jnp.where(here % 2 == 0, here // 2, count - 1 - here // 2)
        there = lax.rem(here + distance % count, count)
        if self.snake:
            there = jnp.where(there < self.half, 2 * there, 2 * (count - 1 - there) + 1)
        return there

    def gather(self, top, bottom, use, paced=False):
        top_left = top_right = top
        bottom_left = bottom_right = bottom
        use((0,), (top, bottom))
        for step in range(1, self.half):
            if paced and step > 1:
                top_left = after(top_left, [top_right])
                bottom_right = after(bottom_right, [bottom_left])
            top_left = self.send(top_left, 1)
            top_right = self.send(top_right, -1)
            bottom_left = self.send(bottom_left, 1)
            bottom_right = self.send(bottom_right, -1)
            use((-step, step), (top_left, bottom_left, top_right, bottom_right))
        use((self.half,), (self.send(top_left, 1), self.send(bottom_right, -1)))

    def scatter(self, parts):
        most = self.half - 1
        top_left = self.send(parts[self.half][0], 1)
        bottom_right = self.send(parts[self.half][1], -1)
        bottom_left = self.send(parts[most][1], 1)
        top_right = self.send(parts[-most][0], -1)
        for step in range(most, 0, -1):
            top_left = self.send(add(parts[step][0], top_left), 1)
            bottom_right = self.send(add(parts[-step][1], bottom_right), -1)
            if step > 1:
                bottom_left = self.send(add(parts[step - 1][1], bottom_left), 1)
                top_right = self.send(add(parts[1 - step][0], top_right), -1)
        return (top_left, top_right), (bottom_left, bottom_right)

    def part_types(self, distances):
        types = []
        for k in distances:
            first = BF16 if k == self.half or k == 1 - self.half else F32
            second = BF16 if k == self.half or k == self.half - 1 else F32
            types += [first, second]
        return types


def add_kernel(block_ref, arrived_ref, out_ref):
    out_ref[...] = (block_ref[...] + arrived_ref[...].astype(F32)).astype(BF16)


def add(block, arrived):
    return call(add_kernel, [(block.shape, BF16)], block, arrived)[0]


def sum_kernel(*refs):
    out_ref = refs[-1]
    rows = refs[0].shape[0]
    for i in range(len(refs) // 3):
        own, left, right = refs[3 * i : 3 * i + 3]
        arrived = left[...].astype(F32) + right[...].astype(F32)
        out_ref[pl.ds(i * rows, rows), :] = (own[...] + arrived).astype(BF16)


class Copies:
    def __init__(self, sems):
        self.sems, self.started = sems, []

    def start(self, source, target):
        copy = pltpu.make_async_copy(source, target, self.sems.at[len(self.started)])
        copy.start()
        self.started.append(copy)

    def wait(self):
        for copy in self.started:
            copy.wait()


def strips(gate_shape, down_shape):
    local_experts, depth, hidden_dim = gate_shape
    _, height, feature_dim = down_shape
    row, places = 0, []
    for _ in range(local_experts):
        pair = [(row, depth), (row + depth, depth)]
        row += 2 * depth
        downs = []
        for begin in range(0, feature_dim, hidden_dim):
            downs.append((row, height, begin, min(hidden_dim, feature_dim - begin)))
            row += height
        places.append((pair, downs))
    return row, places


def pack(ids, scores, tokens, shards):
    rows, cols = tokens.shape
    mid = rows // 2
    quarter = LANES // 4
    inputs = [ids, scores, tokens, *shards]
    packed_shape, places, count = None, [], 0
    if shards:
        hidden_dim = shards[0].shape[2]
        packed_rows, places = strips(shards[0].shape, shards[2].shape)
        packed_shape = (packed_rows, hidden_dim)
        count = sum(len(pair) + len(downs) for pair, downs in places)

    def kernel(*refs):
        ids_hbm, scores_hbm, tokens_hbm, *shards_hbm = refs[: len(inputs)]
        top_ref, bottom_ref, *packed_refs = refs[len(inputs) : -3]
        ids_ref, scores_ref, sems = refs[-3:]
        copies = Copies(sems)
        copies.start(ids_hbm, ids_ref)
        copies.start(scores_hbm, scores_ref)
        copies.start(tokens_hbm.at[pl.ds(0, mid), :], top_ref.at[:, pl.ds(0, cols)])
        copies.start(tokens_hbm.at[pl.ds(mid, mid), :], bottom_ref)
        for local, (pair, downs) in enumerate(places):
            out_ref = packed_refs[0]
            for source, (row, some) in zip(shards_hbm, pair):
                copies.start(source.at[local], out_ref.at[pl.ds(row, some), :])
            for row, some, begin, width in downs:
                source = shards_hbm[2].at[local, :, pl.ds(begin, width)]
                copies.start(source, out_ref.at[pl.ds(row, some), pl.ds(0, width)])
                if width < hidden_dim:
                    rest = hidden_dim - width
                    out_ref[pl.ds(row, some), pl.ds(width, rest)] = jnp.zeros((some, rest), BF16)
        copies.started[0].wait()
        copies.started[1].wait()
        scores = scores_ref[...]
        ids = ids_ref[...]
        route_weight = scores / jnp.sum(scores, axis=0, keepdims=True)
        expert = lax.broadcasted_iota(jnp.int32, (quarter, rows), 0)
        weight_by = jnp.zeros((quarter, rows), F32)
        for choice_k in range(scores.shape[0]):
            one = slice(choice_k, choice_k + 1)
            weight_by = weight_by + jnp.where(ids[one] == expert, route_weight[one], 0.0)
        high = weight_by.astype(BF16).astype(F32)
        weights = jnp.concatenate([high, weight_by - high] * 2, axis=0).T
        lane = lax.broadcasted_iota(jnp.int32, (mid, LANES), 1)
        both = jnp.where(lane < 2 * quarter, weights[:mid], weights[mid:])
        top_ref[:, cols:] = both.astype(BF16)
        for copy in copies.started[2:]:
            copy.wait()

    outs = [pltpu.VMEM((mid, cols + LANES), BF16), pltpu.VMEM((mid, cols), BF16)]
    if shards:
        outs.append(pltpu.VMEM(packed_shape, BF16))
    return pl.pallas_call(
        kernel,
        out_shape=outs,
        in_specs=[pl.BlockSpec(memory_space=pl.ANY)] * len(inputs),
        out_specs=[pl.BlockSpec(memory_space=pltpu.VMEM)] * len(outs),
        scratch_shapes=[
            pltpu.VMEM(ids.shape, ids.dtype),
            pltpu.VMEM(scores.shape, F32),
            pltpu.SemaphoreType.DMA((4 + count,)),
        ],
        compiler_params=pltpu.CompilerParams(vmem_limit_bytes=VMEM_LIMIT),
    )(*[pltpu.with_memory_space_constraint(a, pltpu.HBM) for a in inputs])


def full_weights(shards, packed):
    local_experts, _, hidden_dim = shards[0].shape
    feature_dim = shards[2].shape[2]
    paired = packed is not None
    _, places = strips(shards[0].shape, shards[2].shape)
    depth, height = shards[0].shape[1], shards[2].shape[1]

    def kernel(*refs):
        gate_hbm, up_hbm, down_hbm, *rest = refs
        wide_ref, down_ref, sems = rest[-3:]
        copies = Copies(sems)
        mine = lax.axis_index("group") if paired else 0

        def wide_at(place, local, is_up):
            rows = pl.ds(pl.multiple_of(place * depth, 16), depth)
            return wide_ref.at[rows, pl.ds((2 * local + is_up) * hidden_dim, hidden_dim)]

        def down_at(place, local, begin, cols):
            top = pl.multiple_of(local * hidden_dim + place * height, 16)
            return down_ref.at[pl.ds(top, height), pl.ds(begin, cols)]

        for local in range(local_experts):
            for is_up, source in enumerate((gate_hbm, up_hbm)):
                copies.start(source.at[local], wide_at(mine, local, is_up))
            copies.start(down_hbm.at[local], down_at(mine, local, 0, feature_dim))
        if paired:
            for local, (pair, downs) in enumerate(places):
                for is_up, (row, some) in enumerate(pair):
                    copies.start(rest[0].at[pl.ds(row, some), :], wide_at(1 - mine, local, is_up))
                for row, some, begin, cols in downs:
                    source = rest[0].at[pl.ds(row, some), pl.ds(0, cols)]
                    copies.start(source, down_at(1 - mine, local, begin, cols))
        copies.wait()

    shards = [pltpu.with_memory_space_constraint(w, pltpu.HBM) for w in shards]
    count = 3 * local_experts
    specs = [pl.BlockSpec(memory_space=pl.ANY)] * 3
    if paired:
        count += sum(len(pair) + len(downs) for pair, downs in places)
        specs.append(pl.BlockSpec(memory_space=pltpu.VMEM))
        shards.append(pltpu.with_memory_space_constraint(packed, pltpu.VMEM))
    return pl.pallas_call(
        kernel,
        out_shape=[
            pltpu.VMEM((feature_dim, 2 * local_experts * hidden_dim), BF16),
            pltpu.VMEM((local_experts * hidden_dim, feature_dim), BF16),
        ],
        in_specs=specs,
        out_specs=[pl.BlockSpec(memory_space=pltpu.VMEM)] * 2,
        scratch_shapes=[pltpu.SemaphoreType.DMA((count,))],
        compiler_params=pltpu.CompilerParams(vmem_limit_bytes=VMEM_LIMIT),
    )(*shards)


def transpose_kernel(from_ref, to_ref):
    strip = 2 * LANES

    @pl.loop(0, to_ref.shape[0] // strip)
    def _(i):
        some = pl.ds(pl.multiple_of(i * strip, strip), strip)
        to_ref[some, :] = from_ref[:, some].T


def transposed(weights):
    rows, cols = weights.shape
    return call(transpose_kernel, [((cols, rows), BF16)], weights)[0]


def body(tokens, w_gate, w_up, w_down, route_ids, route_scores, norm_gain, class_head, targets):
    rows_here, feature_dim = tokens.shape
    expert_count = lax.axis_size("expert")
    group_count = lax.axis_size("group")
    local_experts, _, hidden_dim = w_gate.shape
    pair_dim = 2 * hidden_dim
    ring = Ring(expert_count, group_count)
    block = (rows_here, feature_dim)
    mid = rows_here // 2

    shards = [w_gate, w_up, w_down]
    if group_count == 2:
        top, bottom, packed = pack(route_ids.T, route_scores.T, tokens, shards)
        packed = lax.ppermute(packed, "group", [(0, 1), (1, 0)])
    else:
        top, bottom = pack(route_ids.T, route_scores.T, tokens, [])
        shards = [lax.all_gather(w, "group", axis=1, tiled=True) for w in shards]
        packed = None
    wide, down = full_weights(shards, packed)

    def rows_of(refs):
        return jnp.concatenate([ref[...] for ref in refs], axis=0) if len(refs) > 1 else refs[0][...]

    def forward_kernel(count, *refs):
        token_refs, (wide_ref, down_ref) = refs[:count], refs[count : count + 2]
        outs = refs[count + 2 :]
        x = rows_of([ref.at[:, :feature_dim] for ref in token_refs])
        weights = jnp.concatenate([ref[:, feature_dim:] for ref in token_refs[::2]], axis=0).astype(F32)
        lane = lax.broadcasted_iota(jnp.int32, weights.shape, 1)
        quarter = LANES // 4
        hidden = []
        for local in range(local_experts):
            expert = lax.axis_index("expert") * local_experts + local
            scales = []
            for begin in (expert, expert + 2 * quarter):
                here = (lane == begin) | (lane == begin + quarter)
                scales.append(jnp.sum(jnp.where(here, weights, 0.0), axis=1, keepdims=True))
            pieces = [s[i : i + mid] for i in range(0, weights.shape[0], mid) for s in scales]
            scale = jnp.concatenate(pieces, axis=0)
            act = dot(x, wide_ref[:, pl.ds(local * pair_dim, pair_dim)])
            gate_act, up_act = act[:, :hidden_dim], act[:, hidden_dim:]
            sigmoid_gate = jax.nn.sigmoid(gate_act)
            silu = gate_act * sigmoid_gate * scale
            slope = sigmoid_gate * (1.0 + gate_act * (1.0 - sigmoid_gate)) * scale
            cols = pl.ds(local * hidden_dim, hidden_dim)
            outs[0][:, cols] = (up_act * slope).astype(BF16)
            outs[1][:, cols] = silu.astype(BF16)
            hidden.append((silu * up_act).astype(BF16))
        total = dot(jnp.concatenate(hidden, axis=1), down_ref[...])
        for i, out in enumerate(outs[2:]):
            out[...] = total[i * mid : (i + 1) * mid].astype(out.dtype)

    tokens_at, saved_at, part_at = {}, {}, {}
    flops = 2 * rows_here * feature_dim * hidden_dim * local_experts * 3

    def hold(distances, blocks):
        tokens_at[distances] = blocks

    def keep_parts(parts, distances, halves):
        parts.update({k: halves[2 * i : 2 * i + 2] for i, k in enumerate(distances)})

    def part_outs(distances):
        return [((mid, feature_dim), dtype) for dtype in ring.part_types(distances)]

    def forward(distances):
        blocks = tokens_at[distances]
        rows = mid * len(blocks)
        result = call(
            functools.partial(forward_kernel, len(blocks)),
            [((rows, local_experts * hidden_dim), BF16)] * 2 + part_outs(distances),
            *blocks,
            wide,
            down,
            flops=flops * rows // rows_here,
        )
        saved_at[distances] = result[:2]
        keep_parts(part_at, distances, result[2:])

    ring.gather(top, bottom, hold, paced=True)
    for distances in tokens_at:
        forward(distances)
    gain = norm_gain.reshape(1, feature_dim)
    half_shape = (mid, feature_dim)
    moe_top, moe_bottom = [
        call(sum_kernel, [(half_shape, BF16)], own, *arrived)[0]
        for own, arrived in zip(part_at[0], ring.scatter(part_at))
    ]

    norm_at, mean_at = {}, {}

    def residual_of(token_refs, moe_refs):
        token_rows = rows_of([ref.at[:, :feature_dim] for ref in token_refs]).astype(F32)
        return token_rows + rows_of(moe_refs).astype(F32)

    def inv_rms_of(residual):
        return lax.rsqrt(jnp.mean(residual * residual, axis=-1, keepdims=True) + NORM_EPS)

    def norm_kernel(distances, count, *refs):
        residual = residual_of(refs[:count], refs[count : 2 * count])
        gain_ref, so_far, out_ref, residual_ref, inv_ref = refs[2 * count :]
        inv_rms = inv_rms_of(residual)
        residual_ref[...] = residual
        inv_ref[...] = jnp.broadcast_to(inv_rms, inv_ref.shape)
        normed = residual * inv_rms * gain_ref[...]
        pooled = so_far[...]
        row = lax.broadcasted_iota(jnp.int32, pooled.shape, 0)
        for i, k in enumerate(distances):
            part = normed[i * rows_here : (i + 1) * rows_here]
            mean = jnp.mean(part, axis=0, keepdims=True)
            pooled = jnp.where(row == ring.device_at(k), mean, pooled)
        out_ref[...] = pooled

    pooled_shape = (expert_count, feature_dim)
    mean_at["pooled"] = jnp.zeros(pooled_shape, F32)

    def norm(distances, blocks):
        rows = mid * len(blocks)
        mean_at["pooled"], *norm_at[distances] = call(
            functools.partial(norm_kernel, distances, len(blocks)),
            [(pooled_shape, F32), ((rows, feature_dim), F32), ((rows, LANES), F32)],
            *tokens_at[distances],
            *blocks,
            gain,
            mean_at["pooled"],
        )

    ring.gather(moe_top, moe_bottom, norm)
    pooled = mean_at["pooled"].astype(BF16)
    logits = dot(pooled, class_head)
    target_rows = targets.reshape(expert_count, -1).astype(F32)
    logit_grad = (LOSS_SCALE * (jax.nn.sigmoid(logits) - target_rows)).astype(BF16)
    pooled_grad = dot_t(logit_grad, class_head)
    span = 2
    for masks in ([1], list(range(span, expert_count, span))):
        mine = pooled_grad.astype(BF16)
        pooled_grad = mine.astype(F32)
        for mask in masks:
            pairs = [(e, e ^ mask) for e in range(expert_count)]
            pooled_grad = pooled_grad + lax.ppermute(mine, "expert", pairs).astype(F32)

    both = jnp.concatenate([pooled, logit_grad], axis=1)
    if group_count == 2:
        both = jnp.concatenate([both, lax.ppermute(both, "group", [(0, 1), (1, 0)])], axis=0)
    else:
        both = lax.all_gather(both, "group", axis=0, tiled=True)
    head_grad = lax.dot_general(
        both[:, :feature_dim],
        both[:, feature_dim:],
        (((0,), (0,)), ((), ())),
        preferred_element_type=F32,
    )

    def backward_kernel(distances, residual_ref, inv_ref, gate_save, up_save, *refs):
        grad_ref, gain_ref, wide_ref, down_ref, *outs = refs
        residual, inv_rms = residual_ref[...], inv_ref[:, :1]
        cube = inv_rms * inv_rms * inv_rms
        parts = []
        for i, k in enumerate(distances):
            rows = slice(i * rows_here, (i + 1) * rows_here)
            scaled = gain_ref[...] * grad_ref[pl.ds(ring.device_at(k), 1), :] / rows_here
            slope = cube[rows] * jnp.mean(residual[rows] * scaled, axis=-1, keepdims=True)
            parts.append(inv_rms[rows] * scaled - residual[rows] * slope)
        resid_grad = jnp.concatenate(parts, axis=0) if len(parts) > 1 else parts[0]
        down_back = dot(resid_grad.astype(BF16), down_ref[...])
        grads = []
        for local in range(local_experts):
            cols = slice(local * hidden_dim, (local + 1) * hidden_dim)
            for save in (gate_save, up_save):
                grads.append((down_back[:, cols] * save[:, cols].astype(F32)).astype(BF16))
        total = dot(jnp.concatenate(grads, axis=1), wide_ref[...])
        if distances == (0,):
            total = total + resid_grad
        rows = total.shape[0] // len(outs)
        for i, out in enumerate(outs):
            out[...] = total[i * rows : (i + 1) * rows].astype(out.dtype)

    wide_t, down_t = transposed(wide), transposed(down)
    back_at = {}

    def backward(distances):
        result = call(
            functools.partial(backward_kernel, distances),
            part_outs(distances),
            *norm_at[distances],
            *saved_at[distances],
            pooled_grad,
            gain,
            wide_t,
            down_t,
            flops=flops * len(distances),
        )
        keep_parts(back_at, distances, result)

    for distances in reversed(list(tokens_at)):
        backward(distances)
    (top_left, top_right), (bottom_left, bottom_right) = ring.scatter(back_at)
    token_grad = pl.pallas_call(
        sum_kernel,
        out_shape=jax.ShapeDtypeStruct(block, BF16),
        in_specs=[pl.BlockSpec(memory_space=pltpu.VMEM)] * 6,
        out_specs=pl.BlockSpec(memory_space=pltpu.VMEM),
        compiler_params=pltpu.CompilerParams(vmem_limit_bytes=VMEM_LIMIT),
    )(back_at[0][0], top_left, top_right, back_at[0][1], bottom_left, bottom_right)
    return (token_grad, head_grad)


def solution(mesh):
    in_specs = (
        P(("rep", "expert", "group"), None),
        P("expert", "group", None),
        P("expert", "group", None),
        P("expert", "group", None),
        P(("rep", "expert", "group"), None),
        P(("rep", "expert", "group"), None),
        P(),
        P(None, "expert"),
        P("rep", "group", "expert"),
    )
    out_specs = (P(("rep", "expert", "group"), None), P("rep", "expert"))
    return jax.shard_map(body, mesh=mesh, in_specs=in_specs, out_specs=out_specs, check_vma=False)
```

```python
import functools

import jax
import jax.numpy as jnp
from jax import lax
from jax.experimental import pallas as pl
from jax.experimental.pallas import tpu as pltpu
from jax.sharding import PartitionSpec as P

LOSS_SCALE = 8.0
NORM_EPS = 1e-06
F32 = jnp.float32
BF16 = jnp.bfloat16
LANES = 128
VMEM_LIMIT = 32 * 1024 * 1024


def dot(left, right):
    return jnp.dot(left, right, preferred_element_type=F32)


def dot_t(left, right):
    return lax.dot_general(left, right, (((1,), (1,)), ((), ())), preferred_element_type=F32)


def call(kernel, outs, *args, flops=0):
    args = [pltpu.with_memory_space_constraint(a, pltpu.VMEM) for a in args]
    size = sum(a.size * a.dtype.itemsize for a in args)
    return pl.pallas_call(
        kernel,
        out_shape=[pltpu.VMEM(shape, dtype) for shape, dtype in outs],
        in_specs=[pl.BlockSpec(memory_space=pltpu.VMEM)] * len(args),
        out_specs=[pl.BlockSpec(memory_space=pltpu.VMEM)] * len(outs),
        compiler_params=pltpu.CompilerParams(vmem_limit_bytes=VMEM_LIMIT),
        cost_estimate=pl.CostEstimate(flops=flops, bytes_accessed=size, transcendentals=0),
    )(*args)


def after(value, guards):
    def kernel(*refs):
        pass

    args = [pltpu.with_memory_space_constraint(a, pltpu.VMEM) for a in (value, *guards)]
    return pl.pallas_call(
        kernel,
        out_shape=pltpu.VMEM(value.shape, value.dtype),
        in_specs=[pl.BlockSpec(memory_space=pltpu.VMEM)] * len(args),
        out_specs=pl.BlockSpec(memory_space=pltpu.VMEM),
        input_output_aliases={0: 0},
        compiler_params=pltpu.CompilerParams(vmem_limit_bytes=VMEM_LIMIT),
    )(*args)


class Ring:
    def __init__(self, expert_count, group_count):
        self.count = expert_count
        self.half = expert_count // 2
        self.snake = group_count == 2
        if self.snake:
            self.order = list(range(0, expert_count, 2)) + list(range(expert_count - 1, 0, -2))
        else:
            self.order = list(range(expert_count))

    def send(self, value, distance):
        pairs = [
            (self.order[i], self.order[(i + distance) % self.count]) for i in range(self.count)
        ]
        return lax.ppermute(value, "expert", pairs)

    def device_at(self, distance):
        here = lax.axis_index("expert")
        count = self.count
        if self.snake:
            here = jnp.where(here % 2 == 0, here // 2, count - 1 - here // 2)
        there = lax.rem(here + distance % count, count)
        if self.snake:
            there = jnp.where(there < self.half, 2 * there, 2 * (count - 1 - there) + 1)
        return there

    def gather(self, top, bottom, use, guard=None):
        top_left = top_right = top
        bottom_left = bottom_right = bottom
        use((0,), (top, bottom))
        for step in range(1, self.half):
            if guard is not None and step == self.half - 1:
                top_right = after(top_right, [guard])
            top_left = self.send(top_left, 1)
            top_right = self.send(top_right, -1)
            bottom_left = self.send(bottom_left, 1)
            bottom_right = self.send(bottom_right, -1)
            use((-step, step), (top_left, bottom_left, top_right, bottom_right))
        use((self.half,), (self.send(top_left, 1), self.send(bottom_right, -1)))

    def scatter(self, parts):
        most = self.half - 1
        top_left = self.send(parts[self.half][0], 1)
        bottom_right = self.send(parts[self.half][1], -1)
        bottom_left = self.send(parts[most][1], 1)
        top_right = self.send(parts[-most][0], -1)
        for step in range(most, 0, -1):
            top_left = self.send(add(parts[step][0], top_left), 1)
            bottom_right = self.send(add(parts[-step][1], bottom_right), -1)
            if step > 1:
                bottom_left = self.send(add(parts[step - 1][1], bottom_left), 1)
                top_right = self.send(add(parts[1 - step][0], top_right), -1)
        return (top_left, top_right), (bottom_left, bottom_right)

    def part_types(self, distances):
        types = []
        for k in distances:
            first = BF16 if k == self.half or k == 1 - self.half else F32
            second = BF16 if k == self.half or k == self.half - 1 else F32
            types += [first, second]
        return types


def add_kernel(block_ref, arrived_ref, out_ref):
    out_ref[...] = (block_ref[...] + arrived_ref[...].astype(F32)).astype(BF16)


def add(block, arrived):
    return call(add_kernel, [(block.shape, BF16)], block, arrived)[0]


def sum_kernel(*refs):
    out_ref = refs[-1]
    rows = refs[0].shape[0]
    for i in range(len(refs) // 3):
        own, left, right = refs[3 * i : 3 * i + 3]
        arrived = left[...].astype(F32) + right[...].astype(F32)
        out_ref[pl.ds(i * rows, rows), :] = (own[...] + arrived).astype(BF16)


class Copies:
    def __init__(self, sems):
        self.sems, self.started = sems, []

    def start(self, source, target):
        copy = pltpu.make_async_copy(source, target, self.sems.at[len(self.started)])
        copy.start()
        self.started.append(copy)

    def wait(self):
        for copy in self.started:
            copy.wait()


def strips(gate_shape, down_shape):
    local_experts, depth, hidden_dim = gate_shape
    _, height, feature_dim = down_shape
    row, places = 0, []
    for _ in range(local_experts):
        pair = [(row, depth), (row + depth, depth)]
        row += 2 * depth
        downs = []
        for begin in range(0, feature_dim, hidden_dim):
            downs.append((row, height, begin, min(hidden_dim, feature_dim - begin)))
            row += height
        places.append((pair, downs))
    return row, places


def pack(ids, scores, tokens, shards):
    rows, cols = tokens.shape
    mid = rows // 2
    quarter = LANES // 4
    inputs = [ids, scores, tokens, *shards]
    packed_shape, places, count = None, [], 0
    if shards:
        hidden_dim = shards[0].shape[2]
        packed_rows, places = strips(shards[0].shape, shards[2].shape)
        packed_shape = (packed_rows, hidden_dim)
        count = sum(len(pair) + len(downs) for pair, downs in places)

    def kernel(*refs):
        ids_hbm, scores_hbm, tokens_hbm, *shards_hbm = refs[: len(inputs)]
        top_ref, bottom_ref, *packed_refs = refs[len(inputs) : -3]
        ids_ref, scores_ref, sems = refs[-3:]
        copies = Copies(sems)
        copies.start(ids_hbm, ids_ref)
        copies.start(scores_hbm, scores_ref)
        copies.start(tokens_hbm.at[pl.ds(0, mid), :], top_ref.at[:, pl.ds(0, cols)])
        copies.start(tokens_hbm.at[pl.ds(mid, mid), :], bottom_ref)
        for local, (pair, downs) in enumerate(places):
            out_ref = packed_refs[0]
            for source, (row, some) in zip(shards_hbm, pair):
                copies.start(source.at[local], out_ref.at[pl.ds(row, some), :])
            for row, some, begin, width in downs:
                source = shards_hbm[2].at[local, :, pl.ds(begin, width)]
                copies.start(source, out_ref.at[pl.ds(row, some), pl.ds(0, width)])
                if width < hidden_dim:
                    rest = hidden_dim - width
                    out_ref[pl.ds(row, some), pl.ds(width, rest)] = jnp.zeros((some, rest), BF16)
        copies.started[0].wait()
        copies.started[1].wait()
        scores = scores_ref[...]
        ids = ids_ref[...]
        route_weight = scores / jnp.sum(scores, axis=0, keepdims=True)
        expert = lax.broadcasted_iota(jnp.int32, (quarter, rows), 0)
        weight_by = jnp.zeros((quarter, rows), F32)
        for choice_k in range(scores.shape[0]):
            one = slice(choice_k, choice_k + 1)
            weight_by = weight_by + jnp.where(ids[one] == expert, route_weight[one], 0.0)
        high = weight_by.astype(BF16).astype(F32)
        weights = jnp.concatenate([high, weight_by - high] * 2, axis=0).T
        lane = lax.broadcasted_iota(jnp.int32, (mid, LANES), 1)
        both = jnp.where(lane < 2 * quarter, weights[:mid], weights[mid:])
        top_ref[:, cols:] = both.astype(BF16)
        for copy in copies.started[2:]:
            copy.wait()

    outs = [pltpu.VMEM((mid, cols + LANES), BF16), pltpu.VMEM((mid, cols), BF16)]
    if shards:
        outs.append(pltpu.VMEM(packed_shape, BF16))
    return pl.pallas_call(
        kernel,
        out_shape=outs,
        in_specs=[pl.BlockSpec(memory_space=pl.ANY)] * len(inputs),
        out_specs=[pl.BlockSpec(memory_space=pltpu.VMEM)] * len(outs),
        scratch_shapes=[
            pltpu.VMEM(ids.shape, ids.dtype),
            pltpu.VMEM(scores.shape, F32),
            pltpu.SemaphoreType.DMA((4 + count,)),
        ],
        compiler_params=pltpu.CompilerParams(vmem_limit_bytes=VMEM_LIMIT),
    )(*[pltpu.with_memory_space_constraint(a, pltpu.HBM) for a in inputs])


def full_weights(shards, packed):
    local_experts, _, hidden_dim = shards[0].shape
    feature_dim = shards[2].shape[2]
    paired = packed is not None
    _, places = strips(shards[0].shape, shards[2].shape)
    depth, height = shards[0].shape[1], shards[2].shape[1]

    def kernel(*refs):
        gate_hbm, up_hbm, down_hbm, *rest = refs
        wide_ref, down_ref, sems = rest[-3:]
        copies = Copies(sems)
        mine = lax.axis_index("group") if paired else 0

        def wide_at(place, local, is_up):
            rows = pl.ds(pl.multiple_of(place * depth, 16), depth)
            return wide_ref.at[rows, pl.ds((2 * local + is_up) * hidden_dim, hidden_dim)]

        def down_at(place, local, begin, cols):
            top = pl.multiple_of(local * hidden_dim + place * height, 16)
            return down_ref.at[pl.ds(top, height), pl.ds(begin, cols)]

        for local in range(local_experts):
            for is_up, source in enumerate((gate_hbm, up_hbm)):
                copies.start(source.at[local], wide_at(mine, local, is_up))
            copies.start(down_hbm.at[local], down_at(mine, local, 0, feature_dim))
        if paired:
            for local, (pair, downs) in enumerate(places):
                for is_up, (row, some) in enumerate(pair):
                    copies.start(rest[0].at[pl.ds(row, some), :], wide_at(1 - mine, local, is_up))
                for row, some, begin, cols in downs:
                    source = rest[0].at[pl.ds(row, some), pl.ds(0, cols)]
                    copies.start(source, down_at(1 - mine, local, begin, cols))
        copies.wait()

    shards = [pltpu.with_memory_space_constraint(w, pltpu.HBM) for w in shards]
    count = 3 * local_experts
    specs = [pl.BlockSpec(memory_space=pl.ANY)] * 3
    if paired:
        count += sum(len(pair) + len(downs) for pair, downs in places)
        specs.append(pl.BlockSpec(memory_space=pltpu.VMEM))
        shards.append(pltpu.with_memory_space_constraint(packed, pltpu.VMEM))
    return pl.pallas_call(
        kernel,
        out_shape=[
            pltpu.VMEM((feature_dim, 2 * local_experts * hidden_dim), BF16),
            pltpu.VMEM((local_experts * hidden_dim, feature_dim), BF16),
        ],
        in_specs=specs,
        out_specs=[pl.BlockSpec(memory_space=pltpu.VMEM)] * 2,
        scratch_shapes=[pltpu.SemaphoreType.DMA((count,))],
        compiler_params=pltpu.CompilerParams(vmem_limit_bytes=VMEM_LIMIT),
    )(*shards)


def transpose_kernel(from_ref, to_ref):
    strip = 2 * LANES

    @pl.loop(0, to_ref.shape[0] // strip)
    def _(i):
        some = pl.ds(pl.multiple_of(i * strip, strip), strip)
        to_ref[some, :] = from_ref[:, some].T


def transposed(weights):
    rows, cols = weights.shape
    return call(transpose_kernel, [((cols, rows), BF16)], weights)[0]


def body(tokens, w_gate, w_up, w_down, route_ids, route_scores, norm_gain, class_head, targets):
    rows_here, feature_dim = tokens.shape
    expert_count = lax.axis_size("expert")
    group_count = lax.axis_size("group")
    local_experts, _, hidden_dim = w_gate.shape
    pair_dim = 2 * hidden_dim
    ring = Ring(expert_count, group_count)
    block = (rows_here, feature_dim)
    mid = rows_here // 2

    shards = [w_gate, w_up, w_down]
    if group_count == 2:
        top, bottom, packed = pack(route_ids.T, route_scores.T, tokens, shards)
        packed = lax.ppermute(packed, "group", [(0, 1), (1, 0)])
    else:
        top, bottom = pack(route_ids.T, route_scores.T, tokens, [])
        shards = [lax.all_gather(w, "group", axis=1, tiled=True) for w in shards]
        packed = None
    wide, down = full_weights(shards, packed)

    def rows_of(refs):
        return jnp.concatenate([ref[...] for ref in refs], axis=0) if len(refs) > 1 else refs[0][...]

    def forward_kernel(count, *refs):
        token_refs, (wide_ref, down_ref) = refs[:count], refs[count : count + 2]
        outs = refs[count + 2 :]
        x = rows_of([ref.at[:, :feature_dim] for ref in token_refs])
        weights = jnp.concatenate([ref[:, feature_dim:] for ref in token_refs[::2]], axis=0).astype(F32)
        lane = lax.broadcasted_iota(jnp.int32, weights.shape, 1)
        quarter = LANES // 4
        hidden = []
        for local in range(local_experts):
            expert = lax.axis_index("expert") * local_experts + local
            scales = []
            for begin in (expert, expert + 2 * quarter):
                here = (lane == begin) | (lane == begin + quarter)
                scales.append(jnp.sum(jnp.where(here, weights, 0.0), axis=1, keepdims=True))
            pieces = [s[i : i + mid] for i in range(0, weights.shape[0], mid) for s in scales]
            scale = jnp.concatenate(pieces, axis=0)
            act = dot(x, wide_ref[:, pl.ds(local * pair_dim, pair_dim)])
            gate_act, up_act = act[:, :hidden_dim], act[:, hidden_dim:]
            sigmoid_gate = jax.nn.sigmoid(gate_act)
            silu = gate_act * sigmoid_gate * scale
            slope = sigmoid_gate * (1.0 + gate_act * (1.0 - sigmoid_gate)) * scale
            cols = pl.ds(local * hidden_dim, hidden_dim)
            outs[0][:, cols] = (up_act * slope).astype(BF16)
            outs[1][:, cols] = silu.astype(BF16)
            hidden.append((silu * up_act).astype(BF16))
        total = dot(jnp.concatenate(hidden, axis=1), down_ref[...])
        for i, out in enumerate(outs[2:]):
            out[...] = total[i * mid : (i + 1) * mid].astype(out.dtype)

    tokens_at, saved_at, part_at = {}, {}, {}
    flops = 2 * rows_here * feature_dim * hidden_dim * local_experts * 3

    def hold(distances, blocks):
        tokens_at[distances] = blocks

    def keep_parts(parts, distances, halves):
        parts.update({k: halves[2 * i : 2 * i + 2] for i, k in enumerate(distances)})

    def part_outs(distances):
        return [((mid, feature_dim), dtype) for dtype in ring.part_types(distances)]

    def forward(distances):
        blocks = tokens_at[distances]
        rows = mid * len(blocks)
        result = call(
            functools.partial(forward_kernel, len(blocks)),
            [((rows, local_experts * hidden_dim), BF16)] * 2 + part_outs(distances),
            *blocks,
            wide,
            down,
            flops=flops * rows // rows_here,
        )
        saved_at[distances] = result[:2]
        keep_parts(part_at, distances, result[2:])

    ring.gather(top, bottom, hold, wide)
    for distances in tokens_at:
        forward(distances)
    gain = norm_gain.reshape(1, feature_dim)
    half_shape = (mid, feature_dim)
    moe_top, moe_bottom = [
        call(sum_kernel, [(half_shape, BF16)], own, *arrived)[0]
        for own, arrived in zip(part_at[0], ring.scatter(part_at))
    ]

    norm_at, mean_at = {}, {}

    def residual_of(token_refs, moe_refs):
        token_rows = rows_of([ref.at[:, :feature_dim] for ref in token_refs]).astype(F32)
        return token_rows + rows_of(moe_refs).astype(F32)

    def inv_rms_of(residual):
        return lax.rsqrt(jnp.mean(residual * residual, axis=-1, keepdims=True) + NORM_EPS)

    def norm_kernel(distances, count, *refs):
        residual = residual_of(refs[:count], refs[count : 2 * count])
        gain_ref, so_far, out_ref, residual_ref, inv_ref = refs[2 * count :]
        inv_rms = inv_rms_of(residual)
        residual_ref[...] = residual
        inv_ref[...] = jnp.broadcast_to(inv_rms, inv_ref.shape)
        normed = residual * inv_rms * gain_ref[...]
        pooled = so_far[...]
        row = lax.broadcasted_iota(jnp.int32, pooled.shape, 0)
        for i, k in enumerate(distances):
            part = normed[i * rows_here : (i + 1) * rows_here]
            mean = jnp.mean(part, axis=0, keepdims=True)
            pooled = jnp.where(row == ring.device_at(k), mean, pooled)
        out_ref[...] = pooled

    pooled_shape = (expert_count, feature_dim)
    mean_at["pooled"] = jnp.zeros(pooled_shape, F32)

    def norm(distances, blocks):
        rows = mid * len(blocks)
        mean_at["pooled"], *norm_at[distances] = call(
            functools.partial(norm_kernel, distances, len(blocks)),
            [(pooled_shape, F32), ((rows, feature_dim), F32), ((rows, LANES), F32)],
            *tokens_at[distances],
            *blocks,
            gain,
            mean_at["pooled"],
        )

    ring.gather(moe_top, moe_bottom, norm)
    pooled = mean_at["pooled"].astype(BF16)
    logits = dot(pooled, class_head)
    target_rows = targets.reshape(expert_count, -1).astype(F32)
    logit_grad = (LOSS_SCALE * (jax.nn.sigmoid(logits) - target_rows)).astype(BF16)
    pooled_grad = dot_t(logit_grad, class_head)
    span = 2
    for masks in ([1], list(range(span, expert_count, span))):
        mine = pooled_grad.astype(BF16)
        pooled_grad = mine.astype(F32)
        for mask in masks:
            pairs = [(e, e ^ mask) for e in range(expert_count)]
            pooled_grad = pooled_grad + lax.ppermute(mine, "expert", pairs).astype(F32)

    both = jnp.concatenate([pooled, logit_grad], axis=1)
    if group_count == 2:
        both = jnp.concatenate([both, lax.ppermute(both, "group", [(0, 1), (1, 0)])], axis=0)
    else:
        both = lax.all_gather(both, "group", axis=0, tiled=True)
    head_grad = lax.dot_general(
        both[:, :feature_dim],
        both[:, feature_dim:],
        (((0,), (0,)), ((), ())),
        preferred_element_type=F32,
    )

    def backward_kernel(distances, residual_ref, inv_ref, gate_save, up_save, *refs):
        grad_ref, gain_ref, wide_ref, down_ref, *outs = refs
        residual, inv_rms = residual_ref[...], inv_ref[:, :1]
        cube = inv_rms * inv_rms * inv_rms
        parts = []
        for i, k in enumerate(distances):
            rows = slice(i * rows_here, (i + 1) * rows_here)
            scaled = gain_ref[...] * grad_ref[pl.ds(ring.device_at(k), 1), :] / rows_here
            slope = cube[rows] * jnp.mean(residual[rows] * scaled, axis=-1, keepdims=True)
            parts.append(inv_rms[rows] * scaled - residual[rows] * slope)
        resid_grad = jnp.concatenate(parts, axis=0) if len(parts) > 1 else parts[0]
        down_back = dot(resid_grad.astype(BF16), down_ref[...])
        grads = []
        for local in range(local_experts):
            cols = slice(local * hidden_dim, (local + 1) * hidden_dim)
            for save in (gate_save, up_save):
                grads.append((down_back[:, cols] * save[:, cols].astype(F32)).astype(BF16))
        total = dot(jnp.concatenate(grads, axis=1), wide_ref[...])
        if distances == (0,):
            total = total + resid_grad
        rows = total.shape[0] // len(outs)
        for i, out in enumerate(outs):
            out[...] = total[i * rows : (i + 1) * rows].astype(out.dtype)

    wide_t, down_t = transposed(wide), transposed(down)
    back_at = {}

    def backward(distances):
        result = call(
            functools.partial(backward_kernel, distances),
            part_outs(distances),
            *norm_at[distances],
            *saved_at[distances],
            pooled_grad,
            gain,
            wide_t,
            down_t,
            flops=flops * len(distances),
        )
        keep_parts(back_at, distances, result)

    for distances in reversed(list(tokens_at)):
        backward(distances)
    (top_left, top_right), (bottom_left, bottom_right) = ring.scatter(back_at)
    token_grad = pl.pallas_call(
        sum_kernel,
        out_shape=jax.ShapeDtypeStruct(block, BF16),
        in_specs=[pl.BlockSpec(memory_space=pltpu.VMEM)] * 6,
        out_specs=pl.BlockSpec(memory_space=pltpu.VMEM),
        compiler_params=pltpu.CompilerParams(vmem_limit_bytes=VMEM_LIMIT),
    )(back_at[0][0], top_left, top_right, back_at[0][1], bottom_left, bottom_right)
    return (token_grad, head_grad)


def solution(mesh):
    in_specs = (
        P(("rep", "expert", "group"), None),
        P("expert", "group", None),
        P("expert", "group", None),
        P("expert", "group", None),
        P(("rep", "expert", "group"), None),
        P(("rep", "expert", "group"), None),
        P(),
        P(None, "expert"),
        P("rep", "group", "expert"),
    )
    out_specs = (P(("rep", "expert", "group"), None), P("rep", "expert"))
    return jax.shard_map(body, mesh=mesh, in_specs=in_specs, out_specs=out_specs, check_vma=False)
```

```python
import functools

import jax
import jax.numpy as jnp
from jax import lax
from jax.experimental import pallas as pl
from jax.experimental.pallas import tpu as pltpu
from jax.sharding import PartitionSpec as P

LOSS_SCALE = 8.0
NORM_EPS = 1e-06
F32 = jnp.float32
BF16 = jnp.bfloat16
LANES = 128
VMEM_LIMIT = 32 * 1024 * 1024


def dot(left, right):
    return jnp.dot(left, right, preferred_element_type=F32)


def dot_t(left, right):
    return lax.dot_general(left, right, (((1,), (1,)), ((), ())), preferred_element_type=F32)


def call(kernel, outs, *args, flops=0):
    args = [pltpu.with_memory_space_constraint(a, pltpu.VMEM) for a in args]
    size = sum(a.size * a.dtype.itemsize for a in args)
    return pl.pallas_call(
        kernel,
        out_shape=[pltpu.VMEM(shape, dtype) for shape, dtype in outs],
        in_specs=[pl.BlockSpec(memory_space=pltpu.VMEM)] * len(args),
        out_specs=[pl.BlockSpec(memory_space=pltpu.VMEM)] * len(outs),
        compiler_params=pltpu.CompilerParams(vmem_limit_bytes=VMEM_LIMIT),
        cost_estimate=pl.CostEstimate(flops=flops, bytes_accessed=size, transcendentals=0),
    )(*args)


def after(value, guards):
    def kernel(*refs):
        pass

    args = [pltpu.with_memory_space_constraint(a, pltpu.VMEM) for a in (value, *guards)]
    return pl.pallas_call(
        kernel,
        out_shape=pltpu.VMEM(value.shape, value.dtype),
        in_specs=[pl.BlockSpec(memory_space=pltpu.VMEM)] * len(args),
        out_specs=pl.BlockSpec(memory_space=pltpu.VMEM),
        input_output_aliases={0: 0},
        compiler_params=pltpu.CompilerParams(vmem_limit_bytes=VMEM_LIMIT),
    )(*args)


class Ring:
    def __init__(self, expert_count, group_count):
        self.count = expert_count
        self.half = expert_count // 2
        self.snake = group_count == 2
        if self.snake:
            self.order = list(range(0, expert_count, 2)) + list(range(expert_count - 1, 0, -2))
        else:
            self.order = list(range(expert_count))

    def send(self, value, distance):
        pairs = [
            (self.order[i], self.order[(i + distance) % self.count]) for i in range(self.count)
        ]
        return lax.ppermute(value, "expert", pairs)

    def device_at(self, distance):
        here = lax.axis_index("expert")
        count = self.count
        if self.snake:
            here = jnp.where(here % 2 == 0, here // 2, count - 1 - here // 2)
        there = lax.rem(here + distance % count, count)
        if self.snake:
            there = jnp.where(there < self.half, 2 * there, 2 * (count - 1 - there) + 1)
        return there

    def gather(self, top, bottom, use, guard=None):
        top_left = top_right = top
        bottom_left = bottom_right = bottom
        use((0,), (top, bottom))
        for step in range(1, self.half):
            if guard is not None and step == self.half - 1:
                top_right = after(top_right, [guard])
            top_left = self.send(top_left, 1)
            top_right = self.send(top_right, -1)
            bottom_left = self.send(bottom_left, 1)
            bottom_right = self.send(bottom_right, -1)
            use((-step, step), (top_left, bottom_left, top_right, bottom_right))
        use((self.half,), (self.send(top_left, 1), self.send(bottom_right, -1)))

    def scatter(self, parts):
        most = self.half - 1
        top_left = self.send(parts[self.half][0], 1)
        bottom_right = self.send(parts[self.half][1], -1)
        bottom_left = self.send(parts[most][1], 1)
        top_right = self.send(parts[-most][0], -1)
        for step in range(most, 0, -1):
            top_left = self.send(add(parts[step][0], top_left), 1)
            bottom_right = self.send(add(parts[-step][1], bottom_right), -1)
            if step > 1:
                bottom_left = self.send(add(parts[step - 1][1], bottom_left), 1)
                top_right = self.send(add(parts[1 - step][0], top_right), -1)
        return (top_left, top_right), (bottom_left, bottom_right)

    def part_types(self, distances):
        types = []
        for k in distances:
            first = BF16 if k == self.half or k == 1 - self.half else F32
            second = BF16 if k == self.half or k == self.half - 1 else F32
            types += [first, second]
        return types


def add_kernel(block_ref, arrived_ref, out_ref):
    out_ref[...] = (block_ref[...] + arrived_ref[...].astype(F32)).astype(BF16)


def add(block, arrived):
    return call(add_kernel, [(block.shape, BF16)], block, arrived)[0]


def sum_kernel(*refs):
    out_ref = refs[-1]
    rows = refs[0].shape[0]
    for i in range(len(refs) // 3):
        own, left, right = refs[3 * i : 3 * i + 3]
        arrived = left[...].astype(F32) + right[...].astype(F32)
        out_ref[pl.ds(i * rows, rows), :] = (own[...] + arrived).astype(BF16)


class Copies:
    def __init__(self, sems):
        self.sems, self.started = sems, []

    def start(self, source, target):
        copy = pltpu.make_async_copy(source, target, self.sems.at[len(self.started)])
        copy.start()
        self.started.append(copy)

    def wait(self):
        for copy in self.started:
            copy.wait()


def strips(gate_shape, down_shape):
    local_experts, depth, hidden_dim = gate_shape
    _, height, feature_dim = down_shape
    row, places = 0, []
    for _ in range(local_experts):
        pair = [(row, depth), (row + depth, depth)]
        row += 2 * depth
        downs = []
        for begin in range(0, feature_dim, hidden_dim):
            downs.append((row, height, begin, min(hidden_dim, feature_dim - begin)))
            row += height
        places.append((pair, downs))
    return row, places


def pack(ids, scores, tokens, shards):
    rows, cols = tokens.shape
    mid = rows // 2
    quarter = LANES // 4
    inputs = [ids, scores, tokens, *shards]
    packed_shape, places, count = None, [], 0
    if shards:
        hidden_dim = shards[0].shape[2]
        packed_rows, places = strips(shards[0].shape, shards[2].shape)
        packed_shape = (packed_rows, hidden_dim)
        count = sum(len(pair) + len(downs) for pair, downs in places)

    def kernel(*refs):
        ids_hbm, scores_hbm, tokens_hbm, *shards_hbm = refs[: len(inputs)]
        top_ref, bottom_ref, *packed_refs = refs[len(inputs) : -3]
        ids_ref, scores_ref, sems = refs[-3:]
        copies = Copies(sems)
        copies.start(ids_hbm, ids_ref)
        copies.start(scores_hbm, scores_ref)
        copies.start(tokens_hbm.at[pl.ds(0, mid), :], top_ref.at[:, pl.ds(0, cols)])
        copies.start(tokens_hbm.at[pl.ds(mid, mid), :], bottom_ref)
        for local, (pair, downs) in enumerate(places):
            out_ref = packed_refs[0]
            for source, (row, some) in zip(shards_hbm, pair):
                copies.start(source.at[local], out_ref.at[pl.ds(row, some), :])
            for row, some, begin, width in downs:
                source = shards_hbm[2].at[local, :, pl.ds(begin, width)]
                copies.start(source, out_ref.at[pl.ds(row, some), pl.ds(0, width)])
                if width < hidden_dim:
                    rest = hidden_dim - width
                    out_ref[pl.ds(row, some), pl.ds(width, rest)] = jnp.zeros((some, rest), BF16)
        copies.started[0].wait()
        copies.started[1].wait()
        scores = scores_ref[...]
        ids = ids_ref[...]
        route_weight = scores / jnp.sum(scores, axis=0, keepdims=True)
        expert = lax.broadcasted_iota(jnp.int32, (quarter, rows), 0)
        weight_by = jnp.zeros((quarter, rows), F32)
        for choice_k in range(scores.shape[0]):
            one = slice(choice_k, choice_k + 1)
            weight_by = weight_by + jnp.where(ids[one] == expert, route_weight[one], 0.0)
        high = weight_by.astype(BF16).astype(F32)
        weights = jnp.concatenate([high, weight_by - high] * 2, axis=0).T
        lane = lax.broadcasted_iota(jnp.int32, (mid, LANES), 1)
        both = jnp.where(lane < 2 * quarter, weights[:mid], weights[mid:])
        top_ref[:, cols:] = both.astype(BF16)
        for copy in copies.started[2:]:
            copy.wait()

    outs = [pltpu.VMEM((mid, cols + LANES), BF16), pltpu.VMEM((mid, cols), BF16)]
    if shards:
        outs.append(pltpu.VMEM(packed_shape, BF16))
    return pl.pallas_call(
        kernel,
        out_shape=outs,
        in_specs=[pl.BlockSpec(memory_space=pl.ANY)] * len(inputs),
        out_specs=[pl.BlockSpec(memory_space=pltpu.VMEM)] * len(outs),
        scratch_shapes=[
            pltpu.VMEM(ids.shape, ids.dtype),
            pltpu.VMEM(scores.shape, F32),
            pltpu.SemaphoreType.DMA((4 + count,)),
        ],
        compiler_params=pltpu.CompilerParams(vmem_limit_bytes=VMEM_LIMIT),
    )(*[pltpu.with_memory_space_constraint(a, pltpu.HBM) for a in inputs])


def full_weights(shards, packed):
    local_experts, _, hidden_dim = shards[0].shape
    feature_dim = shards[2].shape[2]
    paired = packed is not None
    _, places = strips(shards[0].shape, shards[2].shape)
    depth, height = shards[0].shape[1], shards[2].shape[1]

    def kernel(*refs):
        gate_hbm, up_hbm, down_hbm, *rest = refs
        wide_ref, down_ref, sems = rest[-3:]
        copies = Copies(sems)
        mine = lax.axis_index("group") if paired else 0

        def wide_at(place, local, is_up):
            rows = pl.ds(pl.multiple_of(place * depth, 16), depth)
            return wide_ref.at[rows, pl.ds((2 * local + is_up) * hidden_dim, hidden_dim)]

        def down_at(place, local, begin, cols):
            top = pl.multiple_of(local * hidden_dim + place * height, 16)
            return down_ref.at[pl.ds(top, height), pl.ds(begin, cols)]

        for local in range(local_experts):
            for is_up, source in enumerate((gate_hbm, up_hbm)):
                copies.start(source.at[local], wide_at(mine, local, is_up))
            copies.start(down_hbm.at[local], down_at(mine, local, 0, feature_dim))
        if paired:
            for local, (pair, downs) in enumerate(places):
                for is_up, (row, some) in enumerate(pair):
                    copies.start(rest[0].at[pl.ds(row, some), :], wide_at(1 - mine, local, is_up))
                for row, some, begin, cols in downs:
                    source = rest[0].at[pl.ds(row, some), pl.ds(0, cols)]
                    copies.start(source, down_at(1 - mine, local, begin, cols))
        copies.wait()

    shards = [pltpu.with_memory_space_constraint(w, pltpu.HBM) for w in shards]
    count = 3 * local_experts
    specs = [pl.BlockSpec(memory_space=pl.ANY)] * 3
    if paired:
        count += sum(len(pair) + len(downs) for pair, downs in places)
        specs.append(pl.BlockSpec(memory_space=pltpu.VMEM))
        shards.append(pltpu.with_memory_space_constraint(packed, pltpu.VMEM))
    return pl.pallas_call(
        kernel,
        out_shape=[
            pltpu.VMEM((feature_dim, 2 * local_experts * hidden_dim), BF16),
            pltpu.VMEM((local_experts * hidden_dim, feature_dim), BF16),
        ],
        in_specs=specs,
        out_specs=[pl.BlockSpec(memory_space=pltpu.VMEM)] * 2,
        scratch_shapes=[pltpu.SemaphoreType.DMA((count,))],
        compiler_params=pltpu.CompilerParams(vmem_limit_bytes=VMEM_LIMIT),
        cost_estimate=pl.CostEstimate(
            flops=0,
            bytes_accessed=12 * local_experts * hidden_dim * feature_dim,
            transcendentals=0,
        ),
    )(*shards)


def transpose_kernel(from_ref, to_ref):
    strip = 2 * LANES

    @pl.loop(0, to_ref.shape[0] // strip)
    def _(i):
        some = pl.ds(pl.multiple_of(i * strip, strip), strip)
        to_ref[some, :] = from_ref[:, some].T


def transposed(weights):
    rows, cols = weights.shape
    return call(transpose_kernel, [((cols, rows), BF16)], weights)[0]


def body(tokens, w_gate, w_up, w_down, route_ids, route_scores, norm_gain, class_head, targets):
    rows_here, feature_dim = tokens.shape
    expert_count = lax.axis_size("expert")
    group_count = lax.axis_size("group")
    local_experts, _, hidden_dim = w_gate.shape
    pair_dim = 2 * hidden_dim
    ring = Ring(expert_count, group_count)
    block = (rows_here, feature_dim)
    mid = rows_here // 2

    shards = [w_gate, w_up, w_down]
    if group_count == 2:
        top, bottom, packed = pack(route_ids.T, route_scores.T, tokens, shards)
        packed = lax.ppermute(packed, "group", [(0, 1), (1, 0)])
    else:
        top, bottom = pack(route_ids.T, route_scores.T, tokens, [])
        shards = [lax.all_gather(w, "group", axis=1, tiled=True) for w in shards]
        packed = None
    wide, down = full_weights(shards, packed)

    def rows_of(refs):
        return jnp.concatenate([ref[...] for ref in refs], axis=0) if len(refs) > 1 else refs[0][...]

    def forward_kernel(count, *refs):
        token_refs, (wide_ref, down_ref) = refs[:count], refs[count : count + 2]
        outs = refs[count + 2 :]
        x = rows_of([ref.at[:, :feature_dim] for ref in token_refs])
        weights = jnp.concatenate([ref[:, feature_dim:] for ref in token_refs[::2]], axis=0).astype(F32)
        lane = lax.broadcasted_iota(jnp.int32, weights.shape, 1)
        quarter = LANES // 4
        hidden = []
        for local in range(local_experts):
            expert = lax.axis_index("expert") * local_experts + local
            scales = []
            for begin in (expert, expert + 2 * quarter):
                here = (lane == begin) | (lane == begin + quarter)
                scales.append(jnp.sum(jnp.where(here, weights, 0.0), axis=1, keepdims=True))
            pieces = [s[i : i + mid] for i in range(0, weights.shape[0], mid) for s in scales]
            scale = jnp.concatenate(pieces, axis=0)
            act = dot(x, wide_ref[:, pl.ds(local * pair_dim, pair_dim)])
            gate_act, up_act = act[:, :hidden_dim], act[:, hidden_dim:]
            sigmoid_gate = jax.nn.sigmoid(gate_act)
            silu = gate_act * sigmoid_gate * scale
            slope = sigmoid_gate * (1.0 + gate_act * (1.0 - sigmoid_gate)) * scale
            cols = pl.ds(local * hidden_dim, hidden_dim)
            outs[0][:, cols] = (up_act * slope).astype(BF16)
            outs[1][:, cols] = silu.astype(BF16)
            hidden.append((silu * up_act).astype(BF16))
        total = dot(jnp.concatenate(hidden, axis=1), down_ref[...])
        for i, out in enumerate(outs[2:]):
            out[...] = total[i * mid : (i + 1) * mid].astype(out.dtype)

    tokens_at, saved_at, part_at = {}, {}, {}
    flops = 2 * rows_here * feature_dim * hidden_dim * local_experts * 3

    def hold(distances, blocks):
        tokens_at[distances] = blocks

    def keep_parts(parts, distances, halves):
        parts.update({k: halves[2 * i : 2 * i + 2] for i, k in enumerate(distances)})

    def part_outs(distances):
        return [((mid, feature_dim), dtype) for dtype in ring.part_types(distances)]

    def forward(distances):
        blocks = tokens_at[distances]
        rows = mid * len(blocks)
        result = call(
            functools.partial(forward_kernel, len(blocks)),
            [((rows, local_experts * hidden_dim), BF16)] * 2 + part_outs(distances),
            *blocks,
            wide,
            down,
            flops=flops * rows // rows_here,
        )
        saved_at[distances] = result[:2]
        keep_parts(part_at, distances, result[2:])

    ring.gather(top, bottom, hold, wide)
    for distances in tokens_at:
        forward(distances)
    gain = norm_gain.reshape(1, feature_dim)
    half_shape = (mid, feature_dim)
    moe_top, moe_bottom = [
        call(sum_kernel, [(half_shape, BF16)], own, *arrived)[0]
        for own, arrived in zip(part_at[0], ring.scatter(part_at))
    ]

    norm_at, mean_at = {}, {}

    def residual_of(token_refs, moe_refs):
        token_rows = rows_of([ref.at[:, :feature_dim] for ref in token_refs]).astype(F32)
        return token_rows + rows_of(moe_refs).astype(F32)

    def inv_rms_of(residual):
        return lax.rsqrt(jnp.mean(residual * residual, axis=-1, keepdims=True) + NORM_EPS)

    def norm_kernel(distances, count, *refs):
        residual = residual_of(refs[:count], refs[count : 2 * count])
        gain_ref, so_far, out_ref, residual_ref, inv_ref = refs[2 * count :]
        inv_rms = inv_rms_of(residual)
        residual_ref[...] = residual
        inv_ref[...] = jnp.broadcast_to(inv_rms, inv_ref.shape)
        normed = residual * inv_rms * gain_ref[...]
        pooled = so_far[...]
        row = lax.broadcasted_iota(jnp.int32, pooled.shape, 0)
        for i, k in enumerate(distances):
            part = normed[i * rows_here : (i + 1) * rows_here]
            mean = jnp.mean(part, axis=0, keepdims=True)
            pooled = jnp.where(row == ring.device_at(k), mean, pooled)
        out_ref[...] = pooled

    pooled_shape = (expert_count, feature_dim)
    mean_at["pooled"] = jnp.zeros(pooled_shape, F32)

    def norm(distances, blocks):
        rows = mid * len(blocks)
        mean_at["pooled"], *norm_at[distances] = call(
            functools.partial(norm_kernel, distances, len(blocks)),
            [(pooled_shape, F32), ((rows, feature_dim), F32), ((rows, LANES), F32)],
            *tokens_at[distances],
            *blocks,
            gain,
            mean_at["pooled"],
        )

    ring.gather(moe_top, moe_bottom, norm)
    pooled = mean_at["pooled"].astype(BF16)
    logits = dot(pooled, class_head)
    target_rows = targets.reshape(expert_count, -1).astype(F32)
    logit_grad = (LOSS_SCALE * (jax.nn.sigmoid(logits) - target_rows)).astype(BF16)
    wide_t, down_t = transposed(wide), transposed(down)

    def grad_sum_kernel(count, *refs):
        total = refs[0][...].astype(F32)
        for ref in refs[1:count]:
            total = total + ref[...].astype(F32)
        refs[-1][...] = total.astype(refs[-1].dtype)

    grad_rows = dot_t(logit_grad, class_head).astype(BF16)
    span = 2
    for masks, others, dtype in (
        ([1], [wide_t, down_t], BF16),
        (list(range(span, expert_count, span)), [], F32),
    ):
        terms = [grad_rows]
        for mask in masks:
            pairs = [(e, e ^ mask) for e in range(expert_count)]
            terms.append(lax.ppermute(grad_rows, "expert", pairs))
        grad_rows = call(
            functools.partial(grad_sum_kernel, len(terms)),
            [(pooled_shape, dtype)],
            *terms,
            *others,
        )[0]
    pooled_grad = grad_rows

    both = jnp.concatenate([pooled, logit_grad], axis=1)
    if group_count == 2:
        both = jnp.concatenate([both, lax.ppermute(both, "group", [(0, 1), (1, 0)])], axis=0)
    else:
        both = lax.all_gather(both, "group", axis=0, tiled=True)
    head_grad = lax.dot_general(
        both[:, :feature_dim],
        both[:, feature_dim:],
        (((0,), (0,)), ((), ())),
        preferred_element_type=F32,
    )

    def backward_kernel(distances, residual_ref, inv_ref, gate_save, up_save, *refs):
        grad_ref, gain_ref, wide_ref, down_ref, *outs = refs
        residual, inv_rms = residual_ref[...], inv_ref[:, :1]
        cube = inv_rms * inv_rms * inv_rms
        parts = []
        for i, k in enumerate(distances):
            rows = slice(i * rows_here, (i + 1) * rows_here)
            scaled = gain_ref[...] * grad_ref[pl.ds(ring.device_at(k), 1), :] / rows_here
            slope = cube[rows] * jnp.mean(residual[rows] * scaled, axis=-1, keepdims=True)
            parts.append(inv_rms[rows] * scaled - residual[rows] * slope)
        resid_grad = jnp.concatenate(parts, axis=0) if len(parts) > 1 else parts[0]
        down_back = dot(resid_grad.astype(BF16), down_ref[...])
        grads = []
        for local in range(local_experts):
            cols = slice(local * hidden_dim, (local + 1) * hidden_dim)
            for save in (gate_save, up_save):
                grads.append((down_back[:, cols] * save[:, cols].astype(F32)).astype(BF16))
        total = dot(jnp.concatenate(grads, axis=1), wide_ref[...])
        if distances == (0,):
            total = total + resid_grad
        rows = total.shape[0] // len(outs)
        for i, out in enumerate(outs):
            out[...] = total[i * rows : (i + 1) * rows].astype(out.dtype)

    back_at = {}

    def backward(distances):
        result = call(
            functools.partial(backward_kernel, distances),
            part_outs(distances),
            *norm_at[distances],
            *saved_at[distances],
            pooled_grad,
            gain,
            wide_t,
            down_t,
            flops=flops * len(distances),
        )
        keep_parts(back_at, distances, result)

    for distances in reversed(list(tokens_at)):
        backward(distances)
    (top_left, top_right), (bottom_left, bottom_right) = ring.scatter(back_at)
    token_grad = pl.pallas_call(
        sum_kernel,
        out_shape=jax.ShapeDtypeStruct(block, BF16),
        in_specs=[pl.BlockSpec(memory_space=pltpu.VMEM)] * 6,
        out_specs=pl.BlockSpec(memory_space=pltpu.VMEM),
        compiler_params=pltpu.CompilerParams(vmem_limit_bytes=VMEM_LIMIT),
    )(back_at[0][0], top_left, top_right, back_at[0][1], bottom_left, bottom_right)
    return (token_grad, head_grad)


def solution(mesh):
    in_specs = (
        P(("rep", "expert", "group"), None),
        P("expert", "group", None),
        P("expert", "group", None),
        P("expert", "group", None),
        P(("rep", "expert", "group"), None),
        P(("rep", "expert", "group"), None),
        P(),
        P(None, "expert"),
        P("rep", "group", "expert"),
    )
    out_specs = (P(("rep", "expert", "group"), None), P("rep", "expert"))
    return jax.shard_map(body, mesh=mesh, in_specs=in_specs, out_specs=out_specs, check_vma=False)
```

```python
import functools

import jax
import jax.numpy as jnp
from jax import lax
from jax.experimental import pallas as pl
from jax.experimental.pallas import tpu as pltpu
from jax.sharding import PartitionSpec as P

LOSS_SCALE = 8.0
NORM_EPS = 1e-06
F32 = jnp.float32
BF16 = jnp.bfloat16
LANES = 128
VMEM_LIMIT = 32 * 1024 * 1024


def dot(left, right):
    return jnp.dot(left, right, preferred_element_type=F32)


def dot_t(left, right):
    return lax.dot_general(left, right, (((1,), (1,)), ((), ())), preferred_element_type=F32)


def call(kernel, outs, *args, flops=0):
    args = [pltpu.with_memory_space_constraint(a, pltpu.VMEM) for a in args]
    size = sum(a.size * a.dtype.itemsize for a in args)
    return pl.pallas_call(
        kernel,
        out_shape=[pltpu.VMEM(shape, dtype) for shape, dtype in outs],
        in_specs=[pl.BlockSpec(memory_space=pltpu.VMEM)] * len(args),
        out_specs=[pl.BlockSpec(memory_space=pltpu.VMEM)] * len(outs),
        compiler_params=pltpu.CompilerParams(vmem_limit_bytes=VMEM_LIMIT),
        cost_estimate=pl.CostEstimate(flops=flops, bytes_accessed=size, transcendentals=0),
    )(*args)


def after(value, guards):
    def kernel(*refs):
        pass

    args = [pltpu.with_memory_space_constraint(a, pltpu.VMEM) for a in (value, *guards)]
    return pl.pallas_call(
        kernel,
        out_shape=pltpu.VMEM(value.shape, value.dtype),
        in_specs=[pl.BlockSpec(memory_space=pltpu.VMEM)] * len(args),
        out_specs=pl.BlockSpec(memory_space=pltpu.VMEM),
        input_output_aliases={0: 0},
        compiler_params=pltpu.CompilerParams(vmem_limit_bytes=VMEM_LIMIT),
    )(*args)


class Ring:
    def __init__(self, expert_count, group_count):
        self.count = expert_count
        self.half = expert_count // 2
        self.snake = group_count == 2
        if self.snake:
            self.order = list(range(0, expert_count, 2)) + list(range(expert_count - 1, 0, -2))
        else:
            self.order = list(range(expert_count))

    def send(self, value, distance):
        pairs = [
            (self.order[i], self.order[(i + distance) % self.count]) for i in range(self.count)
        ]
        return lax.ppermute(value, "expert", pairs)

    def device_at(self, distance):
        here = lax.axis_index("expert")
        count = self.count
        if self.snake:
            here = jnp.where(here % 2 == 0, here // 2, count - 1 - here // 2)
        there = lax.rem(here + distance % count, count)
        if self.snake:
            there = jnp.where(there < self.half, 2 * there, 2 * (count - 1 - there) + 1)
        return there

    def gather(self, top, bottom, use, guard=None):
        top_left = top_right = top
        bottom_left = bottom_right = bottom
        use((0,), (top, bottom))
        for step in range(1, self.half):
            if guard is not None and step == self.half - 1:
                top_right = after(top_right, [guard])
            top_left = self.send(top_left, 1)
            top_right = self.send(top_right, -1)
            bottom_left = self.send(bottom_left, 1)
            bottom_right = self.send(bottom_right, -1)
            use((-step, step), (top_left, bottom_left, top_right, bottom_right))
        use((self.half,), (self.send(top_left, 1), self.send(bottom_right, -1)))

    def scatter(self, parts):
        most = self.half - 1
        top_left = self.send(parts[self.half][0], 1)
        bottom_right = self.send(parts[self.half][1], -1)
        bottom_left = top_right = None
        for step in range(most, 0, -1):
            top_sum = add(parts[step][0], top_left)
            bottom_sum = add(parts[-step][1], bottom_right)
            top_left, bottom_right = self.send(top_sum, 1), self.send(bottom_sum, -1)
            if step == most:
                bottom_left = after(parts[step][1], [top_sum])
                top_right = after(parts[-step][0], [bottom_sum])
            else:
                bottom_left = add(parts[step][1], bottom_left)
                top_right = add(parts[-step][0], top_right)
            bottom_left, top_right = self.send(bottom_left, 1), self.send(top_right, -1)
        return (top_left, top_right), (bottom_left, bottom_right)

    def part_types(self, distances):
        types = []
        for k in distances:
            first = BF16 if k == self.half or k == 1 - self.half else F32
            second = BF16 if k == self.half or k == self.half - 1 else F32
            types += [first, second]
        return types


def add_kernel(block_ref, arrived_ref, out_ref):
    out_ref[...] = (block_ref[...] + arrived_ref[...].astype(F32)).astype(BF16)


def add(block, arrived):
    return call(add_kernel, [(block.shape, BF16)], block, arrived)[0]


def sum_kernel(*refs):
    out_ref = refs[-1]
    rows = refs[0].shape[0]
    for i in range(len(refs) // 3):
        own, left, right = refs[3 * i : 3 * i + 3]
        arrived = left[...].astype(F32) + right[...].astype(F32)
        out_ref[pl.ds(i * rows, rows), :] = (own[...] + arrived).astype(BF16)


PIECES = 4


class Copies:
    def __init__(self, sems):
        self.sems, self.started = sems, []

    def start(self, source, target, pieces=1):
        assert source.shape[0] % (16 * pieces) == 0 or pieces == 1
        rows = source.shape[0] // pieces
        for i in range(pieces):
            some = pl.ds(i * rows, rows)
            sem = self.sems.at[len(self.started)]
            copy = pltpu.make_async_copy(source.at[some], target.at[some], sem)
            copy.start()
            self.started.append(copy)

    def wait(self):
        for copy in self.started:
            copy.wait()


def strips(gate_shape, down_shape):
    local_experts, depth, hidden_dim = gate_shape
    _, height, feature_dim = down_shape
    row, places = 0, []
    for _ in range(local_experts):
        pair = [(row, depth), (row + depth, depth)]
        row += 2 * depth
        downs = []
        for begin in range(0, feature_dim, hidden_dim):
            downs.append((row, height, begin, min(hidden_dim, feature_dim - begin)))
            row += height
        places.append((pair, downs))
    return row, places


def pack(ids, scores, tokens, shards):
    rows, cols = tokens.shape
    mid = rows // 2
    quarter = LANES // 4
    inputs = [ids, scores, tokens, *shards]
    packed_shape, places, count = None, [], 0
    if shards:
        hidden_dim = shards[0].shape[2]
        packed_rows, places = strips(shards[0].shape, shards[2].shape)
        packed_shape = (packed_rows, hidden_dim)
        count = sum(PIECES * len(pair) + len(downs) for pair, downs in places)

    def kernel(*refs):
        ids_hbm, scores_hbm, tokens_hbm, *shards_hbm = refs[: len(inputs)]
        top_ref, bottom_ref, *packed_refs = refs[len(inputs) : -3]
        ids_ref, scores_ref, sems = refs[-3:]
        copies = Copies(sems)
        copies.start(ids_hbm, ids_ref)
        copies.start(scores_hbm, scores_ref)
        copies.start(tokens_hbm.at[pl.ds(0, mid), :], top_ref.at[:, pl.ds(0, cols)])
        copies.start(tokens_hbm.at[pl.ds(mid, mid), :], bottom_ref)
        for local, (pair, downs) in enumerate(places):
            out_ref = packed_refs[0]
            for source, (row, some) in zip(shards_hbm, pair):
                copies.start(source.at[local], out_ref.at[pl.ds(row, some), :], PIECES)
            for row, some, begin, width in downs:
                source = shards_hbm[2].at[local, :, pl.ds(begin, width)]
                copies.start(source, out_ref.at[pl.ds(row, some), pl.ds(0, width)])
                if width < hidden_dim:
                    rest = hidden_dim - width
                    out_ref[pl.ds(row, some), pl.ds(width, rest)] = jnp.zeros((some, rest), BF16)
        copies.started[0].wait()
        copies.started[1].wait()
        scores = scores_ref[...]
        ids = ids_ref[...]
        route_weight = scores / jnp.sum(scores, axis=0, keepdims=True)
        expert = lax.broadcasted_iota(jnp.int32, (quarter, rows), 0)
        weight_by = jnp.zeros((quarter, rows), F32)
        for choice_k in range(scores.shape[0]):
            one = slice(choice_k, choice_k + 1)
            weight_by = weight_by + jnp.where(ids[one] == expert, route_weight[one], 0.0)
        high = weight_by.astype(BF16).astype(F32)
        weights = jnp.concatenate([high, weight_by - high] * 2, axis=0).T
        lane = lax.broadcasted_iota(jnp.int32, (mid, LANES), 1)
        both = jnp.where(lane < 2 * quarter, weights[:mid], weights[mid:])
        top_ref[:, cols:] = both.astype(BF16)
        for copy in copies.started[2:]:
            copy.wait()

    outs = [pltpu.VMEM((mid, cols + LANES), BF16), pltpu.VMEM((mid, cols), BF16)]
    if shards:
        outs.append(pltpu.VMEM(packed_shape, BF16))
    return pl.pallas_call(
        kernel,
        out_shape=outs,
        in_specs=[pl.BlockSpec(memory_space=pl.ANY)] * len(inputs),
        out_specs=[pl.BlockSpec(memory_space=pltpu.VMEM)] * len(outs),
        scratch_shapes=[
            pltpu.VMEM(ids.shape, ids.dtype),
            pltpu.VMEM(scores.shape, F32),
            pltpu.SemaphoreType.DMA((4 + count,)),
        ],
        compiler_params=pltpu.CompilerParams(vmem_limit_bytes=VMEM_LIMIT),
    )(*[pltpu.with_memory_space_constraint(a, pltpu.HBM) for a in inputs])


def full_weights(shards, packed):
    local_experts, _, hidden_dim = shards[0].shape
    feature_dim = shards[2].shape[2]
    paired = packed is not None
    _, places = strips(shards[0].shape, shards[2].shape)
    depth, height = shards[0].shape[1], shards[2].shape[1]

    def kernel(*refs):
        gate_hbm, up_hbm, down_hbm, *rest = refs
        wide_ref, down_ref, sems = rest[-3:]
        copies = Copies(sems)
        mine = lax.axis_index("group") if paired else 0

        def wide_at(place, local, is_up):
            rows = pl.ds(pl.multiple_of(place * depth, 16), depth)
            return wide_ref.at[rows, pl.ds((2 * local + is_up) * hidden_dim, hidden_dim)]

        def down_at(place, local, begin, cols):
            top = pl.multiple_of(local * hidden_dim + place * height, 16)
            return down_ref.at[pl.ds(top, height), pl.ds(begin, cols)]

        for local in range(local_experts):
            for is_up, source in enumerate((gate_hbm, up_hbm)):
                copies.start(source.at[local], wide_at(mine, local, is_up), PIECES)
            copies.start(down_hbm.at[local], down_at(mine, local, 0, feature_dim), PIECES)
        if paired:
            for local, (pair, downs) in enumerate(places):
                for is_up, (row, some) in enumerate(pair):
                    source = rest[0].at[pl.ds(row, some), :]
                    copies.start(source, wide_at(1 - mine, local, is_up), PIECES)
                for row, some, begin, cols in downs:
                    source = rest[0].at[pl.ds(row, some), pl.ds(0, cols)]
                    copies.start(source, down_at(1 - mine, local, begin, cols))
        copies.wait()

    shards = [pltpu.with_memory_space_constraint(w, pltpu.HBM) for w in shards]
    count = 3 * PIECES * local_experts
    specs = [pl.BlockSpec(memory_space=pl.ANY)] * 3
    if paired:
        count += sum(PIECES * len(pair) + len(downs) for pair, downs in places)
        specs.append(pl.BlockSpec(memory_space=pltpu.VMEM))
        shards.append(pltpu.with_memory_space_constraint(packed, pltpu.VMEM))
    return pl.pallas_call(
        kernel,
        out_shape=[
            pltpu.VMEM((feature_dim, 2 * local_experts * hidden_dim), BF16),
            pltpu.VMEM((local_experts * hidden_dim, feature_dim), BF16),
        ],
        in_specs=specs,
        out_specs=[pl.BlockSpec(memory_space=pltpu.VMEM)] * 2,
        scratch_shapes=[pltpu.SemaphoreType.DMA((count,))],
        compiler_params=pltpu.CompilerParams(vmem_limit_bytes=VMEM_LIMIT),
        cost_estimate=pl.CostEstimate(
            flops=0,
            bytes_accessed=12 * local_experts * hidden_dim * feature_dim,
            transcendentals=0,
        ),
    )(*shards)


def transpose_kernel(from_ref, to_ref):
    strip = 2 * LANES

    @pl.loop(0, to_ref.shape[0] // strip)
    def _(i):
        some = pl.ds(pl.multiple_of(i * strip, strip), strip)
        to_ref[some, :] = from_ref[:, some].T


def transposed(weights):
    rows, cols = weights.shape
    return call(transpose_kernel, [((cols, rows), BF16)], weights)[0]


def body(tokens, w_gate, w_up, w_down, route_ids, route_scores, norm_gain, class_head, targets):
    rows_here, feature_dim = tokens.shape
    expert_count = lax.axis_size("expert")
    group_count = lax.axis_size("group")
    local_experts, _, hidden_dim = w_gate.shape
    pair_dim = 2 * hidden_dim
    ring = Ring(expert_count, group_count)
    block = (rows_here, feature_dim)
    mid = rows_here // 2

    shards = [w_gate, w_up, w_down]
    if group_count == 2:
        top, bottom, packed = pack(route_ids.T, route_scores.T, tokens, shards)
        packed = lax.ppermute(packed, "group", [(0, 1), (1, 0)])
    else:
        top, bottom = pack(route_ids.T, route_scores.T, tokens, [])
        shards = [lax.all_gather(w, "group", axis=1, tiled=True) for w in shards]
        packed = None
    wide, down = full_weights(shards, packed)

    def rows_of(refs):
        return jnp.concatenate([ref[...] for ref in refs], axis=0) if len(refs) > 1 else refs[0][...]

    def forward_kernel(count, *refs):
        token_refs, (wide_ref, down_ref) = refs[:count], refs[count : count + 2]
        outs = refs[count + 2 :]
        x = rows_of([ref.at[:, :feature_dim] for ref in token_refs])
        weights = jnp.concatenate([ref[:, feature_dim:] for ref in token_refs[::2]], axis=0).astype(F32)
        lane = lax.broadcasted_iota(jnp.int32, weights.shape, 1)
        quarter = LANES // 4
        hidden = []
        for local in range(local_experts):
            expert = lax.axis_index("expert") * local_experts + local
            scales = []
            for begin in (expert, expert + 2 * quarter):
                here = (lane == begin) | (lane == begin + quarter)
                scales.append(jnp.sum(jnp.where(here, weights, 0.0), axis=1, keepdims=True))
            pieces = [s[i : i + mid] for i in range(0, weights.shape[0], mid) for s in scales]
            scale = jnp.concatenate(pieces, axis=0)
            act = dot(x, wide_ref[:, pl.ds(local * pair_dim, pair_dim)])
            gate_act, up_act = act[:, :hidden_dim], act[:, hidden_dim:]
            sigmoid_gate = jax.nn.sigmoid(gate_act)
            silu = gate_act * sigmoid_gate * scale
            slope = sigmoid_gate * (1.0 + gate_act * (1.0 - sigmoid_gate)) * scale
            cols = pl.ds(local * hidden_dim, hidden_dim)
            outs[0][:, cols] = (up_act * slope).astype(BF16)
            outs[1][:, cols] = silu.astype(BF16)
            hidden.append((silu * up_act).astype(BF16))
        total = dot(jnp.concatenate(hidden, axis=1), down_ref[...])
        for i, out in enumerate(outs[2:]):
            out[...] = total[i * mid : (i + 1) * mid].astype(out.dtype)

    tokens_at, saved_at, part_at = {}, {}, {}
    flops = 2 * rows_here * feature_dim * hidden_dim * local_experts * 3

    def hold(distances, blocks):
        tokens_at[distances] = blocks

    def keep_parts(parts, distances, halves):
        parts.update({k: halves[2 * i : 2 * i + 2] for i, k in enumerate(distances)})

    def part_outs(distances):
        return [((mid, feature_dim), dtype) for dtype in ring.part_types(distances)]

    def forward(distances):
        blocks = tokens_at[distances]
        rows = mid * len(blocks)
        result = call(
            functools.partial(forward_kernel, len(blocks)),
            [((rows, local_experts * hidden_dim), BF16)] * 2 + part_outs(distances),
            *blocks,
            wide,
            down,
            flops=flops * rows // rows_here,
        )
        saved_at[distances] = result[:2]
        keep_parts(part_at, distances, result[2:])

    ring.gather(top, bottom, hold, wide)
    for distances in tokens_at:
        forward(distances)
    gain = norm_gain.reshape(1, feature_dim)
    half_shape = (mid, feature_dim)
    moe_top, moe_bottom = [
        call(sum_kernel, [(half_shape, BF16)], own, *arrived)[0]
        for own, arrived in zip(part_at[0], ring.scatter(part_at))
    ]

    norm_at, mean_at = {}, {}

    def residual_of(token_refs, moe_refs):
        token_rows = rows_of([ref.at[:, :feature_dim] for ref in token_refs]).astype(F32)
        return token_rows + rows_of(moe_refs).astype(F32)

    def inv_rms_of(residual):
        return lax.rsqrt(jnp.mean(residual * residual, axis=-1, keepdims=True) + NORM_EPS)

    def norm_kernel(distances, count, *refs):
        residual = residual_of(refs[:count], refs[count : 2 * count])
        gain_ref, so_far, out_ref, residual_ref, inv_ref = refs[2 * count :]
        inv_rms = inv_rms_of(residual)
        residual_ref[...] = residual
        inv_ref[...] = jnp.broadcast_to(inv_rms, inv_ref.shape)
        normed = residual * inv_rms * gain_ref[...]
        pooled = so_far[...]
        row = lax.broadcasted_iota(jnp.int32, pooled.shape, 0)
        for i, k in enumerate(distances):
            part = normed[i * rows_here : (i + 1) * rows_here]
            mean = jnp.mean(part, axis=0, keepdims=True)
            pooled = jnp.where(row == ring.device_at(k), mean, pooled)
        out_ref[...] = pooled

    pooled_shape = (expert_count, feature_dim)
    mean_at["pooled"] = jnp.zeros(pooled_shape, F32)

    def norm(distances, blocks):
        rows = mid * len(blocks)
        mean_at["pooled"], *norm_at[distances] = call(
            functools.partial(norm_kernel, distances, len(blocks)),
            [(pooled_shape, F32), ((rows, feature_dim), F32), ((rows, LANES), F32)],
            *tokens_at[distances],
            *blocks,
            gain,
            mean_at["pooled"],
        )

    ring.gather(moe_top, moe_bottom, norm)
    pooled = mean_at["pooled"].astype(BF16)
    logits = dot(pooled, class_head)
    target_rows = targets.reshape(expert_count, -1).astype(F32)
    logit_grad = (LOSS_SCALE * (jax.nn.sigmoid(logits) - target_rows)).astype(BF16)
    wide_t, down_t = transposed(wide), transposed(down)

    def grad_sum_kernel(count, *refs):
        total = refs[0][...].astype(F32)
        for ref in refs[1:count]:
            total = total + ref[...].astype(F32)
        refs[-1][...] = total.astype(refs[-1].dtype)

    grad_rows = dot_t(logit_grad, class_head).astype(BF16)
    span = 2
    for masks, others, dtype in (
        ([1], [wide_t, down_t], BF16),
        (list(range(span, expert_count, span)), [], F32),
    ):
        terms = [grad_rows]
        for mask in masks:
            pairs = [(e, e ^ mask) for e in range(expert_count)]
            terms.append(lax.ppermute(grad_rows, "expert", pairs))
        grad_rows = call(
            functools.partial(grad_sum_kernel, len(terms)),
            [(pooled_shape, dtype)],
            *terms,
            *others,
        )[0]
    pooled_grad = grad_rows

    both = jnp.concatenate([pooled, logit_grad], axis=1)
    if group_count == 2:
        both = jnp.concatenate([both, lax.ppermute(both, "group", [(0, 1), (1, 0)])], axis=0)
    else:
        both = lax.all_gather(both, "group", axis=0, tiled=True)
    head_grad = lax.dot_general(
        both[:, :feature_dim],
        both[:, feature_dim:],
        (((0,), (0,)), ((), ())),
        preferred_element_type=F32,
    )

    def backward_kernel(distances, residual_ref, inv_ref, gate_save, up_save, *refs):
        grad_ref, gain_ref, wide_ref, down_ref, *outs = refs
        residual, inv_rms = residual_ref[...], inv_ref[:, :1]
        cube = inv_rms * inv_rms * inv_rms
        parts = []
        for i, k in enumerate(distances):
            rows = slice(i * rows_here, (i + 1) * rows_here)
            scaled = gain_ref[...] * grad_ref[pl.ds(ring.device_at(k), 1), :] / rows_here
            slope = cube[rows] * jnp.mean(residual[rows] * scaled, axis=-1, keepdims=True)
            parts.append(inv_rms[rows] * scaled - residual[rows] * slope)
        resid_grad = jnp.concatenate(parts, axis=0) if len(parts) > 1 else parts[0]
        down_back = dot(resid_grad.astype(BF16), down_ref[...])
        grads = []
        for local in range(local_experts):
            cols = slice(local * hidden_dim, (local + 1) * hidden_dim)
            for save in (gate_save, up_save):
                grads.append((down_back[:, cols] * save[:, cols].astype(F32)).astype(BF16))
        total = dot(jnp.concatenate(grads, axis=1), wide_ref[...])
        if distances == (0,):
            total = total + resid_grad
        rows = total.shape[0] // len(outs)
        for i, out in enumerate(outs):
            out[...] = total[i * rows : (i + 1) * rows].astype(out.dtype)

    back_at = {}

    def backward(distances):
        result = call(
            functools.partial(backward_kernel, distances),
            part_outs(distances),
            *norm_at[distances],
            *saved_at[distances],
            pooled_grad,
            gain,
            wide_t,
            down_t,
            flops=flops * len(distances),
        )
        keep_parts(back_at, distances, result)

    for distances in reversed(list(tokens_at)):
        backward(distances)
    (top_left, top_right), (bottom_left, bottom_right) = ring.scatter(back_at)
    token_grad = pl.pallas_call(
        sum_kernel,
        out_shape=jax.ShapeDtypeStruct(block, BF16),
        in_specs=[pl.BlockSpec(memory_space=pltpu.VMEM)] * 6,
        out_specs=pl.BlockSpec(memory_space=pltpu.VMEM),
        compiler_params=pltpu.CompilerParams(vmem_limit_bytes=VMEM_LIMIT),
    )(back_at[0][0], top_left, top_right, back_at[0][1], bottom_left, bottom_right)
    return (token_grad, head_grad)


def solution(mesh):
    in_specs = (
        P(("rep", "expert", "group"), None),
        P("expert", "group", None),
        P("expert", "group", None),
        P("expert", "group", None),
        P(("rep", "expert", "group"), None),
        P(("rep", "expert", "group"), None),
        P(),
        P(None, "expert"),
        P("rep", "group", "expert"),
    )
    out_specs = (P(("rep", "expert", "group"), None), P("rep", "expert"))
    return jax.shard_map(body, mesh=mesh, in_specs=in_specs, out_specs=out_specs, check_vma=False)
```

```python
import functools

import jax
import jax.numpy as jnp
from jax import lax
from jax.experimental import pallas as pl
from jax.experimental.pallas import tpu as pltpu
from jax.sharding import PartitionSpec as P

LOSS_SCALE = 8.0
NORM_EPS = 1e-06
F32 = jnp.float32
BF16 = jnp.bfloat16
LANES = 128
VMEM_LIMIT = 32 * 1024 * 1024


def dot(left, right):
    return jnp.dot(left, right, preferred_element_type=F32)


def dot_t(left, right):
    return lax.dot_general(left, right, (((1,), (1,)), ((), ())), preferred_element_type=F32)


def call(kernel, outs, *args, flops=0):
    args = [pltpu.with_memory_space_constraint(a, pltpu.VMEM) for a in args]
    size = sum(a.size * a.dtype.itemsize for a in args)
    return pl.pallas_call(
        kernel,
        out_shape=[pltpu.VMEM(shape, dtype) for shape, dtype in outs],
        in_specs=[pl.BlockSpec(memory_space=pltpu.VMEM)] * len(args),
        out_specs=[pl.BlockSpec(memory_space=pltpu.VMEM)] * len(outs),
        compiler_params=pltpu.CompilerParams(vmem_limit_bytes=VMEM_LIMIT),
        cost_estimate=pl.CostEstimate(flops=flops, bytes_accessed=size, transcendentals=0),
    )(*args)


def after(value, guards):
    def kernel(*refs):
        pass

    args = [pltpu.with_memory_space_constraint(a, pltpu.VMEM) for a in (value, *guards)]
    return pl.pallas_call(
        kernel,
        out_shape=pltpu.VMEM(value.shape, value.dtype),
        in_specs=[pl.BlockSpec(memory_space=pltpu.VMEM)] * len(args),
        out_specs=pl.BlockSpec(memory_space=pltpu.VMEM),
        input_output_aliases={0: 0},
        compiler_params=pltpu.CompilerParams(vmem_limit_bytes=VMEM_LIMIT),
    )(*args)


class Ring:
    def __init__(self, expert_count, group_count):
        self.count = expert_count
        self.half = expert_count // 2
        self.snake = group_count == 2
        self.groups = group_count
        self.token = None
        if self.snake:
            self.order = list(range(0, expert_count, 2)) + list(range(expert_count - 1, 0, -2))
        else:
            self.order = list(range(expert_count))

    def send(self, value, distance):
        pairs = [
            (self.order[i], self.order[(i + distance) % self.count]) for i in range(self.count)
        ]
        return lax.ppermute(value, "expert", pairs)

    def in_step(self, value, behind):
        if self.groups != 2:
            return value
        token = after(self.token, [behind])
        self.token = lax.ppermute(token, "group", [(0, 1), (1, 0)])
        return after(value, [self.token])

    def device_at(self, distance):
        here = lax.axis_index("expert")
        count = self.count
        if self.snake:
            here = jnp.where(here % 2 == 0, here // 2, count - 1 - here // 2)
        there = lax.rem(here + distance % count, count)
        if self.snake:
            there = jnp.where(there < self.half, 2 * there, 2 * (count - 1 - there) + 1)
        return there

    def gather(self, top, bottom, use, guard=None):
        top_left = top_right = top
        bottom_left = bottom_right = bottom
        use((0,), (top, bottom))
        for step in range(1, self.half):
            if guard is not None and step == self.half - 1:
                top_right = after(top_right, [guard])
            if step > 1:
                top_right = self.in_step(top_right, top_left)
            top_left = self.send(top_left, 1)
            top_right = self.send(top_right, -1)
            bottom_left = self.send(bottom_left, 1)
            bottom_right = self.send(bottom_right, -1)
            use((-step, step), (top_left, bottom_left, top_right, bottom_right))
        use((self.half,), (self.send(top_left, 1), self.send(bottom_right, -1)))

    def scatter(self, parts, paced=False):
        most = self.half - 1
        top_left = self.send(parts[self.half][0], 1)
        bottom_right = self.send(parts[self.half][1], -1)
        bottom_left = self.send(parts[most][1], 1)
        top_right = self.send(parts[-most][0], -1)
        for step in range(most, 0, -1):
            top_sum = add(parts[step][0], top_left)
            top_left = self.send(top_sum, 1)
            bottom_right = self.send(add(parts[-step][1], bottom_right), -1)
            if step > 1:
                bottom_left = self.send(add(parts[step - 1][1], bottom_left), 1)
                top_right = add(parts[1 - step][0], top_right)
                if paced:
                    top_right = self.in_step(top_right, top_sum)
                top_right = self.send(top_right, -1)
        return (top_left, top_right), (bottom_left, bottom_right)

    def part_types(self, distances):
        types = []
        for k in distances:
            first = BF16 if k == self.half or k == 1 - self.half else F32
            second = BF16 if k == self.half or k == self.half - 1 else F32
            types += [first, second]
        return types


def add_kernel(block_ref, arrived_ref, out_ref):
    out_ref[...] = (block_ref[...] + arrived_ref[...].astype(F32)).astype(BF16)


def add(block, arrived):
    return call(add_kernel, [(block.shape, BF16)], block, arrived)[0]


def sum_kernel(*refs):
    out_ref = refs[-1]
    rows = refs[0].shape[0]
    for i in range(len(refs) // 3):
        own, left, right = refs[3 * i : 3 * i + 3]
        arrived = left[...].astype(F32) + right[...].astype(F32)
        out_ref[pl.ds(i * rows, rows), :] = (own[...] + arrived).astype(BF16)


class Copies:
    def __init__(self, sems):
        self.sems, self.started = sems, []

    def start(self, source, target):
        copy = pltpu.make_async_copy(source, target, self.sems.at[len(self.started)])
        copy.start()
        self.started.append(copy)

    def wait(self):
        for copy in self.started:
            copy.wait()


def strips(gate_shape, down_shape):
    local_experts, depth, hidden_dim = gate_shape
    _, height, feature_dim = down_shape
    row, places = 0, []
    for _ in range(local_experts):
        pair = [(row, depth), (row + depth, depth)]
        row += 2 * depth
        downs = []
        for begin in range(0, feature_dim, hidden_dim):
            downs.append((row, height, begin, min(hidden_dim, feature_dim - begin)))
            row += height
        places.append((pair, downs))
    return row, places


def pack(ids, scores, tokens, shards):
    rows, cols = tokens.shape
    mid = rows // 2
    quarter = LANES // 4
    inputs = [ids, scores, tokens, *shards]
    packed_shape, places, count = None, [], 0
    if shards:
        hidden_dim = shards[0].shape[2]
        packed_rows, places = strips(shards[0].shape, shards[2].shape)
        packed_shape = (packed_rows, hidden_dim)
        count = sum(len(pair) + len(downs) for pair, downs in places)

    def kernel(*refs):
        ids_hbm, scores_hbm, tokens_hbm, *shards_hbm = refs[: len(inputs)]
        top_ref, bottom_ref, *packed_refs = refs[len(inputs) : -3]
        ids_ref, scores_ref, sems = refs[-3:]
        copies = Copies(sems)
        copies.start(ids_hbm, ids_ref)
        copies.start(scores_hbm, scores_ref)
        copies.start(tokens_hbm.at[pl.ds(0, mid), :], top_ref.at[:, pl.ds(0, cols)])
        copies.start(tokens_hbm.at[pl.ds(mid, mid), :], bottom_ref)
        for local, (pair, downs) in enumerate(places):
            out_ref = packed_refs[0]
            for source, (row, some) in zip(shards_hbm, pair):
                copies.start(source.at[local], out_ref.at[pl.ds(row, some), :])
            for row, some, begin, width in downs:
                source = shards_hbm[2].at[local, :, pl.ds(begin, width)]
                copies.start(source, out_ref.at[pl.ds(row, some), pl.ds(0, width)])
                if width < hidden_dim:
                    rest = hidden_dim - width
                    out_ref[pl.ds(row, some), pl.ds(width, rest)] = jnp.zeros((some, rest), BF16)
        copies.started[0].wait()
        copies.started[1].wait()
        scores = scores_ref[...]
        ids = ids_ref[...]
        route_weight = scores / jnp.sum(scores, axis=0, keepdims=True)
        expert = lax.broadcasted_iota(jnp.int32, (quarter, rows), 0)
        weight_by = jnp.zeros((quarter, rows), F32)
        for choice_k in range(scores.shape[0]):
            one = slice(choice_k, choice_k + 1)
            weight_by = weight_by + jnp.where(ids[one] == expert, route_weight[one], 0.0)
        high = weight_by.astype(BF16).astype(F32)
        weights = jnp.concatenate([high, weight_by - high] * 2, axis=0).T
        lane = lax.broadcasted_iota(jnp.int32, (mid, LANES), 1)
        both = jnp.where(lane < 2 * quarter, weights[:mid], weights[mid:])
        top_ref[:, cols:] = both.astype(BF16)
        for copy in copies.started[2:]:
            copy.wait()

    outs = [pltpu.VMEM((mid, cols + LANES), BF16), pltpu.VMEM((mid, cols), BF16)]
    if shards:
        outs.append(pltpu.VMEM(packed_shape, BF16))
    return pl.pallas_call(
        kernel,
        out_shape=outs,
        in_specs=[pl.BlockSpec(memory_space=pl.ANY)] * len(inputs),
        out_specs=[pl.BlockSpec(memory_space=pltpu.VMEM)] * len(outs),
        scratch_shapes=[
            pltpu.VMEM(ids.shape, ids.dtype),
            pltpu.VMEM(scores.shape, F32),
            pltpu.SemaphoreType.DMA((4 + count,)),
        ],
        compiler_params=pltpu.CompilerParams(vmem_limit_bytes=VMEM_LIMIT),
    )(*[pltpu.with_memory_space_constraint(a, pltpu.HBM) for a in inputs])


def full_weights(shards, packed):
    local_experts, _, hidden_dim = shards[0].shape
    feature_dim = shards[2].shape[2]
    paired = packed is not None
    _, places = strips(shards[0].shape, shards[2].shape)
    depth, height = shards[0].shape[1], shards[2].shape[1]

    def kernel(*refs):
        gate_hbm, up_hbm, down_hbm, *rest = refs
        wide_ref, down_ref, sems = rest[-3:]
        copies = Copies(sems)
        mine = lax.axis_index("group") if paired else 0

        def wide_at(place, local, is_up):
            rows = pl.ds(pl.multiple_of(place * depth, 16), depth)
            return wide_ref.at[rows, pl.ds((2 * local + is_up) * hidden_dim, hidden_dim)]

        def down_at(place, local, begin, cols):
            top = pl.multiple_of(local * hidden_dim + place * height, 16)
            return down_ref.at[pl.ds(top, height), pl.ds(begin, cols)]

        for local in range(local_experts):
            for is_up, source in enumerate((gate_hbm, up_hbm)):
                copies.start(source.at[local], wide_at(mine, local, is_up))
            copies.start(down_hbm.at[local], down_at(mine, local, 0, feature_dim))
        if paired:
            for local, (pair, downs) in enumerate(places):
                for is_up, (row, some) in enumerate(pair):
                    copies.start(rest[0].at[pl.ds(row, some), :], wide_at(1 - mine, local, is_up))
                for row, some, begin, cols in downs:
                    source = rest[0].at[pl.ds(row, some), pl.ds(0, cols)]
                    copies.start(source, down_at(1 - mine, local, begin, cols))
        copies.wait()

    shards = [pltpu.with_memory_space_constraint(w, pltpu.HBM) for w in shards]
    count = 3 * local_experts
    specs = [pl.BlockSpec(memory_space=pl.ANY)] * 3
    if paired:
        count += sum(len(pair) + len(downs) for pair, downs in places)
        specs.append(pl.BlockSpec(memory_space=pltpu.VMEM))
        shards.append(pltpu.with_memory_space_constraint(packed, pltpu.VMEM))
    return pl.pallas_call(
        kernel,
        out_shape=[
            pltpu.VMEM((feature_dim, 2 * local_experts * hidden_dim), BF16),
            pltpu.VMEM((local_experts * hidden_dim, feature_dim), BF16),
        ],
        in_specs=specs,
        out_specs=[pl.BlockSpec(memory_space=pltpu.VMEM)] * 2,
        scratch_shapes=[pltpu.SemaphoreType.DMA((count,))],
        compiler_params=pltpu.CompilerParams(vmem_limit_bytes=VMEM_LIMIT),
        cost_estimate=pl.CostEstimate(
            flops=0,
            bytes_accessed=12 * local_experts * hidden_dim * feature_dim,
            transcendentals=0,
        ),
    )(*shards)


def transpose_kernel(from_ref, to_ref):
    strip = 2 * LANES

    @pl.loop(0, to_ref.shape[0] // strip)
    def _(i):
        some = pl.ds(pl.multiple_of(i * strip, strip), strip)
        to_ref[some, :] = from_ref[:, some].T


def transposed(weights):
    rows, cols = weights.shape
    return call(transpose_kernel, [((cols, rows), BF16)], weights)[0]


def body(tokens, w_gate, w_up, w_down, route_ids, route_scores, norm_gain, class_head, targets):
    rows_here, feature_dim = tokens.shape
    expert_count = lax.axis_size("expert")
    group_count = lax.axis_size("group")
    local_experts, _, hidden_dim = w_gate.shape
    pair_dim = 2 * hidden_dim
    ring = Ring(expert_count, group_count)
    block = (rows_here, feature_dim)
    mid = rows_here // 2

    shards = [w_gate, w_up, w_down]
    if group_count == 2:
        top, bottom, packed = pack(route_ids.T, route_scores.T, tokens, shards)
        packed = lax.ppermute(packed, "group", [(0, 1), (1, 0)])
    else:
        top, bottom = pack(route_ids.T, route_scores.T, tokens, [])
        shards = [lax.all_gather(w, "group", axis=1, tiled=True) for w in shards]
        packed = None
    wide, down = full_weights(shards, packed)

    def rows_of(refs):
        return jnp.concatenate([ref[...] for ref in refs], axis=0) if len(refs) > 1 else refs[0][...]

    def forward_kernel(count, *refs):
        token_refs, (wide_ref, down_ref) = refs[:count], refs[count : count + 2]
        outs = refs[count + 2 :]
        x = rows_of([ref.at[:, :feature_dim] for ref in token_refs])
        weights = jnp.concatenate([ref[:, feature_dim:] for ref in token_refs[::2]], axis=0).astype(F32)
        lane = lax.broadcasted_iota(jnp.int32, weights.shape, 1)
        quarter = LANES // 4
        hidden = []
        for local in range(local_experts):
            expert = lax.axis_index("expert") * local_experts + local
            scales = []
            for begin in (expert, expert + 2 * quarter):
                here = (lane == begin) | (lane == begin + quarter)
                scales.append(jnp.sum(jnp.where(here, weights, 0.0), axis=1, keepdims=True))
            pieces = [s[i : i + mid] for i in range(0, weights.shape[0], mid) for s in scales]
            scale = jnp.concatenate(pieces, axis=0)
            act = dot(x, wide_ref[:, pl.ds(local * pair_dim, pair_dim)])
            gate_act, up_act = act[:, :hidden_dim], act[:, hidden_dim:]
            sigmoid_gate = jax.nn.sigmoid(gate_act)
            silu = gate_act * sigmoid_gate * scale
            slope = sigmoid_gate * (1.0 + gate_act * (1.0 - sigmoid_gate)) * scale
            cols = pl.ds(local * hidden_dim, hidden_dim)
            outs[0][:, cols] = (up_act * slope).astype(BF16)
            outs[1][:, cols] = silu.astype(BF16)
            hidden.append((silu * up_act).astype(BF16))
        total = dot(jnp.concatenate(hidden, axis=1), down_ref[...])
        for i, out in enumerate(outs[2:]):
            out[...] = total[i * mid : (i + 1) * mid].astype(out.dtype)

    tokens_at, saved_at, part_at = {}, {}, {}
    flops = 2 * rows_here * feature_dim * hidden_dim * local_experts * 3

    def hold(distances, blocks):
        tokens_at[distances] = blocks

    def keep_parts(parts, distances, halves):
        parts.update({k: halves[2 * i : 2 * i + 2] for i, k in enumerate(distances)})

    def part_outs(distances):
        return [((mid, feature_dim), dtype) for dtype in ring.part_types(distances)]

    def forward(distances):
        blocks = tokens_at[distances]
        rows = mid * len(blocks)
        result = call(
            functools.partial(forward_kernel, len(blocks)),
            [((rows, local_experts * hidden_dim), BF16)] * 2 + part_outs(distances),
            *blocks,
            wide,
            down,
            flops=flops * rows // rows_here,
        )
        saved_at[distances] = result[:2]
        keep_parts(part_at, distances, result[2:])

    ring.token = norm_gain[: 8 * LANES].reshape(8, LANES)
    ring.gather(top, bottom, hold, wide)
    for distances in tokens_at:
        forward(distances)
    gain = norm_gain.reshape(1, feature_dim)
    half_shape = (mid, feature_dim)
    moe_top, moe_bottom = [
        call(sum_kernel, [(half_shape, BF16)], own, *arrived)[0]
        for own, arrived in zip(part_at[0], ring.scatter(part_at, paced=True))
    ]

    norm_at, mean_at = {}, {}

    def residual_of(token_refs, moe_refs):
        token_rows = rows_of([ref.at[:, :feature_dim] for ref in token_refs]).astype(F32)
        return token_rows + rows_of(moe_refs).astype(F32)

    def inv_rms_of(residual):
        return lax.rsqrt(jnp.mean(residual * residual, axis=-1, keepdims=True) + NORM_EPS)

    def norm_kernel(distances, count, *refs):
        residual = residual_of(refs[:count], refs[count : 2 * count])
        gain_ref, so_far, out_ref, residual_ref, inv_ref = refs[2 * count :]
        inv_rms = inv_rms_of(residual)
        residual_ref[...] = residual
        inv_ref[...] = jnp.broadcast_to(inv_rms, inv_ref.shape)
        normed = residual * inv_rms * gain_ref[...]
        pooled = so_far[...]
        row = lax.broadcasted_iota(jnp.int32, pooled.shape, 0)
        for i, k in enumerate(distances):
            part = normed[i * rows_here : (i + 1) * rows_here]
            mean = jnp.mean(part, axis=0, keepdims=True)
            pooled = jnp.where(row == ring.device_at(k), mean, pooled)
        out_ref[...] = pooled

    pooled_shape = (expert_count, feature_dim)
    mean_at["pooled"] = jnp.zeros(pooled_shape, F32)

    def norm(distances, blocks):
        rows = mid * len(blocks)
        mean_at["pooled"], *norm_at[distances] = call(
            functools.partial(norm_kernel, distances, len(blocks)),
            [(pooled_shape, F32), ((rows, feature_dim), F32), ((rows, LANES), F32)],
            *tokens_at[distances],
            *blocks,
            gain,
            mean_at["pooled"],
        )

    ring.gather(moe_top, moe_bottom, norm)
    pooled = mean_at["pooled"].astype(BF16)
    logits = dot(pooled, class_head)
    target_rows = targets.reshape(expert_count, -1).astype(F32)
    logit_grad = (LOSS_SCALE * (jax.nn.sigmoid(logits) - target_rows)).astype(BF16)
    wide_t, down_t = transposed(wide), transposed(down)

    def grad_sum_kernel(count, *refs):
        total = refs[0][...].astype(F32)
        for ref in refs[1:count]:
            total = total + ref[...].astype(F32)
        refs[-1][...] = total.astype(refs[-1].dtype)

    grad_rows = dot_t(logit_grad, class_head).astype(BF16)
    span = 2
    for masks, others, dtype in (
        ([1], [wide_t, down_t], BF16),
        (list(range(span, expert_count, span)), [], F32),
    ):
        terms = [grad_rows]
        for mask in masks:
            pairs = [(e, e ^ mask) for e in range(expert_count)]
            terms.append(lax.ppermute(grad_rows, "expert", pairs))
        grad_rows = call(
            functools.partial(grad_sum_kernel, len(terms)),
            [(pooled_shape, dtype)],
            *terms,
            *others,
        )[0]
    pooled_grad = grad_rows

    both = jnp.concatenate([pooled, logit_grad], axis=1)
    if group_count == 2:
        both = jnp.concatenate([both, lax.ppermute(both, "group", [(0, 1), (1, 0)])], axis=0)
    else:
        both = lax.all_gather(both, "group", axis=0, tiled=True)
    head_grad = lax.dot_general(
        both[:, :feature_dim],
        both[:, feature_dim:],
        (((0,), (0,)), ((), ())),
        preferred_element_type=F32,
    )

    def backward_kernel(distances, residual_ref, inv_ref, gate_save, up_save, *refs):
        grad_ref, gain_ref, wide_ref, down_ref, *outs = refs
        residual, inv_rms = residual_ref[...], inv_ref[:, :1]
        cube = inv_rms * inv_rms * inv_rms
        parts = []
        for i, k in enumerate(distances):
            rows = slice(i * rows_here, (i + 1) * rows_here)
            scaled = gain_ref[...] * grad_ref[pl.ds(ring.device_at(k), 1), :] / rows_here
            slope = cube[rows] * jnp.mean(residual[rows] * scaled, axis=-1, keepdims=True)
            parts.append(inv_rms[rows] * scaled - residual[rows] * slope)
        resid_grad = jnp.concatenate(parts, axis=0) if len(parts) > 1 else parts[0]
        down_back = dot(resid_grad.astype(BF16), down_ref[...])
        grads = []
        for local in range(local_experts):
            cols = slice(local * hidden_dim, (local + 1) * hidden_dim)
            for save in (gate_save, up_save):
                grads.append((down_back[:, cols] * save[:, cols].astype(F32)).astype(BF16))
        total = dot(jnp.concatenate(grads, axis=1), wide_ref[...])
        if distances == (0,):
            total = total + resid_grad
        rows = total.shape[0] // len(outs)
        for i, out in enumerate(outs):
            out[...] = total[i * rows : (i + 1) * rows].astype(out.dtype)

    back_at = {}

    def backward(distances):
        result = call(
            functools.partial(backward_kernel, distances),
            part_outs(distances),
            *norm_at[distances],
            *saved_at[distances],
            pooled_grad,
            gain,
            wide_t,
            down_t,
            flops=flops * len(distances),
        )
        keep_parts(back_at, distances, result)

    for distances in reversed(list(tokens_at)):
        backward(distances)
    (top_left, top_right), (bottom_left, bottom_right) = ring.scatter(back_at)
    token_grad = pl.pallas_call(
        sum_kernel,
        out_shape=jax.ShapeDtypeStruct(block, BF16),
        in_specs=[pl.BlockSpec(memory_space=pltpu.VMEM)] * 6,
        out_specs=pl.BlockSpec(memory_space=pltpu.VMEM),
        compiler_params=pltpu.CompilerParams(vmem_limit_bytes=VMEM_LIMIT),
    )(back_at[0][0], top_left, top_right, back_at[0][1], bottom_left, bottom_right)
    return (token_grad, head_grad)


def solution(mesh):
    in_specs = (
        P(("rep", "expert", "group"), None),
        P("expert", "group", None),
        P("expert", "group", None),
        P("expert", "group", None),
        P(("rep", "expert", "group"), None),
        P(("rep", "expert", "group"), None),
        P(),
        P(None, "expert"),
        P("rep", "group", "expert"),
    )
    out_specs = (P(("rep", "expert", "group"), None), P("rep", "expert"))
    return jax.shard_map(body, mesh=mesh, in_specs=in_specs, out_specs=out_specs, check_vma=False)
```

```python
import functools

import jax
import jax.numpy as jnp
from jax import lax
from jax.experimental import pallas as pl
from jax.experimental.pallas import tpu as pltpu
from jax.sharding import PartitionSpec as P

LOSS_SCALE = 8.0
NORM_EPS = 1e-06
F32 = jnp.float32
BF16 = jnp.bfloat16
LANES = 128
VMEM_LIMIT = 32 * 1024 * 1024


def dot(left, right):
    return jnp.dot(left, right, preferred_element_type=F32)


def dot_t(left, right):
    return lax.dot_general(left, right, (((1,), (1,)), ((), ())), preferred_element_type=F32)


def call(kernel, outs, *args, flops=0):
    args = [pltpu.with_memory_space_constraint(a, pltpu.VMEM) for a in args]
    size = sum(a.size * a.dtype.itemsize for a in args)
    return pl.pallas_call(
        kernel,
        out_shape=[pltpu.VMEM(shape, dtype) for shape, dtype in outs],
        in_specs=[pl.BlockSpec(memory_space=pltpu.VMEM)] * len(args),
        out_specs=[pl.BlockSpec(memory_space=pltpu.VMEM)] * len(outs),
        compiler_params=pltpu.CompilerParams(vmem_limit_bytes=VMEM_LIMIT),
        cost_estimate=pl.CostEstimate(flops=flops, bytes_accessed=size, transcendentals=0),
    )(*args)


def after(value, guards):
    def kernel(*refs):
        pass

    args = [pltpu.with_memory_space_constraint(a, pltpu.VMEM) for a in (value, *guards)]
    return pl.pallas_call(
        kernel,
        out_shape=pltpu.VMEM(value.shape, value.dtype),
        in_specs=[pl.BlockSpec(memory_space=pltpu.VMEM)] * len(args),
        out_specs=pl.BlockSpec(memory_space=pltpu.VMEM),
        input_output_aliases={0: 0},
        compiler_params=pltpu.CompilerParams(vmem_limit_bytes=VMEM_LIMIT),
    )(*args)


class Ring:
    def __init__(self, expert_count, group_count):
        self.count = expert_count
        self.half = expert_count // 2
        self.snake = group_count == 2
        if self.snake:
            self.order = list(range(0, expert_count, 2)) + list(range(expert_count - 1, 0, -2))
        else:
            self.order = list(range(expert_count))

    def send(self, value, distance):
        pairs = [
            (self.order[i], self.order[(i + distance) % self.count]) for i in range(self.count)
        ]
        return lax.ppermute(value, "expert", pairs)

    def device_at(self, distance):
        here = lax.axis_index("expert")
        count = self.count
        if self.snake:
            here = jnp.where(here % 2 == 0, here // 2, count - 1 - here // 2)
        there = lax.rem(here + distance % count, count)
        if self.snake:
            there = jnp.where(there < self.half, 2 * there, 2 * (count - 1 - there) + 1)
        return there

    def gather(self, top, bottom, use, guard=None):
        top_left = top_right = top
        bottom_left = bottom_right = bottom
        use((0,), (top, bottom))
        for step in range(1, self.half):
            if guard is not None and step == self.half - 1:
                top_right = after(top_right, [guard])
            top_left = self.send(top_left, 1)
            top_right = self.send(top_right, -1)
            bottom_left = self.send(bottom_left, 1)
            bottom_right = self.send(bottom_right, -1)
            use((-step, step), (top_left, bottom_left, top_right, bottom_right))
        use((self.half,), (self.send(top_left, 1), self.send(bottom_right, -1)))

    def scatter(self, parts):
        most = self.half - 1
        mid, cols = parts[most][0].shape

        def join_kernel(first, sum_ref, arrived_ref, other_ref, out_ref):
            out_ref[pl.ds(first, mid), :] = (sum_ref[...] + arrived_ref[...].astype(F32)).astype(BF16)
            out_ref[pl.ds(mid - first, mid), :] = other_ref[...]

        def part_kernel(first, block_ref, arrived_ref, out_ref):
            arrived = arrived_ref[pl.ds(first, mid), :].astype(F32)
            out_ref[...] = (block_ref[...] + arrived).astype(BF16)

        def joined(first, halves, arrived):
            kernel = functools.partial(join_kernel, first)
            own, other = (halves[1], halves[0]) if first else halves
            return call(kernel, [((2 * mid, cols), BF16)], own, arrived, other)[0]

        def parted(first, block, arrived):
            return call(functools.partial(part_kernel, first), [((mid, cols), BF16)], block, arrived)[0]

        from_left = self.send(parts[self.half][0], 1)
        from_right = self.send(parts[self.half][1], -1)
        from_left = self.send(joined(0, parts[most], from_left), 1)
        from_right = self.send(joined(mid, parts[-most], from_right), -1)
        top_left = bottom_left = from_left
        top_right = bottom_right = from_right
        for step in range(most - 1, 0, -1):
            plus = add
            if step == most - 1:
                plus = None
            sums = []
            for first, block, arrived in (
                (0, parts[step][0], top_left),
                (mid, parts[-step][1], bottom_right),
                (mid, parts[step][1], bottom_left),
                (0, parts[-step][0], top_right),
            ):
                sums.append(plus(block, arrived) if plus else parted(first, block, arrived))
            top_left, bottom_right = self.send(sums[0], 1), self.send(sums[1], -1)
            bottom_left, top_right = self.send(sums[2], 1), self.send(sums[3], -1)
        return (top_left, top_right), (bottom_left, bottom_right)

    def part_types(self, distances):
        types = []
        for k in distances:
            first = BF16 if k == self.half or k == 1 - self.half else F32
            second = BF16 if k == self.half or k == self.half - 1 else F32
            types += [first, second]
        return types


def add_kernel(block_ref, arrived_ref, out_ref):
    out_ref[...] = (block_ref[...] + arrived_ref[...].astype(F32)).astype(BF16)


def add(block, arrived):
    return call(add_kernel, [(block.shape, BF16)], block, arrived)[0]


def sum_kernel(*refs):
    out_ref = refs[-1]
    rows = refs[0].shape[0]
    for i in range(len(refs) // 3):
        own, left, right = refs[3 * i : 3 * i + 3]
        arrived = left[...].astype(F32) + right[...].astype(F32)
        out_ref[pl.ds(i * rows, rows), :] = (own[...] + arrived).astype(BF16)


class Copies:
    def __init__(self, sems):
        self.sems, self.started = sems, []

    def start(self, source, target):
        copy = pltpu.make_async_copy(source, target, self.sems.at[len(self.started)])
        copy.start()
        self.started.append(copy)

    def wait(self):
        for copy in self.started:
            copy.wait()


def strips(gate_shape, down_shape):
    local_experts, depth, hidden_dim = gate_shape
    _, height, feature_dim = down_shape
    row, places = 0, []
    for _ in range(local_experts):
        pair = [(row, depth), (row + depth, depth)]
        row += 2 * depth
        downs = []
        for begin in range(0, feature_dim, hidden_dim):
            downs.append((row, height, begin, min(hidden_dim, feature_dim - begin)))
            row += height
        places.append((pair, downs))
    return row, places


def pack(ids, scores, tokens, shards):
    rows, cols = tokens.shape
    mid = rows // 2
    quarter = LANES // 4
    inputs = [ids, scores, tokens, *shards]
    packed_shape, places, count = None, [], 0
    if shards:
        hidden_dim = shards[0].shape[2]
        packed_rows, places = strips(shards[0].shape, shards[2].shape)
        packed_shape = (packed_rows, hidden_dim)
        count = sum(len(pair) + len(downs) for pair, downs in places)

    def kernel(*refs):
        ids_hbm, scores_hbm, tokens_hbm, *shards_hbm = refs[: len(inputs)]
        top_ref, bottom_ref, *packed_refs = refs[len(inputs) : -3]
        ids_ref, scores_ref, sems = refs[-3:]
        copies = Copies(sems)
        copies.start(ids_hbm, ids_ref)
        copies.start(scores_hbm, scores_ref)
        copies.start(tokens_hbm.at[pl.ds(0, mid), :], top_ref.at[:, pl.ds(0, cols)])
        copies.start(tokens_hbm.at[pl.ds(mid, mid), :], bottom_ref)
        for local, (pair, downs) in enumerate(places):
            out_ref = packed_refs[0]
            for source, (row, some) in zip(shards_hbm, pair):
                copies.start(source.at[local], out_ref.at[pl.ds(row, some), :])
            for row, some, begin, width in downs:
                source = shards_hbm[2].at[local, :, pl.ds(begin, width)]
                copies.start(source, out_ref.at[pl.ds(row, some), pl.ds(0, width)])
                if width < hidden_dim:
                    rest = hidden_dim - width
                    out_ref[pl.ds(row, some), pl.ds(width, rest)] = jnp.zeros((some, rest), BF16)
        copies.started[0].wait()
        copies.started[1].wait()
        scores = scores_ref[...]
        ids = ids_ref[...]
        route_weight = scores / jnp.sum(scores, axis=0, keepdims=True)
        expert = lax.broadcasted_iota(jnp.int32, (quarter, rows), 0)
        weight_by = jnp.zeros((quarter, rows), F32)
        for choice_k in range(scores.shape[0]):
            one = slice(choice_k, choice_k + 1)
            weight_by = weight_by + jnp.where(ids[one] == expert, route_weight[one], 0.0)
        high = weight_by.astype(BF16).astype(F32)
        weights = jnp.concatenate([high, weight_by - high] * 2, axis=0).T
        lane = lax.broadcasted_iota(jnp.int32, (mid, LANES), 1)
        both = jnp.where(lane < 2 * quarter, weights[:mid], weights[mid:])
        top_ref[:, cols:] = both.astype(BF16)
        for copy in copies.started[2:]:
            copy.wait()

    outs = [pltpu.VMEM((mid, cols + LANES), BF16), pltpu.VMEM((mid, cols), BF16)]
    if shards:
        outs.append(pltpu.VMEM(packed_shape, BF16))
    return pl.pallas_call(
        kernel,
        out_shape=outs,
        in_specs=[pl.BlockSpec(memory_space=pl.ANY)] * len(inputs),
        out_specs=[pl.BlockSpec(memory_space=pltpu.VMEM)] * len(outs),
        scratch_shapes=[
            pltpu.VMEM(ids.shape, ids.dtype),
            pltpu.VMEM(scores.shape, F32),
            pltpu.SemaphoreType.DMA((4 + count,)),
        ],
        compiler_params=pltpu.CompilerParams(vmem_limit_bytes=VMEM_LIMIT),
    )(*[pltpu.with_memory_space_constraint(a, pltpu.HBM) for a in inputs])


def full_weights(shards, packed):
    local_experts, _, hidden_dim = shards[0].shape
    feature_dim = shards[2].shape[2]
    paired = packed is not None
    _, places = strips(shards[0].shape, shards[2].shape)
    depth, height = shards[0].shape[1], shards[2].shape[1]

    def kernel(*refs):
        gate_hbm, up_hbm, down_hbm, *rest = refs
        wide_ref, down_ref, sems = rest[-3:]
        copies = Copies(sems)
        mine = lax.axis_index("group") if paired else 0

        def wide_at(place, local, is_up):
            rows = pl.ds(pl.multiple_of(place * depth, 16), depth)
            return wide_ref.at[rows, pl.ds((2 * local + is_up) * hidden_dim, hidden_dim)]

        def down_at(place, local, begin, cols):
            top = pl.multiple_of(local * hidden_dim + place * height, 16)
            return down_ref.at[pl.ds(top, height), pl.ds(begin, cols)]

        for local in range(local_experts):
            for is_up, source in enumerate((gate_hbm, up_hbm)):
                copies.start(source.at[local], wide_at(mine, local, is_up))
            copies.start(down_hbm.at[local], down_at(mine, local, 0, feature_dim))
        if paired:
            for local, (pair, downs) in enumerate(places):
                for is_up, (row, some) in enumerate(pair):
                    copies.start(rest[0].at[pl.ds(row, some), :], wide_at(1 - mine, local, is_up))
                for row, some, begin, cols in downs:
                    source = rest[0].at[pl.ds(row, some), pl.ds(0, cols)]
                    copies.start(source, down_at(1 - mine, local, begin, cols))
        copies.wait()

    shards = [pltpu.with_memory_space_constraint(w, pltpu.HBM) for w in shards]
    count = 3 * local_experts
    specs = [pl.BlockSpec(memory_space=pl.ANY)] * 3
    if paired:
        count += sum(len(pair) + len(downs) for pair, downs in places)
        specs.append(pl.BlockSpec(memory_space=pltpu.VMEM))
        shards.append(pltpu.with_memory_space_constraint(packed, pltpu.VMEM))
    return pl.pallas_call(
        kernel,
        out_shape=[
            pltpu.VMEM((feature_dim, 2 * local_experts * hidden_dim), BF16),
            pltpu.VMEM((local_experts * hidden_dim, feature_dim), BF16),
        ],
        in_specs=specs,
        out_specs=[pl.BlockSpec(memory_space=pltpu.VMEM)] * 2,
        scratch_shapes=[pltpu.SemaphoreType.DMA((count,))],
        compiler_params=pltpu.CompilerParams(vmem_limit_bytes=VMEM_LIMIT),
        cost_estimate=pl.CostEstimate(
            flops=0,
            bytes_accessed=12 * local_experts * hidden_dim * feature_dim,
            transcendentals=0,
        ),
    )(*shards)


def transpose_kernel(from_ref, to_ref):
    strip = 2 * LANES

    @pl.loop(0, to_ref.shape[0] // strip)
    def _(i):
        some = pl.ds(pl.multiple_of(i * strip, strip), strip)
        to_ref[some, :] = from_ref[:, some].T


def transposed(weights):
    rows, cols = weights.shape
    return call(transpose_kernel, [((cols, rows), BF16)], weights)[0]


def body(tokens, w_gate, w_up, w_down, route_ids, route_scores, norm_gain, class_head, targets):
    rows_here, feature_dim = tokens.shape
    expert_count = lax.axis_size("expert")
    group_count = lax.axis_size("group")
    local_experts, _, hidden_dim = w_gate.shape
    pair_dim = 2 * hidden_dim
    ring = Ring(expert_count, group_count)
    block = (rows_here, feature_dim)
    mid = rows_here // 2

    shards = [w_gate, w_up, w_down]
    if group_count == 2:
        top, bottom, packed = pack(route_ids.T, route_scores.T, tokens, shards)
        packed = lax.ppermute(packed, "group", [(0, 1), (1, 0)])
    else:
        top, bottom = pack(route_ids.T, route_scores.T, tokens, [])
        shards = [lax.all_gather(w, "group", axis=1, tiled=True) for w in shards]
        packed = None
    wide, down = full_weights(shards, packed)

    def rows_of(refs):
        return jnp.concatenate([ref[...] for ref in refs], axis=0) if len(refs) > 1 else refs[0][...]

    def forward_kernel(count, *refs):
        token_refs, (wide_ref, down_ref) = refs[:count], refs[count : count + 2]
        outs = refs[count + 2 :]
        x = rows_of([ref.at[:, :feature_dim] for ref in token_refs])
        weights = jnp.concatenate([ref[:, feature_dim:] for ref in token_refs[::2]], axis=0).astype(F32)
        lane = lax.broadcasted_iota(jnp.int32, weights.shape, 1)
        quarter = LANES // 4
        hidden = []
        for local in range(local_experts):
            expert = lax.axis_index("expert") * local_experts + local
            scales = []
            for begin in (expert, expert + 2 * quarter):
                here = (lane == begin) | (lane == begin + quarter)
                scales.append(jnp.sum(jnp.where(here, weights, 0.0), axis=1, keepdims=True))
            pieces = [s[i : i + mid] for i in range(0, weights.shape[0], mid) for s in scales]
            scale = jnp.concatenate(pieces, axis=0)
            act = dot(x, wide_ref[:, pl.ds(local * pair_dim, pair_dim)])
            gate_act, up_act = act[:, :hidden_dim], act[:, hidden_dim:]
            sigmoid_gate = jax.nn.sigmoid(gate_act)
            silu = gate_act * sigmoid_gate * scale
            slope = sigmoid_gate * (1.0 + gate_act * (1.0 - sigmoid_gate)) * scale
            cols = pl.ds(local * hidden_dim, hidden_dim)
            outs[0][:, cols] = (up_act * slope).astype(BF16)
            outs[1][:, cols] = silu.astype(BF16)
            hidden.append((silu * up_act).astype(BF16))
        total = dot(jnp.concatenate(hidden, axis=1), down_ref[...])
        for i, out in enumerate(outs[2:]):
            out[...] = total[i * mid : (i + 1) * mid].astype(out.dtype)

    tokens_at, saved_at, part_at = {}, {}, {}
    flops = 2 * rows_here * feature_dim * hidden_dim * local_experts * 3

    def hold(distances, blocks):
        tokens_at[distances] = blocks

    def keep_parts(parts, distances, halves):
        parts.update({k: halves[2 * i : 2 * i + 2] for i, k in enumerate(distances)})

    def part_outs(distances):
        return [((mid, feature_dim), dtype) for dtype in ring.part_types(distances)]

    def forward(distances):
        blocks = tokens_at[distances]
        rows = mid * len(blocks)
        result = call(
            functools.partial(forward_kernel, len(blocks)),
            [((rows, local_experts * hidden_dim), BF16)] * 2 + part_outs(distances),
            *blocks,
            wide,
            down,
            flops=flops * rows // rows_here,
        )
        saved_at[distances] = result[:2]
        keep_parts(part_at, distances, result[2:])

    ring.gather(top, bottom, hold, wide)
    for distances in tokens_at:
        forward(distances)
    gain = norm_gain.reshape(1, feature_dim)
    half_shape = (mid, feature_dim)
    moe_top, moe_bottom = [
        call(sum_kernel, [(half_shape, BF16)], own, *arrived)[0]
        for own, arrived in zip(part_at[0], ring.scatter(part_at))
    ]

    norm_at, mean_at = {}, {}

    def residual_of(token_refs, moe_refs):
        token_rows = rows_of([ref.at[:, :feature_dim] for ref in token_refs]).astype(F32)
        return token_rows + rows_of(moe_refs).astype(F32)

    def inv_rms_of(residual):
        return lax.rsqrt(jnp.mean(residual * residual, axis=-1, keepdims=True) + NORM_EPS)

    def norm_kernel(distances, count, *refs):
        residual = residual_of(refs[:count], refs[count : 2 * count])
        gain_ref, so_far, out_ref, residual_ref, inv_ref = refs[2 * count :]
        inv_rms = inv_rms_of(residual)
        residual_ref[...] = residual
        inv_ref[...] = jnp.broadcast_to(inv_rms, inv_ref.shape)
        normed = residual * inv_rms * gain_ref[...]
        pooled = so_far[...]
        row = lax.broadcasted_iota(jnp.int32, pooled.shape, 0)
        for i, k in enumerate(distances):
            part = normed[i * rows_here : (i + 1) * rows_here]
            mean = jnp.mean(part, axis=0, keepdims=True)
            pooled = jnp.where(row == ring.device_at(k), mean, pooled)
        out_ref[...] = pooled

    pooled_shape = (expert_count, feature_dim)
    mean_at["pooled"] = jnp.zeros(pooled_shape, F32)

    def norm(distances, blocks):
        rows = mid * len(blocks)
        mean_at["pooled"], *norm_at[distances] = call(
            functools.partial(norm_kernel, distances, len(blocks)),
            [(pooled_shape, F32), ((rows, feature_dim), F32), ((rows, LANES), F32)],
            *tokens_at[distances],
            *blocks,
            gain,
            mean_at["pooled"],
        )

    ring.gather(moe_top, moe_bottom, norm)
    pooled = mean_at["pooled"].astype(BF16)
    logits = dot(pooled, class_head)
    target_rows = targets.reshape(expert_count, -1).astype(F32)
    logit_grad = (LOSS_SCALE * (jax.nn.sigmoid(logits) - target_rows)).astype(BF16)
    wide_t, down_t = transposed(wide), transposed(down)

    def grad_sum_kernel(count, *refs):
        total = refs[0][...].astype(F32)
        for ref in refs[1:count]:
            total = total + ref[...].astype(F32)
        refs[-1][...] = total.astype(refs[-1].dtype)

    grad_rows = dot_t(logit_grad, class_head).astype(BF16)
    span = 2
    for masks, others, dtype in (
        ([1], [wide_t, down_t], BF16),
        (list(range(span, expert_count, span)), [], F32),
    ):
        terms = [grad_rows]
        for mask in masks:
            pairs = [(e, e ^ mask) for e in range(expert_count)]
            terms.append(lax.ppermute(grad_rows, "expert", pairs))
        grad_rows = call(
            functools.partial(grad_sum_kernel, len(terms)),
            [(pooled_shape, dtype)],
            *terms,
            *others,
        )[0]
    pooled_grad = grad_rows

    both = jnp.concatenate([pooled, logit_grad], axis=1)
    if group_count == 2:
        both = jnp.concatenate([both, lax.ppermute(both, "group", [(0, 1), (1, 0)])], axis=0)
    else:
        both = lax.all_gather(both, "group", axis=0, tiled=True)
    head_grad = lax.dot_general(
        both[:, :feature_dim],
        both[:, feature_dim:],
        (((0,), (0,)), ((), ())),
        preferred_element_type=F32,
    )

    def backward_kernel(distances, residual_ref, inv_ref, gate_save, up_save, *refs):
        grad_ref, gain_ref, wide_ref, down_ref, *outs = refs
        residual, inv_rms = residual_ref[...], inv_ref[:, :1]
        cube = inv_rms * inv_rms * inv_rms
        parts = []
        for i, k in enumerate(distances):
            rows = slice(i * rows_here, (i + 1) * rows_here)
            scaled = gain_ref[...] * grad_ref[pl.ds(ring.device_at(k), 1), :] / rows_here
            slope = cube[rows] * jnp.mean(residual[rows] * scaled, axis=-1, keepdims=True)
            parts.append(inv_rms[rows] * scaled - residual[rows] * slope)
        resid_grad = jnp.concatenate(parts, axis=0) if len(parts) > 1 else parts[0]
        down_back = dot(resid_grad.astype(BF16), down_ref[...])
        grads = []
        for local in range(local_experts):
            cols = slice(local * hidden_dim, (local + 1) * hidden_dim)
            for save in (gate_save, up_save):
                grads.append((down_back[:, cols] * save[:, cols].astype(F32)).astype(BF16))
        total = dot(jnp.concatenate(grads, axis=1), wide_ref[...])
        if distances == (0,):
            total = total + resid_grad
        rows = total.shape[0] // len(outs)
        for i, out in enumerate(outs):
            out[...] = total[i * rows : (i + 1) * rows].astype(out.dtype)

    back_at = {}

    def backward(distances):
        result = call(
            functools.partial(backward_kernel, distances),
            part_outs(distances),
            *norm_at[distances],
            *saved_at[distances],
            pooled_grad,
            gain,
            wide_t,
            down_t,
            flops=flops * len(distances),
        )
        keep_parts(back_at, distances, result)

    for distances in reversed(list(tokens_at)):
        backward(distances)
    (top_left, top_right), (bottom_left, bottom_right) = ring.scatter(back_at)
    token_grad = pl.pallas_call(
        sum_kernel,
        out_shape=jax.ShapeDtypeStruct(block, BF16),
        in_specs=[pl.BlockSpec(memory_space=pltpu.VMEM)] * 6,
        out_specs=pl.BlockSpec(memory_space=pltpu.VMEM),
        compiler_params=pltpu.CompilerParams(vmem_limit_bytes=VMEM_LIMIT),
    )(back_at[0][0], top_left, top_right, back_at[0][1], bottom_left, bottom_right)
    return (token_grad, head_grad)


def solution(mesh):
    in_specs = (
        P(("rep", "expert", "group"), None),
        P("expert", "group", None),
        P("expert", "group", None),
        P("expert", "group", None),
        P(("rep", "expert", "group"), None),
        P(("rep", "expert", "group"), None),
        P(),
        P(None, "expert"),
        P("rep", "group", "expert"),
    )
    out_specs = (P(("rep", "expert", "group"), None), P("rep", "expert"))
    return jax.shard_map(body, mesh=mesh, in_specs=in_specs, out_specs=out_specs, check_vma=False)
```

```python
import functools

import jax
import jax.numpy as jnp
from jax import lax
from jax.experimental import pallas as pl
from jax.experimental.pallas import tpu as pltpu
from jax.sharding import PartitionSpec as P

LOSS_SCALE = 8.0
NORM_EPS = 1e-06
F32 = jnp.float32
BF16 = jnp.bfloat16
LANES = 128
VMEM_LIMIT = 32 * 1024 * 1024


def dot(left, right):
    return jnp.dot(left, right, preferred_element_type=F32)


def dot_t(left, right):
    return lax.dot_general(left, right, (((1,), (1,)), ((), ())), preferred_element_type=F32)


def call(kernel, outs, *args, flops=0):
    args = [pltpu.with_memory_space_constraint(a, pltpu.VMEM) for a in args]
    size = sum(a.size * a.dtype.itemsize for a in args)
    return pl.pallas_call(
        kernel,
        out_shape=[pltpu.VMEM(shape, dtype) for shape, dtype in outs],
        in_specs=[pl.BlockSpec(memory_space=pltpu.VMEM)] * len(args),
        out_specs=[pl.BlockSpec(memory_space=pltpu.VMEM)] * len(outs),
        compiler_params=pltpu.CompilerParams(vmem_limit_bytes=VMEM_LIMIT),
        cost_estimate=pl.CostEstimate(flops=flops, bytes_accessed=size, transcendentals=0),
    )(*args)


def after(value, guards):
    def kernel(*refs):
        pass

    args = [pltpu.with_memory_space_constraint(a, pltpu.VMEM) for a in (value, *guards)]
    return pl.pallas_call(
        kernel,
        out_shape=pltpu.VMEM(value.shape, value.dtype),
        in_specs=[pl.BlockSpec(memory_space=pltpu.VMEM)] * len(args),
        out_specs=pl.BlockSpec(memory_space=pltpu.VMEM),
        input_output_aliases={0: 0},
        compiler_params=pltpu.CompilerParams(vmem_limit_bytes=VMEM_LIMIT),
    )(*args)


class Ring:
    def __init__(self, expert_count, group_count):
        self.count = expert_count
        self.half = expert_count // 2
        self.snake = group_count == 2
        if self.snake:
            self.order = list(range(0, expert_count, 2)) + list(range(expert_count - 1, 0, -2))
        else:
            self.order = list(range(expert_count))

    def send(self, value, distance):
        pairs = [
            (self.order[i], self.order[(i + distance) % self.count]) for i in range(self.count)
        ]
        return lax.ppermute(value, "expert", pairs)

    def device_at(self, distance):
        here = lax.axis_index("expert")
        count = self.count
        if self.snake:
            here = jnp.where(here % 2 == 0, here // 2, count - 1 - here // 2)
        there = lax.rem(here + distance % count, count)
        if self.snake:
            there = jnp.where(there < self.half, 2 * there, 2 * (count - 1 - there) + 1)
        return there

    def gather(self, top, bottom, use, guard=None):
        top_left = top_right = top
        bottom_left = bottom_right = bottom
        use((0,), (top, bottom))
        for step in range(1, self.half):
            if guard is not None and step == self.half - 1:
                top_right = after(top_right, [guard])
            top_left = self.send(top_left, 1)
            top_right = self.send(top_right, -1)
            bottom_left = self.send(bottom_left, 1)
            bottom_right = self.send(bottom_right, -1)
            use((-step, step), (top_left, bottom_left, top_right, bottom_right))
        use((self.half,), (self.send(top_left, 1), self.send(bottom_right, -1)))

    def scatter(self, parts):
        most = self.half - 1
        top_left = self.send(parts[self.half][0], 1)
        bottom_right = self.send(parts[self.half][1], -1)
        bottom_left = self.send(parts[most][1], 1)
        top_right = self.send(parts[-most][0], -1)
        for step in range(most, 0, -1):
            top_left = self.send(add(parts[step][0], top_left), 1)
            bottom_right = self.send(add(parts[-step][1], bottom_right), -1)
            if step > 1:
                bottom_left = self.send(add(parts[step - 1][1], bottom_left), 1)
                top_right = self.send(add(parts[1 - step][0], top_right), -1)
        return (top_left, top_right), (bottom_left, bottom_right)

    def part_types(self, distances):
        types = []
        for k in distances:
            first = BF16 if k == self.half or k == 1 - self.half else F32
            second = BF16 if k == self.half or k == self.half - 1 else F32
            types += [first, second]
        return types


def add_kernel(block_ref, arrived_ref, out_ref):
    out_ref[...] = (block_ref[...] + arrived_ref[...].astype(F32)).astype(BF16)


def add(block, arrived):
    return call(add_kernel, [(block.shape, BF16)], block, arrived)[0]


def sum_kernel(*refs):
    out_ref = refs[-1]
    rows = refs[0].shape[0]
    for i in range(len(refs) // 3):
        own, left, right = refs[3 * i : 3 * i + 3]
        arrived = left[...].astype(F32) + right[...].astype(F32)
        out_ref[pl.ds(i * rows, rows), :] = (own[...] + arrived).astype(BF16)


class Copies:
    def __init__(self, sems):
        self.sems, self.started = sems, []

    def start(self, source, target):
        copy = pltpu.make_async_copy(source, target, self.sems.at[len(self.started)])
        copy.start()
        self.started.append(copy)

    def wait(self):
        for copy in self.started:
            copy.wait()


def strips(gate_shape, down_shape):
    local_experts, depth, hidden_dim = gate_shape
    _, height, feature_dim = down_shape
    row, places = 0, []
    for _ in range(local_experts):
        pair = [(row, depth), (row + depth, depth)]
        row += 2 * depth
        downs = []
        for begin in range(0, feature_dim, hidden_dim):
            downs.append((row, height, begin, min(hidden_dim, feature_dim - begin)))
            row += height
        places.append((pair, downs))
    return row, places


def pack(ids, scores, tokens, shards):
    rows, cols = tokens.shape
    mid = rows // 2
    quarter = LANES // 4
    inputs = [ids, scores, tokens, *shards]
    packed_shape, places, count = None, [], 0
    if shards:
        hidden_dim = shards[0].shape[2]
        packed_rows, places = strips(shards[0].shape, shards[2].shape)
        packed_shape = (packed_rows, hidden_dim)
        count = sum(len(pair) + len(downs) for pair, downs in places)

    def kernel(*refs):
        ids_hbm, scores_hbm, tokens_hbm, *shards_hbm = refs[: len(inputs)]
        top_ref, bottom_ref, *packed_refs = refs[len(inputs) : -3]
        ids_ref, scores_ref, sems = refs[-3:]
        copies = Copies(sems)
        copies.start(ids_hbm, ids_ref)
        copies.start(scores_hbm, scores_ref)
        copies.start(tokens_hbm.at[pl.ds(0, mid), :], top_ref.at[:, pl.ds(0, cols)])
        copies.start(tokens_hbm.at[pl.ds(mid, mid), :], bottom_ref)
        for local, (pair, downs) in enumerate(places):
            out_ref = packed_refs[0]
            for source, (row, some) in zip(shards_hbm, pair):
                copies.start(source.at[local], out_ref.at[pl.ds(row, some), :])
            for row, some, begin, width in downs:
                source = shards_hbm[2].at[local, :, pl.ds(begin, width)]
                copies.start(source, out_ref.at[pl.ds(row, some), pl.ds(0, width)])
                if width < hidden_dim:
                    rest = hidden_dim - width
                    out_ref[pl.ds(row, some), pl.ds(width, rest)] = jnp.zeros((some, rest), BF16)
        copies.started[0].wait()
        copies.started[1].wait()
        scores = scores_ref[...]
        ids = ids_ref[...]
        route_weight = scores / jnp.sum(scores, axis=0, keepdims=True)
        expert = lax.broadcasted_iota(jnp.int32, (quarter, rows), 0)
        weight_by = jnp.zeros((quarter, rows), F32)
        for choice_k in range(scores.shape[0]):
            one = slice(choice_k, choice_k + 1)
            weight_by = weight_by + jnp.where(ids[one] == expert, route_weight[one], 0.0)
        high = weight_by.astype(BF16).astype(F32)
        weights = jnp.concatenate([high, weight_by - high] * 2, axis=0).T
        lane = lax.broadcasted_iota(jnp.int32, (mid, LANES), 1)
        both = jnp.where(lane < 2 * quarter, weights[:mid], weights[mid:])
        top_ref[:, cols:] = both.astype(BF16)
        for copy in copies.started[2:]:
            copy.wait()

    outs = [pltpu.VMEM((mid, cols + LANES), BF16), pltpu.VMEM((mid, cols), BF16)]
    if shards:
        outs.append(pltpu.VMEM(packed_shape, BF16))
    return pl.pallas_call(
        kernel,
        out_shape=outs,
        in_specs=[pl.BlockSpec(memory_space=pl.ANY)] * len(inputs),
        out_specs=[pl.BlockSpec(memory_space=pltpu.VMEM)] * len(outs),
        scratch_shapes=[
            pltpu.VMEM(ids.shape, ids.dtype),
            pltpu.VMEM(scores.shape, F32),
            pltpu.SemaphoreType.DMA((4 + count,)),
        ],
        compiler_params=pltpu.CompilerParams(vmem_limit_bytes=VMEM_LIMIT),
    )(*[pltpu.with_memory_space_constraint(a, pltpu.HBM) for a in inputs])


def full_weights(shards, packed):
    local_experts, _, hidden_dim = shards[0].shape
    feature_dim = shards[2].shape[2]
    paired = packed is not None
    _, places = strips(shards[0].shape, shards[2].shape)
    depth, height = shards[0].shape[1], shards[2].shape[1]

    def kernel(*refs):
        gate_hbm, up_hbm, down_hbm, *rest = refs
        wide_ref, down_ref, sems = rest[-3:]
        copies = Copies(sems)
        mine = lax.axis_index("group") if paired else 0

        def wide_at(place, local, is_up):
            rows = pl.ds(pl.multiple_of(place * depth, 16), depth)
            return wide_ref.at[rows, pl.ds((2 * local + is_up) * hidden_dim, hidden_dim)]

        def down_at(place, local, begin, cols):
            top = pl.multiple_of(local * hidden_dim + place * height, 16)
            return down_ref.at[pl.ds(top, height), pl.ds(begin, cols)]

        for local in range(local_experts):
            for is_up, source in enumerate((gate_hbm, up_hbm)):
                copies.start(source.at[local], wide_at(mine, local, is_up))
            copies.start(down_hbm.at[local], down_at(mine, local, 0, feature_dim))
        if paired:
            for local, (pair, downs) in enumerate(places):
                for is_up, (row, some) in enumerate(pair):
                    copies.start(rest[0].at[pl.ds(row, some), :], wide_at(1 - mine, local, is_up))
                for row, some, begin, cols in downs:
                    source = rest[0].at[pl.ds(row, some), pl.ds(0, cols)]
                    copies.start(source, down_at(1 - mine, local, begin, cols))
        copies.wait()

    shards = [pltpu.with_memory_space_constraint(w, pltpu.HBM) for w in shards]
    count = 3 * local_experts
    specs = [pl.BlockSpec(memory_space=pl.ANY)] * 3
    if paired:
        count += sum(len(pair) + len(downs) for pair, downs in places)
        specs.append(pl.BlockSpec(memory_space=pltpu.VMEM))
        shards.append(pltpu.with_memory_space_constraint(packed, pltpu.VMEM))
    return pl.pallas_call(
        kernel,
        out_shape=[
            pltpu.VMEM((feature_dim, 2 * local_experts * hidden_dim), BF16),
            pltpu.VMEM((local_experts * hidden_dim, feature_dim), BF16),
        ],
        in_specs=specs,
        out_specs=[pl.BlockSpec(memory_space=pltpu.VMEM)] * 2,
        scratch_shapes=[pltpu.SemaphoreType.DMA((count,))],
        compiler_params=pltpu.CompilerParams(vmem_limit_bytes=VMEM_LIMIT),
        cost_estimate=pl.CostEstimate(
            flops=0,
            bytes_accessed=12 * local_experts * hidden_dim * feature_dim,
            transcendentals=0,
        ),
    )(*shards)


def transpose_kernel(from_ref, to_ref):
    strip = 2 * LANES

    @pl.loop(0, to_ref.shape[0] // strip)
    def _(i):
        some = pl.ds(pl.multiple_of(i * strip, strip), strip)
        to_ref[some, :] = from_ref[:, some].T


def transposed(weights):
    rows, cols = weights.shape
    return call(transpose_kernel, [((cols, rows), BF16)], weights)[0]


def body(tokens, w_gate, w_up, w_down, route_ids, route_scores, norm_gain, class_head, targets):
    rows_here, feature_dim = tokens.shape
    expert_count = lax.axis_size("expert")
    group_count = lax.axis_size("group")
    local_experts, _, hidden_dim = w_gate.shape
    pair_dim = 2 * hidden_dim
    ring = Ring(expert_count, group_count)
    block = (rows_here, feature_dim)
    mid = rows_here // 2

    shards = [w_gate, w_up, w_down]
    if group_count == 2:
        top, bottom, packed = pack(route_ids.T, route_scores.T, tokens, shards)
        packed = lax.ppermute(packed, "group", [(0, 1), (1, 0)])
    else:
        top, bottom = pack(route_ids.T, route_scores.T, tokens, [])
        shards = [lax.all_gather(w, "group", axis=1, tiled=True) for w in shards]
        packed = None
    wide, down = full_weights(shards, packed)

    def rows_of(refs):
        return jnp.concatenate([ref[...] for ref in refs], axis=0) if len(refs) > 1 else refs[0][...]

    def forward_kernel(count, *refs):
        token_refs, (wide_ref, down_ref) = refs[:count], refs[count : count + 2]
        outs = refs[count + 2 :]
        x = rows_of([ref.at[:, :feature_dim] for ref in token_refs])
        weights = jnp.concatenate([ref[:, feature_dim:] for ref in token_refs[::2]], axis=0).astype(F32)
        lane = lax.broadcasted_iota(jnp.int32, weights.shape, 1)
        quarter = LANES // 4
        hidden = []
        for local in range(local_experts):
            expert = lax.axis_index("expert") * local_experts + local
            scales = []
            for begin in (expert, expert + 2 * quarter):
                here = (lane == begin) | (lane == begin + quarter)
                scales.append(jnp.sum(jnp.where(here, weights, 0.0), axis=1, keepdims=True))
            pieces = [s[i : i + mid] for i in range(0, weights.shape[0], mid) for s in scales]
            scale = jnp.concatenate(pieces, axis=0)
            act = dot(x, wide_ref[:, pl.ds(local * pair_dim, pair_dim)])
            gate_act, up_act = act[:, :hidden_dim], act[:, hidden_dim:]
            sigmoid_gate = jax.nn.sigmoid(gate_act)
            silu = gate_act * sigmoid_gate * scale
            slope = sigmoid_gate * (1.0 + gate_act * (1.0 - sigmoid_gate)) * scale
            cols = pl.ds(local * hidden_dim, hidden_dim)
            outs[0][:, cols] = (up_act * slope).astype(BF16)
            outs[1][:, cols] = silu.astype(BF16)
            hidden.append((silu * up_act).astype(BF16))
        total = dot(jnp.concatenate(hidden, axis=1), down_ref[...])
        for i, out in enumerate(outs[2:]):
            out[...] = total[i * mid : (i + 1) * mid].astype(out.dtype)

    tokens_at, saved_at, part_at = {}, {}, {}
    flops = 2 * rows_here * feature_dim * hidden_dim * local_experts * 3

    def hold(distances, blocks):
        tokens_at[distances] = blocks

    def keep_parts(parts, distances, halves):
        parts.update({k: halves[2 * i : 2 * i + 2] for i, k in enumerate(distances)})

    def part_outs(distances):
        return [((mid, feature_dim), dtype) for dtype in ring.part_types(distances)]

    def forward(distances):
        blocks = tokens_at[distances]
        rows = mid * len(blocks)
        result = call(
            functools.partial(forward_kernel, len(blocks)),
            [((rows, local_experts * hidden_dim), BF16)] * 2 + part_outs(distances),
            *blocks,
            wide,
            down,
            flops=flops * rows // rows_here,
        )
        saved_at[distances] = result[:2]
        keep_parts(part_at, distances, result[2:])

    ring.gather(top, bottom, hold, wide)
    for distances in tokens_at:
        forward(distances)
    gain = norm_gain.reshape(1, feature_dim)
    half_shape = (mid, feature_dim)
    moe_top, moe_bottom = [
        call(sum_kernel, [(half_shape, BF16)], own, *arrived)[0]
        for own, arrived in zip(part_at[0], ring.scatter(part_at))
    ]

    norm_at, mean_at, moe_at = {}, {}, {}

    def residual_of(token_refs, moe_refs):
        token_rows = rows_of([ref.at[:, :feature_dim] for ref in token_refs]).astype(F32)
        return token_rows + rows_of(moe_refs).astype(F32)

    def inv_rms_of(residual):
        return lax.rsqrt(jnp.mean(residual * residual, axis=-1, keepdims=True) + NORM_EPS)

    def norm_kernel(distances, count, *refs):
        residual = residual_of(refs[:count], refs[count : 2 * count])
        gain_ref, so_far, out_ref, residual_ref, inv_ref = refs[2 * count :]
        inv_rms = inv_rms_of(residual)
        residual_ref[...] = residual
        inv_ref[...] = jnp.broadcast_to(inv_rms, inv_ref.shape)
        normed = residual * inv_rms * gain_ref[...]
        pooled = so_far[...]
        row = lax.broadcasted_iota(jnp.int32, pooled.shape, 0)
        for i, k in enumerate(distances):
            part = normed[i * rows_here : (i + 1) * rows_here]
            mean = jnp.mean(part, axis=0, keepdims=True)
            pooled = jnp.where(row == ring.device_at(k), mean, pooled)
        out_ref[...] = pooled

    pooled_shape = (expert_count, feature_dim)
    mean_at["pooled"] = jnp.zeros(pooled_shape, F32)

    def norm(distances, blocks):
        moe_at[distances] = blocks
        rows = mid * len(blocks)
        mean_at["pooled"], *norm_at[distances] = call(
            functools.partial(norm_kernel, distances, len(blocks)),
            [(pooled_shape, F32), ((rows, feature_dim), F32), ((rows, LANES), F32)],
            *tokens_at[distances],
            *blocks,
            gain,
            mean_at["pooled"],
        )

    ring.gather(moe_top, moe_bottom, norm)
    pooled = mean_at["pooled"].astype(BF16)
    logits = dot(pooled, class_head)
    target_rows = targets.reshape(expert_count, -1).astype(F32)
    logit_grad = (LOSS_SCALE * (jax.nn.sigmoid(logits) - target_rows)).astype(BF16)
    wide_t, down_t = transposed(wide), transposed(down)

    def grad_sum_kernel(count, *refs):
        total = refs[0][...].astype(F32)
        for ref in refs[1:count]:
            total = total + ref[...].astype(F32)
        refs[-1][...] = total.astype(refs[-1].dtype)

    def grad_kernel(count, *refs):
        gain_ref, down_ref, *_, scaled_ref, back_ref = refs[count:]
        total = refs[0][...].astype(F32)
        for ref in refs[1:count]:
            total = total + ref[...].astype(F32)
        scaled = gain_ref[...] * total / rows_here
        scaled_ref[...] = scaled
        high = scaled.astype(BF16)
        low = (scaled - high.astype(F32)).astype(BF16)
        back_ref[...] = dot(high, down_ref[...]) + dot(low, down_ref[...])

    def project_kernel(count, *refs):
        down_ref, out_ref = refs[2 * count :]
        tokens_here = [ref[:, :feature_dim] for ref in refs[:count]]
        moe_here = [ref[...] for ref in refs[count : 2 * count]]
        out = dot(jnp.concatenate(tokens_here, axis=0), down_ref[...])
        out_ref[...] = out + dot(jnp.concatenate(moe_here, axis=0), down_ref[...])

    def terms_of(rows, masks):
        pairs = [[(e, e ^ mask) for e in range(expert_count)] for mask in masks]
        return [rows] + [lax.ppermute(rows, "expert", p) for p in pairs]

    project_at = {}
    for distances, blocks in moe_at.items():
        rows = mid * len(blocks)
        project_at[distances] = call(
            functools.partial(project_kernel, len(blocks)),
            [((rows, local_experts * hidden_dim), F32)],
            *tokens_at[distances],
            *blocks,
            down_t,
            flops=4 * rows * feature_dim * hidden_dim * local_experts,
        )[0]

    near = [d for d in project_at if 0 < d[-1] < ring.half - 1]
    last = [d for d in project_at if d not in near]
    terms = terms_of(dot_t(logit_grad, class_head).astype(BF16), [1])
    grad_rows = call(
        functools.partial(grad_sum_kernel, 2),
        [(pooled_shape, BF16)],
        *terms,
        wide_t,
        *[project_at[d] for d in near],
    )[0]
    span = 2
    terms = terms_of(grad_rows, range(span, expert_count, span))
    scaled_rows, back_rows = call(
        functools.partial(grad_kernel, len(terms)),
        [(pooled_shape, F32), ((expert_count, local_experts * hidden_dim), F32)],
        *terms,
        gain,
        down_t,
        *[project_at[d] for d in last],
    )
    both = jnp.concatenate([pooled, logit_grad], axis=1)
    if group_count == 2:
        both = jnp.concatenate([both, lax.ppermute(both, "group", [(0, 1), (1, 0)])], axis=0)
    else:
        both = lax.all_gather(both, "group", axis=0, tiled=True)
    head_grad = lax.dot_general(
        both[:, :feature_dim],
        both[:, feature_dim:],
        (((0,), (0,)), ((), ())),
        preferred_element_type=F32,
    )

    def backward_kernel(distances, residual_ref, inv_ref, gate_save, up_save, project_ref, *refs):
        scaled_ref, back_ref, wide_ref, *outs = refs
        residual, inv_rms = residual_ref[...], inv_ref[:, :1]
        cube = inv_rms * inv_rms * inv_rms
        parts = []
        for i, k in enumerate(distances):
            rows = slice(i * rows_here, (i + 1) * rows_here)
            device = pl.ds(ring.device_at(k), 1)
            scaled = scaled_ref[device, :]
            slope = cube[rows] * jnp.mean(residual[rows] * scaled, axis=-1, keepdims=True)
            parts.append(inv_rms[rows] * back_ref[device, :] - project_ref[rows, :] * slope)
        down_back = jnp.concatenate(parts, axis=0) if len(parts) > 1 else parts[0]
        if distances == (0,):
            resid_grad = inv_rms * scaled - residual * slope
        grads = []
        for local in range(local_experts):
            cols = slice(local * hidden_dim, (local + 1) * hidden_dim)
            for save in (gate_save, up_save):
                grads.append((down_back[:, cols] * save[:, cols].astype(F32)).astype(BF16))
        total = dot(jnp.concatenate(grads, axis=1), wide_ref[...])
        if distances == (0,):
            total = total + resid_grad
        rows = total.shape[0] // len(outs)
        for i, out in enumerate(outs):
            out[...] = total[i * rows : (i + 1) * rows].astype(out.dtype)

    back_at = {}

    def backward(distances):
        result = call(
            functools.partial(backward_kernel, distances),
            part_outs(distances),
            *norm_at[distances],
            *saved_at[distances],
            project_at[distances],
            scaled_rows,
            back_rows,
            wide_t,
            flops=flops * len(distances),
        )
        keep_parts(back_at, distances, result)

    for distances in reversed(list(tokens_at)):
        backward(distances)
    (top_left, top_right), (bottom_left, bottom_right) = ring.scatter(back_at)
    token_grad = pl.pallas_call(
        sum_kernel,
        out_shape=jax.ShapeDtypeStruct(block, BF16),
        in_specs=[pl.BlockSpec(memory_space=pltpu.VMEM)] * 6,
        out_specs=pl.BlockSpec(memory_space=pltpu.VMEM),
        compiler_params=pltpu.CompilerParams(vmem_limit_bytes=VMEM_LIMIT),
    )(back_at[0][0], top_left, top_right, back_at[0][1], bottom_left, bottom_right)
    return (token_grad, head_grad)


def solution(mesh):
    in_specs = (
        P(("rep", "expert", "group"), None),
        P("expert", "group", None),
        P("expert", "group", None),
        P("expert", "group", None),
        P(("rep", "expert", "group"), None),
        P(("rep", "expert", "group"), None),
        P(),
        P(None, "expert"),
        P("rep", "group", "expert"),
    )
    out_specs = (P(("rep", "expert", "group"), None), P("rep", "expert"))
    return jax.shard_map(body, mesh=mesh, in_specs=in_specs, out_specs=out_specs, check_vma=False)
```

```python
import functools

import jax
import jax.numpy as jnp
from jax import lax
from jax.experimental import pallas as pl
from jax.experimental.pallas import tpu as pltpu
from jax.sharding import PartitionSpec as P

LOSS_SCALE = 8.0
NORM_EPS = 1e-06
F32 = jnp.float32
BF16 = jnp.bfloat16
LANES = 128
VMEM_LIMIT = 32 * 1024 * 1024


def dot(left, right):
    return jnp.dot(left, right, preferred_element_type=F32)


def dot_t(left, right):
    return lax.dot_general(left, right, (((1,), (1,)), ((), ())), preferred_element_type=F32)


def call(kernel, outs, *args, flops=0):
    args = [pltpu.with_memory_space_constraint(a, pltpu.VMEM) for a in args]
    size = sum(a.size * a.dtype.itemsize for a in args)
    return pl.pallas_call(
        kernel,
        out_shape=[pltpu.VMEM(shape, dtype) for shape, dtype in outs],
        in_specs=[pl.BlockSpec(memory_space=pltpu.VMEM)] * len(args),
        out_specs=[pl.BlockSpec(memory_space=pltpu.VMEM)] * len(outs),
        compiler_params=pltpu.CompilerParams(vmem_limit_bytes=VMEM_LIMIT),
        cost_estimate=pl.CostEstimate(flops=flops, bytes_accessed=size, transcendentals=0),
    )(*args)


def after(value, guards):
    def kernel(*refs):
        pass

    args = [pltpu.with_memory_space_constraint(a, pltpu.VMEM) for a in (value, *guards)]
    return pl.pallas_call(
        kernel,
        out_shape=pltpu.VMEM(value.shape, value.dtype),
        in_specs=[pl.BlockSpec(memory_space=pltpu.VMEM)] * len(args),
        out_specs=pl.BlockSpec(memory_space=pltpu.VMEM),
        input_output_aliases={0: 0},
        compiler_params=pltpu.CompilerParams(vmem_limit_bytes=VMEM_LIMIT),
    )(*args)


class Ring:
    def __init__(self, expert_count, group_count):
        self.count = expert_count
        self.half = expert_count // 2
        self.snake = group_count == 2
        if self.snake:
            self.order = list(range(0, expert_count, 2)) + list(range(expert_count - 1, 0, -2))
        else:
            self.order = list(range(expert_count))

    def send(self, value, distance):
        pairs = [
            (self.order[i], self.order[(i + distance) % self.count]) for i in range(self.count)
        ]
        return lax.ppermute(value, "expert", pairs)

    def device_at(self, distance):
        here = lax.axis_index("expert")
        count = self.count
        if self.snake:
            here = jnp.where(here % 2 == 0, here // 2, count - 1 - here // 2)
        there = lax.rem(here + distance % count, count)
        if self.snake:
            there = jnp.where(there < self.half, 2 * there, 2 * (count - 1 - there) + 1)
        return there

    def gather(self, top, bottom, use, guard=None):
        top_left = top_right = top
        bottom_left = bottom_right = bottom
        use((0,), (top, bottom))
        for step in range(1, self.half):
            if guard is not None and step == self.half - 1:
                top_right = after(top_right, [guard])
            top_left = self.send(top_left, 1)
            top_right = self.send(top_right, -1)
            bottom_left = self.send(bottom_left, 1)
            bottom_right = self.send(bottom_right, -1)
            use((-step, step), (top_left, bottom_left, top_right, bottom_right))
        use((self.half,), (self.send(top_left, 1), self.send(bottom_right, -1)))

    def scatter(self, parts):
        most = self.half - 1
        top_left = self.send(parts[self.half][0], 1)
        bottom_right = self.send(parts[self.half][1], -1)
        bottom_left = self.send(parts[most][1], 1)
        top_right = self.send(parts[-most][0], -1)
        for step in range(most, 0, -1):
            last = add(parts[step][0], top_left)
            top_left = self.send(last, 1)
            bottom_right = self.send(add(parts[-step][1], bottom_right), -1)
            if step > 1:
                bottom_left = self.send(add(parts[step - 1][1], bottom_left), 1)
                top_right = self.send(add(parts[1 - step][0], top_right), -1)
        return (top_left, top_right), (bottom_left, bottom_right), last

    def part_types(self, distances):
        types = []
        for k in distances:
            first = BF16 if k == self.half or k == 1 - self.half else F32
            second = BF16 if k == self.half or k == self.half - 1 else F32
            types += [first, second]
        return types


def add_kernel(block_ref, arrived_ref, out_ref):
    out_ref[...] = (block_ref[...] + arrived_ref[...].astype(F32)).astype(BF16)


def add(block, arrived):
    return call(add_kernel, [(block.shape, BF16)], block, arrived)[0]


def sum_kernel(*refs):
    out_ref = refs[-1]
    rows = refs[0].shape[0]
    for i in range(len(refs) // 3):
        own, left, right = refs[3 * i : 3 * i + 3]
        arrived = left[...].astype(F32) + right[...].astype(F32)
        out_ref[pl.ds(i * rows, rows), :] = (own[...] + arrived).astype(BF16)


class Copies:
    def __init__(self, sems):
        self.sems, self.started = sems, []

    def start(self, source, target):
        copy = pltpu.make_async_copy(source, target, self.sems.at[len(self.started)])
        copy.start()
        self.started.append(copy)

    def wait(self):
        for copy in self.started:
            copy.wait()


def strips(gate_shape, down_shape):
    local_experts, depth, hidden_dim = gate_shape
    _, height, feature_dim = down_shape
    row, places = 0, []
    for _ in range(local_experts):
        pair = [(row, depth), (row + depth, depth)]
        row += 2 * depth
        downs = []
        for begin in range(0, feature_dim, hidden_dim):
            downs.append((row, height, begin, min(hidden_dim, feature_dim - begin)))
            row += height
        places.append((pair, downs))
    return row, places


def pack(ids, scores, tokens, shards):
    rows, cols = tokens.shape
    mid = rows // 2
    quarter = LANES // 4
    inputs = [ids, scores, tokens, *shards]
    packed_shape, places, count = None, [], 0
    if shards:
        hidden_dim = shards[0].shape[2]
        packed_rows, places = strips(shards[0].shape, shards[2].shape)
        packed_shape = (packed_rows, hidden_dim)
        count = sum(len(pair) + len(downs) for pair, downs in places)

    def kernel(*refs):
        ids_hbm, scores_hbm, tokens_hbm, *shards_hbm = refs[: len(inputs)]
        top_ref, bottom_ref, *packed_refs = refs[len(inputs) : -3]
        ids_ref, scores_ref, sems = refs[-3:]
        copies = Copies(sems)
        copies.start(ids_hbm, ids_ref)
        copies.start(scores_hbm, scores_ref)
        copies.start(tokens_hbm.at[pl.ds(0, mid), :], top_ref.at[:, pl.ds(0, cols)])
        copies.start(tokens_hbm.at[pl.ds(mid, mid), :], bottom_ref)
        for local, (pair, downs) in enumerate(places):
            out_ref = packed_refs[0]
            for source, (row, some) in zip(shards_hbm, pair):
                copies.start(source.at[local], out_ref.at[pl.ds(row, some), :])
            for row, some, begin, width in downs:
                source = shards_hbm[2].at[local, :, pl.ds(begin, width)]
                copies.start(source, out_ref.at[pl.ds(row, some), pl.ds(0, width)])
                if width < hidden_dim:
                    rest = hidden_dim - width
                    out_ref[pl.ds(row, some), pl.ds(width, rest)] = jnp.zeros((some, rest), BF16)
        copies.started[0].wait()
        copies.started[1].wait()
        scores = scores_ref[...]
        ids = ids_ref[...]
        route_weight = scores / jnp.sum(scores, axis=0, keepdims=True)
        expert = lax.broadcasted_iota(jnp.int32, (quarter, rows), 0)
        weight_by = jnp.zeros((quarter, rows), F32)
        for choice_k in range(scores.shape[0]):
            one = slice(choice_k, choice_k + 1)
            weight_by = weight_by + jnp.where(ids[one] == expert, route_weight[one], 0.0)
        high = weight_by.astype(BF16).astype(F32)
        weights = jnp.concatenate([high, weight_by - high] * 2, axis=0).T
        lane = lax.broadcasted_iota(jnp.int32, (mid, LANES), 1)
        both = jnp.where(lane < 2 * quarter, weights[:mid], weights[mid:])
        top_ref[:, cols:] = both.astype(BF16)
        for copy in copies.started[2:]:
            copy.wait()

    outs = [pltpu.VMEM((mid, cols + LANES), BF16), pltpu.VMEM((mid, cols), BF16)]
    if shards:
        outs.append(pltpu.VMEM(packed_shape, BF16))
    return pl.pallas_call(
        kernel,
        out_shape=outs,
        in_specs=[pl.BlockSpec(memory_space=pl.ANY)] * len(inputs),
        out_specs=[pl.BlockSpec(memory_space=pltpu.VMEM)] * len(outs),
        scratch_shapes=[
            pltpu.VMEM(ids.shape, ids.dtype),
            pltpu.VMEM(scores.shape, F32),
            pltpu.SemaphoreType.DMA((4 + count,)),
        ],
        compiler_params=pltpu.CompilerParams(vmem_limit_bytes=VMEM_LIMIT),
    )(*[pltpu.with_memory_space_constraint(a, pltpu.HBM) for a in inputs])


def full_weights(shards, packed):
    local_experts, _, hidden_dim = shards[0].shape
    feature_dim = shards[2].shape[2]
    paired = packed is not None
    _, places = strips(shards[0].shape, shards[2].shape)
    depth, height = shards[0].shape[1], shards[2].shape[1]

    def kernel(*refs):
        gate_hbm, up_hbm, down_hbm, *rest = refs
        wide_ref, down_ref, sems = rest[-3:]
        copies = Copies(sems)
        mine = lax.axis_index("group") if paired else 0

        def wide_at(place, local, is_up):
            rows = pl.ds(pl.multiple_of(place * depth, 16), depth)
            return wide_ref.at[rows, pl.ds((2 * local + is_up) * hidden_dim, hidden_dim)]

        def down_at(place, local, begin, cols):
            top = pl.multiple_of(local * hidden_dim + place * height, 16)
            return down_ref.at[pl.ds(top, height), pl.ds(begin, cols)]

        for local in range(local_experts):
            for is_up, source in enumerate((gate_hbm, up_hbm)):
                copies.start(source.at[local], wide_at(mine, local, is_up))
            copies.start(down_hbm.at[local], down_at(mine, local, 0, feature_dim))
        if paired:
            for local, (pair, downs) in enumerate(places):
                for is_up, (row, some) in enumerate(pair):
                    copies.start(rest[0].at[pl.ds(row, some), :], wide_at(1 - mine, local, is_up))
                for row, some, begin, cols in downs:
                    source = rest[0].at[pl.ds(row, some), pl.ds(0, cols)]
                    copies.start(source, down_at(1 - mine, local, begin, cols))
        copies.wait()

    shards = [pltpu.with_memory_space_constraint(w, pltpu.HBM) for w in shards]
    count = 3 * local_experts
    specs = [pl.BlockSpec(memory_space=pl.ANY)] * 3
    if paired:
        count += sum(len(pair) + len(downs) for pair, downs in places)
        specs.append(pl.BlockSpec(memory_space=pltpu.VMEM))
        shards.append(pltpu.with_memory_space_constraint(packed, pltpu.VMEM))
    return pl.pallas_call(
        kernel,
        out_shape=[
            pltpu.VMEM((feature_dim, 2 * local_experts * hidden_dim), BF16),
            pltpu.VMEM((local_experts * hidden_dim, feature_dim), BF16),
        ],
        in_specs=specs,
        out_specs=[pl.BlockSpec(memory_space=pltpu.VMEM)] * 2,
        scratch_shapes=[pltpu.SemaphoreType.DMA((count,))],
        compiler_params=pltpu.CompilerParams(vmem_limit_bytes=VMEM_LIMIT),
    )(*shards)


def transpose_kernel(from_ref, to_ref):
    strip = 2 * LANES

    @pl.loop(0, to_ref.shape[0] // strip)
    def _(i):
        some = pl.ds(pl.multiple_of(i * strip, strip), strip)
        to_ref[some, :] = from_ref[:, some].T


def transposed(weights):
    rows, cols = weights.shape
    return call(transpose_kernel, [((cols, rows), BF16)], weights)[0]


def body(tokens, w_gate, w_up, w_down, route_ids, route_scores, norm_gain, class_head, targets):
    rows_here, feature_dim = tokens.shape
    expert_count = lax.axis_size("expert")
    group_count = lax.axis_size("group")
    local_experts, _, hidden_dim = w_gate.shape
    pair_dim = 2 * hidden_dim
    ring = Ring(expert_count, group_count)
    block = (rows_here, feature_dim)
    mid = rows_here // 2

    shards = [w_gate, w_up, w_down]
    if group_count == 2:
        top, bottom, packed = pack(route_ids.T, route_scores.T, tokens, shards)
        packed = lax.ppermute(packed, "group", [(0, 1), (1, 0)])
    else:
        top, bottom = pack(route_ids.T, route_scores.T, tokens, [])
        shards = [lax.all_gather(w, "group", axis=1, tiled=True) for w in shards]
        packed = None
    wide, down = full_weights(shards, packed)

    def rows_of(refs):
        return jnp.concatenate([ref[...] for ref in refs], axis=0) if len(refs) > 1 else refs[0][...]

    def forward_kernel(count, *refs):
        token_refs, (wide_ref, down_ref) = refs[:count], refs[count : count + 2]
        outs = refs[count + 2 :]
        x = rows_of([ref.at[:, :feature_dim] for ref in token_refs])
        weights = jnp.concatenate([ref[:, feature_dim:] for ref in token_refs[::2]], axis=0).astype(F32)
        lane = lax.broadcasted_iota(jnp.int32, weights.shape, 1)
        quarter = LANES // 4
        hidden = []
        for local in range(local_experts):
            expert = lax.axis_index("expert") * local_experts + local
            scales = []
            for begin in (expert, expert + 2 * quarter):
                here = (lane == begin) | (lane == begin + quarter)
                scales.append(jnp.sum(jnp.where(here, weights, 0.0), axis=1, keepdims=True))
            pieces = [s[i : i + mid] for i in range(0, weights.shape[0], mid) for s in scales]
            scale = jnp.concatenate(pieces, axis=0)
            act = dot(x, wide_ref[:, pl.ds(local * pair_dim, pair_dim)])
            gate_act, up_act = act[:, :hidden_dim], act[:, hidden_dim:]
            sigmoid_gate = jax.nn.sigmoid(gate_act)
            silu = gate_act * sigmoid_gate * scale
            slope = sigmoid_gate * (1.0 + gate_act * (1.0 - sigmoid_gate)) * scale
            cols = pl.ds(local * hidden_dim, hidden_dim)
            outs[0][:, cols] = (up_act * slope).astype(BF16)
            outs[1][:, cols] = silu.astype(BF16)
            hidden.append((silu * up_act).astype(BF16))
        total = dot(jnp.concatenate(hidden, axis=1), down_ref[...])
        for i, out in enumerate(outs[2:]):
            out[...] = total[i * mid : (i + 1) * mid].astype(out.dtype)

    tokens_at, saved_at, part_at = {}, {}, {}
    flops = 2 * rows_here * feature_dim * hidden_dim * local_experts * 3

    def hold(distances, blocks):
        tokens_at[distances] = blocks

    def keep_parts(parts, distances, halves):
        parts.update({k: halves[2 * i : 2 * i + 2] for i, k in enumerate(distances)})

    def part_outs(distances):
        return [((mid, feature_dim), dtype) for dtype in ring.part_types(distances)]

    def forward(distances):
        blocks = tokens_at[distances]
        rows = mid * len(blocks)
        result = call(
            functools.partial(forward_kernel, len(blocks)),
            [((rows, local_experts * hidden_dim), BF16)] * 2 + part_outs(distances),
            *blocks,
            wide,
            down,
            flops=flops * rows // rows_here,
        )
        saved_at[distances] = result[:2]
        keep_parts(part_at, distances, result[2:])

    ring.gather(top, bottom, hold, wide)
    for distances in tokens_at:
        forward(distances)
    gain = norm_gain.reshape(1, feature_dim)
    half_shape = (mid, feature_dim)
    moe_top, moe_bottom = [
        call(sum_kernel, [(half_shape, BF16)], own, *arrived)[0]
        for own, arrived in zip(part_at[0], ring.scatter(part_at))
    ]

    norm_at, mean_at = {}, {}

    def residual_of(token_refs, moe_refs):
        token_rows = rows_of([ref.at[:, :feature_dim] for ref in token_refs]).astype(F32)
        return token_rows + rows_of(moe_refs).astype(F32)

    def inv_rms_of(residual):
        return lax.rsqrt(jnp.mean(residual * residual, axis=-1, keepdims=True) + NORM_EPS)

    def norm_kernel(distances, count, *refs):
        residual = residual_of(refs[:count], refs[count : 2 * count])
        gain_ref, so_far, out_ref, residual_ref, inv_ref = refs[2 * count :]
        inv_rms = inv_rms_of(residual)
        residual_ref[...] = residual
        inv_ref[...] = jnp.broadcast_to(inv_rms, inv_ref.shape)
        normed = residual * inv_rms * gain_ref[...]
        pooled = so_far[...]
        row = lax.broadcasted_iota(jnp.int32, pooled.shape, 0)
        for i, k in enumerate(distances):
            part = normed[i * rows_here : (i + 1) * rows_here]
            mean = jnp.mean(part, axis=0, keepdims=True)
            pooled = jnp.where(row == ring.device_at(k), mean, pooled)
        out_ref[...] = pooled

    pooled_shape = (expert_count, feature_dim)
    mean_at["pooled"] = jnp.zeros(pooled_shape, F32)

    def norm(distances, blocks):
        rows = mid * len(blocks)
        mean_at["pooled"], *norm_at[distances] = call(
            functools.partial(norm_kernel, distances, len(blocks)),
            [(pooled_shape, F32), ((rows, feature_dim), F32), ((rows, LANES), F32)],
            *tokens_at[distances],
            *blocks,
            gain,
            mean_at["pooled"],
        )

    ring.gather(moe_top, moe_bottom, norm)
    pooled = mean_at["pooled"].astype(BF16)
    logits = dot(pooled, class_head)
    target_rows = targets.reshape(expert_count, -1).astype(F32)
    logit_grad = (LOSS_SCALE * (jax.nn.sigmoid(logits) - target_rows)).astype(BF16)
    pooled_grad = dot_t(logit_grad, class_head)
    span = 2
    for masks in ([1], list(range(span, expert_count, span))):
        mine = pooled_grad.astype(BF16)
        pooled_grad = mine.astype(F32)
        for mask in masks:
            pairs = [(e, e ^ mask) for e in range(expert_count)]
            pooled_grad = pooled_grad + lax.ppermute(mine, "expert", pairs).astype(F32)

    def backward_kernel(distances, residual_ref, inv_ref, gate_save, up_save, *refs):
        grad_ref, gain_ref, wide_ref, down_ref, *outs = refs
        residual, inv_rms = residual_ref[...], inv_ref[:, :1]
        cube = inv_rms * inv_rms * inv_rms
        parts = []
        for i, k in enumerate(distances):
            rows = slice(i * rows_here, (i + 1) * rows_here)
            scaled = gain_ref[...] * grad_ref[pl.ds(ring.device_at(k), 1), :] / rows_here
            slope = cube[rows] * jnp.mean(residual[rows] * scaled, axis=-1, keepdims=True)
            parts.append(inv_rms[rows] * scaled - residual[rows] * slope)
        resid_grad = jnp.concatenate(parts, axis=0) if len(parts) > 1 else parts[0]
        down_back = dot(resid_grad.astype(BF16), down_ref[...])
        grads = []
        for local in range(local_experts):
            cols = slice(local * hidden_dim, (local + 1) * hidden_dim)
            for save in (gate_save, up_save):
                grads.append((down_back[:, cols] * save[:, cols].astype(F32)).astype(BF16))
        total = dot(jnp.concatenate(grads, axis=1), wide_ref[...])
        if distances == (0,):
            total = total + resid_grad
        rows = total.shape[0] // len(outs)
        for i, out in enumerate(outs):
            out[...] = total[i * rows : (i + 1) * rows].astype(out.dtype)

    wide_t, down_t = transposed(wide), transposed(down)
    back_at = {}

    def backward(distances):
        result = call(
            functools.partial(backward_kernel, distances),
            part_outs(distances),
            *norm_at[distances],
            *saved_at[distances],
            pooled_grad,
            gain,
            wide_t,
            down_t,
            flops=flops * len(distances),
        )
        keep_parts(back_at, distances, result)

    for distances in reversed(list(tokens_at)):
        backward(distances)
    (top_left, top_right), (bottom_left, bottom_right), last = ring.scatter(back_at)
    token_grad = pl.pallas_call(
        sum_kernel,
        out_shape=jax.ShapeDtypeStruct(block, BF16),
        in_specs=[pl.BlockSpec(memory_space=pltpu.VMEM)] * 6,
        out_specs=pl.BlockSpec(memory_space=pltpu.VMEM),
        compiler_params=pltpu.CompilerParams(vmem_limit_bytes=VMEM_LIMIT),
    )(back_at[0][0], top_left, top_right, back_at[0][1], bottom_left, bottom_right)

    both = after(jnp.concatenate([pooled, logit_grad], axis=1), [last])
    if group_count == 2:
        both = jnp.concatenate([both, lax.ppermute(both, "group", [(0, 1), (1, 0)])], axis=0)
    else:
        both = lax.all_gather(both, "group", axis=0, tiled=True)
    head_grad = lax.dot_general(
        both[:, :feature_dim],
        both[:, feature_dim:],
        (((0,), (0,)), ((), ())),
        preferred_element_type=F32,
    )
    return (token_grad, head_grad)


def solution(mesh):
    in_specs = (
        P(("rep", "expert", "group"), None),
        P("expert", "group", None),
        P("expert", "group", None),
        P("expert", "group", None),
        P(("rep", "expert", "group"), None),
        P(("rep", "expert", "group"), None),
        P(),
        P(None, "expert"),
        P("rep", "group", "expert"),
    )
    out_specs = (P(("rep", "expert", "group"), None), P("rep", "expert"))
    return jax.shard_map(body, mesh=mesh, in_specs=in_specs, out_specs=out_specs, check_vma=False)
```

```python
import functools

import jax
import jax.numpy as jnp
from jax import lax
from jax.experimental import pallas as pl
from jax.experimental.pallas import tpu as pltpu
from jax.sharding import PartitionSpec as P

LOSS_SCALE = 8.0
NORM_EPS = 1e-06
F32 = jnp.float32
BF16 = jnp.bfloat16
LANES = 128
VMEM_LIMIT = 32 * 1024 * 1024


def dot(left, right):
    return jnp.dot(left, right, preferred_element_type=F32)


def dot_t(left, right):
    return lax.dot_general(left, right, (((1,), (1,)), ((), ())), preferred_element_type=F32)


def call(kernel, outs, *args, flops=0):
    args = [pltpu.with_memory_space_constraint(a, pltpu.VMEM) for a in args]
    size = sum(a.size * a.dtype.itemsize for a in args)
    return pl.pallas_call(
        kernel,
        out_shape=[pltpu.VMEM(shape, dtype) for shape, dtype in outs],
        in_specs=[pl.BlockSpec(memory_space=pltpu.VMEM)] * len(args),
        out_specs=[pl.BlockSpec(memory_space=pltpu.VMEM)] * len(outs),
        compiler_params=pltpu.CompilerParams(vmem_limit_bytes=VMEM_LIMIT),
        cost_estimate=pl.CostEstimate(flops=flops, bytes_accessed=size, transcendentals=0),
    )(*args)


def after(value, guards):
    def kernel(*refs):
        pass

    args = [pltpu.with_memory_space_constraint(a, pltpu.VMEM) for a in (value, *guards)]
    return pl.pallas_call(
        kernel,
        out_shape=pltpu.VMEM(value.shape, value.dtype),
        in_specs=[pl.BlockSpec(memory_space=pltpu.VMEM)] * len(args),
        out_specs=pl.BlockSpec(memory_space=pltpu.VMEM),
        input_output_aliases={0: 0},
        compiler_params=pltpu.CompilerParams(vmem_limit_bytes=VMEM_LIMIT),
    )(*args)


class Ring:
    def __init__(self, expert_count, group_count):
        self.count = expert_count
        self.half = expert_count // 2
        self.groups = group_count
        self.snake = group_count == 2
        if self.snake:
            self.order = list(range(0, expert_count, 2)) + list(range(expert_count - 1, 0, -2))
        else:
            self.order = list(range(expert_count))

    def send(self, value, distance):
        pairs = []
        for i in range(self.count):
            for g in range(self.groups):
                there = self.order[(i + (-distance if g % 2 else distance)) % self.count]
                pairs.append((self.order[i] * self.groups + g, there * self.groups + g))
        return lax.ppermute(value, ("expert", "group"), pairs)

    def device_at(self, distance):
        here = lax.axis_index("expert")
        count = self.count
        if self.snake:
            here = jnp.where(here % 2 == 0, here // 2, count - 1 - here // 2)
        ahead = distance % count
        step = jnp.where(lax.rem(lax.axis_index("group"), 2) == 0, ahead, count - ahead)
        there = lax.rem(here + step, count)
        if self.snake:
            there = jnp.where(there < self.half, 2 * there, 2 * (count - 1 - there) + 1)
        return there

    def gather(self, top, bottom, use, guard=None):
        top_left = top_right = top
        bottom_left = bottom_right = bottom
        use((0,), (top, bottom))
        for step in range(1, self.half):
            if guard is not None and step == self.half - 1:
                top_right = after(top_right, [guard])
            top_left = self.send(top_left, 1)
            top_right = self.send(top_right, -1)
            bottom_left = self.send(bottom_left, 1)
            bottom_right = self.send(bottom_right, -1)
            use((-step, step), (top_left, bottom_left, top_right, bottom_right))
        use((self.half,), (self.send(top_left, 1), self.send(bottom_right, -1)))

    def scatter(self, parts):
        most = self.half - 1
        top_left = self.send(parts[self.half][0], 1)
        bottom_right = self.send(parts[self.half][1], -1)
        bottom_left = self.send(parts[most][1], 1)
        top_right = self.send(parts[-most][0], -1)
        for step in range(most, 0, -1):
            top_left = self.send(add(parts[step][0], top_left), 1)
            bottom_right = self.send(add(parts[-step][1], bottom_right), -1)
            if step > 1:
                bottom_left = self.send(add(parts[step - 1][1], bottom_left), 1)
                top_right = self.send(add(parts[1 - step][0], top_right), -1)
        return (top_left, top_right), (bottom_left, bottom_right)

    def part_types(self, distances):
        types = []
        for k in distances:
            first = BF16 if k == self.half or k == 1 - self.half else F32
            second = BF16 if k == self.half or k == self.half - 1 else F32
            types += [first, second]
        return types


def add_kernel(block_ref, arrived_ref, out_ref):
    out_ref[...] = (block_ref[...] + arrived_ref[...].astype(F32)).astype(BF16)


def add(block, arrived):
    return call(add_kernel, [(block.shape, BF16)], block, arrived)[0]


def sum_kernel(*refs):
    out_ref = refs[-1]
    rows = refs[0].shape[0]
    for i in range(len(refs) // 3):
        own, left, right = refs[3 * i : 3 * i + 3]
        arrived = left[...].astype(F32) + right[...].astype(F32)
        out_ref[pl.ds(i * rows, rows), :] = (own[...] + arrived).astype(BF16)


class Copies:
    def __init__(self, sems):
        self.sems, self.started = sems, []

    def start(self, source, target):
        copy = pltpu.make_async_copy(source, target, self.sems.at[len(self.started)])
        copy.start()
        self.started.append(copy)

    def wait(self):
        for copy in self.started:
            copy.wait()


def strips(gate_shape, down_shape):
    local_experts, depth, hidden_dim = gate_shape
    _, height, feature_dim = down_shape
    row, places = 0, []
    for _ in range(local_experts):
        pair = [(row, depth), (row + depth, depth)]
        row += 2 * depth
        downs = []
        for begin in range(0, feature_dim, hidden_dim):
            downs.append((row, height, begin, min(hidden_dim, feature_dim - begin)))
            row += height
        places.append((pair, downs))
    return row, places


def pack(ids, scores, tokens, shards):
    rows, cols = tokens.shape
    mid = rows // 2
    quarter = LANES // 4
    inputs = [ids, scores, tokens, *shards]
    packed_shape, places, count = None, [], 0
    if shards:
        hidden_dim = shards[0].shape[2]
        packed_rows, places = strips(shards[0].shape, shards[2].shape)
        packed_shape = (packed_rows, hidden_dim)
        count = sum(len(pair) + len(downs) for pair, downs in places)

    def kernel(*refs):
        ids_hbm, scores_hbm, tokens_hbm, *shards_hbm = refs[: len(inputs)]
        top_ref, bottom_ref, *packed_refs = refs[len(inputs) : -3]
        ids_ref, scores_ref, sems = refs[-3:]
        copies = Copies(sems)
        copies.start(ids_hbm, ids_ref)
        copies.start(scores_hbm, scores_ref)
        copies.start(tokens_hbm.at[pl.ds(0, mid), :], top_ref.at[:, pl.ds(0, cols)])
        copies.start(tokens_hbm.at[pl.ds(mid, mid), :], bottom_ref)
        for local, (pair, downs) in enumerate(places):
            out_ref = packed_refs[0]
            for source, (row, some) in zip(shards_hbm, pair):
                copies.start(source.at[local], out_ref.at[pl.ds(row, some), :])
            for row, some, begin, width in downs:
                source = shards_hbm[2].at[local, :, pl.ds(begin, width)]
                copies.start(source, out_ref.at[pl.ds(row, some), pl.ds(0, width)])
                if width < hidden_dim:
                    rest = hidden_dim - width
                    out_ref[pl.ds(row, some), pl.ds(width, rest)] = jnp.zeros((some, rest), BF16)
        copies.started[0].wait()
        copies.started[1].wait()
        scores = scores_ref[...]
        ids = ids_ref[...]
        route_weight = scores / jnp.sum(scores, axis=0, keepdims=True)
        expert = lax.broadcasted_iota(jnp.int32, (quarter, rows), 0)
        weight_by = jnp.zeros((quarter, rows), F32)
        for choice_k in range(scores.shape[0]):
            one = slice(choice_k, choice_k + 1)
            weight_by = weight_by + jnp.where(ids[one] == expert, route_weight[one], 0.0)
        high = weight_by.astype(BF16).astype(F32)
        weights = jnp.concatenate([high, weight_by - high] * 2, axis=0).T
        lane = lax.broadcasted_iota(jnp.int32, (mid, LANES), 1)
        both = jnp.where(lane < 2 * quarter, weights[:mid], weights[mid:])
        top_ref[:, cols:] = both.astype(BF16)
        for copy in copies.started[2:]:
            copy.wait()

    outs = [pltpu.VMEM((mid, cols + LANES), BF16), pltpu.VMEM((mid, cols), BF16)]
    if shards:
        outs.append(pltpu.VMEM(packed_shape, BF16))
    return pl.pallas_call(
        kernel,
        out_shape=outs,
        in_specs=[pl.BlockSpec(memory_space=pl.ANY)] * len(inputs),
        out_specs=[pl.BlockSpec(memory_space=pltpu.VMEM)] * len(outs),
        scratch_shapes=[
            pltpu.VMEM(ids.shape, ids.dtype),
            pltpu.VMEM(scores.shape, F32),
            pltpu.SemaphoreType.DMA((4 + count,)),
        ],
        compiler_params=pltpu.CompilerParams(vmem_limit_bytes=VMEM_LIMIT),
    )(*[pltpu.with_memory_space_constraint(a, pltpu.HBM) for a in inputs])


def full_weights(shards, packed):
    local_experts, _, hidden_dim = shards[0].shape
    feature_dim = shards[2].shape[2]
    paired = packed is not None
    _, places = strips(shards[0].shape, shards[2].shape)
    depth, height = shards[0].shape[1], shards[2].shape[1]

    def kernel(*refs):
        gate_hbm, up_hbm, down_hbm, *rest = refs
        wide_ref, down_ref, sems = rest[-3:]
        copies = Copies(sems)
        mine = lax.axis_index("group") if paired else 0

        def wide_at(place, local, is_up):
            rows = pl.ds(pl.multiple_of(place * depth, 16), depth)
            return wide_ref.at[rows, pl.ds((2 * local + is_up) * hidden_dim, hidden_dim)]

        def down_at(place, local, begin, cols):
            top = pl.multiple_of(local * hidden_dim + place * height, 16)
            return down_ref.at[pl.ds(top, height), pl.ds(begin, cols)]

        for local in range(local_experts):
            for is_up, source in enumerate((gate_hbm, up_hbm)):
                copies.start(source.at[local], wide_at(mine, local, is_up))
            copies.start(down_hbm.at[local], down_at(mine, local, 0, feature_dim))
        if paired:
            for local, (pair, downs) in enumerate(places):
                for is_up, (row, some) in enumerate(pair):
                    copies.start(rest[0].at[pl.ds(row, some), :], wide_at(1 - mine, local, is_up))
                for row, some, begin, cols in downs:
                    source = rest[0].at[pl.ds(row, some), pl.ds(0, cols)]
                    copies.start(source, down_at(1 - mine, local, begin, cols))
        copies.wait()

    shards = [pltpu.with_memory_space_constraint(w, pltpu.HBM) for w in shards]
    count = 3 * local_experts
    specs = [pl.BlockSpec(memory_space=pl.ANY)] * 3
    if paired:
        count += sum(len(pair) + len(downs) for pair, downs in places)
        specs.append(pl.BlockSpec(memory_space=pltpu.VMEM))
        shards.append(pltpu.with_memory_space_constraint(packed, pltpu.VMEM))
    return pl.pallas_call(
        kernel,
        out_shape=[
            pltpu.VMEM((feature_dim, 2 * local_experts * hidden_dim), BF16),
            pltpu.VMEM((local_experts * hidden_dim, feature_dim), BF16),
        ],
        in_specs=specs,
        out_specs=[pl.BlockSpec(memory_space=pltpu.VMEM)] * 2,
        scratch_shapes=[pltpu.SemaphoreType.DMA((count,))],
        compiler_params=pltpu.CompilerParams(vmem_limit_bytes=VMEM_LIMIT),
    )(*shards)


def transpose_kernel(from_ref, to_ref):
    strip = 2 * LANES

    @pl.loop(0, to_ref.shape[0] // strip)
    def _(i):
        some = pl.ds(pl.multiple_of(i * strip, strip), strip)
        to_ref[some, :] = from_ref[:, some].T


def transposed(weights):
    rows, cols = weights.shape
    return call(transpose_kernel, [((cols, rows), BF16)], weights)[0]


def body(tokens, w_gate, w_up, w_down, route_ids, route_scores, norm_gain, class_head, targets):
    rows_here, feature_dim = tokens.shape
    expert_count = lax.axis_size("expert")
    group_count = lax.axis_size("group")
    local_experts, _, hidden_dim = w_gate.shape
    pair_dim = 2 * hidden_dim
    ring = Ring(expert_count, group_count)
    block = (rows_here, feature_dim)
    mid = rows_here // 2

    shards = [w_gate, w_up, w_down]
    if group_count == 2:
        top, bottom, packed = pack(route_ids.T, route_scores.T, tokens, shards)
        packed = lax.ppermute(packed, "group", [(0, 1), (1, 0)])
    else:
        top, bottom = pack(route_ids.T, route_scores.T, tokens, [])
        shards = [lax.all_gather(w, "group", axis=1, tiled=True) for w in shards]
        packed = None
    wide, down = full_weights(shards, packed)

    def rows_of(refs):
        return jnp.concatenate([ref[...] for ref in refs], axis=0) if len(refs) > 1 else refs[0][...]

    def forward_kernel(count, *refs):
        token_refs, (wide_ref, down_ref) = refs[:count], refs[count : count + 2]
        outs = refs[count + 2 :]
        x = rows_of([ref.at[:, :feature_dim] for ref in token_refs])
        weights = jnp.concatenate([ref[:, feature_dim:] for ref in token_refs[::2]], axis=0).astype(F32)
        lane = lax.broadcasted_iota(jnp.int32, weights.shape, 1)
        quarter = LANES // 4
        hidden = []
        for local in range(local_experts):
            expert = lax.axis_index("expert") * local_experts + local
            scales = []
            for begin in (expert, expert + 2 * quarter):
                here = (lane == begin) | (lane == begin + quarter)
                scales.append(jnp.sum(jnp.where(here, weights, 0.0), axis=1, keepdims=True))
            pieces = [s[i : i + mid] for i in range(0, weights.shape[0], mid) for s in scales]
            scale = jnp.concatenate(pieces, axis=0)
            act = dot(x, wide_ref[:, pl.ds(local * pair_dim, pair_dim)])
            gate_act, up_act = act[:, :hidden_dim], act[:, hidden_dim:]
            sigmoid_gate = jax.nn.sigmoid(gate_act)
            silu = gate_act * sigmoid_gate * scale
            slope = sigmoid_gate * (1.0 + gate_act * (1.0 - sigmoid_gate)) * scale
            cols = pl.ds(local * hidden_dim, hidden_dim)
            outs[0][:, cols] = (up_act * slope).astype(BF16)
            outs[1][:, cols] = silu.astype(BF16)
            hidden.append((silu * up_act).astype(BF16))
        total = dot(jnp.concatenate(hidden, axis=1), down_ref[...])
        for i, out in enumerate(outs[2:]):
            out[...] = total[i * mid : (i + 1) * mid].astype(out.dtype)

    tokens_at, saved_at, part_at = {}, {}, {}
    flops = 2 * rows_here * feature_dim * hidden_dim * local_experts * 3

    def hold(distances, blocks):
        tokens_at[distances] = blocks

    def keep_parts(parts, distances, halves):
        parts.update({k: halves[2 * i : 2 * i + 2] for i, k in enumerate(distances)})

    def part_outs(distances):
        return [((mid, feature_dim), dtype) for dtype in ring.part_types(distances)]

    def forward(distances):
        blocks = tokens_at[distances]
        rows = mid * len(blocks)
        result = call(
            functools.partial(forward_kernel, len(blocks)),
            [((rows, local_experts * hidden_dim), BF16)] * 2 + part_outs(distances),
            *blocks,
            wide,
            down,
            flops=flops * rows // rows_here,
        )
        saved_at[distances] = result[:2]
        keep_parts(part_at, distances, result[2:])

    ring.gather(top, bottom, hold, wide)
    for distances in tokens_at:
        forward(distances)
    gain = norm_gain.reshape(1, feature_dim)
    half_shape = (mid, feature_dim)
    moe_top, moe_bottom = [
        call(sum_kernel, [(half_shape, BF16)], own, *arrived)[0]
        for own, arrived in zip(part_at[0], ring.scatter(part_at))
    ]

    norm_at, mean_at = {}, {}

    def residual_of(token_refs, moe_refs):
        token_rows = rows_of([ref.at[:, :feature_dim] for ref in token_refs]).astype(F32)
        return token_rows + rows_of(moe_refs).astype(F32)

    def inv_rms_of(residual):
        return lax.rsqrt(jnp.mean(residual * residual, axis=-1, keepdims=True) + NORM_EPS)

    def norm_kernel(distances, count, *refs):
        residual = residual_of(refs[:count], refs[count : 2 * count])
        gain_ref, so_far, out_ref, residual_ref, inv_ref = refs[2 * count :]
        inv_rms = inv_rms_of(residual)
        residual_ref[...] = residual
        inv_ref[...] = jnp.broadcast_to(inv_rms, inv_ref.shape)
        normed = residual * inv_rms * gain_ref[...]
        pooled = so_far[...]
        row = lax.broadcasted_iota(jnp.int32, pooled.shape, 0)
        for i, k in enumerate(distances):
            part = normed[i * rows_here : (i + 1) * rows_here]
            mean = jnp.mean(part, axis=0, keepdims=True)
            pooled = jnp.where(row == ring.device_at(k), mean, pooled)
        out_ref[...] = pooled

    pooled_shape = (expert_count, feature_dim)
    mean_at["pooled"] = jnp.zeros(pooled_shape, F32)

    def norm(distances, blocks):
        rows = mid * len(blocks)
        mean_at["pooled"], *norm_at[distances] = call(
            functools.partial(norm_kernel, distances, len(blocks)),
            [(pooled_shape, F32), ((rows, feature_dim), F32), ((rows, LANES), F32)],
            *tokens_at[distances],
            *blocks,
            gain,
            mean_at["pooled"],
        )

    ring.gather(moe_top, moe_bottom, norm)
    pooled = mean_at["pooled"].astype(BF16)
    logits = dot(pooled, class_head)
    target_rows = targets.reshape(expert_count, -1).astype(F32)
    logit_grad = (LOSS_SCALE * (jax.nn.sigmoid(logits) - target_rows)).astype(BF16)
    pooled_grad = dot_t(logit_grad, class_head)
    span = 2
    for masks in ([1], list(range(span, expert_count, span))):
        mine = pooled_grad.astype(BF16)
        pooled_grad = mine.astype(F32)
        for mask in masks:
            pairs = [(e, e ^ mask) for e in range(expert_count)]
            pooled_grad = pooled_grad + lax.ppermute(mine, "expert", pairs).astype(F32)

    both = jnp.concatenate([pooled, logit_grad], axis=1)
    if group_count == 2:
        both = jnp.concatenate([both, lax.ppermute(both, "group", [(0, 1), (1, 0)])], axis=0)
    else:
        both = lax.all_gather(both, "group", axis=0, tiled=True)
    head_grad = lax.dot_general(
        both[:, :feature_dim],
        both[:, feature_dim:],
        (((0,), (0,)), ((), ())),
        preferred_element_type=F32,
    )

    def backward_kernel(distances, residual_ref, inv_ref, gate_save, up_save, *refs):
        grad_ref, gain_ref, wide_ref, down_ref, *outs = refs
        residual, inv_rms = residual_ref[...], inv_ref[:, :1]
        cube = inv_rms * inv_rms * inv_rms
        parts = []
        for i, k in enumerate(distances):
            rows = slice(i * rows_here, (i + 1) * rows_here)
            scaled = gain_ref[...] * grad_ref[pl.ds(ring.device_at(k), 1), :] / rows_here
            slope = cube[rows] * jnp.mean(residual[rows] * scaled, axis=-1, keepdims=True)
            parts.append(inv_rms[rows] * scaled - residual[rows] * slope)
        resid_grad = jnp.concatenate(parts, axis=0) if len(parts) > 1 else parts[0]
        down_back = dot(resid_grad.astype(BF16), down_ref[...])
        grads = []
        for local in range(local_experts):
            cols = slice(local * hidden_dim, (local + 1) * hidden_dim)
            for save in (gate_save, up_save):
                grads.append((down_back[:, cols] * save[:, cols].astype(F32)).astype(BF16))
        total = dot(jnp.concatenate(grads, axis=1), wide_ref[...])
        if distances == (0,):
            total = total + resid_grad
        rows = total.shape[0] // len(outs)
        for i, out in enumerate(outs):
            out[...] = total[i * rows : (i + 1) * rows].astype(out.dtype)

    wide_t, down_t = transposed(wide), transposed(down)
    back_at = {}

    def backward(distances):
        result = call(
            functools.partial(backward_kernel, distances),
            part_outs(distances),
            *norm_at[distances],
            *saved_at[distances],
            pooled_grad,
            gain,
            wide_t,
            down_t,
            flops=flops * len(distances),
        )
        keep_parts(back_at, distances, result)

    for distances in reversed(list(tokens_at)):
        backward(distances)
    (top_left, top_right), (bottom_left, bottom_right) = ring.scatter(back_at)
    token_grad = pl.pallas_call(
        sum_kernel,
        out_shape=jax.ShapeDtypeStruct(block, BF16),
        in_specs=[pl.BlockSpec(memory_space=pltpu.VMEM)] * 6,
        out_specs=pl.BlockSpec(memory_space=pltpu.VMEM),
        compiler_params=pltpu.CompilerParams(vmem_limit_bytes=VMEM_LIMIT),
    )(back_at[0][0], top_left, top_right, back_at[0][1], bottom_left, bottom_right)
    return (token_grad, head_grad)


def solution(mesh):
    in_specs = (
        P(("rep", "expert", "group"), None),
        P("expert", "group", None),
        P("expert", "group", None),
        P("expert", "group", None),
        P(("rep", "expert", "group"), None),
        P(("rep", "expert", "group"), None),
        P(),
        P(None, "expert"),
        P("rep", "group", "expert"),
    )
    out_specs = (P(("rep", "expert", "group"), None), P("rep", "expert"))
    return jax.shard_map(body, mesh=mesh, in_specs=in_specs, out_specs=out_specs, check_vma=False)
```

```python
import functools

import jax
import jax.numpy as jnp
from jax import lax
from jax.experimental import pallas as pl
from jax.experimental.pallas import tpu as pltpu
from jax.sharding import PartitionSpec as P

LOSS_SCALE = 8.0
NORM_EPS = 1e-06
F32 = jnp.float32
BF16 = jnp.bfloat16
LANES = 128
VMEM_LIMIT = 32 * 1024 * 1024


def dot(left, right):
    return jnp.dot(left, right, preferred_element_type=F32)


def dot_t(left, right):
    return lax.dot_general(left, right, (((1,), (1,)), ((), ())), preferred_element_type=F32)


def call(kernel, outs, *args, flops=0):
    args = [pltpu.with_memory_space_constraint(a, pltpu.VMEM) for a in args]
    size = sum(a.size * a.dtype.itemsize for a in args)
    return pl.pallas_call(
        kernel,
        out_shape=[pltpu.VMEM(shape, dtype) for shape, dtype in outs],
        in_specs=[pl.BlockSpec(memory_space=pltpu.VMEM)] * len(args),
        out_specs=[pl.BlockSpec(memory_space=pltpu.VMEM)] * len(outs),
        compiler_params=pltpu.CompilerParams(vmem_limit_bytes=VMEM_LIMIT),
        cost_estimate=pl.CostEstimate(flops=flops, bytes_accessed=size, transcendentals=0),
    )(*args)


def after(value, guards):
    def kernel(*refs):
        pass

    args = [pltpu.with_memory_space_constraint(a, pltpu.VMEM) for a in (value, *guards)]
    return pl.pallas_call(
        kernel,
        out_shape=pltpu.VMEM(value.shape, value.dtype),
        in_specs=[pl.BlockSpec(memory_space=pltpu.VMEM)] * len(args),
        out_specs=pl.BlockSpec(memory_space=pltpu.VMEM),
        input_output_aliases={0: 0},
        compiler_params=pltpu.CompilerParams(vmem_limit_bytes=VMEM_LIMIT),
    )(*args)


class Ring:
    def __init__(self, expert_count, group_count):
        self.count = expert_count
        self.half = expert_count // 2
        self.snake = group_count == 2
        if self.snake:
            self.order = list(range(0, expert_count, 2)) + list(range(expert_count - 1, 0, -2))
        else:
            self.order = list(range(expert_count))

    def send(self, value, distance):
        pairs = [
            (self.order[i], self.order[(i + distance) % self.count]) for i in range(self.count)
        ]
        return lax.ppermute(value, "expert", pairs)

    def device_at(self, distance):
        here = lax.axis_index("expert")
        count = self.count
        if self.snake:
            here = jnp.where(here % 2 == 0, here // 2, count - 1 - here // 2)
        there = lax.rem(here + distance % count, count)
        if self.snake:
            there = jnp.where(there < self.half, 2 * there, 2 * (count - 1 - there) + 1)
        return there

    def gather(self, top, bottom, use, guard=None):
        top_left = top_right = top
        bottom_left = bottom_right = bottom
        use((0,), (top, bottom))
        for step in range(1, self.half):
            if guard is not None and step == self.half - 1:
                bottom_right = after(bottom_right, [guard])
            top_left = self.send(top_left, 1)
            top_right = self.send(top_right, -1)
            bottom_left = self.send(bottom_left, 1)
            bottom_right = self.send(bottom_right, -1)
            use((-step, step), (top_left, bottom_left, top_right, bottom_right))
        use((self.half,), (self.send(top_left, 1), self.send(bottom_right, -1)))

    def scatter(self, parts):
        most = self.half - 1
        top_left = self.send(parts[self.half][0], 1)
        bottom_right = self.send(parts[self.half][1], -1)
        bottom_left = self.send(parts[most][1], 1)
        top_right = self.send(parts[-most][0], -1)
        for step in range(most, 0, -1):
            top_left = self.send(add(parts[step][0], top_left), 1)
            bottom_right = self.send(add(parts[-step][1], bottom_right), -1)
            if step > 1:
                bottom_left = self.send(add(parts[step - 1][1], bottom_left), 1)
                top_right = self.send(add(parts[1 - step][0], top_right), -1)
        return (top_left, top_right), (bottom_left, bottom_right)

    def part_types(self, distances):
        types = []
        for k in distances:
            first = BF16 if k == self.half or k == 1 - self.half else F32
            second = BF16 if k == self.half or k == self.half - 1 else F32
            types += [first, second]
        return types


def add_kernel(block_ref, arrived_ref, out_ref):
    out_ref[...] = (block_ref[...] + arrived_ref[...].astype(F32)).astype(BF16)


def add(block, arrived):
    return call(add_kernel, [(block.shape, BF16)], block, arrived)[0]


def sum_kernel(*refs):
    out_ref = refs[-1]
    rows = refs[0].shape[0]
    for i in range(len(refs) // 3):
        own, left, right = refs[3 * i : 3 * i + 3]
        arrived = left[...].astype(F32) + right[...].astype(F32)
        out_ref[pl.ds(i * rows, rows), :] = (own[...] + arrived).astype(BF16)


class Copies:
    def __init__(self, sems):
        self.sems, self.started = sems, []

    def start(self, source, target):
        copy = pltpu.make_async_copy(source, target, self.sems.at[len(self.started)])
        copy.start()
        self.started.append(copy)

    def wait(self):
        for copy in self.started:
            copy.wait()


def strips(gate_shape, down_shape):
    local_experts, depth, hidden_dim = gate_shape
    _, height, feature_dim = down_shape
    row, places = 0, []
    for _ in range(local_experts):
        pair = [(row, depth), (row + depth, depth)]
        row += 2 * depth
        downs = []
        for begin in range(0, feature_dim, hidden_dim):
            downs.append((row, height, begin, min(hidden_dim, feature_dim - begin)))
            row += height
        places.append((pair, downs))
    return row, places


def pack(ids, scores, tokens, shards):
    rows, cols = tokens.shape
    mid = rows // 2
    quarter = LANES // 4
    inputs = [ids, scores, tokens, *shards]
    packed_shape, places, count = None, [], 0
    if shards:
        hidden_dim = shards[0].shape[2]
        packed_rows, places = strips(shards[0].shape, shards[2].shape)
        packed_shape = (packed_rows, hidden_dim)
        count = sum(len(pair) + len(downs) for pair, downs in places)

    def kernel(*refs):
        ids_hbm, scores_hbm, tokens_hbm, *shards_hbm = refs[: len(inputs)]
        top_ref, bottom_ref, *packed_refs = refs[len(inputs) : -3]
        ids_ref, scores_ref, sems = refs[-3:]
        copies = Copies(sems)
        copies.start(ids_hbm, ids_ref)
        copies.start(scores_hbm, scores_ref)
        copies.start(tokens_hbm.at[pl.ds(0, mid), :], top_ref.at[:, pl.ds(0, cols)])
        copies.start(tokens_hbm.at[pl.ds(mid, mid), :], bottom_ref)
        for local, (pair, downs) in enumerate(places):
            out_ref = packed_refs[0]
            for source, (row, some) in zip(shards_hbm, pair):
                copies.start(source.at[local], out_ref.at[pl.ds(row, some), :])
            for row, some, begin, width in downs:
                source = shards_hbm[2].at[local, :, pl.ds(begin, width)]
                copies.start(source, out_ref.at[pl.ds(row, some), pl.ds(0, width)])
                if width < hidden_dim:
                    rest = hidden_dim - width
                    out_ref[pl.ds(row, some), pl.ds(width, rest)] = jnp.zeros((some, rest), BF16)
        copies.started[0].wait()
        copies.started[1].wait()
        scores = scores_ref[...]
        ids = ids_ref[...]
        route_weight = scores / jnp.sum(scores, axis=0, keepdims=True)
        expert = lax.broadcasted_iota(jnp.int32, (quarter, rows), 0)
        weight_by = jnp.zeros((quarter, rows), F32)
        for choice_k in range(scores.shape[0]):
            one = slice(choice_k, choice_k + 1)
            weight_by = weight_by + jnp.where(ids[one] == expert, route_weight[one], 0.0)
        high = weight_by.astype(BF16).astype(F32)
        weights = jnp.concatenate([high, weight_by - high] * 2, axis=0).T
        lane = lax.broadcasted_iota(jnp.int32, (mid, LANES), 1)
        both = jnp.where(lane < 2 * quarter, weights[:mid], weights[mid:])
        top_ref[:, cols:] = both.astype(BF16)
        for copy in copies.started[2:]:
            copy.wait()

    outs = [pltpu.VMEM((mid, cols + LANES), BF16), pltpu.VMEM((mid, cols), BF16)]
    if shards:
        outs.append(pltpu.VMEM(packed_shape, BF16))
    return pl.pallas_call(
        kernel,
        out_shape=outs,
        in_specs=[pl.BlockSpec(memory_space=pl.ANY)] * len(inputs),
        out_specs=[pl.BlockSpec(memory_space=pltpu.VMEM)] * len(outs),
        scratch_shapes=[
            pltpu.VMEM(ids.shape, ids.dtype),
            pltpu.VMEM(scores.shape, F32),
            pltpu.SemaphoreType.DMA((4 + count,)),
        ],
        compiler_params=pltpu.CompilerParams(vmem_limit_bytes=VMEM_LIMIT),
    )(*[pltpu.with_memory_space_constraint(a, pltpu.HBM) for a in inputs])


def full_weights(shards, packed):
    local_experts, _, hidden_dim = shards[0].shape
    feature_dim = shards[2].shape[2]
    paired = packed is not None
    _, places = strips(shards[0].shape, shards[2].shape)
    depth, height = shards[0].shape[1], shards[2].shape[1]

    def kernel(*refs):
        gate_hbm, up_hbm, down_hbm, *rest = refs
        wide_ref, down_ref, sems = rest[-3:]
        copies = Copies(sems)
        mine = lax.axis_index("group") if paired else 0

        def wide_at(place, local, is_up):
            rows = pl.ds(pl.multiple_of(place * depth, 16), depth)
            return wide_ref.at[rows, pl.ds((2 * local + is_up) * hidden_dim, hidden_dim)]

        def down_at(place, local, begin, cols):
            top = pl.multiple_of(local * hidden_dim + place * height, 16)
            return down_ref.at[pl.ds(top, height), pl.ds(begin, cols)]

        for local in range(local_experts):
            for is_up, source in enumerate((gate_hbm, up_hbm)):
                copies.start(source.at[local], wide_at(mine, local, is_up))
            copies.start(down_hbm.at[local], down_at(mine, local, 0, feature_dim))
        if paired:
            for local, (pair, downs) in enumerate(places):
                for is_up, (row, some) in enumerate(pair):
                    copies.start(rest[0].at[pl.ds(row, some), :], wide_at(1 - mine, local, is_up))
                for row, some, begin, cols in downs:
                    source = rest[0].at[pl.ds(row, some), pl.ds(0, cols)]
                    copies.start(source, down_at(1 - mine, local, begin, cols))
        copies.wait()

    shards = [pltpu.with_memory_space_constraint(w, pltpu.HBM) for w in shards]
    count = 3 * local_experts
    specs = [pl.BlockSpec(memory_space=pl.ANY)] * 3
    if paired:
        count += sum(len(pair) + len(downs) for pair, downs in places)
        specs.append(pl.BlockSpec(memory_space=pltpu.VMEM))
        shards.append(pltpu.with_memory_space_constraint(packed, pltpu.VMEM))
    return pl.pallas_call(
        kernel,
        out_shape=[
            pltpu.VMEM((feature_dim, 2 * local_experts * hidden_dim), BF16),
            pltpu.VMEM((local_experts * hidden_dim, feature_dim), BF16),
        ],
        in_specs=specs,
        out_specs=[pl.BlockSpec(memory_space=pltpu.VMEM)] * 2,
        scratch_shapes=[pltpu.SemaphoreType.DMA((count,))],
        compiler_params=pltpu.CompilerParams(vmem_limit_bytes=VMEM_LIMIT),
    )(*shards)


def transpose_kernel(from_ref, to_ref):
    strip = 2 * LANES

    @pl.loop(0, to_ref.shape[0] // strip)
    def _(i):
        some = pl.ds(pl.multiple_of(i * strip, strip), strip)
        to_ref[some, :] = from_ref[:, some].T


def transposed(weights):
    rows, cols = weights.shape
    return call(transpose_kernel, [((cols, rows), BF16)], weights)[0]


def body(tokens, w_gate, w_up, w_down, route_ids, route_scores, norm_gain, class_head, targets):
    rows_here, feature_dim = tokens.shape
    expert_count = lax.axis_size("expert")
    group_count = lax.axis_size("group")
    local_experts, _, hidden_dim = w_gate.shape
    pair_dim = 2 * hidden_dim
    ring = Ring(expert_count, group_count)
    block = (rows_here, feature_dim)
    mid = rows_here // 2

    shards = [w_gate, w_up, w_down]
    if group_count == 2:
        top, bottom, packed = pack(route_ids.T, route_scores.T, tokens, shards)
        packed = lax.ppermute(packed, "group", [(0, 1), (1, 0)])
    else:
        top, bottom = pack(route_ids.T, route_scores.T, tokens, [])
        shards = [lax.all_gather(w, "group", axis=1, tiled=True) for w in shards]
        packed = None
    wide, down = full_weights(shards, packed)

    def rows_of(refs):
        return jnp.concatenate([ref[...] for ref in refs], axis=0) if len(refs) > 1 else refs[0][...]

    def forward_kernel(count, *refs):
        token_refs, (wide_ref, down_ref) = refs[:count], refs[count : count + 2]
        outs = refs[count + 2 :]
        x = rows_of([ref.at[:, :feature_dim] for ref in token_refs])
        weights = jnp.concatenate([ref[:, feature_dim:] for ref in token_refs[::2]], axis=0).astype(F32)
        lane = lax.broadcasted_iota(jnp.int32, weights.shape, 1)
        quarter = LANES // 4
        hidden = []
        for local in range(local_experts):
            expert = lax.axis_index("expert") * local_experts + local
            scales = []
            for begin in (expert, expert + 2 * quarter):
                here = (lane == begin) | (lane == begin + quarter)
                scales.append(jnp.sum(jnp.where(here, weights, 0.0), axis=1, keepdims=True))
            pieces = [s[i : i + mid] for i in range(0, weights.shape[0], mid) for s in scales]
            scale = jnp.concatenate(pieces, axis=0)
            act = dot(x, wide_ref[:, pl.ds(local * pair_dim, pair_dim)])
            gate_act, up_act = act[:, :hidden_dim], act[:, hidden_dim:]
            sigmoid_gate = 0.5 + 0.5 * jnp.tanh(0.5 * gate_act)
            silu = gate_act * sigmoid_gate * scale
            slope = sigmoid_gate * (1.0 + gate_act * (1.0 - sigmoid_gate)) * scale
            cols = pl.ds(local * hidden_dim, hidden_dim)
            outs[0][:, cols] = (up_act * slope).astype(BF16)
            outs[1][:, cols] = silu.astype(BF16)
            hidden.append((silu * up_act).astype(BF16))
        total = dot(jnp.concatenate(hidden, axis=1), down_ref[...])
        for i, out in enumerate(outs[2:]):
            out[...] = total[i * mid : (i + 1) * mid].astype(out.dtype)

    tokens_at, saved_at, part_at = {}, {}, {}
    flops = 2 * rows_here * feature_dim * hidden_dim * local_experts * 3

    def hold(distances, blocks):
        tokens_at[distances] = blocks

    def keep_parts(parts, distances, halves):
        parts.update({k: halves[2 * i : 2 * i + 2] for i, k in enumerate(distances)})

    def part_outs(distances):
        return [((mid, feature_dim), dtype) for dtype in ring.part_types(distances)]

    def forward(distances):
        blocks = tokens_at[distances]
        rows = mid * len(blocks)
        result = call(
            functools.partial(forward_kernel, len(blocks)),
            [((rows, local_experts * hidden_dim), BF16)] * 2 + part_outs(distances),
            *blocks,
            wide,
            down,
            flops=flops * rows // rows_here,
        )
        saved_at[distances] = result[:2]
        keep_parts(part_at, distances, result[2:])

    ring.gather(top, bottom, hold, wide)
    for distances in tokens_at:
        forward(distances)
    gain = norm_gain.reshape(1, feature_dim)
    half_shape = (mid, feature_dim)
    moe_top, moe_bottom = [
        call(sum_kernel, [(half_shape, BF16)], own, *arrived)[0]
        for own, arrived in zip(part_at[0], ring.scatter(part_at))
    ]

    norm_at, mean_at = {}, {}

    def residual_of(token_refs, moe_refs):
        token_rows = rows_of([ref.at[:, :feature_dim] for ref in token_refs]).astype(F32)
        return token_rows + rows_of(moe_refs).astype(F32)

    def inv_rms_of(residual):
        return lax.rsqrt(jnp.mean(residual * residual, axis=-1, keepdims=True) + NORM_EPS)

    def norm_kernel(distances, count, *refs):
        residual = residual_of(refs[:count], refs[count : 2 * count])
        gain_ref, so_far, out_ref, residual_ref, inv_ref = refs[2 * count :]
        inv_rms = inv_rms_of(residual)
        residual_ref[...] = residual
        inv_ref[...] = jnp.broadcast_to(inv_rms, inv_ref.shape)
        normed = residual * inv_rms * gain_ref[...]
        pooled = so_far[...]
        row = lax.broadcasted_iota(jnp.int32, pooled.shape, 0)
        for i, k in enumerate(distances):
            part = normed[i * rows_here : (i + 1) * rows_here]
            mean = jnp.mean(part, axis=0, keepdims=True)
            pooled = jnp.where(row == ring.device_at(k), mean, pooled)
        out_ref[...] = pooled

    pooled_shape = (expert_count, feature_dim)
    mean_at["pooled"] = jnp.zeros(pooled_shape, F32)

    def norm(distances, blocks):
        rows = mid * len(blocks)
        mean_at["pooled"], *norm_at[distances] = call(
            functools.partial(norm_kernel, distances, len(blocks)),
            [(pooled_shape, F32), ((rows, feature_dim), F32), ((rows, LANES), F32)],
            *tokens_at[distances],
            *blocks,
            gain,
            mean_at["pooled"],
        )

    ring.gather(moe_top, moe_bottom, norm)
    pooled = mean_at["pooled"].astype(BF16)
    logits = dot(pooled, class_head)
    target_rows = targets.reshape(expert_count, -1).astype(F32)
    logit_grad = (LOSS_SCALE * (jax.nn.sigmoid(logits) - target_rows)).astype(BF16)
    pooled_grad = dot_t(logit_grad, class_head)
    span = 2
    for masks in ([1], list(range(span, expert_count, span))):
        mine = pooled_grad.astype(BF16)
        pooled_grad = mine.astype(F32)
        for mask in masks:
            pairs = [(e, e ^ mask) for e in range(expert_count)]
            pooled_grad = pooled_grad + lax.ppermute(mine, "expert", pairs).astype(F32)

    both = jnp.concatenate([pooled, logit_grad], axis=1)
    if group_count == 2:
        both = jnp.concatenate([both, lax.ppermute(both, "group", [(0, 1), (1, 0)])], axis=0)
    else:
        both = lax.all_gather(both, "group", axis=0, tiled=True)
    head_grad = lax.dot_general(
        both[:, :feature_dim],
        both[:, feature_dim:],
        (((0,), (0,)), ((), ())),
        preferred_element_type=F32,
    )

    def backward_kernel(distances, residual_ref, inv_ref, gate_save, up_save, *refs):
        grad_ref, gain_ref, wide_ref, down_ref, *outs = refs
        residual, inv_rms = residual_ref[...], inv_ref[:, :1]
        cube = inv_rms * inv_rms * inv_rms
        parts = []
        for i, k in enumerate(distances):
            rows = slice(i * rows_here, (i + 1) * rows_here)
            scaled = gain_ref[...] * grad_ref[pl.ds(ring.device_at(k), 1), :] / rows_here
            slope = cube[rows] * jnp.mean(residual[rows] * scaled, axis=-1, keepdims=True)
            parts.append(inv_rms[rows] * scaled - residual[rows] * slope)
        resid_grad = jnp.concatenate(parts, axis=0) if len(parts) > 1 else parts[0]
        down_back = dot(resid_grad.astype(BF16), down_ref[...])
        grads = []
        for local in range(local_experts):
            cols = slice(local * hidden_dim, (local + 1) * hidden_dim)
            for save in (gate_save, up_save):
                grads.append((down_back[:, cols] * save[:, cols].astype(F32)).astype(BF16))
        total = dot(jnp.concatenate(grads, axis=1), wide_ref[...])
        if distances == (0,):
            total = total + resid_grad
        rows = total.shape[0] // len(outs)
        for i, out in enumerate(outs):
            out[...] = total[i * rows : (i + 1) * rows].astype(out.dtype)

    wide_t, down_t = transposed(wide), transposed(down)
    back_at = {}

    def backward(distances):
        result = call(
            functools.partial(backward_kernel, distances),
            part_outs(distances),
            *norm_at[distances],
            *saved_at[distances],
            pooled_grad,
            gain,
            wide_t,
            down_t,
            flops=flops * len(distances),
        )
        keep_parts(back_at, distances, result)

    for distances in reversed(list(tokens_at)):
        backward(distances)
    (top_left, top_right), (bottom_left, bottom_right) = ring.scatter(back_at)
    token_grad = pl.pallas_call(
        sum_kernel,
        out_shape=jax.ShapeDtypeStruct(block, BF16),
        in_specs=[pl.BlockSpec(memory_space=pltpu.VMEM)] * 6,
        out_specs=pl.BlockSpec(memory_space=pltpu.VMEM),
        compiler_params=pltpu.CompilerParams(vmem_limit_bytes=VMEM_LIMIT),
    )(back_at[0][0], top_left, top_right, back_at[0][1], bottom_left, bottom_right)
    return (token_grad, head_grad)


def solution(mesh):
    in_specs = (
        P(("rep", "expert", "group"), None),
        P("expert", "group", None),
        P("expert", "group", None),
        P("expert", "group", None),
        P(("rep", "expert", "group"), None),
        P(("rep", "expert", "group"), None),
        P(),
        P(None, "expert"),
        P("rep", "group", "expert"),
    )
    out_specs = (P(("rep", "expert", "group"), None), P("rep", "expert"))
    return jax.shard_map(body, mesh=mesh, in_specs=in_specs, out_specs=out_specs, check_vma=False)
```

```python
import functools

import jax
import jax.numpy as jnp
from jax import lax
from jax.experimental import pallas as pl
from jax.experimental.pallas import tpu as pltpu
from jax.sharding import PartitionSpec as P

LOSS_SCALE = 8.0
NORM_EPS = 1e-06
F32 = jnp.float32
BF16 = jnp.bfloat16
LANES = 128
VMEM_LIMIT = 32 * 1024 * 1024


def dot(left, right):
    return jnp.dot(left, right, preferred_element_type=F32)


def dot_t(left, right):
    return lax.dot_general(left, right, (((1,), (1,)), ((), ())), preferred_element_type=F32)


def call(kernel, outs, *args, flops=0):
    args = [pltpu.with_memory_space_constraint(a, pltpu.VMEM) for a in args]
    size = sum(a.size * a.dtype.itemsize for a in args)
    return pl.pallas_call(
        kernel,
        out_shape=[pltpu.VMEM(shape, dtype) for shape, dtype in outs],
        in_specs=[pl.BlockSpec(memory_space=pltpu.VMEM)] * len(args),
        out_specs=[pl.BlockSpec(memory_space=pltpu.VMEM)] * len(outs),
        compiler_params=pltpu.CompilerParams(vmem_limit_bytes=VMEM_LIMIT),
        cost_estimate=pl.CostEstimate(flops=flops, bytes_accessed=size, transcendentals=0),
    )(*args)


def after(value, guards):
    def kernel(*refs):
        pass

    args = [pltpu.with_memory_space_constraint(a, pltpu.VMEM) for a in (value, *guards)]
    return pl.pallas_call(
        kernel,
        out_shape=pltpu.VMEM(value.shape, value.dtype),
        in_specs=[pl.BlockSpec(memory_space=pltpu.VMEM)] * len(args),
        out_specs=pl.BlockSpec(memory_space=pltpu.VMEM),
        input_output_aliases={0: 0},
        compiler_params=pltpu.CompilerParams(vmem_limit_bytes=VMEM_LIMIT),
    )(*args)


class Ring:
    def __init__(self, expert_count, group_count):
        self.count = expert_count
        self.half = expert_count // 2
        self.snake = group_count == 2
        if self.snake:
            self.order = list(range(0, expert_count, 2)) + list(range(expert_count - 1, 0, -2))
        else:
            self.order = list(range(expert_count))

    def send(self, value, distance):
        pairs = [
            (self.order[i], self.order[(i + distance) % self.count]) for i in range(self.count)
        ]
        return lax.ppermute(value, "expert", pairs)

    def device_at(self, distance):
        here = lax.axis_index("expert")
        count = self.count
        if self.snake:
            here = jnp.where(here % 2 == 0, here // 2, count - 1 - here // 2)
        there = lax.rem(here + distance % count, count)
        if self.snake:
            there = jnp.where(there < self.half, 2 * there, 2 * (count - 1 - there) + 1)
        return there

    def gather(self, top, bottom, use, guard=None):
        top_left = top_right = top
        bottom_left = bottom_right = bottom
        use((0,), (top, bottom))
        for step in range(1, self.half):
            if guard is not None and step == self.half - 1:
                top_right = after(top_right, [guard])
            top_left = self.send(top_left, 1)
            top_right = self.send(top_right, -1)
            bottom_left = self.send(bottom_left, 1)
            bottom_right = self.send(bottom_right, -1)
            use((-step, step), (top_left, bottom_left, top_right, bottom_right))
        use((self.half,), (self.send(top_left, 1), self.send(bottom_right, -1)))

    def scatter(self, parts):
        most = self.half - 1
        top_left = self.send(parts[self.half][0], 1)
        bottom_right = self.send(parts[self.half][1], -1)
        bottom_left = self.send(parts[most][1], 1)
        top_right = self.send(parts[-most][0], -1)
        for step in range(most, 0, -1):
            top_left = self.send(add(parts[step][0], top_left), 1)
            bottom_right = self.send(add(parts[-step][1], bottom_right), -1)
            if step > 1:
                bottom_left = self.send(add(parts[step - 1][1], bottom_left), 1)
                top_right = self.send(add(parts[1 - step][0], top_right), -1)
        return (top_left, top_right), (bottom_left, bottom_right)

    def part_types(self, distances):
        types = []
        for k in distances:
            first = BF16 if k == self.half or k == 1 - self.half else F32
            second = BF16 if k == self.half or k == self.half - 1 else F32
            types += [first, second]
        return types


def add_kernel(block_ref, arrived_ref, out_ref):
    out_ref[...] = (block_ref[...] + arrived_ref[...].astype(F32)).astype(BF16)


def add(block, arrived):
    return call(add_kernel, [(block.shape, BF16)], block, arrived)[0]


def sum_kernel(*refs):
    out_ref = refs[-1]
    rows = refs[0].shape[0]
    for i in range(len(refs) // 3):
        own, left, right = refs[3 * i : 3 * i + 3]
        arrived = left[...].astype(F32) + right[...].astype(F32)
        out_ref[pl.ds(i * rows, rows), :] = (own[...] + arrived).astype(BF16)


class Copies:
    def __init__(self, sems):
        self.sems, self.started = sems, []

    def start(self, source, target):
        copy = pltpu.make_async_copy(source, target, self.sems.at[len(self.started)])
        copy.start()
        self.started.append(copy)

    def wait(self):
        for copy in self.started:
            copy.wait()


def strips(gate_shape, down_shape):
    local_experts, depth, hidden_dim = gate_shape
    _, height, feature_dim = down_shape
    row, places = 0, []
    for _ in range(local_experts):
        pair = [(row, depth), (row + depth, depth)]
        row += 2 * depth
        downs = []
        for begin in range(0, feature_dim, hidden_dim):
            downs.append((row, height, begin, min(hidden_dim, feature_dim - begin)))
            row += height
        places.append((pair, downs))
    return row, places


def pack(ids, scores, tokens, shards):
    rows, cols = tokens.shape
    mid = rows // 2
    quarter = LANES // 4
    inputs = [ids, scores, tokens, *shards]
    packed_shape, places, count = None, [], 0
    if shards:
        hidden_dim = shards[0].shape[2]
        packed_rows, places = strips(shards[0].shape, shards[2].shape)
        packed_shape = (packed_rows, hidden_dim)
        count = sum(len(pair) + len(downs) for pair, downs in places)

    def kernel(*refs):
        ids_hbm, scores_hbm, tokens_hbm, *shards_hbm = refs[: len(inputs)]
        top_ref, bottom_ref, *packed_refs = refs[len(inputs) : -3]
        ids_ref, scores_ref, sems = refs[-3:]
        copies = Copies(sems)
        copies.start(ids_hbm, ids_ref)
        copies.start(scores_hbm, scores_ref)
        copies.start(tokens_hbm.at[pl.ds(0, mid), :], top_ref.at[:, pl.ds(0, cols)])
        copies.start(tokens_hbm.at[pl.ds(mid, mid), :], bottom_ref)
        for local, (pair, downs) in enumerate(places):
            out_ref = packed_refs[0]
            for source, (row, some) in zip(shards_hbm, pair):
                copies.start(source.at[local], out_ref.at[pl.ds(row, some), :])
            for row, some, begin, width in downs:
                source = shards_hbm[2].at[local, :, pl.ds(begin, width)]
                copies.start(source, out_ref.at[pl.ds(row, some), pl.ds(0, width)])
                if width < hidden_dim:
                    rest = hidden_dim - width
                    out_ref[pl.ds(row, some), pl.ds(width, rest)] = jnp.zeros((some, rest), BF16)
        copies.started[0].wait()
        copies.started[1].wait()
        scores = scores_ref[...]
        ids = ids_ref[...]
        route_weight = scores / jnp.sum(scores, axis=0, keepdims=True)
        expert = lax.broadcasted_iota(jnp.int32, (quarter, rows), 0)
        weight_by = jnp.zeros((quarter, rows), F32)
        for choice_k in range(scores.shape[0]):
            one = slice(choice_k, choice_k + 1)
            weight_by = weight_by + jnp.where(ids[one] == expert, route_weight[one], 0.0)
        high = weight_by.astype(BF16).astype(F32)
        weights = jnp.concatenate([high, weight_by - high] * 2, axis=0).T
        lane = lax.broadcasted_iota(jnp.int32, (mid, LANES), 1)
        both = jnp.where(lane < 2 * quarter, weights[:mid], weights[mid:])
        top_ref[:, cols:] = both.astype(BF16)
        for copy in copies.started[2:]:
            copy.wait()

    outs = [pltpu.VMEM((mid, cols + LANES), BF16), pltpu.VMEM((mid, cols), BF16)]
    if shards:
        outs.append(pltpu.VMEM(packed_shape, BF16))
    return pl.pallas_call(
        kernel,
        out_shape=outs,
        in_specs=[pl.BlockSpec(memory_space=pl.ANY)] * len(inputs),
        out_specs=[pl.BlockSpec(memory_space=pltpu.VMEM)] * len(outs),
        scratch_shapes=[
            pltpu.VMEM(ids.shape, ids.dtype),
            pltpu.VMEM(scores.shape, F32),
            pltpu.SemaphoreType.DMA((4 + count,)),
        ],
        compiler_params=pltpu.CompilerParams(vmem_limit_bytes=VMEM_LIMIT),
    )(*[pltpu.with_memory_space_constraint(a, pltpu.HBM) for a in inputs])


def full_weights(shards, packed):
    local_experts, _, hidden_dim = shards[0].shape
    feature_dim = shards[2].shape[2]
    paired = packed is not None
    _, places = strips(shards[0].shape, shards[2].shape)
    depth, height = shards[0].shape[1], shards[2].shape[1]

    def kernel(*refs):
        gate_hbm, up_hbm, down_hbm, *rest = refs
        wide_ref, down_ref, sems = rest[-3:]
        copies = Copies(sems)
        mine = lax.axis_index("group") if paired else 0

        def wide_at(place, local, is_up):
            rows = pl.ds(pl.multiple_of(place * depth, 16), depth)
            return wide_ref.at[rows, pl.ds((2 * local + is_up) * hidden_dim, hidden_dim)]

        def down_at(place, local, begin, cols):
            top = pl.multiple_of(local * hidden_dim + place * height, 16)
            return down_ref.at[pl.ds(top, height), pl.ds(begin, cols)]

        for local in range(local_experts):
            for is_up, source in enumerate((gate_hbm, up_hbm)):
                copies.start(source.at[local], wide_at(mine, local, is_up))
            copies.start(down_hbm.at[local], down_at(mine, local, 0, feature_dim))
        if paired:
            for local, (pair, downs) in enumerate(places):
                for is_up, (row, some) in enumerate(pair):
                    copies.start(rest[0].at[pl.ds(row, some), :], wide_at(1 - mine, local, is_up))
                for row, some, begin, cols in downs:
                    source = rest[0].at[pl.ds(row, some), pl.ds(0, cols)]
                    copies.start(source, down_at(1 - mine, local, begin, cols))
        copies.wait()

    shards = [pltpu.with_memory_space_constraint(w, pltpu.HBM) for w in shards]
    count = 3 * local_experts
    specs = [pl.BlockSpec(memory_space=pl.ANY)] * 3
    if paired:
        count += sum(len(pair) + len(downs) for pair, downs in places)
        specs.append(pl.BlockSpec(memory_space=pltpu.VMEM))
        shards.append(pltpu.with_memory_space_constraint(packed, pltpu.VMEM))
    return pl.pallas_call(
        kernel,
        out_shape=[
            pltpu.VMEM((feature_dim, 2 * local_experts * hidden_dim), BF16),
            pltpu.VMEM((local_experts * hidden_dim, feature_dim), BF16),
        ],
        in_specs=specs,
        out_specs=[pl.BlockSpec(memory_space=pltpu.VMEM)] * 2,
        scratch_shapes=[pltpu.SemaphoreType.DMA((count,))],
        compiler_params=pltpu.CompilerParams(vmem_limit_bytes=VMEM_LIMIT),
    )(*shards)


def transpose_kernel(from_ref, to_ref):
    strip = 2 * LANES

    @pl.loop(0, to_ref.shape[0] // strip)
    def _(i):
        some = pl.ds(pl.multiple_of(i * strip, strip), strip)
        to_ref[some, :] = from_ref[:, some].T


def transposed(weights):
    rows, cols = weights.shape
    return call(transpose_kernel, [((cols, rows), BF16)], weights)[0]


def body(tokens, w_gate, w_up, w_down, route_ids, route_scores, norm_gain, class_head, targets):
    rows_here, feature_dim = tokens.shape
    expert_count = lax.axis_size("expert")
    group_count = lax.axis_size("group")
    local_experts, _, hidden_dim = w_gate.shape
    pair_dim = 2 * hidden_dim
    ring = Ring(expert_count, group_count)
    block = (rows_here, feature_dim)
    mid = rows_here // 2

    shards = [w_gate, w_up, w_down]
    if group_count == 2:
        top, bottom, packed = pack(route_ids.T, route_scores.T, tokens, shards)
        packed = lax.ppermute(packed, "group", [(0, 1), (1, 0)])
    else:
        top, bottom = pack(route_ids.T, route_scores.T, tokens, [])
        shards = [lax.all_gather(w, "group", axis=1, tiled=True) for w in shards]
        packed = None
    wide, down = full_weights(shards, packed)

    def rows_of(refs):
        return jnp.concatenate([ref[...] for ref in refs], axis=0) if len(refs) > 1 else refs[0][...]

    def forward_kernel(count, *refs):
        token_refs, (wide_ref, down_ref) = refs[:count], refs[count : count + 2]
        outs = refs[count + 2 :]
        x = rows_of([ref.at[:, :feature_dim] for ref in token_refs])
        weights = jnp.concatenate([ref[:, feature_dim:] for ref in token_refs[::2]], axis=0).astype(F32)
        lane = lax.broadcasted_iota(jnp.int32, weights.shape, 1)
        quarter = LANES // 4
        hidden = []
        for local in range(local_experts):
            expert = lax.axis_index("expert") * local_experts + local
            scales = []
            for begin in (expert, expert + 2 * quarter):
                here = (lane == begin) | (lane == begin + quarter)
                scales.append(jnp.sum(jnp.where(here, weights, 0.0), axis=1, keepdims=True))
            pieces = [s[i : i + mid] for i in range(0, weights.shape[0], mid) for s in scales]
            scale = jnp.concatenate(pieces, axis=0)
            act = dot(x, wide_ref[:, pl.ds(local * pair_dim, pair_dim)])
            gate_act, up_act = act[:, :hidden_dim], act[:, hidden_dim:]
            sigmoid_gate = jax.nn.sigmoid(gate_act)
            silu = gate_act * sigmoid_gate * scale
            slope = sigmoid_gate * (1.0 + gate_act * (1.0 - sigmoid_gate)) * scale
            cols = pl.ds(local * hidden_dim, hidden_dim)
            outs[0][:, cols] = (up_act * slope).astype(BF16)
            outs[1][:, cols] = silu.astype(BF16)
            hidden.append((silu * up_act).astype(BF16))
        total = dot(jnp.concatenate(hidden, axis=1), down_ref[...])
        for i, out in enumerate(outs[2:]):
            out[...] = total[i * mid : (i + 1) * mid].astype(out.dtype)

    tokens_at, saved_at, part_at = {}, {}, {}
    flops = 2 * rows_here * feature_dim * hidden_dim * local_experts * 3

    def hold(distances, blocks):
        tokens_at[distances] = blocks

    def keep_parts(parts, distances, halves):
        parts.update({k: halves[2 * i : 2 * i + 2] for i, k in enumerate(distances)})

    def part_outs(distances):
        return [((mid, feature_dim), dtype) for dtype in ring.part_types(distances)]

    def forward(distances):
        blocks = tokens_at[distances]
        rows = mid * len(blocks)
        result = call(
            functools.partial(forward_kernel, len(blocks)),
            [((rows, local_experts * hidden_dim), BF16)] * 2 + part_outs(distances),
            *blocks,
            wide,
            down,
            flops=flops * rows // rows_here,
        )
        saved_at[distances] = result[:2]
        keep_parts(part_at, distances, result[2:])

    ring.gather(top, bottom, hold, wide)
    for distances in tokens_at:
        forward(distances)
    gain = norm_gain.reshape(1, feature_dim)
    half_shape = (mid, feature_dim)
    moe_top, moe_bottom = [
        call(sum_kernel, [(half_shape, BF16)], own, *arrived)[0]
        for own, arrived in zip(part_at[0], ring.scatter(part_at))
    ]

    norm_at, mean_at = {}, {}

    def residual_of(token_refs, moe_refs):
        token_rows = rows_of([ref.at[:, :feature_dim] for ref in token_refs]).astype(F32)
        return token_rows + rows_of(moe_refs).astype(F32)

    def inv_rms_of(residual):
        return lax.rsqrt(jnp.mean(residual * residual, axis=-1, keepdims=True) + NORM_EPS)

    def norm_kernel(distances, count, *refs):
        residual = residual_of(refs[:count], refs[count : 2 * count])
        gain_ref, so_far, out_ref, residual_ref, inv_ref = refs[2 * count :]
        inv_rms = inv_rms_of(residual)
        residual_ref[...] = residual
        inv_ref[...] = jnp.broadcast_to(inv_rms, inv_ref.shape)
        normed = residual * inv_rms * gain_ref[...]
        pooled = so_far[...]
        row = lax.broadcasted_iota(jnp.int32, pooled.shape, 0)
        for i, k in enumerate(distances):
            part = normed[i * rows_here : (i + 1) * rows_here]
            mean = jnp.mean(part, axis=0, keepdims=True)
            pooled = jnp.where(row == ring.device_at(k), mean, pooled)
        out_ref[...] = pooled

    pooled_shape = (expert_count, feature_dim)
    mean_at["pooled"] = jnp.zeros(pooled_shape, F32)

    def norm(distances, blocks):
        rows = mid * len(blocks)
        mean_at["pooled"], *norm_at[distances] = call(
            functools.partial(norm_kernel, distances, len(blocks)),
            [(pooled_shape, F32), ((rows, feature_dim), F32), ((rows, LANES), F32)],
            *tokens_at[distances],
            *blocks,
            gain,
            mean_at["pooled"],
        )

    ring.gather(moe_top, moe_bottom, norm)
    pooled = mean_at["pooled"].astype(BF16)
    logits = dot(pooled, class_head)
    target_rows = targets.reshape(expert_count, -1).astype(F32)
    logit_grad = (LOSS_SCALE * (jax.nn.sigmoid(logits) - target_rows)).astype(BF16)
    pooled_grad = dot_t(logit_grad, class_head)
    span = 2
    for masks in ([1], list(range(span, expert_count, span))):
        mine = pooled_grad.astype(BF16)
        pooled_grad = mine.astype(F32)
        for mask in masks:
            pairs = [(e, e ^ mask) for e in range(expert_count)]
            pooled_grad = pooled_grad + lax.ppermute(mine, "expert", pairs).astype(F32)

    both = jnp.concatenate([pooled, logit_grad], axis=1)
    if group_count == 2:
        both = jnp.concatenate([both, lax.ppermute(both, "group", [(0, 1), (1, 0)])], axis=0)
    else:
        both = lax.all_gather(both, "group", axis=0, tiled=True)
    head_grad = lax.dot_general(
        both[:, :feature_dim],
        both[:, feature_dim:],
        (((0,), (0,)), ((), ())),
        preferred_element_type=F32,
    )

    def backward_kernel(distances, residual_ref, inv_ref, gate_save, up_save, *refs):
        grad_ref, gain_ref, wide_ref, down_ref, *outs = refs
        residual, inv_rms = residual_ref[...], inv_ref[:, :1]
        cube = inv_rms * inv_rms * inv_rms
        parts = []
        for i, k in enumerate(distances):
            rows = slice(i * rows_here, (i + 1) * rows_here)
            scaled = gain_ref[...] * grad_ref[pl.ds(ring.device_at(k), 1), :] / rows_here
            slope = cube[rows] * jnp.mean(residual[rows] * scaled, axis=-1, keepdims=True)
            parts.append(inv_rms[rows] * scaled - residual[rows] * slope)
        resid_grad = jnp.concatenate(parts, axis=0) if len(parts) > 1 else parts[0]
        down_back = dot(resid_grad.astype(BF16), down_ref[...])
        grads = []
        for local in range(local_experts):
            cols = slice(local * hidden_dim, (local + 1) * hidden_dim)
            for save in (gate_save, up_save):
                grads.append((down_back[:, cols] * save[:, cols].astype(F32)).astype(BF16))
        total = dot(jnp.concatenate(grads, axis=1), wide_ref[...])
        if distances == (0,):
            total = total + resid_grad
        rows = total.shape[0] // len(outs)
        for i, out in enumerate(outs):
            out[...] = total[i * rows : (i + 1) * rows].astype(out.dtype)

    wide_t, down_t = transposed(wide), transposed(down)
    back_at = {}

    def backward(distances):
        result = call(
            functools.partial(backward_kernel, distances),
            part_outs(distances),
            *norm_at[distances],
            *saved_at[distances],
            pooled_grad,
            gain,
            wide_t,
            down_t,
            flops=flops * len(distances),
        )
        keep_parts(back_at, distances, result)

    for distances in reversed(list(tokens_at)):
        backward(distances)
    (top_left, top_right), (bottom_left, bottom_right) = ring.scatter(back_at)

    def last_kernel(*refs):
        out_hbm, rows_ref, sems = refs[-3:]
        copies = Copies(sems)
        for i in range(2):
            own, left, right = refs[3 * i : 3 * i + 3]
            some = pl.ds(i * mid, mid)
            arrived = left[...].astype(F32) + right[...].astype(F32)
            rows_ref[some, :] = (own[...] + arrived).astype(BF16)
            copies.start(rows_ref.at[some, :], out_hbm.at[some, :])
        copies.wait()

    token_grad = pl.pallas_call(
        last_kernel,
        out_shape=jax.ShapeDtypeStruct(block, BF16),
        in_specs=[pl.BlockSpec(memory_space=pltpu.VMEM)] * 6,
        out_specs=pl.BlockSpec(memory_space=pl.ANY),
        scratch_shapes=[pltpu.VMEM(block, BF16), pltpu.SemaphoreType.DMA((2,))],
        compiler_params=pltpu.CompilerParams(vmem_limit_bytes=VMEM_LIMIT),
    )(back_at[0][0], top_left, top_right, back_at[0][1], bottom_left, bottom_right)
    return (token_grad, head_grad)


def solution(mesh):
    in_specs = (
        P(("rep", "expert", "group"), None),
        P("expert", "group", None),
        P("expert", "group", None),
        P("expert", "group", None),
        P(("rep", "expert", "group"), None),
        P(("rep", "expert", "group"), None),
        P(),
        P(None, "expert"),
        P("rep", "group", "expert"),
    )
    out_specs = (P(("rep", "expert", "group"), None), P("rep", "expert"))
    return jax.shard_map(body, mesh=mesh, in_specs=in_specs, out_specs=out_specs, check_vma=False)
```
